32 devices in a mesh: dp: 16 (over z, y, x), seq: 2 (over core).
Axes of the slice: x: 2, y: 2, z: 4, core: 2. Of those that a mesh axis runs over, the one named last changes fastest.
Arguments:
- patches: bfloat16 [64, 324, 512], P('dp', 'seq'), may hold values from -6 to 6
- resolution: int32 [64], P('dp'), may hold values from 0 to 2, as said below
- out_grad: bfloat16 [64, 324, 512], P('dp', 'seq'), may hold values from -6 to 6
- dense_in: float32 [512, 3072], P(('dp', 'seq')), may hold values from -0.25 to 0.25
- dense_out: float32 [1536, 512], P(('dp', 'seq')), may hold values from -0.15625 to 0.15625
- vectors: float32 [7680], P(('dp', 'seq')), may hold values from -1 to 2, as said below
- spatial: float32 [3, 324, 324], P(None, 'seq'), may hold values from -0.3125 to 0.3125
- spatial_bias: float32 [3, 324], P(None, 'seq'), may hold values from 0.5 to 1.5
- in_first: float32 [512, 3072], P(('dp', 'seq')), may hold values from -24 to 24
- in_second: float32 [512, 3072], P(('dp', 'seq')), may hold values from 11.904 to 47.616
- out_first: float32 [1536, 512], P(('dp', 'seq')), may hold values from -56 to 56
- out_second: float32 [1536, 512], P(('dp', 'seq')), may hold values from 67.456 to 265.856
- vec_first: float32 [7680], P(('dp', 'seq')), may hold values from -40 to 40
- vec_second: float32 [7680], P(('dp', 'seq')), may hold values from 32.9344 to 130.944
- spat_first: float32 [3, 324, 324], P(None, 'seq'), may hold values from -40 to 40
- spat_second: float32 [3, 324, 324], P(None, 'seq'), may hold values from 39.3216 to 157.2864
- bias_first: float32 [3, 324], P(None, 'seq'), may hold values from -40 to 40
- bias_second: float32 [3, 324], P(None, 'seq'), may hold values from 39.3216 to 157.2864
Outputs:
- mixed: bfloat16 [64, 324, 512], P('dp', 'seq')
- patches_grad: bfloat16 [64, 324, 512], P('dp', 'seq')
- next_dense_in: float32 [512, 3072], P(('dp', 'seq'))
- next_in_first: float32 [512, 3072], P(('dp', 'seq'))
- next_in_second: float32 [512, 3072], P(('dp', 'seq'))
- next_dense_out: float32 [1536, 512], P(('dp', 'seq'))
- next_out_first: float32 [1536, 512], P(('dp', 'seq'))
- next_out_second: float32 [1536, 512], P(('dp', 'seq'))
- next_vectors: float32 [7680], P(('dp', 'seq'))
- next_vec_first: float32 [7680], P(('dp', 'seq'))
- next_vec_second: float32 [7680], P(('dp', 'seq'))
- next_spatial: float32 [3, 324, 324], P(None, 'seq')
- next_spat_first: float32 [3, 324, 324], P(None, 'seq')
- next_spat_second: float32 [3, 324, 324], P(None, 'seq')
- next_spatial_bias: float32 [3, 324], P(None, 'seq')
- next_bias_first: float32 [3, 324], P(None, 'seq')
- next_bias_second: float32 [3, 324], P(None, 'seq')
The draws below stay inside these ranges and needn't reach their ends.
Inputs may be any that keep to these rules, and one draw needn't show every extreme that they name: `resolution`: 0, 1, 2 name images of 100, 196 and 324 patches; among the 4 images of each index of dp at least one has index 2. `vectors`: gains and biases, gains near one.
All inputs are finite; a program needn't handle non-finite values.
Results may differ from the reference program's by a relative error of at most 0.012.
Values may be sent and summed in bfloat16 or wider, within the bound.
No kernel may reach another device: no remote copies, remote signals or barrier semaphores. Data moves between devices by JAX's collectives and lax.ppermute only.
A program may use at most 128 MiB of HBM per device.

```python
import jax
import jax.numpy as jnp
from jax import lax

D = 512
FF = 3072
HALF = 1536
VEC = 7680
PMAX = 324
P_MID = 196
P_LOW = 100
IMG_MB = 2
STEP = 10
IMG_DEV = 4
IMAGES = 64


def draw_resolution(key, part):
    key = jax.random.fold_in(key, 11)
    first_key, second_key = jax.random.split(key)
    values = jax.random.randint(first_key, (IMAGES,), 0, 3)
    owners = IMAGES // IMG_DEV
    spots = jax.random.randint(second_key, (owners,), 0, IMG_DEV)
    places = jnp.arange(owners) * IMG_DEV + spots
    return values.at[places].set(2).astype(jnp.int32)


def draw_vectors(key, part):
    key = jax.random.fold_in(key, 23)
    noise = jnp.clip(jax.random.normal(key, (VEC,), jnp.float32), -3.0, 3.0)
    spot = jnp.arange(VEC)
    is_gain = (spot < D) | (spot >= 2 * D + FF) & (spot < 2 * D + FF + HALF)
    return jnp.where(is_gain, 1.0 + 0.25 * noise, 0.3 * noise).astype(jnp.float32)


def block_levels(key, shape, shards, least, largest):
    def one(position, parts):
        heights = jax.random.uniform(jax.random.fold_in(jax.random.fold_in(key, 6), position), (parts,), jnp.float32, least / len(shards), largest / len(shards))
        return jnp.repeat(jnp.exp(heights), shape[position] // parts).reshape((-1,) + (1,) * (len(shape) - position - 1))

    loudness = one(*shards[0])
    for cut in shards[1:]:
        loudness = loudness * one(*cut)
    return loudness


def bell_draw(rng, dims, scale, reach, cuts=(), dtype=jnp.bfloat16):
    values = jax.random.normal(rng, dims, jnp.float32) * scale
    if len(cuts) > 0:
        values = block_levels(rng, dims, cuts, -0.22, 0.18) * values
    return jnp.clip(values, min=-reach, max=reach).astype(dtype)


def setup_inputs(seed: int = 0) -> dict:
    key_list = jax.random.split(jax.random.key(seed), 19)
    return {
        "patches": bell_draw(key_list[0], (IMAGES, PMAX, D), 1.0, 6.0, ((0, 16), (1, 2))),
        "resolution": draw_resolution(jax.random.fold_in(key_list[18], 71), 0),
        "out_grad": bell_draw(key_list[2], (IMAGES, PMAX, D), 1.0, 6.0, ((0, 16), (1, 2))),
        "dense_in": bell_draw(key_list[3], (D, FF), D ** -0.5, 0.25, ((0, 32),), jnp.float32),
        "dense_out": bell_draw(key_list[4], (HALF, D), HALF ** -0.5, 0.15625, ((0, 32),), jnp.float32),
        "vectors": draw_vectors(jax.random.fold_in(key_list[18], 71), 0),
        "spatial": bell_draw(key_list[6], (3, PMAX, PMAX), PMAX ** -0.5, 0.3125, ((1, 2),), jnp.float32),
        "spatial_bias": jnp.clip(1.0 + 0.1 * jax.random.normal(key_list[7], (3, PMAX), jnp.float32), 0.5, 1.5),
        "in_first": bell_draw(key_list[8], (D, FF), (0.019 * (IMAGES * (P_LOW + P_MID + PMAX)) ** 0.5), 24.0, ((0, 32),), jnp.float32),
        "in_second": jnp.clip(11.904 + 35.712 * jax.random.uniform(key_list[9], (D, FF), jnp.float32) ** block_levels(key_list[9], (D, FF), ((0, 32),), -0.2, 0.2), 11.904, 47.616),
        "out_first": bell_draw(key_list[10], (HALF, D), (0.044 * (IMAGES * (P_LOW + P_MID + PMAX)) ** 0.5), 56.0, ((0, 32),), jnp.float32),
        "out_second": jnp.clip(67.456 + 198.4 * jax.random.uniform(key_list[11], (HALF, D), jnp.float32) ** block_levels(key_list[11], (HALF, D), ((0, 32),), -0.2, 0.2), 67.456, 265.856),
        "vec_first": bell_draw(key_list[12], (VEC,), (0.032 * (IMAGES * (P_LOW + P_MID + PMAX)) ** 0.5), 40.0, ((0, 32),), jnp.float32),
        "vec_second": jnp.clip(32.9344 + 98.0096 * jax.random.uniform(key_list[13], (VEC,), jnp.float32) ** block_levels(key_list[13], (VEC,), ((0, 32),), -0.2, 0.2), 32.9344, 130.944),
        "spat_first": bell_draw(key_list[14], (3, PMAX, PMAX), (0.0222 * (HALF * IMAGES) ** 0.5), 40.0, ((1, 2),), jnp.float32),
        "spat_second": jnp.clip(39.3216 + 117.964806 * jax.random.uniform(key_list[15], (3, PMAX, PMAX), jnp.float32) ** block_levels(key_list[15], (3, PMAX, PMAX), ((1, 2),), -0.2, 0.2), 39.3216, 157.2864),
        "bias_first": bell_draw(key_list[16], (3, PMAX), (0.0222 * (HALF * IMAGES) ** 0.5), 40.0, ((1, 2),), jnp.float32),
        "bias_second": jnp.clip(39.3216 + 117.964806 * jax.random.uniform(key_list[17], (3, PMAX), jnp.float32) ** block_levels(key_list[17], (3, PMAX), ((1, 2),), -0.2, 0.2), 39.3216, 157.2864),
    }


NORM_EPS = 1e-05
BETA_ONE = 0.9
BETA_TWO = 0.99
ADAM_EPS = 1e-08
DENSE_RATE = 0.02
SMALL_RATE = 0.2
DENSE_DECAY = 0.05
HIGHEST = lax.Precision.HIGHEST

@jax.custom_vjp
def low(v):
    return lax.optimization_barrier(v.astype(jnp.bfloat16)).astype(jnp.float32)

@jax.custom_vjp
def low_back(v):
    return v

def low_keep(v):
    return (low(v), None)

def low_pass(kept, grad):
    return (grad,)

def back_keep(v):
    return (v, None)

def back_low(kept, grad):
    return (low(grad),)
low.defvjp(low_keep, low_pass)
low_back.defvjp(back_keep, back_low)

def layer_norm(values, gain, shift):
    center = values - lax.optimization_barrier(jnp.mean(values, axis=-1, keepdims=True))
    spread = lax.optimization_barrier(jnp.mean(center * center, axis=-1, keepdims=True))
    return center * lax.rsqrt(spread + NORM_EPS) * gain + shift

def counts_of(levels):
    return jnp.where(levels == 0, P_LOW, jnp.where(levels == 1, P_MID, PMAX))

def split_vectors(vecs):
    gain_one = vecs[:D]
    shift_one = vecs[D:2 * D]
    bias_in = vecs[2 * D:2 * D + FF]
    gain_two = vecs[2 * D + FF:2 * D + FF + HALF]
    shift_two = vecs[2 * D + FF + HALF:2 * D + FF + 2 * HALF]
    bias_out = vecs[2 * D + FF + 2 * HALF:]
    return (gain_one, shift_one, bias_in, gain_two, shift_two, bias_out)

def group_forward(item, weight_in, weight_out, vec_low, spat_low, spat_bias):
    inputs, levels = item
    gain_one, shift_one, bias_in, gain_two, shift_two, bias_out = split_vectors(vec_low)
    counts = counts_of(levels)
    live = (jnp.arange(PMAX)[None, :] < counts[:, None]).astype(jnp.float32)
    normed = low(layer_norm(inputs, gain_one, shift_one))
    pre = low_back(jnp.einsum('gpd,df->gpf', normed, weight_in, precision=HIGHEST) + bias_in)
    act = jax.nn.gelu(pre, approximate=False)
    left = act[..., :HALF]
    right = act[..., HALF:]
    gate_in = low(layer_norm(right, gain_two, shift_two))
    mixing = spat_low[levels] * live[:, :, None] * live[:, None, :]
    summed = jnp.einsum('gij,gjf->gif', mixing, gate_in, precision=HIGHEST)
    spat = low_back(live[:, :, None] * (summed + spat_bias[levels][:, :, None]))
    gated = low(left * spat)
    branch = low_back(jnp.einsum('gpf,fd->gpd', gated, weight_out, precision=HIGHEST) + bias_out)
    return inputs + live[:, :, None] * branch

def adamw(weight, grad, first, second, rate, decay):
    first = BETA_ONE * first + (1.0 - BETA_ONE) * grad
    second = BETA_TWO * second + (1.0 - BETA_TWO) * grad * grad
    first_hat = first / (1.0 - BETA_ONE ** STEP)
    second_hat = second / (1.0 - BETA_TWO ** STEP)
    weight = weight - rate * (first_hat / (jnp.sqrt(second_hat) + ADAM_EPS) + decay * weight)
    return (weight, first, second)

def reference(patches, resolution, out_grad, dense_in, dense_out, vectors, spatial, spatial_bias, in_first, in_second, out_first, out_second, vec_first, vec_second, spat_first, spat_second, bias_first, bias_second):
    groups = IMAGES // IMG_MB

    def forward(inputs, weight_in, weight_out, vecs, spat, spat_bias):
        w_in_low = low(weight_in)
        w_out_low = low(weight_out)
        vec_low = low(vecs)
        spat_low = low(spat)
        stacked = inputs.reshape(groups, IMG_MB, PMAX, D)
        grouped_levels = resolution.reshape(groups, IMG_MB)
        step_fn = jax.checkpoint(lambda item: group_forward(item, w_in_low, w_out_low, vec_low, spat_low, spat_bias))
        result = lax.map(step_fn, (stacked, grouped_levels))
        return result.reshape(IMAGES, PMAX, D)
    inputs = patches.astype(jnp.float32)
    mixed, pullback = jax.vjp(forward, inputs, dense_in, dense_out, vectors, spatial, spatial_bias)
    grads = pullback(out_grad.astype(jnp.float32))
    new_in = adamw(dense_in, grads[1], in_first, in_second, DENSE_RATE, DENSE_DECAY)
    new_out = adamw(dense_out, grads[2], out_first, out_second, DENSE_RATE, DENSE_DECAY)
    new_vec = adamw(vectors, grads[3], vec_first, vec_second, SMALL_RATE, 0.0)
    new_spat = adamw(spatial, grads[4], spat_first, spat_second, DENSE_RATE, DENSE_DECAY)
    new_bias = adamw(spatial_bias, grads[5], bias_first, bias_second, SMALL_RATE, 0.0)
    return (mixed.astype(jnp.bfloat16), grads[0].astype(jnp.bfloat16), new_in[0], new_in[1], new_in[2], new_out[0], new_out[1], new_out[2], new_vec[0], new_vec[1], new_vec[2], new_spat[0], new_spat[1], new_spat[2], new_bias[0], new_bias[1], new_bias[2])
```

```python
import functools

import jax
import jax.numpy as jnp
from jax import lax
from jax.experimental import pallas as pl
from jax.experimental.pallas import tpu as pltpu
from jax.sharding import PartitionSpec as P

D = 512
FF = 3072
HALF = 1536
PMAX = 324
PPAD = 336
P_MID = 196
P_LOW = 100
VCOLS = 256
ROWS = 2 * PPAD
GROUPS = 16
DEVS = 2 * GROUPS
VPER = 240
SCOLS = 384
BIAS_AT = 336
TOTAL_AT = 324
LSTRIDE = 168
MIB = 1024 * 1024
STEP = 10

NORM_EPS = 1e-05
BETA_ONE = 0.9
BETA_TWO = 0.99
ADAM_EPS = 1e-08
DENSE_RATE = 0.02
SMALL_RATE = 0.2
DENSE_DECAY = 0.05

BF = jnp.bfloat16
F32 = jnp.float32
AXES = ("dp", "seq")
VM = pl.BlockSpec(memory_space=pltpu.VMEM)
SM = pl.BlockSpec(memory_space=pltpu.SMEM)
HB = pl.BlockSpec(memory_space=pl.ANY)


class Route:
    def __init__(self, n):
        bits = n.bit_length() - 1
        assert n == 1 << bits and bits >= 2
        self.n = n
        top = n // 4
        self.direct = [top, 2 * top, 3 * top]
        low = [1 << b for b in range(bits - 2)]
        self.low = list(zip(low[::-1], low))
        masks = [(0, 0)] + [(m, m) for m in self.direct]
        for step in self.low:
            masks = masks + [(m[0] ^ step[0], m[1] ^ step[1]) for m in masks]
        self.masks = masks

    def swap(self, block, mask):
        pairs = []
        for dp in range(self.n):
            for seq in range(2):
                pairs.append((dp * 2 + seq, (dp ^ mask[seq]) * 2 + seq))
        return lax.ppermute(block, AXES, pairs)

    def cross(self, block):
        pairs = []
        for dp in range(self.n):
            for seq in range(2):
                pairs.append((dp * 2 + seq, dp * 2 + 1 - seq))
        return lax.ppermute(block, AXES, pairs)

    def order(self, seq_flip):
        place = lax.axis_index("dp")
        seq = lax.axis_index("seq")
        if seq_flip:
            seq = 1 - seq
        zero = jnp.array([m[0] for m in self.masks], jnp.int32)
        one = jnp.array([m[1] for m in self.masks], jnp.int32)
        return place ^ jnp.where(seq == 0, zero, one), seq

    def table(self):
        mine, seq = self.order(False)
        other, flip = self.order(True)
        return jnp.concatenate([mine * 2 + seq, other * 2 + flip])

    def spread(self, shard):
        first = jnp.concatenate([shard] + [self.swap(shard, (m, m)) for m in self.direct], axis=0)
        return self.widen(first)

    def widen(self, first):
        blocks = [first]
        for step in self.low:
            blocks = blocks + [self.swap(b, step) for b in blocks]
        return blocks

    def gather(self, shard):
        blocks = self.spread(shard)
        return blocks + [self.cross(b) for b in blocks]

    def collect(self, terms):
        cur = terms[0].shape[0]
        rows = cur // self.n

        def part(lower, upper):
            total = terms[0][lower:upper].astype(F32)
            for t in terms[1:]:
                total = total + t[lower:upper].astype(F32)
            return total

        terms = list(terms)
        for step in reversed(self.low):
            half = cur // 2
            terms.append(self.swap(part(half, cur).astype(BF), step))
            cur = half
        got = []
        for j, m in enumerate(self.direct):
            got.append(self.swap(part((j + 1) * rows, (j + 2) * rows).astype(BF), (m, m)))
        total = part(0, rows)
        return (total + got[0].astype(F32)) + (got[1].astype(F32) + got[2].astype(F32))

    def next_term(self, terms, stage):
        cur = self.n * 16 >> stage
        half = cur // 2
        total = terms[0][half:cur].astype(F32)
        for t in terms[1:]:
            total = total + t[half:cur].astype(F32)
        total = total.astype(BF)
        return terms + [self.swap(total, self.low[-1 - stage])], [total]

    def scatter(self, keep, send):
        return self.collect([keep, self.cross(send)])


def dot(a, b, dims):
    return lax.dot_general(a, b, (dims, ((), ())), preferred_element_type=F32)


NN = ((1,), (0,))
NT = ((1,), (1,))
TN = ((0,), (0,))


def gelu_parts(p):
    bell = jnp.exp(p * p * -0.5)
    d = 1.0 + jnp.abs(p) * (0.3275911 * 0.7071067811865476)
    t = pl.reciprocal(d, approx=True)
    t = t * (2.0 - d * t)
    poly = t * (
        0.127414796
        + t * (-0.142248368 + t * (0.7107068705 + t * (-0.7265760135 + t * 0.5307027145)))
    )
    tail = poly * bell
    phi_sum = jnp.where(p >= 0.0, 1.0 - tail, tail)
    return p * phi_sum, phi_sum + p * bell * 0.3989422804014327


def count_of(level):
    return jnp.where(level == 0, P_LOW, jnp.where(level == 1, P_MID, PMAX))


def masked_mix(mix, count):
    i = lax.broadcasted_iota(jnp.int32, (PPAD, SCOLS), 0)
    j = lax.broadcasted_iota(jnp.int32, (PPAD, SCOLS), 1)
    return jnp.where((i < count) & (j < count), mix.astype(F32), 0.0).astype(BF)


def live_rows(count, shape, start=0):
    return lax.broadcasted_iota(jnp.int32, shape, 0) + start < count


def live_mask(levels_ref, b, width):
    return live_rows(count_of(levels_ref[b]), (PPAD, width))


def fold(value):
    total = value[:, 0:128]
    for n in range(128, value.shape[1], 128):
        total = total + value[:, n : n + 128]
    return total


def spread_sum(ref, factor):
    return jnp.broadcast_to(jnp.sum(ref[...], axis=-1, keepdims=True) * factor, ref.shape)


def wide(value, times):
    return jnp.concatenate([value] * times, axis=1)


def start_blocks(table_ref, pieces, rows, cols, target, sem, extra=0):
    copies = []
    k = 0
    for piece in pieces:
        for j in range(piece.shape[0] // 16):
            at = pl.multiple_of(table_ref[k] * rows, 16)
            c = pltpu.make_async_copy(
                piece.at[pl.ds(j * 16, 16), pl.ds(cols[0], cols[1])], target.at[pl.ds(at + extra, 16)], sem.at[k]
            )
            c.start()
            copies.append(c)
            k += 1
    return copies


def row_loop(step, body):
    def run(i, carry):
        body(pl.multiple_of(i * step, step))
        return carry

    lax.fori_loop(0, ROWS // step, run, 0)


def call(kernel, out_shape, in_specs, scratch, flops, nbytes, *args, room=12):
    vm = pl.BlockSpec(memory_space=pltpu.VMEM)
    return pl.pallas_call(
        kernel,
        out_shape=out_shape,
        in_specs=in_specs,
        out_specs=jax.tree.map(lambda _: vm, out_shape),
        scratch_shapes=scratch,
        compiler_params=pltpu.CompilerParams(vmem_limit_bytes=room * MIB),
        cost_estimate=pl.CostEstimate(flops=flops, bytes_accessed=nbytes, transcendentals=0),
    )(*args)


def norm_parts(values):
    center = values - jnp.mean(values, axis=-1, keepdims=True)
    scale = lax.rsqrt(jnp.mean(center * center, axis=-1, keepdims=True) + NORM_EPS)
    return center * scale, scale


VSEG = {
    "g1": (0, D),
    "b1": (D, D),
    "c1l": (2 * D, HALF),
    "c1r": (2 * D + HALF, HALF),
    "g2": (2 * D + FF, HALF),
    "b2": (2 * D + FF + HALF, HALF),
    "c2": (2 * D + FF + 2 * HALF, D),
}
VEC = 2 * D + FF + 2 * HALF + D


def seg(ref, name):
    start, size = VSEG[name]
    return ref[0:1, start : start + size]

def adamw(weight, grad, first, second, rate, decay):
    first = BETA_ONE * first + (1.0 - BETA_ONE) * grad
    second = BETA_TWO * second + (1.0 - BETA_TWO) * grad * grad
    first_hat = first / (1.0 - BETA_ONE**STEP)
    second_hat = second / (1.0 - BETA_TWO**STEP)
    weight = weight - rate * (first_hat / (jnp.sqrt(second_hat) + ADAM_EPS) + decay * weight)
    return (weight, first, second)


CHUNK = 16
TILE = 256
BODY = 32
STRIPE = 112
LO = 2 * HALF
SPC = 2 * SCOLS


def sds(shape, dtype):
    return jax.ShapeDtypeStruct(shape, dtype)


def pack_dense(dense_in, dense_out, vec_row):
    rows = dense_in.shape[0]
    per = vec_row.shape[1]

    def kernel(w_ref, o_ref, v_ref, out_ref, lo_ref, row):
        out_ref[:, 0:HALF] = w_ref[:, HALF:].astype(BF)
        row[...] = jnp.zeros_like(row)
        row[0:1, 0:per] = v_ref[...]
        out_ref[:, HALF:] = row[...].astype(BF)
        lo_ref[:, 0:HALF] = w_ref[:, 0:HALF].astype(BF)
        for g in range(3):
            lo_ref[:, HALF + g * D : HALF + (g + 1) * D] = o_ref[g * rows : (g + 1) * rows, :].astype(BF)

    scratch = [pltpu.VMEM((rows, VCOLS), F32)]
    shapes = (sds((rows, HALF + VCOLS), BF), sds((rows, LO), BF))
    return call(kernel, shapes, [VM] * 3, scratch, 1000, 600000, dense_in, dense_out, vec_row)


def pack_images(sides, spatial, bias_col, patches, out_grad):
    half = patches.shape[1]

    def kernel(sides_ref, s_ref, b_ref, x_ref, g_ref, spat_ref, xs_ref, gs_ref, buf):
        away = 2 - 2 * sides_ref[0]
        for b in range(2):
            xs_ref[b] = x_ref[away + b]
            gs_ref[b] = g_ref[away + b]
        buf[...] = jnp.zeros_like(buf)
        for level in range(3):
            buf[:, 0:PMAX] = s_ref[level]
            rest = b_ref[level]
            for c in range(3):
                piece = rest.astype(BF).astype(F32)
                buf[:, BIAS_AT + c : BIAS_AT + c + 1] = piece
                rest = rest - piece
            spat_ref[level] = buf[...].astype(BF)

    pair = sds((2, half, D), BF)
    return call(
        kernel,
        (sds((3, half, SCOLS), BF), pair, pair),
        [SM] + [VM] * 4,
        [pltpu.VMEM((half, SCOLS), F32)],
        1000,
        3000000,
        sides,
        spatial,
        bias_col,
        patches,
        out_grad,
    )


def stack(pieces, after):
    count = len(pieces)
    rows, cols = pieces[0].shape

    def kernel(*refs):
        for k in range(count):
            refs[count + 1][k * rows : (k + 1) * rows, :] = refs[k][...]

    return call(kernel, sds((count * rows, cols), BF), [VM] * count + [HB], [], 1000, 1000000, *pieces, after)


def two_halves(is_first, own, got):
    own = own.astype(F32)
    got = got.astype(F32)
    return jnp.where(is_first, own, got), jnp.where(is_first, got, own)


def spatial_mix(levels, sides, gate, spat_own, spat_got, after):
    half = spat_own.shape[1]
    count = len(after)

    def kernel(levels_ref, sides_ref, gate_ref, so_ref, sg_ref, *refs):
        spat_ref, mm_ref, mixf = refs[count:]
        is_first = sides_ref[0] == 0
        for b in range(2):
            level = levels_ref[b]
            live = count_of(level)
            one, two = two_halves(is_first, so_ref[level], sg_ref[level])
            mixf[0:half, :] = one
            mixf[half : 2 * half, :] = two
            mixf[2 * half :, :] = jnp.zeros((PPAD - 2 * half, SCOLS), F32)
            bias = jnp.sum(mixf[:, TOTAL_AT:], axis=-1, keepdims=True)
            mm_ref[b] = masked_mix(mixf[...], live)

            def mix_tile(n, carry):
                cols = pl.ds(pl.multiple_of(n * 512, 512), 512)
                got = dot(mm_ref[b], gate_ref[b * PPAD : b * PPAD + SCOLS, cols], NN) + bias
                got = jnp.where(live_rows(live, (PPAD, 512)), got, 0.0)
                spat_ref[b * PPAD : (b + 1) * PPAD, cols] = got.astype(BF)
                return carry

            lax.fori_loop(0, HALF // 512, mix_tile, 0)

    return call(
        kernel,
        (sds((ROWS, HALF), BF), sds((2, PPAD, SCOLS), BF)),
        [SM] * 2 + [VM] * 3 + [HB] * count,
        [pltpu.VMEM((PPAD, SCOLS), F32)],
        3000000000,
        6000000,
        levels,
        sides,
        gate,
        spat_own,
        spat_got,
        *after,
        room=14,
    )


def gate_forward(table, sides, patches, x_got, out_grad, g_got, pieces):
    count = len(pieces)
    half = patches.shape[1]

    def kernel(table_ref, sides_ref, p_ref, xg_ref, o_ref, gg_ref, *refs):
        ins = refs[:count]
        outs = refs[count : count + 9]
        x_ref, og_ref, h_ref, gate_ref, hat_ref, slope_ref, scale_ref, w_ref, vec_ref = outs
        vblk, xbuf, pre, part, mean, sem, vsem = refs[count + 9 :]
        vcopies = start_blocks(table_ref, ins, 16, (HALF, VCOLS), vblk, vsem)
        copies = start_blocks(table_ref, ins, 16, (0, HALF), w_ref, sem)
        me = sides_ref[0]
        is_first = me == 0

        for src, got, target in ((o_ref, gg_ref, og_ref), (p_ref, xg_ref, x_ref)):
            for b in range(2):
                one, two = two_halves(is_first, src[2 * me + b], got[b])
                xbuf[b * PPAD : b * PPAD + half, :] = one
                xbuf[b * PPAD + half : b * PPAD + 2 * half, :] = two
                xbuf[b * PPAD + 2 * half : (b + 1) * PPAD, :] = jnp.zeros((PPAD - 2 * half, D), F32)
            target[...] = xbuf[...].astype(BF)
        for c in vcopies:
            c.wait()
        for s in range(DEVS):
            row = vblk[16 * s : 16 * s + 16, :].astype(F32)[0:1, :VPER]
            vec_ref[0:1, VPER * s : VPER * s + VPER] = row

        def norm_one(r):
            hat, _ = norm_parts(xbuf[pl.ds(r, STRIPE), :])
            h_ref[pl.ds(r, STRIPE), :] = (hat * seg(vec_ref, "g1") + seg(vec_ref, "b1")).astype(BF)

        row_loop(STRIPE, norm_one)
        for c in copies:
            c.wait()
        c_start = VSEG["c1r"][0]
        g_start = VSEG["g2"][0]
        b_start = VSEG["b2"][0]

        def matmul(n, carry):
            at = pl.multiple_of(n * TILE, TILE)
            pre[:, pl.ds(at, TILE)] = dot(h_ref[...], w_ref[:, pl.ds(at, TILE)], NN)
            return carry

        lax.fori_loop(0, HALF // TILE, matmul, 0)

        def gelu_rows(r):
            for k in range(0, BODY, CHUNK):
                rows = pl.ds(r + k, CHUNK)
                total = jnp.zeros((CHUNK, 128), F32)
                for n in range(0, HALF, TILE):
                    v, slope = gelu_parts(pre[rows, n : n + TILE] + vec_ref[0:1, c_start + n : c_start + n + TILE])
                    pre[rows, n : n + TILE] = v
                    slope_ref[rows, n : n + TILE] = slope.astype(BF)
                    total = total + fold(v)
                part[rows, :] = total

        row_loop(BODY, gelu_rows)
        mean[...] = spread_sum(part, 1.0 / HALF)

        def square_rows(r):
            for k in range(0, BODY, CHUNK):
                rows = pl.ds(r + k, CHUNK)
                mid = mean[rows, :]
                total = jnp.zeros((CHUNK, 128), F32)
                for n in range(0, HALF, 128):
                    center = pre[rows, n : n + 128] - mid
                    total = total + center * center
                part[rows, :] = total

        row_loop(BODY, square_rows)
        scale_ref[...] = lax.rsqrt(spread_sum(part, 1.0 / HALF) + NORM_EPS)

        def gate_rows(r):
            for k in range(0, BODY, CHUNK):
                rows = pl.ds(r + k, CHUNK)
                mid = wide(mean[rows, :], 2)
                scale = wide(scale_ref[rows, :], 2)
                for n in range(0, HALF, TILE):
                    hat = (pre[rows, n : n + TILE] - mid) * scale
                    hat_ref[rows, n : n + TILE] = hat.astype(BF)
                    gate = hat * vec_ref[0:1, g_start + n : g_start + n + TILE]
                    gate = (gate + vec_ref[0:1, b_start + n : b_start + n + TILE]).astype(BF)
                    gate_ref[rows, n : n + TILE] = gate

        row_loop(BODY, gate_rows)
        gate_ref[ROWS:, :] = jnp.zeros((SCOLS - PPAD, HALF), BF)

    broad = sds((ROWS, HALF), BF)
    narrow = sds((ROWS, D), BF)
    out_shape = (
        narrow,
        narrow,
        narrow,
        sds((ROWS + SCOLS - PPAD, HALF), BF),
        broad,
        broad,
        sds((ROWS, 128), F32),
        sds((D, HALF), BF),
        sds((1, VEC), F32),
    )
    scratch = [
        pltpu.VMEM((D, VCOLS), BF),
        pltpu.VMEM((ROWS, D), F32),
        pltpu.VMEM((ROWS, HALF), F32),
        pltpu.VMEM((ROWS, 128), F32),
        pltpu.VMEM((ROWS, 128), F32),
        pltpu.SemaphoreType.DMA((DEVS,)),
        pltpu.SemaphoreType.DMA((DEVS,)),
    ]
    return call(
        kernel,
        out_shape,
        [SM] * 2 + [VM] * 4 + [HB] * count,
        scratch,
        10000000000,
        20000000,
        table,
        sides,
        patches,
        x_got,
        out_grad,
        g_got,
        *pieces,
        room=26,
    )


def split_rows(target, first, second, seq, value):
    half = first.shape[1]
    target[...] = value
    for b in range(2):
        one = target[b * PPAD : b * PPAD + half, :]
        two = target[b * PPAD + half : b * PPAD + 2 * half, :]
        first[b] = jnp.where(seq == 0, one, two).astype(BF)
        second[b] = jnp.where(seq == 0, two, one).astype(BF)


def middle(table, levels, sides, vec, h, spat, gate, grad_out, pieces):
    count = len(pieces)

    def kernel(table_ref, levels_ref, sides_ref, vec_ref, h_ref, spat_ref, gate_ref, og_ref, *refs):
        ins = refs[:count]
        gs_ref, gated_ref, q_ref, gb, wl, wo, keep, send, gsum_ref = refs[count : count + 9]
        pbuf, gbuf, cells, flat, sem = refs[count + 9 :]
        copies = start_blocks(table_ref, ins, 16, (0, HALF), wl, sem.at[0])
        for g in range(3):
            copies += start_blocks(table_ref, ins, 48, (HALF + g * D, D), wo, sem.at[1 + g], 16 * g)
        for b in range(2):
            rows = slice(b * PPAD, (b + 1) * PPAD)
            gb[rows, :] = jnp.where(live_mask(levels_ref, b, D), og_ref[rows, :].astype(F32), 0.0).astype(BF)
        gsum_ref[0:1, HALF : HALF + D] = jnp.sum(gb[...].astype(F32), axis=0, keepdims=True)
        cells[...] = jnp.zeros_like(cells)
        flat[...] = jnp.zeros_like(flat)
        for c in copies:
            c.wait()
        c_start = VSEG["c1l"][0]

        def tile(n, carry):
            at = pl.multiple_of(n * TILE, TILE)
            cols = pl.ds(at, TILE)
            pbuf[...] = dot(h_ref[...], wl[:, cols], NN)
            gbuf[...] = dot(gb[...], wo[cols, :], NT)
            shift = vec_ref[0:1, pl.ds(c_start + at, TILE)]
            total = jnp.zeros((CHUNK, TILE), F32)
            for k in range(0, ROWS, CHUNK):
                r = slice(k, k + CHUNK)
                u, slope = gelu_parts(pbuf[r, :] + shift)
                sp = spat_ref[r, cols].astype(F32)
                gg = gbuf[r, :]
                gated_ref[r, cols] = (u * sp).astype(BF)
                gs_ref[r, cols] = (gg * u).astype(BF)
                q = (gg * sp * slope).astype(BF)
                q_ref[r, cols] = q
                total = total + q.astype(F32)
            gsum_ref[0:1, cols] = jnp.sum(total, axis=0, keepdims=True)
            return carry

        lax.fori_loop(0, HALF // TILE, tile, 0)

        me = sides_ref[0]
        for b in range(2):
            level = levels_ref[b]
            count_b = count_of(level)
            gs = gs_ref[b * PPAD : (b + 1) * PPAD, :]
            got = dot(gs, gate_ref[b * PPAD : (b + 1) * PPAD, :], NT)
            sums = jnp.sum(gs.astype(F32), axis=-1, keepdims=True)
            j = lax.broadcasted_iota(jnp.int32, (PPAD, PPAD), 1)
            got = jnp.where(j < count_b, got, jnp.where(j == TOTAL_AT, sums, 0.0))
            cells[level, :, 0:PPAD] += got
        part = PMAX // 2
        for level in range(3):
            for k in range(2):
                flat[k, level * LSTRIDE : level * LSTRIDE + part, 0:PPAD] = cells[level, k * part : (k + 1) * part, 0:PPAD]
        for k in range(DEVS):
            target, side = (keep, me) if k < GROUPS else (send, 1 - me)
            r = pl.ds(k % GROUPS * 16, 16)
            block = flat[side, pl.ds(pl.multiple_of(sides_ref[1 + k] * 32, 32), 32), :].astype(BF)
            target[r, 0:SCOLS] = block[0:16]
            target[r, SCOLS:SPC] = block[16:32]

    broad = sds((ROWS, HALF), BF)
    payload = sds((D // 2, SPC), BF)
    out_shape = (
        broad,
        broad,
        broad,
        sds((ROWS, D), BF),
        sds((D, HALF), BF),
        sds((HALF, D), BF),
        payload,
        payload,
        sds((1, HALF + D), F32),
    )
    scratch = [
        pltpu.VMEM((ROWS, TILE), F32),
        pltpu.VMEM((ROWS, TILE), F32),
        pltpu.VMEM((3, PPAD, SCOLS), F32),
        pltpu.VMEM((2, 512, SCOLS), F32),
        pltpu.SemaphoreType.DMA((4, DEVS)),
    ]
    return call(
        kernel,
        out_shape,
        [SM] * 3 + [VM] * 5 + [HB] * count,
        scratch,
        8000000000,
        16000000,
        table,
        levels,
        sides,
        vec,
        h,
        spat,
        gate,
        grad_out,
        *pieces,
        room=28,
    )


def weight_grads(table, levels, sides, vec, gated, q, gb, h, wl, wo, x, half):
    def kernel(
        table_ref, levels_ref, sides_ref, vec_ref, t_ref, q_ref, gb_ref, h_ref, wl_ref, wo_ref, x_ref,
        keep, send, stay_ref, away_ref, gh_ref, branch, gwo, gwl,
    ):
        def out_tile(n, carry):
            cols = pl.ds(pl.multiple_of(n * TILE, TILE), TILE)
            gwo[cols, :] = dot(t_ref[:, cols], gb_ref[...], TN).astype(BF)
            return carry

        lax.fori_loop(0, HALF // TILE, out_tile, 0)

        def in_tile(n, carry):
            cols = pl.ds(pl.multiple_of(n * TILE, TILE), TILE)
            gwl[cols, :] = dot(h_ref[:, cols], q_ref[...], TN).astype(BF)
            branch[:, cols] = dot(t_ref[...], wo_ref[:, cols], NN)
            gh_ref[:, cols] = dot(q_ref[...], wl_ref[cols, :], NT)
            return carry

        lax.fori_loop(0, D // TILE, in_tile, 0)
        me = sides_ref[0]
        live = jnp.concatenate([live_mask(levels_ref, b, D) for b in range(2)], axis=0)
        out = branch[...] + seg(vec_ref, "c2")
        split_rows(branch, stay_ref, away_ref, me, x_ref[...].astype(F32) + jnp.where(live, out, 0.0))
        for k in range(DEVS):
            dev = table_ref[k]
            target = keep if k < GROUPS else send
            r = pl.ds(k % GROUPS * 16, 16)
            target[r, 0:HALF] = gwl[pl.ds(pl.multiple_of(dev * 16, 16), 16), :]
            for g in range(3):
                target[r, HALF + g * D : HALF + (g + 1) * D] = gwo[pl.ds(pl.multiple_of(dev * 48 + 16 * g, 16), 16), :]

    pair = sds((2, half, D), BF)
    payload = sds((D // 2, LO), BF)
    return call(
        kernel,
        (payload, payload, pair, pair, sds((ROWS, D), F32)),
        [SM] * 3 + [VM] * 8,
        [pltpu.VMEM((ROWS, D), F32), pltpu.VMEM((HALF, D), BF), pltpu.VMEM((D, HALF), BF)],
        5000000000,
        15000000,
        table,
        levels,
        sides,
        vec,
        gated,
        q,
        gb,
        h,
        wl,
        wo,
        x,
        room=24,
    )


def gate_backward(vec, gs, mm, hat, slope, scale):
    def kernel(vec_ref, gs_ref, mm_ref, hat_ref, slope_ref, scale_ref, gp, gsum_ref, dbuf, one, two, acc):
        for b in range(2):

            def mix_tile(n, carry):
                cols = pl.ds(pl.multiple_of(n * 512, 512), 512)
                got = dot(mm_ref[b], gs_ref[b * PPAD : (b + 1) * PPAD, cols], TN)
                dbuf[b * PPAD : (b + 1) * PPAD, cols] = got[0:PPAD]
                return carry

            lax.fori_loop(0, HALF // 512, mix_tile, 0)
        g_start = VSEG["g2"][0]

        def sum_rows(r):
            for k in range(0, BODY, CHUNK):
                rows = pl.ds(r + k, CHUNK)
                a = jnp.zeros((CHUNK, 128), F32)
                c = jnp.zeros((CHUNK, 128), F32)
                for n in range(0, HALF, TILE):
                    e = dbuf[rows, n : n + TILE] * vec_ref[0:1, g_start + n : g_start + n + TILE]
                    a = a + fold(e)
                    c = c + fold(e * hat_ref[rows, n : n + TILE].astype(F32))
                one[rows, :] = a
                two[rows, :] = c

        row_loop(BODY, sum_rows)
        one[...] = spread_sum(one, 1.0 / HALF)
        two[...] = spread_sum(two, 1.0 / HALF)
        acc[...] = jnp.zeros_like(acc)

        def grad_rows(r):
            for n in range(0, HALF, TILE):
                gain = vec_ref[0:1, g_start + n : g_start + n + TILE]
                sums = [jnp.zeros((CHUNK, TILE), F32) for _ in range(3)]
                for k in range(0, BODY, CHUNK):
                    rows = pl.ds(r + k, CHUNK)
                    d = dbuf[rows, n : n + TILE]
                    xh = hat_ref[rows, n : n + TILE].astype(F32)
                    inner = d * gain - wide(one[rows, :], 2) - xh * wide(two[rows, :], 2)
                    q = inner * wide(scale_ref[rows, :], 2) * slope_ref[rows, n : n + TILE].astype(F32)
                    q = q.astype(BF)
                    gp[rows, n : n + TILE] = q
                    sums = [sums[0] + d * xh, sums[1] + d, sums[2] + q.astype(F32)]
                for i in range(3):
                    acc[i, :, n : n + TILE] += sums[i]

        row_loop(BODY, grad_rows)
        for i in range(3):
            gsum_ref[0:1, i * HALF : (i + 1) * HALF] = jnp.sum(acc[i], axis=0, keepdims=True)

    return call(
        kernel,
        (sds((ROWS, HALF), BF), sds((1, 3 * HALF), F32)),
        [VM] * 6,
        [
            pltpu.VMEM((ROWS, HALF), F32),
            pltpu.VMEM((ROWS, 128), F32),
            pltpu.VMEM((ROWS, 128), F32),
            pltpu.VMEM((3, CHUNK, HALF), F32),
        ],
        3000000000,
        10000000,
        vec,
        gs,
        mm,
        hat,
        slope,
        scale,
        room=20,
    )


def in_grads(gp, h, w, gh, after):
    count = len(after)

    def kernel(gp_ref, h_ref, w_ref, gh_ref, *refs):
        gwr, ghb = refs[count:]

        def in_tile(n, carry):
            cols = pl.ds(pl.multiple_of(n * TILE, TILE), TILE)
            ghb[:, cols] = gh_ref[:, cols] + dot(gp_ref[...], w_ref[cols, :], NT)
            gwr[cols, :] = dot(h_ref[:, cols], gp_ref[...], TN).astype(BF)
            return carry

        lax.fori_loop(0, D // TILE, in_tile, 0)

    return call(
        kernel,
        (sds((D, HALF), BF), sds((ROWS, D), F32)),
        [VM] * 4 + [HB] * count,
        [],
        3000000000,
        8000000,
        gp,
        h,
        w,
        gh,
        *after,
        room=14,
    )


def in_backward(table, sides, vec, gsum, gate_sum, gwr, ghb, x, grad_out, half, after):
    count = len(after)

    def kernel(table_ref, sides_ref, vec_ref, gsum_ref, gate_ref, gwr, ghb, x_ref, og_ref, *refs):
        keep, send, stay_ref, away_ref, acc, gvec, blocks, pgb = refs[count:]

        def put(name, value):
            start, size = VSEG[name]
            gvec[0:1, start : start + size] = value

        put("g2", gate_ref[0:1, 0:HALF])
        put("b2", gate_ref[0:1, HALF : 2 * HALF])
        put("c1r", gate_ref[0:1, 2 * HALF : 3 * HALF])
        put("c1l", gsum_ref[0:1, 0:HALF])
        put("c2", gsum_ref[0:1, HALF : HALF + D])
        acc[...] = jnp.zeros_like(acc)
        def in_rows(r):
            rows = pl.ds(r, STRIPE)
            xh, scale = norm_parts(x_ref[rows, :].astype(F32))
            d = ghb[rows, :]
            e = d * seg(vec_ref, "g1")
            one = jnp.mean(e, axis=-1, keepdims=True)
            two = jnp.mean(e * xh, axis=-1, keepdims=True)
            pgb[rows, :] = og_ref[rows, :].astype(F32) + scale * (e - one - xh * two)
            acc[0:1, :] += jnp.sum(d * xh, axis=0, keepdims=True)
            acc[1:2, :] += jnp.sum(d, axis=0, keepdims=True)

        row_loop(STRIPE, in_rows)
        put("g1", acc[0:1, :])
        put("b1", acc[1:2, :])
        split_rows(pgb, stay_ref, away_ref, sides_ref[0], pgb[...])
        blocks[...] = jnp.zeros_like(blocks)
        for s in range(DEVS):
            blocks[s, 0:1, 0:VPER] = gvec[0:1, VPER * s : VPER * s + VPER]
        for k in range(DEVS):
            dev = table_ref[k]
            target = keep if k < GROUPS else send
            r = pl.ds(k % GROUPS * 16, 16)
            target[r, 0:HALF] = gwr[pl.ds(pl.multiple_of(dev * 16, 16), 16), :]
            target[r, HALF : HALF + VCOLS] = blocks[dev].astype(BF)

    payload = sds((D // 2, HALF + VCOLS), BF)
    pair = sds((2, half, D), BF)
    return call(
        kernel,
        (payload, payload, pair, pair),
        [SM] * 2 + [VM] * 7 + [HB] * count,
        [
            pltpu.VMEM((8, D), F32),
            pltpu.VMEM((1, VEC), F32),
            pltpu.VMEM((DEVS, 16, VCOLS), F32),
            pltpu.VMEM((ROWS, D), F32),
        ],
        2000000000,
        6000000,
        table,
        sides,
        vec,
        gsum,
        gate_sum,
        gwr,
        ghb,
        x,
        grad_out,
        *after,
        room=16,
    )


def line_parts(terms):
    cols = terms[0].shape[1]
    count = len(terms)

    def kernel(*refs):
        own, outs = refs[count], refs[count + 1 :]
        for m in range(4):
            rows = slice(16 * m, 16 * (m + 1))
            value = refs[0][rows, :].astype(F32)
            for t in refs[1:count]:
                value = value + t[rows, :].astype(F32)
            if m == 0:
                own[...] = value
            else:
                outs[m - 1][...] = value.astype(BF)

    block = pl.BlockSpec((64, cols), lambda i: (0, 0))
    one = pl.BlockSpec((16, cols), lambda i: (0, 0))
    return pl.pallas_call(
        kernel,
        grid=(1,),
        out_shape=[sds((16, cols), F32)] + [sds((16, cols), BF)] * 3,
        in_specs=[block] * count,
        out_specs=[one] * 4,
        compiler_params=pltpu.CompilerParams(vmem_limit_bytes=8 * MIB),
        cost_estimate=pl.CostEstimate(flops=1000000, bytes_accessed=3000000, transcendentals=0),
    )(*terms)


def line_sum(total, got):
    rows = total.shape[0]

    def kernel(own_ref, a_ref, b_ref, c_ref, out_ref):
        near = own_ref[...].astype(F32) + a_ref[...].astype(F32)
        far = b_ref[...].astype(F32) + c_ref[...].astype(F32)
        out_ref[...] = (near + far).astype(BF)

    return call(kernel, sds((rows, SPC), BF), [VM] * 4, [], 1000000, 500000, total, *got)


def line_spread(terms):
    count = len(terms)
    cols = terms[0].shape[1]

    def kernel(*refs):
        outs = refs[count:]
        for m in range(4):
            rows = slice(16 * m, 16 * (m + 1))
            value = refs[0][rows, :].astype(F32)
            for t in refs[1:count]:
                value = value + t[rows, :].astype(F32)
            value = value.astype(BF)
            for j in range(4):
                at = 16 * (m ^ j)
                outs[j][at : at + 16, :] = value

    block = pl.BlockSpec((64, cols), lambda i: (0, 0))
    return pl.pallas_call(
        kernel,
        grid=(1,),
        out_shape=[sds((64, cols), BF)] * 4,
        in_specs=[block] * count,
        out_specs=[block] * 4,
        compiler_params=pltpu.CompilerParams(vmem_limit_bytes=8 * MIB),
        cost_estimate=pl.CostEstimate(flops=1000000, bytes_accessed=1000000, transcendentals=0),
    )(*terms)


def finish_out(own, got, weight, first, second):
    def kernel(own_ref, a_ref, b_ref, c_ref, w_ref, m_ref, s_ref, left_ref, nw, nm, ns):
        total = own_ref[...] + a_ref[...].astype(F32)
        total = total + (b_ref[...].astype(F32) + c_ref[...].astype(F32))
        left_ref[...] = total[:, 0:HALF]
        for g in range(3):
            rows = slice(16 * g, 16 * (g + 1))
            grad = total[:, HALF + g * D : HALF + (g + 1) * D]
            new = adamw(w_ref[rows, :], grad, m_ref[rows, :], s_ref[rows, :], DENSE_RATE, DENSE_DECAY)
            nw[rows, :] = new[0]
            nm[rows, :] = new[1]
            ns[rows, :] = new[2]

    same = sds(weight.shape, F32)
    return call(
        kernel,
        (sds((16, HALF), F32), same, same, same),
        [VM] * 7,
        [],
        1000000,
        2000000,
        own,
        *got,
        weight,
        first,
        second,
    )


def finish_in(own, got, left, weight, first, second):
    def kernel(own_ref, a_ref, b_ref, c_ref, l_ref, w_ref, m_ref, s_ref, nw, nm, ns, vec_ref):
        total = own_ref[...] + a_ref[...].astype(F32)
        total = total + (b_ref[...].astype(F32) + c_ref[...].astype(F32))
        vec_ref[...] = total[0:1, HALF:]
        for cols, grad in ((slice(0, HALF), l_ref[...]), (slice(HALF, FF), total[:, 0:HALF])):
            new = adamw(w_ref[:, cols], grad, m_ref[:, cols], s_ref[:, cols], DENSE_RATE, DENSE_DECAY)
            nw[:, cols] = new[0]
            nm[:, cols] = new[1]
            ns[:, cols] = new[2]

    same = sds(weight.shape, F32)
    return call(
        kernel,
        (same, same, same, sds((1, VCOLS), F32)),
        [VM] * 8,
        [],
        1000000,
        2000000,
        own,
        *got,
        left,
        weight,
        first,
        second,
    )


def spatial_update(order, pieces, spatial, first, second):
    count = len(pieces)
    rows = spatial.shape[1]

    def kernel(order_ref, *refs):
        ins = refs[:count]
        w_ref, m_ref, s_ref, nw, nm, ns, nb, flat = refs[count:]
        k = 0
        for piece in ins:
            for j in range(piece.shape[0] // 16):
                at = pl.multiple_of(order_ref[k] * 32, 32)
                block = piece[16 * j : 16 * j + 16, :].astype(F32)
                flat[pl.ds(at, 16), :] = block[:, 0:SCOLS]
                flat[pl.ds(at + 16, 16), :] = block[:, SCOLS:]
                k += 1
        for level in range(3):
            got = flat[level * LSTRIDE : level * LSTRIDE + rows, :]
            new = adamw(w_ref[level], got[:, 0:PMAX], m_ref[level], s_ref[level], DENSE_RATE, DENSE_DECAY)
            nw[level] = new[0]
            nm[level] = new[1]
            ns[level] = new[2]
            nb[level] = got[:, TOTAL_AT : TOTAL_AT + 1]

    vm = pl.BlockSpec(memory_space=pltpu.VMEM)
    sm = pl.BlockSpec(memory_space=pltpu.SMEM)
    same = jax.ShapeDtypeStruct(spatial.shape, F32)
    return pl.pallas_call(
        kernel,
        out_shape=(same, same, same, jax.ShapeDtypeStruct((3, rows, 1), F32)),
        in_specs=[sm] + [vm] * (count + 3),
        out_specs=(vm,) * 4,
        scratch_shapes=[pltpu.VMEM((512, SCOLS), F32)],
        compiler_params=pltpu.CompilerParams(vmem_limit_bytes=12 * MIB),
        cost_estimate=pl.CostEstimate(flops=10000000, bytes_accessed=6000000, transcendentals=0),
    )(order, *pieces, spatial, first, second)


def in_order(blocks, table, rows):
    cols = blocks[0].shape[1]
    whole = jnp.concatenate(blocks, axis=0).reshape(-1, rows, cols)
    back = jnp.zeros_like(table).at[table].set(jnp.arange(table.shape[0], dtype=table.dtype))
    return jnp.take(whole, back, axis=0)


def local(
    patches,
    resolution,
    out_grad,
    dense_in,
    dense_out,
    vectors,
    spatial,
    spatial_bias,
    in_first,
    in_second,
    out_first,
    out_second,
    vec_first,
    vec_second,
    spat_first,
    spat_second,
    bias_first,
    bias_second,
):
    route = Route(lax.axis_size("dp"))
    ndev = 2 * route.n
    fits = route.n == GROUPS
    seq = lax.axis_index("seq").astype(jnp.int32)
    rows = patches.shape[1]
    table = route.table()
    order = route.order(False)[0]
    in_rows = dense_in.shape[0]
    out_rows = dense_out.shape[0]
    vec_len = vectors.shape[0]
    if fits:
        ktable = table
        korder = table // 2
    else:
        ktable = jnp.arange(DEVS, dtype=jnp.int32)
        korder = jnp.arange(DEVS, dtype=jnp.int32) % GROUPS
    sides = jnp.concatenate([seq[None], korder])
    levels = lax.dynamic_slice_in_dim(resolution, seq * 2, 2, 0)

    right_shard, lo_shard = pack_dense(dense_in, dense_out, vectors.reshape(1, vec_len))
    line = [route.swap(right_shard, (m, m)) for m in route.direct]
    lo_line = [route.swap(lo_shard, (m, m)) for m in route.direct]
    spat_own, x_send, g_send = pack_images(sides, spatial, spatial_bias.reshape(3, rows, 1), patches, out_grad)
    x_got = route.cross(x_send)
    g_got = route.cross(g_send)
    spat_got = route.cross(spat_own)
    right_blocks = route.widen(jnp.concatenate([right_shard] + line, axis=0))
    if fits:
        lo_first = stack([lo_shard] + lo_line, right_blocks[1])
    else:
        lo_first = jnp.concatenate([lo_shard] + lo_line, axis=0)
    lo_blocks = route.widen(lo_first)
    lo_second = lo_blocks[1]
    right_blocks = right_blocks + [route.cross(b) for b in right_blocks]
    lo_blocks = lo_blocks + [route.cross(b) for b in lo_blocks]
    if not fits:
        whole = in_order(right_blocks, table, in_rows)
        all_vec = whole[:, 0, HALF : HALF + vec_len].reshape(DEVS, 1, VPER)
        all_vec = jnp.pad(all_vec, ((0, 0), (0, 15), (0, VCOLS - VPER))).reshape(D, VCOLS)
        right_blocks = [jnp.concatenate([whole[:, :, :HALF].reshape(D, HALF), all_vec], axis=1)]
        whole = in_order(lo_blocks, table, in_rows)
        outs = whole[:, :, HALF:].reshape(ndev, in_rows, 3, D).transpose(0, 2, 1, 3).reshape(DEVS, 3, 16, D)
        outs = outs.transpose(0, 2, 1, 3).reshape(D, HALF)
        lo_blocks = [jnp.concatenate([whole[:, :, :HALF].reshape(D, HALF), outs], axis=1)]

    x, grad_out, h, gate, hat, slope, scale, weight_right, vec = gate_forward(
        ktable, sides, patches, x_got, out_grad, g_got, right_blocks
    )
    spat, mm = spatial_mix(levels, sides, gate, spat_own, spat_got, [lo_second])
    gs, gated, q, gb, wl, wo, sp_keep, sp_send, gsum = middle(ktable, levels, sides, vec, h, spat, gate, grad_out, lo_blocks)
    sp_got = route.cross(sp_send) if fits else sp_send
    lo_keep, lo_send, mixed_stay, mixed_away, gh = weight_grads(
        ktable, levels, sides, vec, gated, q, gb, h, wl, wo, x, rows
    )
    mixed_got = route.cross(mixed_away)
    gp, gate_sum = gate_backward(vec, gs, mm, hat, slope, scale)
    after = [[], []]
    if fits:
        terms = [lo_keep, route.cross(lo_send)]
        terms, lo_part = route.next_term(terms, 0)
        sp_terms = [sp_keep, sp_got]
        sp_terms, _ = route.next_term(sp_terms, 0)
        after[0] = [sp_terms[-1]]
        sp_terms, _ = route.next_term(sp_terms, 1)
        after[1] = [sp_terms[-1]] + lo_part
    gwr, ghb = in_grads(gp, h, weight_right, gh, after[0])
    right_keep, right_send, grad_stay, grad_away = in_backward(
        ktable, sides, vec, gsum, gate_sum, gwr, ghb, x, grad_out, rows, after[1]
    )
    if fits:
        sp_own, *sends = line_spread(sp_terms)
        got = [route.swap(p, (m, m)) for p, m in zip(sends, route.direct)]
        spat_pieces = route.widen(line_sum(sp_own, got))
        right_terms = [right_keep, route.cross(right_send)]
        terms, _ = route.next_term(terms, 1)
        right_terms, _ = route.next_term(right_terms, 0)
        own, *sends = line_parts(terms)
        got = [route.swap(p, (m, m)) for p, m in zip(sends, route.direct)]
        right_terms, _ = route.next_term(right_terms, 1)
        left_sum, *new_out = finish_out(own, got, dense_out, out_first, out_second)
        own, *sends = line_parts(right_terms)
        got = [route.swap(p, (m, m)) for p, m in zip(sends, route.direct)]
        *new_in, vec_sum = finish_in(own, got, left_sum, dense_in, in_first, in_second)
        vec_sum = vec_sum[0, :vec_len]
        korder = order
    else:
        both = jnp.concatenate([lo_keep, lo_send])
        outs = both[:, HALF:LO].reshape(DEVS, 16, 3, D).transpose(0, 2, 1, 3).reshape(ndev, out_rows, D)
        outs = jnp.take(outs, table, axis=0).reshape(HALF, D)
        out_sum = route.scatter(outs[: HALF // 2], outs[HALF // 2 :])
        lefts = jnp.take(both[:, :HALF].reshape(ndev, in_rows, HALF), table, axis=0).reshape(D, HALF)
        left_sum = route.scatter(lefts[: D // 2], lefts[D // 2 :])
        per = 512 // route.n

        def spat_blocks(part, flip):
            flat = part.reshape(GROUPS, 16, 2, SCOLS).transpose(0, 2, 1, 3).reshape(route.n, per, SCOLS)
            return jnp.take(flat, route.order(flip)[0], axis=0).reshape(512, SCOLS)

        spat_part = route.scatter(spat_blocks(sp_keep, False), spat_blocks(sp_send, True)).astype(BF)
        flat = in_order(route.spread(spat_part), order, per).reshape(GROUPS, 2, 16, SCOLS)
        spat_pieces = [flat.transpose(0, 2, 1, 3).reshape(GROUPS * 16, SPC)]
        korder = jnp.arange(GROUPS, dtype=jnp.int32)
        both = jnp.concatenate([right_keep, right_send])
        vecs = jnp.take(both[::16, HALF : HALF + VPER].reshape(ndev, vec_len), table, axis=0)
        vec_sum = route.scatter(vecs[: route.n], vecs[route.n :]).reshape(vec_len)
        rights = jnp.take(both[:, :HALF].reshape(ndev, in_rows, HALF), table, axis=0).reshape(D, HALF)
        right_sum = route.scatter(rights[: D // 2], rights[D // 2 :])
        in_sum = jnp.concatenate([left_sum, right_sum], axis=1)
        new_in = adamw(dense_in, in_sum, in_first, in_second, DENSE_RATE, DENSE_DECAY)
        new_out = adamw(dense_out, out_sum, out_first, out_second, DENSE_RATE, DENSE_DECAY)

    def whole_images(stays, came):
        return jnp.concatenate([jnp.where(seq == 0, stays, came), jnp.where(seq == 0, came, stays)], axis=0)

    mixed = whole_images(mixed_stay, mixed_got)
    patches_grad = whole_images(grad_stay, route.cross(grad_away))
    new_vec = adamw(vectors, vec_sum, vec_first, vec_second, SMALL_RATE, 0.0)
    spat_new = spatial_update(korder, spat_pieces, spatial, spat_first, spat_second)
    new_bias = adamw(spatial_bias, spat_new[3].reshape(3, rows), bias_first, bias_second, SMALL_RATE, 0.0)
    return (mixed, patches_grad) + tuple(new_in) + tuple(new_out) + new_vec + tuple(spat_new[:3]) + new_bias


def solution(mesh):
    rows3 = P("dp", "seq", None)
    dense = P(AXES, None)
    vec = P(AXES)
    spat = P(None, "seq", None)
    bias = P(None, "seq")
    in_specs = (rows3, P("dp"), rows3, dense, dense, vec, spat, bias)
    in_specs += (dense,) * 4 + (vec,) * 2 + (spat,) * 2 + (bias,) * 2
    out_specs = (rows3, rows3) + (dense,) * 6 + (vec,) * 3 + (spat,) * 3 + (bias,) * 3
    return jax.shard_map(local, mesh=mesh, in_specs=in_specs, out_specs=out_specs, check_vma=False)
```

```python
import functools

import jax
import jax.numpy as jnp
from jax import lax
from jax.experimental import pallas as pl
from jax.experimental.pallas import tpu as pltpu
from jax.sharding import PartitionSpec as P

D = 512
FF = 3072
HALF = 1536
PMAX = 324
PPAD = 336
P_MID = 196
P_LOW = 100
VCOLS = 256
ROWS = 2 * PPAD
GROUPS = 16
DEVS = 2 * GROUPS
VPER = 240
SCOLS = 384
BIAS_AT = 336
TOTAL_AT = 324
LSTRIDE = 168
MIB = 1024 * 1024
STEP = 10

NORM_EPS = 1e-05
BETA_ONE = 0.9
BETA_TWO = 0.99
ADAM_EPS = 1e-08
DENSE_RATE = 0.02
SMALL_RATE = 0.2
DENSE_DECAY = 0.05

BF = jnp.bfloat16
F32 = jnp.float32
AXES = ("dp", "seq")
VM = pl.BlockSpec(memory_space=pltpu.VMEM)
SM = pl.BlockSpec(memory_space=pltpu.SMEM)
HB = pl.BlockSpec(memory_space=pl.ANY)


class Route:
    def __init__(self, n):
        bits = n.bit_length() - 1
        assert n == 1 << bits and bits >= 2
        self.n = n
        top = n // 4
        self.direct = [top, 2 * top, 3 * top]
        low = [1 << b for b in range(bits - 2)]
        self.low = list(zip(low[::-1], low))
        masks = [(0, 0)] + [(m, m) for m in self.direct]
        for step in self.low:
            masks = masks + [(m[0] ^ step[0], m[1] ^ step[1]) for m in masks]
        self.masks = masks

    def swap(self, block, mask):
        pairs = []
        for dp in range(self.n):
            for seq in range(2):
                pairs.append((dp * 2 + seq, (dp ^ mask[seq]) * 2 + seq))
        return lax.ppermute(block, AXES, pairs)

    def cross(self, block):
        pairs = []
        for dp in range(self.n):
            for seq in range(2):
                pairs.append((dp * 2 + seq, dp * 2 + 1 - seq))
        return lax.ppermute(block, AXES, pairs)

    def order(self, seq_flip):
        place = lax.axis_index("dp")
        seq = lax.axis_index("seq")
        if seq_flip:
            seq = 1 - seq
        zero = jnp.array([m[0] for m in self.masks], jnp.int32)
        one = jnp.array([m[1] for m in self.masks], jnp.int32)
        return place ^ jnp.where(seq == 0, zero, one), seq

    def table(self):
        mine, seq = self.order(False)
        other, flip = self.order(True)
        return jnp.concatenate([mine * 2 + seq, other * 2 + flip])

    def spread(self, shard):
        first = jnp.concatenate([shard] + [self.swap(shard, (m, m)) for m in self.direct], axis=0)
        return self.widen(first)

    def widen(self, first):
        blocks = [first]
        for step in self.low:
            blocks = blocks + [self.swap(b, step) for b in blocks]
        return blocks

    def widen_in_turn(self, first):
        second = self.swap(first, self.low[0])
        third = self.swap(first, self.low[1])
        return [first, second, third, self.swap(stack([second], third), self.low[1])]

    def gather(self, shard):
        blocks = self.spread(shard)
        return blocks + [self.cross(b) for b in blocks]

    def collect(self, terms):
        cur = terms[0].shape[0]
        rows = cur // self.n

        def part(lower, upper):
            total = terms[0][lower:upper].astype(F32)
            for t in terms[1:]:
                total = total + t[lower:upper].astype(F32)
            return total

        terms = list(terms)
        for step in reversed(self.low):
            half = cur // 2
            terms.append(self.swap(part(half, cur).astype(BF), step))
            cur = half
        got = []
        for j, m in enumerate(self.direct):
            got.append(self.swap(part((j + 1) * rows, (j + 2) * rows).astype(BF), (m, m)))
        total = part(0, rows)
        return (total + got[0].astype(F32)) + (got[1].astype(F32) + got[2].astype(F32))

    def scatter(self, keep, send):
        return self.collect([keep, self.cross(send)])


def dot(a, b, dims):
    return lax.dot_general(a, b, (dims, ((), ())), preferred_element_type=F32)


NN = ((1,), (0,))
NT = ((1,), (1,))
TN = ((0,), (0,))


def gelu_parts(p):
    bell = jnp.exp(p * p * -0.5)
    d = 1.0 + jnp.abs(p) * (0.3275911 * 0.7071067811865476)
    t = pl.reciprocal(d, approx=True)
    t = t * (2.0 - d * t)
    poly = t * (
        0.127414796
        + t * (-0.142248368 + t * (0.7107068705 + t * (-0.7265760135 + t * 0.5307027145)))
    )
    tail = poly * bell
    phi_sum = jnp.where(p >= 0.0, 1.0 - tail, tail)
    return p * phi_sum, phi_sum + p * bell * 0.3989422804014327


def count_of(level):
    return jnp.where(level == 0, P_LOW, jnp.where(level == 1, P_MID, PMAX))


def masked_mix(mix, count):
    i = lax.broadcasted_iota(jnp.int32, (PPAD, SCOLS), 0)
    j = lax.broadcasted_iota(jnp.int32, (PPAD, SCOLS), 1)
    return jnp.where((i < count) & (j < count), mix.astype(F32), 0.0).astype(BF)


def live_rows(count, shape, start=0):
    return lax.broadcasted_iota(jnp.int32, shape, 0) + start < count


def live_mask(levels_ref, b, width):
    return live_rows(count_of(levels_ref[b]), (PPAD, width))


def fold(value):
    total = value[:, 0:128]
    for n in range(128, value.shape[1], 128):
        total = total + value[:, n : n + 128]
    return total


def spread_sum(ref, factor):
    return jnp.broadcast_to(jnp.sum(ref[...], axis=-1, keepdims=True) * factor, ref.shape)


def wide(value, times):
    return jnp.concatenate([value] * times, axis=1)


def start_blocks(table_ref, pieces, rows, cols, target, sem, extra=0):
    copies = []
    k = 0
    for piece in pieces:
        for j in range(piece.shape[0] // 16):
            at = pl.multiple_of(table_ref[k] * rows, 16)
            c = pltpu.make_async_copy(
                piece.at[pl.ds(j * 16, 16), pl.ds(cols[0], cols[1])], target.at[pl.ds(at + extra, 16)], sem.at[k]
            )
            c.start()
            copies.append(c)
            k += 1
    return copies


def row_loop(step, body):
    def run(i, carry):
        body(pl.multiple_of(i * step, step))
        return carry

    lax.fori_loop(0, ROWS // step, run, 0)


def call(kernel, out_shape, in_specs, scratch, flops, nbytes, *args, room=12):
    vm = pl.BlockSpec(memory_space=pltpu.VMEM)
    return pl.pallas_call(
        kernel,
        out_shape=out_shape,
        in_specs=in_specs,
        out_specs=jax.tree.map(lambda _: vm, out_shape),
        scratch_shapes=scratch,
        compiler_params=pltpu.CompilerParams(vmem_limit_bytes=room * MIB),
        cost_estimate=pl.CostEstimate(flops=flops, bytes_accessed=nbytes, transcendentals=0),
    )(*args)


def norm_parts(values):
    center = values - jnp.mean(values, axis=-1, keepdims=True)
    scale = lax.rsqrt(jnp.mean(center * center, axis=-1, keepdims=True) + NORM_EPS)
    return center * scale, scale


VSEG = {
    "g1": (0, D),
    "b1": (D, D),
    "c1l": (2 * D, HALF),
    "c1r": (2 * D + HALF, HALF),
    "g2": (2 * D + FF, HALF),
    "b2": (2 * D + FF + HALF, HALF),
    "c2": (2 * D + FF + 2 * HALF, D),
}
VEC = 2 * D + FF + 2 * HALF + D


def seg(ref, name):
    start, size = VSEG[name]
    return ref[0:1, start : start + size]

def adamw(weight, grad, first, second, rate, decay):
    first = BETA_ONE * first + (1.0 - BETA_ONE) * grad
    second = BETA_TWO * second + (1.0 - BETA_TWO) * grad * grad
    first_hat = first / (1.0 - BETA_ONE**STEP)
    second_hat = second / (1.0 - BETA_TWO**STEP)
    weight = weight - rate * (first_hat / (jnp.sqrt(second_hat) + ADAM_EPS) + decay * weight)
    return (weight, first, second)


CHUNK = 16
TILE = 256
BODY = 32
STRIPE = 112
LO = 2 * HALF
SPC = 2 * SCOLS


def sds(shape, dtype):
    return jax.ShapeDtypeStruct(shape, dtype)


def pack_dense(dense_in, dense_out, vec_row):
    rows = dense_in.shape[0]
    per = vec_row.shape[1]

    def kernel(w_hbm, o_hbm, v_ref, out_ref, lo_ref, w_ref, o_ref, row, sem):
        first = pltpu.make_async_copy(w_hbm, w_ref, sem.at[0])
        second = pltpu.make_async_copy(o_hbm, o_ref, sem.at[1])
        first.start()
        second.start()
        row[...] = jnp.zeros_like(row)
        row[0:1, 0:per] = v_ref[...]
        out_ref[:, HALF:] = row[...].astype(BF)
        first.wait()
        out_ref[:, 0:HALF] = w_ref[:, HALF:].astype(BF)
        lo_ref[:, 0:HALF] = w_ref[:, 0:HALF].astype(BF)
        second.wait()
        for g in range(3):
            lo_ref[:, HALF + g * D : HALF + (g + 1) * D] = o_ref[g * rows : (g + 1) * rows, :].astype(BF)

    scratch = [
        pltpu.VMEM(dense_in.shape, F32),
        pltpu.VMEM(dense_out.shape, F32),
        pltpu.VMEM((rows, VCOLS), F32),
        pltpu.SemaphoreType.DMA((2,)),
    ]
    shapes = (sds((rows, HALF + VCOLS), BF), sds((rows, LO), BF))
    return call(kernel, shapes, [HB, HB, VM], scratch, 1000, 600000, dense_in, dense_out, vec_row)


def pack_images(sides, spatial, bias_col, patches, out_grad):
    half = patches.shape[1]

    def kernel(sides_ref, s_ref, b_ref, x_ref, g_ref, spat_ref, xs_ref, gs_ref, buf):
        away = 2 - 2 * sides_ref[0]
        for b in range(2):
            xs_ref[b] = x_ref[away + b]
            gs_ref[b] = g_ref[away + b]
        buf[...] = jnp.zeros_like(buf)
        for level in range(3):
            buf[:, 0:PMAX] = s_ref[level]
            rest = b_ref[level]
            for c in range(3):
                piece = rest.astype(BF).astype(F32)
                buf[:, BIAS_AT + c : BIAS_AT + c + 1] = piece
                rest = rest - piece
            spat_ref[level] = buf[...].astype(BF)

    pair = sds((2, half, D), BF)
    return call(
        kernel,
        (sds((3, half, SCOLS), BF), pair, pair),
        [SM] + [VM] * 4,
        [pltpu.VMEM((half, SCOLS), F32)],
        1000,
        3000000,
        sides,
        spatial,
        bias_col,
        patches,
        out_grad,
    )


def stack(pieces, after):
    count = len(pieces)
    rows, cols = pieces[0].shape

    def kernel(*refs):
        for k in range(count):
            refs[count + 1][k * rows : (k + 1) * rows, :] = refs[k][...]

    return call(kernel, sds((count * rows, cols), BF), [VM] * count + [HB], [], 1000, 1000000, *pieces, after)


def two_halves(is_first, own, got):
    own = own.astype(F32)
    got = got.astype(F32)
    return jnp.where(is_first, own, got), jnp.where(is_first, got, own)


def gate_norm(levels, sides, vec, v, part, spat_own, spat_got, after):
    half = spat_own.shape[1]
    count = len(after)

    def kernel(levels_ref, sides_ref, vec_ref, v_ref, part_ref, so_ref, sg_ref, *refs):
        gate_ref, hat_ref, scale_ref, spat_ref, mm_ref, mixf, mean, buf = refs[count:]
        is_first = sides_ref[0] == 0
        g_start = VSEG["g2"][0]
        b_start = VSEG["b2"][0]
        mean[...] = spread_sum(part_ref, 1.0 / HALF)

        def square_rows(r):
            for k in range(0, BODY, CHUNK):
                rows = pl.ds(r + k, CHUNK)
                mid = mean[rows, :]
                total = jnp.zeros((CHUNK, 128), F32)
                for n in range(0, HALF, 128):
                    center = v_ref[rows, n : n + 128] - mid
                    total = total + center * center
                buf[rows, :] = total

        row_loop(BODY, square_rows)
        scale_ref[...] = lax.rsqrt(spread_sum(buf, 1.0 / HALF) + NORM_EPS)

        def gate_rows(r):
            for k in range(0, BODY, CHUNK):
                rows = pl.ds(r + k, CHUNK)
                mid = wide(mean[rows, :], 2)
                scale = wide(scale_ref[rows, :], 2)
                for n in range(0, HALF, TILE):
                    hat = (v_ref[rows, n : n + TILE] - mid) * scale
                    hat_ref[rows, n : n + TILE] = hat.astype(BF)
                    gate = hat * vec_ref[0:1, g_start + n : g_start + n + TILE]
                    gate = (gate + vec_ref[0:1, b_start + n : b_start + n + TILE]).astype(BF)
                    gate_ref[rows, n : n + TILE] = gate

        row_loop(BODY, gate_rows)
        gate_ref[ROWS:, :] = jnp.zeros((SCOLS - PPAD, HALF), BF)
        for b in range(2):
            level = levels_ref[b]
            live = count_of(level)
            one, two = two_halves(is_first, so_ref[level], sg_ref[level])
            mixf[0:half, :] = one
            mixf[half : 2 * half, :] = two
            mixf[2 * half :, :] = jnp.zeros((PPAD - 2 * half, SCOLS), F32)
            bias = jnp.sum(mixf[:, TOTAL_AT:], axis=-1, keepdims=True)
            mm_ref[b] = masked_mix(mixf[...], live)

            def mix_tile(n, carry):
                cols = pl.ds(pl.multiple_of(n * 512, 512), 512)
                got = dot(mm_ref[b], gate_ref[b * PPAD : b * PPAD + SCOLS, cols], NN) + bias
                got = jnp.where(live_rows(live, (PPAD, 512)), got, 0.0)
                spat_ref[b * PPAD : (b + 1) * PPAD, cols] = got.astype(BF)
                return carry

            lax.fori_loop(0, HALF // 512, mix_tile, 0)

    return call(
        kernel,
        (
            sds((ROWS + SCOLS - PPAD, HALF), BF),
            sds((ROWS, HALF), BF),
            sds((ROWS, 128), F32),
            sds((ROWS, HALF), BF),
            sds((2, PPAD, SCOLS), BF),
        ),
        [SM] * 2 + [VM] * 5 + [HB] * count,
        [pltpu.VMEM((PPAD, SCOLS), F32), pltpu.VMEM((ROWS, 128), F32), pltpu.VMEM((ROWS, 128), F32)],
        6000000000,
        12000000,
        levels,
        sides,
        vec,
        v,
        part,
        spat_own,
        spat_got,
        *after,
        room=22,
    )


def gate_forward(table, sides, patches, x_got, out_grad, g_got, pieces):
    count = len(pieces)
    half = patches.shape[1]

    def kernel(table_ref, sides_ref, p_ref, xg_ref, o_ref, gg_ref, *refs):
        ins = refs[:count]
        outs = refs[count : count + 8]
        x_ref, og_ref, h_ref, pre, slope_ref, part, w_ref, vec_ref = outs
        vblk, xbuf, sem, vsem = refs[count + 8 :]
        vcopies = start_blocks(table_ref, ins, 16, (HALF, VCOLS), vblk, vsem)
        copies = start_blocks(table_ref, ins, 16, (0, HALF), w_ref, sem)
        me = sides_ref[0]
        is_first = me == 0

        for src, got, target in ((o_ref, gg_ref, og_ref), (p_ref, xg_ref, x_ref)):
            for b in range(2):
                one, two = two_halves(is_first, src[2 * me + b], got[b])
                xbuf[b * PPAD : b * PPAD + half, :] = one
                xbuf[b * PPAD + half : b * PPAD + 2 * half, :] = two
                xbuf[b * PPAD + 2 * half : (b + 1) * PPAD, :] = jnp.zeros((PPAD - 2 * half, D), F32)
            target[...] = xbuf[...].astype(BF)
        for c in vcopies:
            c.wait()
        for s in range(DEVS):
            row = vblk[16 * s : 16 * s + 16, :].astype(F32)[0:1, :VPER]
            vec_ref[0:1, VPER * s : VPER * s + VPER] = row

        def norm_one(r):
            hat, _ = norm_parts(xbuf[pl.ds(r, STRIPE), :])
            h_ref[pl.ds(r, STRIPE), :] = (hat * seg(vec_ref, "g1") + seg(vec_ref, "b1")).astype(BF)

        row_loop(STRIPE, norm_one)
        for c in copies:
            c.wait()
        c_start = VSEG["c1r"][0]

        def matmul(n, carry):
            at = pl.multiple_of(n * TILE, TILE)
            pre[:, pl.ds(at, TILE)] = dot(h_ref[...], w_ref[:, pl.ds(at, TILE)], NN)
            return carry

        lax.fori_loop(0, HALF // TILE, matmul, 0)

        def gelu_rows(r):
            for k in range(0, BODY, CHUNK):
                rows = pl.ds(r + k, CHUNK)
                total = jnp.zeros((CHUNK, 128), F32)
                for n in range(0, HALF, TILE):
                    v, slope = gelu_parts(pre[rows, n : n + TILE] + vec_ref[0:1, c_start + n : c_start + n + TILE])
                    pre[rows, n : n + TILE] = v
                    slope_ref[rows, n : n + TILE] = slope.astype(BF)
                    total = total + fold(v)
                part[rows, :] = total

        row_loop(BODY, gelu_rows)

    broad = sds((ROWS, HALF), BF)
    narrow = sds((ROWS, D), BF)
    out_shape = (
        narrow,
        narrow,
        narrow,
        sds((ROWS, HALF), F32),
        broad,
        sds((ROWS, 128), F32),
        sds((D, HALF), BF),
        sds((1, VEC), F32),
    )
    scratch = [
        pltpu.VMEM((D, VCOLS), BF),
        pltpu.VMEM((ROWS, D), F32),
        pltpu.SemaphoreType.DMA((DEVS,)),
        pltpu.SemaphoreType.DMA((DEVS,)),
    ]
    return call(
        kernel,
        out_shape,
        [SM] * 2 + [VM] * 4 + [HB] * count,
        scratch,
        10000000000,
        20000000,
        table,
        sides,
        patches,
        x_got,
        out_grad,
        g_got,
        *pieces,
        room=26,
    )


def split_rows(target, first, second, seq, value):
    half = first.shape[1]
    target[...] = value
    for b in range(2):
        one = target[b * PPAD : b * PPAD + half, :]
        two = target[b * PPAD + half : b * PPAD + 2 * half, :]
        first[b] = jnp.where(seq == 0, one, two).astype(BF)
        second[b] = jnp.where(seq == 0, two, one).astype(BF)


def middle(table, levels, sides, vec, h, spat, gate, grad_out, pieces):
    count = len(pieces)

    def kernel(table_ref, levels_ref, sides_ref, vec_ref, h_ref, spat_ref, gate_ref, og_ref, *refs):
        ins = refs[:count]
        gs_ref, gated_ref, q_ref, gb, wl, wo, keep, send, gsum_ref = refs[count : count + 9]
        pbuf, gbuf, cells, flat, sem = refs[count + 9 :]
        copies = start_blocks(table_ref, ins, 16, (0, HALF), wl, sem.at[0])
        for g in range(3):
            copies += start_blocks(table_ref, ins, 48, (HALF + g * D, D), wo, sem.at[1 + g], 16 * g)
        for b in range(2):
            rows = slice(b * PPAD, (b + 1) * PPAD)
            gb[rows, :] = jnp.where(live_mask(levels_ref, b, D), og_ref[rows, :].astype(F32), 0.0).astype(BF)
        gsum_ref[0:1, HALF : HALF + D] = jnp.sum(gb[...].astype(F32), axis=0, keepdims=True)
        cells[...] = jnp.zeros_like(cells)
        flat[...] = jnp.zeros_like(flat)
        for c in copies:
            c.wait()
        c_start = VSEG["c1l"][0]

        def tile(n, carry):
            at = pl.multiple_of(n * TILE, TILE)
            cols = pl.ds(at, TILE)
            pbuf[...] = dot(h_ref[...], wl[:, cols], NN)
            gbuf[...] = dot(gb[...], wo[cols, :], NT)
            shift = vec_ref[0:1, pl.ds(c_start + at, TILE)]
            total = jnp.zeros((CHUNK, TILE), F32)
            for k in range(0, ROWS, CHUNK):
                r = slice(k, k + CHUNK)
                u, slope = gelu_parts(pbuf[r, :] + shift)
                sp = spat_ref[r, cols].astype(F32)
                gg = gbuf[r, :]
                gated_ref[r, cols] = (u * sp).astype(BF)
                gs_ref[r, cols] = (gg * u).astype(BF)
                q = (gg * sp * slope).astype(BF)
                q_ref[r, cols] = q
                total = total + q.astype(F32)
            gsum_ref[0:1, cols] = jnp.sum(total, axis=0, keepdims=True)
            return carry

        lax.fori_loop(0, HALF // TILE, tile, 0)

        me = sides_ref[0]
        for b in range(2):
            level = levels_ref[b]
            count_b = count_of(level)
            gs = gs_ref[b * PPAD : (b + 1) * PPAD, :]
            got = dot(gs, gate_ref[b * PPAD : (b + 1) * PPAD, :], NT)
            sums = jnp.sum(gs.astype(F32), axis=-1, keepdims=True)
            j = lax.broadcasted_iota(jnp.int32, (PPAD, PPAD), 1)
            got = jnp.where(j < count_b, got, jnp.where(j == TOTAL_AT, sums, 0.0))
            cells[level, :, 0:PPAD] += got
        part = PMAX // 2
        for level in range(3):
            for k in range(2):
                flat[k, level * LSTRIDE : level * LSTRIDE + part, 0:PPAD] = cells[level, k * part : (k + 1) * part, 0:PPAD]
        for k in range(DEVS):
            target, side = (keep, me) if k < GROUPS else (send, 1 - me)
            r = pl.ds(k % GROUPS * 16, 16)
            block = flat[side, pl.ds(pl.multiple_of(sides_ref[1 + k] * 32, 32), 32), :].astype(BF)
            target[r, 0:SCOLS] = block[0:16]
            target[r, SCOLS:SPC] = block[16:32]

    broad = sds((ROWS, HALF), BF)
    payload = sds((D // 2, SPC), BF)
    out_shape = (
        broad,
        broad,
        broad,
        sds((ROWS, D), BF),
        sds((D, HALF), BF),
        sds((HALF, D), BF),
        payload,
        payload,
        sds((1, HALF + D), F32),
    )
    scratch = [
        pltpu.VMEM((ROWS, TILE), F32),
        pltpu.VMEM((ROWS, TILE), F32),
        pltpu.VMEM((3, PPAD, SCOLS), F32),
        pltpu.VMEM((2, 512, SCOLS), F32),
        pltpu.SemaphoreType.DMA((4, DEVS)),
    ]
    return call(
        kernel,
        out_shape,
        [SM] * 3 + [VM] * 5 + [HB] * count,
        scratch,
        8000000000,
        16000000,
        table,
        levels,
        sides,
        vec,
        h,
        spat,
        gate,
        grad_out,
        *pieces,
        room=28,
    )


def weight_grads(table, levels, sides, vec, gated, q, gb, h, wl, wo, x, half):
    def kernel(
        table_ref, levels_ref, sides_ref, vec_ref, t_ref, q_ref, gb_ref, h_ref, wl_ref, wo_ref, x_ref,
        keep, send, stay_ref, away_ref, gh_ref, branch, gwo, gwl,
    ):
        def out_tile(n, carry):
            cols = pl.ds(pl.multiple_of(n * TILE, TILE), TILE)
            gwo[cols, :] = dot(t_ref[:, cols], gb_ref[...], TN).astype(BF)
            return carry

        lax.fori_loop(0, HALF // TILE, out_tile, 0)

        def in_tile(n, carry):
            cols = pl.ds(pl.multiple_of(n * TILE, TILE), TILE)
            gwl[cols, :] = dot(h_ref[:, cols], q_ref[...], TN).astype(BF)
            branch[:, cols] = dot(t_ref[...], wo_ref[:, cols], NN)
            gh_ref[:, cols] = dot(q_ref[...], wl_ref[cols, :], NT)
            return carry

        lax.fori_loop(0, D // TILE, in_tile, 0)
        me = sides_ref[0]
        live = jnp.concatenate([live_mask(levels_ref, b, D) for b in range(2)], axis=0)
        out = branch[...] + seg(vec_ref, "c2")
        split_rows(branch, stay_ref, away_ref, me, x_ref[...].astype(F32) + jnp.where(live, out, 0.0))
        for k in range(DEVS):
            dev = table_ref[k]
            target = keep if k < GROUPS else send
            r = pl.ds(k % GROUPS * 16, 16)
            target[r, 0:HALF] = gwl[pl.ds(pl.multiple_of(dev * 16, 16), 16), :]
            for g in range(3):
                target[r, HALF + g * D : HALF + (g + 1) * D] = gwo[pl.ds(pl.multiple_of(dev * 48 + 16 * g, 16), 16), :]

    pair = sds((2, half, D), BF)
    payload = sds((D // 2, LO), BF)
    return call(
        kernel,
        (payload, payload, pair, pair, sds((ROWS, D), F32)),
        [SM] * 3 + [VM] * 8,
        [pltpu.VMEM((ROWS, D), F32), pltpu.VMEM((HALF, D), BF), pltpu.VMEM((D, HALF), BF)],
        5000000000,
        15000000,
        table,
        levels,
        sides,
        vec,
        gated,
        q,
        gb,
        h,
        wl,
        wo,
        x,
        room=24,
    )


def gate_backward(vec, gs, mm, hat, slope, scale, after):
    count = len(after)

    def kernel(vec_ref, gs_ref, mm_ref, hat_ref, slope_ref, scale_ref, *refs):
        gp, gsum_ref, dbuf, one, two, acc = refs[count:]

        for b in range(2):

            def mix_tile(n, carry):
                cols = pl.ds(pl.multiple_of(n * 512, 512), 512)
                got = dot(mm_ref[b], gs_ref[b * PPAD : (b + 1) * PPAD, cols], TN)
                dbuf[b * PPAD : (b + 1) * PPAD, cols] = got[0:PPAD]
                return carry

            lax.fori_loop(0, HALF // 512, mix_tile, 0)
        g_start = VSEG["g2"][0]

        def sum_rows(r):
            for k in range(0, BODY, CHUNK):
                rows = pl.ds(r + k, CHUNK)
                a = jnp.zeros((CHUNK, 128), F32)
                c = jnp.zeros((CHUNK, 128), F32)
                for n in range(0, HALF, TILE):
                    e = dbuf[rows, n : n + TILE] * vec_ref[0:1, g_start + n : g_start + n + TILE]
                    a = a + fold(e)
                    c = c + fold(e * hat_ref[rows, n : n + TILE].astype(F32))
                one[rows, :] = a
                two[rows, :] = c

        row_loop(BODY, sum_rows)
        one[...] = spread_sum(one, 1.0 / HALF)
        two[...] = spread_sum(two, 1.0 / HALF)
        acc[...] = jnp.zeros_like(acc)

        def grad_rows(r):
            for n in range(0, HALF, TILE):
                gain = vec_ref[0:1, g_start + n : g_start + n + TILE]
                sums = [jnp.zeros((CHUNK, TILE), F32) for _ in range(3)]
                for k in range(0, BODY, CHUNK):
                    rows = pl.ds(r + k, CHUNK)
                    d = dbuf[rows, n : n + TILE]
                    xh = hat_ref[rows, n : n + TILE].astype(F32)
                    inner = d * gain - wide(one[rows, :], 2) - xh * wide(two[rows, :], 2)
                    q = inner * wide(scale_ref[rows, :], 2) * slope_ref[rows, n : n + TILE].astype(F32)
                    q = q.astype(BF)
                    gp[rows, n : n + TILE] = q
                    sums = [sums[0] + d * xh, sums[1] + d, sums[2] + q.astype(F32)]
                for i in range(3):
                    acc[i, :, n : n + TILE] += sums[i]

        row_loop(BODY, grad_rows)
        for i in range(3):
            gsum_ref[0:1, i * HALF : (i + 1) * HALF] = jnp.sum(acc[i], axis=0, keepdims=True)

    return call(
        kernel,
        (sds((ROWS, HALF), BF), sds((1, 3 * HALF), F32)),
        [VM] * 6 + [HB] * count,
        [
            pltpu.VMEM((ROWS, HALF), F32),
            pltpu.VMEM((ROWS, 128), F32),
            pltpu.VMEM((ROWS, 128), F32),
            pltpu.VMEM((3, CHUNK, HALF), F32),
        ],
        3000000000,
        10000000,
        vec,
        gs,
        mm,
        hat,
        slope,
        scale,
        *after,
        room=20,
    )


def in_grads(gp, h, w, gh, after):
    count = len(after)

    def kernel(gp_ref, h_ref, w_ref, gh_ref, *refs):
        gwr, ghb = refs[count:]

        def in_tile(n, carry):
            cols = pl.ds(pl.multiple_of(n * TILE, TILE), TILE)
            ghb[:, cols] = gh_ref[:, cols] + dot(gp_ref[...], w_ref[cols, :], NT)
            gwr[cols, :] = dot(h_ref[:, cols], gp_ref[...], TN).astype(BF)
            return carry

        lax.fori_loop(0, D // TILE, in_tile, 0)

    return call(
        kernel,
        (sds((D, HALF), BF), sds((ROWS, D), F32)),
        [VM] * 4 + [HB] * count,
        [],
        3000000000,
        8000000,
        gp,
        h,
        w,
        gh,
        *after,
        room=14,
    )


def in_backward(table, sides, vec, gsum, gate_sum, gwr, ghb, x, grad_out, half, after):
    count = len(after)

    def kernel(table_ref, sides_ref, vec_ref, gsum_ref, gate_ref, gwr, ghb, x_ref, og_ref, *refs):
        keep, send, send_up, stay_ref, away_ref, acc, gvec, blocks, pgb = refs[count:]

        def put(name, value):
            start, size = VSEG[name]
            gvec[0:1, start : start + size] = value

        put("g2", gate_ref[0:1, 0:HALF])
        put("b2", gate_ref[0:1, HALF : 2 * HALF])
        put("c1r", gate_ref[0:1, 2 * HALF : 3 * HALF])
        put("c1l", gsum_ref[0:1, 0:HALF])
        put("c2", gsum_ref[0:1, HALF : HALF + D])
        acc[...] = jnp.zeros_like(acc)
        def in_rows(r):
            rows = pl.ds(r, STRIPE)
            xh, scale = norm_parts(x_ref[rows, :].astype(F32))
            d = ghb[rows, :]
            e = d * seg(vec_ref, "g1")
            one = jnp.mean(e, axis=-1, keepdims=True)
            two = jnp.mean(e * xh, axis=-1, keepdims=True)
            pgb[rows, :] = og_ref[rows, :].astype(F32) + scale * (e - one - xh * two)
            acc[0:1, :] += jnp.sum(d * xh, axis=0, keepdims=True)
            acc[1:2, :] += jnp.sum(d, axis=0, keepdims=True)

        row_loop(STRIPE, in_rows)
        put("g1", acc[0:1, :])
        put("b1", acc[1:2, :])
        split_rows(pgb, stay_ref, away_ref, sides_ref[0], pgb[...])
        blocks[...] = jnp.zeros_like(blocks)
        for s in range(DEVS):
            blocks[s, 0:1, 0:VPER] = gvec[0:1, VPER * s : VPER * s + VPER]
        for k in range(DEVS):
            dev = table_ref[k]
            target = keep if k < GROUPS else send if k < GROUPS * 3 // 2 else send_up
            r = pl.ds(k % (GROUPS if k < GROUPS else GROUPS // 2) * 16, 16)
            target[r, 0:HALF] = gwr[pl.ds(pl.multiple_of(dev * 16, 16), 16), :]
            target[r, HALF : HALF + VCOLS] = blocks[dev].astype(BF)

    payload = sds((D // 2, HALF + VCOLS), BF)
    part = sds((D // 4, HALF + VCOLS), BF)
    pair = sds((2, half, D), BF)
    return call(
        kernel,
        (payload, part, part, pair, pair),
        [SM] * 2 + [VM] * 7 + [HB] * count,
        [
            pltpu.VMEM((8, D), F32),
            pltpu.VMEM((1, VEC), F32),
            pltpu.VMEM((DEVS, 16, VCOLS), F32),
            pltpu.VMEM((ROWS, D), F32),
        ],
        2000000000,
        6000000,
        table,
        sides,
        vec,
        gsum,
        gate_sum,
        gwr,
        ghb,
        x,
        grad_out,
        *after,
        room=16,
    )


def add_part(terms, size, after, places=None):
    cols = terms[0].shape[1]
    count = len(terms)

    def kernel(*refs):
        for r in range(0, size, 16):
            rows = slice(r, r + 16)
            value = refs[0][rows, :].astype(F32)
            for t in refs[1:count]:
                value = value + t[rows, :].astype(F32)
            refs[count + len(after)][rows, :] = value.astype(BF)

    places = places or [1] * count
    blocks = [pl.BlockSpec((size, cols), lambda i, p=p: (p, 0)) for p in places]
    return pl.pallas_call(
        kernel,
        grid=(1,),
        out_shape=sds((size, cols), BF),
        in_specs=blocks + [HB] * len(after),
        out_specs=pl.BlockSpec((size, cols), lambda i: (0, 0)),
        compiler_params=pltpu.CompilerParams(vmem_limit_bytes=10 * MIB),
        cost_estimate=pl.CostEstimate(flops=1000000, bytes_accessed=3000000, transcendentals=0),
    )(*terms, *after)


def line_parts(terms, after):
    cols = terms[0].shape[1]
    count = len(terms)

    def kernel(*refs):
        own, outs = refs[count + 1], refs[count + 2 :]
        for m in range(4):
            rows = slice(16 * m, 16 * (m + 1))
            value = refs[0][rows, :].astype(F32)
            for t in refs[1:count]:
                value = value + t[rows, :].astype(F32)
            if m == 0:
                own[...] = value
            else:
                outs[m - 1][...] = value.astype(BF)

    block = pl.BlockSpec((64, cols), lambda i: (0, 0))
    one = pl.BlockSpec((16, cols), lambda i: (0, 0))
    return pl.pallas_call(
        kernel,
        grid=(1,),
        out_shape=[sds((16, cols), F32)] + [sds((16, cols), BF)] * 3,
        in_specs=[block] * count + [HB],
        out_specs=[one] * 4,
        compiler_params=pltpu.CompilerParams(vmem_limit_bytes=8 * MIB),
        cost_estimate=pl.CostEstimate(flops=1000000, bytes_accessed=3000000, transcendentals=0),
    )(*terms, after)


def line_sum(total, got, after):
    rows = total.shape[0]

    def kernel(own_ref, a_ref, b_ref, c_ref, after_ref, out_ref):
        near = own_ref[...].astype(F32) + a_ref[...].astype(F32)
        far = b_ref[...].astype(F32) + c_ref[...].astype(F32)
        out_ref[...] = (near + far).astype(BF)

    return call(kernel, sds((rows, SPC), BF), [VM] * 4 + [HB], [], 1000000, 500000, total, *got, after)


def line_spread(terms, after):
    count = len(terms)
    cols = terms[0].shape[1]

    def kernel(*refs):
        outs = refs[count + 1 :]
        for m in range(4):
            rows = slice(16 * m, 16 * (m + 1))
            value = refs[0][rows, :].astype(F32)
            for t in refs[1:count]:
                value = value + t[rows, :].astype(F32)
            value = value.astype(BF)
            for j in range(4):
                at = 16 * (m ^ j)
                outs[j][at : at + 16, :] = value

    block = pl.BlockSpec((64, cols), lambda i: (0, 0))
    return pl.pallas_call(
        kernel,
        grid=(1,),
        out_shape=[sds((64, cols), BF)] * 4,
        in_specs=[block] * count + [HB],
        out_specs=[block] * 4,
        compiler_params=pltpu.CompilerParams(vmem_limit_bytes=8 * MIB),
        cost_estimate=pl.CostEstimate(flops=1000000, bytes_accessed=1000000, transcendentals=0),
    )(*terms, after)


def finish_out(own, got, weight, first, second, after):
    def kernel(own_ref, a_ref, b_ref, c_ref, w_ref, m_ref, s_ref, after_ref, left_ref, nw, nm, ns):
        total = own_ref[...] + a_ref[...].astype(F32)
        total = total + (b_ref[...].astype(F32) + c_ref[...].astype(F32))
        left_ref[...] = total[:, 0:HALF]
        for g in range(3):
            rows = slice(16 * g, 16 * (g + 1))
            grad = total[:, HALF + g * D : HALF + (g + 1) * D]
            new = adamw(w_ref[rows, :], grad, m_ref[rows, :], s_ref[rows, :], DENSE_RATE, DENSE_DECAY)
            nw[rows, :] = new[0]
            nm[rows, :] = new[1]
            ns[rows, :] = new[2]

    same = sds(weight.shape, F32)
    return call(
        kernel,
        (sds((16, HALF), F32), same, same, same),
        [VM] * 7 + [HB],
        [],
        1000000,
        2000000,
        own,
        *got,
        weight,
        first,
        second,
        after,
    )


def finish_in(own, got, left, weight, first, second, after):
    def kernel(own_ref, a_ref, b_ref, c_ref, l_ref, w_ref, m_ref, s_ref, after_ref, nw, nm, ns, vec_ref):
        total = own_ref[...] + a_ref[...].astype(F32)
        total = total + (b_ref[...].astype(F32) + c_ref[...].astype(F32))
        vec_ref[...] = total[0:1, HALF:]
        for cols, grad in ((slice(0, HALF), l_ref[...]), (slice(HALF, FF), total[:, 0:HALF])):
            new = adamw(w_ref[:, cols], grad, m_ref[:, cols], s_ref[:, cols], DENSE_RATE, DENSE_DECAY)
            nw[:, cols] = new[0]
            nm[:, cols] = new[1]
            ns[:, cols] = new[2]

    same = sds(weight.shape, F32)
    return call(
        kernel,
        (same, same, same, sds((1, VCOLS), F32)),
        [VM] * 8 + [HB],
        [],
        1000000,
        2000000,
        own,
        *got,
        left,
        weight,
        first,
        second,
        after,
    )


def spatial_update(order, pieces, spatial, first, second, bias, bias_first, bias_second, after):
    count = len(pieces)
    rows = spatial.shape[1]

    def kernel(order_ref, *refs):
        ins = refs[:count]
        w_ref, m_ref, s_ref, bw, bm, bs = refs[count : count + 6]
        nw, nm, ns, nbw, nbm, nbs, flat = refs[count + 6 + len(after) :]
        k = 0
        for piece in ins:
            for j in range(piece.shape[0] // 16):
                at = pl.multiple_of(order_ref[k] * 32, 32)
                block = piece[16 * j : 16 * j + 16, :].astype(F32)
                flat[pl.ds(at, 16), :] = block[:, 0:SCOLS]
                flat[pl.ds(at + 16, 16), :] = block[:, SCOLS:]
                k += 1
        at = TOTAL_AT // 128 * 128
        totals = flat[:, at : at + 128].T[TOTAL_AT - at : TOTAL_AT - at + 1, :]
        for level in range(3):
            got = flat[level * LSTRIDE : level * LSTRIDE + rows, :]
            new = adamw(w_ref[level], got[:, 0:PMAX], m_ref[level], s_ref[level], DENSE_RATE, DENSE_DECAY)
            nw[level] = new[0]
            nm[level] = new[1]
            ns[level] = new[2]
            got = totals[:, level * LSTRIDE : level * LSTRIDE + rows]
            r = slice(level, level + 1)
            new = adamw(bw[r, :], got, bm[r, :], bs[r, :], SMALL_RATE, 0.0)
            nbw[r, :] = new[0]
            nbm[r, :] = new[1]
            nbs[r, :] = new[2]

    same = sds(spatial.shape, F32)
    small = sds(bias.shape, F32)
    return call(
        kernel,
        (same, same, same, small, small, small),
        [SM] + [VM] * (count + 6) + [HB] * len(after),
        [pltpu.VMEM((512, SCOLS), F32)],
        10000000,
        6000000,
        order,
        *pieces,
        spatial,
        first,
        second,
        bias,
        bias_first,
        bias_second,
        *after,
    )


def in_order(blocks, table, rows):
    cols = blocks[0].shape[1]
    whole = jnp.concatenate(blocks, axis=0).reshape(-1, rows, cols)
    back = jnp.zeros_like(table).at[table].set(jnp.arange(table.shape[0], dtype=table.dtype))
    return jnp.take(whole, back, axis=0)


def local(
    patches,
    resolution,
    out_grad,
    dense_in,
    dense_out,
    vectors,
    spatial,
    spatial_bias,
    in_first,
    in_second,
    out_first,
    out_second,
    vec_first,
    vec_second,
    spat_first,
    spat_second,
    bias_first,
    bias_second,
):
    route = Route(lax.axis_size("dp"))
    ndev = 2 * route.n
    fits = route.n == GROUPS
    seq = lax.axis_index("seq").astype(jnp.int32)
    rows = patches.shape[1]
    table = route.table()
    order = route.order(False)[0]
    in_rows = dense_in.shape[0]
    out_rows = dense_out.shape[0]
    vec_len = vectors.shape[0]
    if fits:
        ktable = table
        korder = table // 2
    else:
        ktable = jnp.arange(DEVS, dtype=jnp.int32)
        korder = jnp.arange(DEVS, dtype=jnp.int32) % GROUPS
    sides = jnp.concatenate([seq[None], korder])
    levels = lax.dynamic_slice_in_dim(resolution, seq * 2, 2, 0)

    right_shard, lo_shard = pack_dense(dense_in, dense_out, vectors.reshape(1, vec_len))
    line = [route.swap(right_shard, (m, m)) for m in route.direct]
    lo_line = [route.swap(lo_shard, (m, m)) for m in route.direct]
    spat_own, x_send, g_send = pack_images(sides, spatial, spatial_bias.reshape(3, rows, 1), patches, out_grad)
    x_got = route.cross(x_send)
    g_got = route.cross(g_send)
    spat_got = route.cross(spat_own)
    if fits:
        right_blocks = route.widen_in_turn(stack([right_shard] + line, lo_line[0]))
        lo_blocks = route.widen_in_turn(stack([lo_shard] + lo_line, right_blocks[3]))
    else:
        right_blocks = route.widen(jnp.concatenate([right_shard] + line, axis=0))
        lo_blocks = route.widen(jnp.concatenate([lo_shard] + lo_line, axis=0))
    lo_second = lo_blocks[1]
    right_blocks = right_blocks + [route.cross(b) for b in right_blocks]
    lo_blocks = lo_blocks + [route.cross(b) for b in lo_blocks]
    if not fits:
        whole = in_order(right_blocks, table, in_rows)
        all_vec = whole[:, 0, HALF : HALF + vec_len].reshape(DEVS, 1, VPER)
        all_vec = jnp.pad(all_vec, ((0, 0), (0, 15), (0, VCOLS - VPER))).reshape(D, VCOLS)
        right_blocks = [jnp.concatenate([whole[:, :, :HALF].reshape(D, HALF), all_vec], axis=1)]
        whole = in_order(lo_blocks, table, in_rows)
        outs = whole[:, :, HALF:].reshape(ndev, in_rows, 3, D).transpose(0, 2, 1, 3).reshape(DEVS, 3, 16, D)
        outs = outs.transpose(0, 2, 1, 3).reshape(D, HALF)
        lo_blocks = [jnp.concatenate([whole[:, :, :HALF].reshape(D, HALF), outs], axis=1)]

    x, grad_out, h, v, slope, part, weight_right, vec = gate_forward(
        ktable, sides, patches, x_got, out_grad, g_got, right_blocks
    )
    gate, hat, scale, spat, mm = gate_norm(levels, sides, vec, v, part, spat_own, spat_got, [lo_second])
    gs, gated, q, gb, wl, wo, sp_keep, sp_send, gsum = middle(ktable, levels, sides, vec, h, spat, gate, grad_out, lo_blocks)
    near, far = route.low[-1], route.low[0]
    if fits:
        sp_terms = [sp_keep, route.cross(sp_send)]
    lo_keep, lo_send, mixed_stay, mixed_away, gh = weight_grads(
        ktable, levels, sides, vec, gated, q, gb, h, wl, wo, x, rows
    )
    mixed_got = route.cross(mixed_away)
    after = [[], []]
    if fits:
        sp_part = add_part(sp_terms, 128, [])
        sp_terms.append(route.swap(sp_part, near))
        lo_terms = [lo_keep, route.cross(lo_send)]
        after[0] = [sp_part]
    gp, gate_sum = gate_backward(vec, gs, mm, hat, slope, scale, after[0])
    if fits:
        lo_part = add_part(lo_terms, 128, [gate_sum])
        lo_terms.append(route.swap(lo_part, near))
        sp_part = add_part(sp_terms, 64, [lo_part])
        sp_terms.append(route.swap(sp_part, far))
        after[1] = [sp_part]
    gwr, ghb = in_grads(gp, h, weight_right, gh, after[1])
    if fits:
        after[0] = [sp_terms[-1]]
    else:
        after[0] = []
    right_keep, right_send, right_up, grad_stay, grad_away = in_backward(
        ktable, sides, vec, gsum, gate_sum, gwr, ghb, x, grad_out, rows, after[0]
    )
    if fits:
        right_up = route.cross(right_up)
        right_terms = [right_keep, route.cross(right_send)]
        right_part = add_part([right_keep, right_up], 128, [], [1, 0])
        right_terms.append(route.swap(right_part, near))
        sp_own, *sends = line_spread(sp_terms, right_part)
        sp_got = [route.swap(p, (m, m)) for p, m in zip(sends, route.direct)]
        lo_part = add_part(lo_terms, 64, [sp_own])
        lo_terms.append(route.swap(lo_part, far))
        right_part = add_part(right_terms, 64, [lo_part])
        right_terms.append(route.swap(right_part, far))
        sp_sum = line_sum(sp_own, sp_got, right_part)
        spat_pieces = route.widen(sp_sum)
        lo_own, *sends = line_parts(lo_terms, sp_sum)
        lo_got = [route.swap(p, (m, m)) for p, m in zip(sends, route.direct)]
        right_own, *sends = line_parts(right_terms, lo_own)
        right_got = [route.swap(p, (m, m)) for p, m in zip(sends, route.direct)]
        left_sum, *new_out = finish_out(lo_own, lo_got, dense_out, out_first, out_second, right_own)
        korder = order
        after = [left_sum]
    else:
        both = jnp.concatenate([lo_keep, lo_send])
        outs = both[:, HALF:LO].reshape(DEVS, 16, 3, D).transpose(0, 2, 1, 3).reshape(ndev, out_rows, D)
        outs = jnp.take(outs, table, axis=0).reshape(HALF, D)
        out_sum = route.scatter(outs[: HALF // 2], outs[HALF // 2 :])
        lefts = jnp.take(both[:, :HALF].reshape(ndev, in_rows, HALF), table, axis=0).reshape(D, HALF)
        left_sum = route.scatter(lefts[: D // 2], lefts[D // 2 :])
        per = 512 // route.n

        def spat_blocks(part, flip):
            flat = part.reshape(GROUPS, 16, 2, SCOLS).transpose(0, 2, 1, 3).reshape(route.n, per, SCOLS)
            return jnp.take(flat, route.order(flip)[0], axis=0).reshape(512, SCOLS)

        spat_part = route.scatter(spat_blocks(sp_keep, False), spat_blocks(sp_send, True)).astype(BF)
        flat = in_order(route.spread(spat_part), order, per).reshape(GROUPS, 2, 16, SCOLS)
        spat_pieces = [flat.transpose(0, 2, 1, 3).reshape(GROUPS * 16, SPC)]
        korder = jnp.arange(GROUPS, dtype=jnp.int32)
        after = []
        both = jnp.concatenate([right_keep, right_send, right_up])
        vecs = jnp.take(both[::16, HALF : HALF + VPER].reshape(ndev, vec_len), table, axis=0)
        vec_sum = route.scatter(vecs[: route.n], vecs[route.n :]).reshape(vec_len)
        rights = jnp.take(both[:, :HALF].reshape(ndev, in_rows, HALF), table, axis=0).reshape(D, HALF)
        right_sum = route.scatter(rights[: D // 2], rights[D // 2 :])
        in_sum = jnp.concatenate([left_sum, right_sum], axis=1)
        new_in = adamw(dense_in, in_sum, in_first, in_second, DENSE_RATE, DENSE_DECAY)
        new_out = adamw(dense_out, out_sum, out_first, out_second, DENSE_RATE, DENSE_DECAY)

    def whole_images(stays, came):
        return jnp.concatenate([jnp.where(seq == 0, stays, came), jnp.where(seq == 0, came, stays)], axis=0)

    mixed = whole_images(mixed_stay, mixed_got)
    patches_grad = whole_images(grad_stay, route.cross(grad_away))
    spat_new = spatial_update(
        korder, spat_pieces, spatial, spat_first, spat_second, spatial_bias, bias_first, bias_second, after
    )
    if fits:
        *new_in, vec_sum = finish_in(right_own, right_got, left_sum, dense_in, in_first, in_second, spat_new[0])
        vec_sum = vec_sum[0, :vec_len]
    new_vec = adamw(vectors, vec_sum, vec_first, vec_second, SMALL_RATE, 0.0)
    return (mixed, patches_grad) + tuple(new_in) + tuple(new_out) + new_vec + tuple(spat_new)


def solution(mesh):
    rows3 = P("dp", "seq", None)
    dense = P(AXES, None)
    vec = P(AXES)
    spat = P(None, "seq", None)
    bias = P(None, "seq")
    in_specs = (rows3, P("dp"), rows3, dense, dense, vec, spat, bias)
    in_specs += (dense,) * 4 + (vec,) * 2 + (spat,) * 2 + (bias,) * 2
    out_specs = (rows3, rows3) + (dense,) * 6 + (vec,) * 3 + (spat,) * 3 + (bias,) * 3
    return jax.shard_map(local, mesh=mesh, in_specs=in_specs, out_specs=out_specs, check_vma=False)
```

```python
import functools

import jax
import jax.numpy as jnp
from jax import lax
from jax.experimental import pallas as pl
from jax.experimental.pallas import tpu as pltpu
from jax.sharding import PartitionSpec as P

D = 512
FF = 3072
HALF = 1536
PMAX = 324
PPAD = 336
P_MID = 196
P_LOW = 100
VCOLS = 256
ROWS = 2 * PPAD
GROUPS = 16
DEVS = 2 * GROUPS
VPER = 240
SCOLS = 384
BIAS_AT = 336
TOTAL_AT = 324
LSTRIDE = 168
MIB = 1024 * 1024
STEP = 10

NORM_EPS = 1e-05
BETA_ONE = 0.9
BETA_TWO = 0.99
ADAM_EPS = 1e-08
DENSE_RATE = 0.02
SMALL_RATE = 0.2
DENSE_DECAY = 0.05

BF = jnp.bfloat16
F32 = jnp.float32
AXES = ("dp", "seq")
VM = pl.BlockSpec(memory_space=pltpu.VMEM)
SM = pl.BlockSpec(memory_space=pltpu.SMEM)
HB = pl.BlockSpec(memory_space=pl.ANY)


class Route:
    def __init__(self, n):
        bits = n.bit_length() - 1
        assert n == 1 << bits and bits >= 2
        self.n = n
        top = n // 4
        self.direct = [top, 2 * top, 3 * top]
        low = [1 << b for b in range(bits - 2)]
        self.low = list(zip(low[::-1], low))
        masks = [(0, 0)] + [(m, m) for m in self.direct]
        for step in self.low:
            masks = masks + [(m[0] ^ step[0], m[1] ^ step[1]) for m in masks]
        self.masks = masks

    def swap(self, block, mask):
        pairs = []
        for dp in range(self.n):
            for seq in range(2):
                pairs.append((dp * 2 + seq, (dp ^ mask[seq]) * 2 + seq))
        return lax.ppermute(block, AXES, pairs)

    def cross(self, block):
        pairs = []
        for dp in range(self.n):
            for seq in range(2):
                pairs.append((dp * 2 + seq, dp * 2 + 1 - seq))
        return lax.ppermute(block, AXES, pairs)

    def order(self, seq_flip):
        place = lax.axis_index("dp")
        seq = lax.axis_index("seq")
        if seq_flip:
            seq = 1 - seq
        zero = jnp.array([m[0] for m in self.masks], jnp.int32)
        one = jnp.array([m[1] for m in self.masks], jnp.int32)
        return place ^ jnp.where(seq == 0, zero, one), seq

    def table(self):
        mine, seq = self.order(False)
        other, flip = self.order(True)
        return jnp.concatenate([mine * 2 + seq, other * 2 + flip])

    def spread(self, shard):
        first = jnp.concatenate([shard] + [self.swap(shard, (m, m)) for m in self.direct], axis=0)
        return self.widen(first)

    def widen(self, first):
        blocks = [first]
        for step in self.low:
            blocks = blocks + [self.swap(b, step) for b in blocks]
        return blocks

    def widen_direct(self, first):
        one, two = self.low
        return [first] + [self.swap(first, m) for m in (one, two, (one[0] ^ two[0], one[1] ^ two[1]))]

    def gather(self, shard):
        blocks = self.spread(shard)
        return blocks + [self.cross(b) for b in blocks]

    def collect(self, terms):
        cur = terms[0].shape[0]
        rows = cur // self.n

        def part(lower, upper):
            total = terms[0][lower:upper].astype(F32)
            for t in terms[1:]:
                total = total + t[lower:upper].astype(F32)
            return total

        terms = list(terms)
        for step in reversed(self.low):
            half = cur // 2
            terms.append(self.swap(part(half, cur).astype(BF), step))
            cur = half
        got = []
        for j, m in enumerate(self.direct):
            got.append(self.swap(part((j + 1) * rows, (j + 2) * rows).astype(BF), (m, m)))
        total = part(0, rows)
        return (total + got[0].astype(F32)) + (got[1].astype(F32) + got[2].astype(F32))

    def scatter(self, keep, send):
        return self.collect([keep, self.cross(send)])


def dot(a, b, dims):
    return lax.dot_general(a, b, (dims, ((), ())), preferred_element_type=F32)


NN = ((1,), (0,))
NT = ((1,), (1,))
TN = ((0,), (0,))


def gelu_parts(p):
    bell = jnp.exp(p * p * -0.5)
    d = 1.0 + jnp.abs(p) * (0.3275911 * 0.7071067811865476)
    t = pl.reciprocal(d, approx=True)
    t = t * (2.0 - d * t)
    poly = t * (
        0.127414796
        + t * (-0.142248368 + t * (0.7107068705 + t * (-0.7265760135 + t * 0.5307027145)))
    )
    tail = poly * bell
    phi_sum = jnp.where(p >= 0.0, 1.0 - tail, tail)
    return p * phi_sum, phi_sum + p * bell * 0.3989422804014327


def count_of(level):
    return jnp.where(level == 0, P_LOW, jnp.where(level == 1, P_MID, PMAX))


def masked_mix(mix, count):
    i = lax.broadcasted_iota(jnp.int32, (PPAD, SCOLS), 0)
    j = lax.broadcasted_iota(jnp.int32, (PPAD, SCOLS), 1)
    return jnp.where((i < count) & (j < count), mix.astype(F32), 0.0).astype(BF)


def live_rows(count, shape, start=0):
    return lax.broadcasted_iota(jnp.int32, shape, 0) + start < count


def live_mask(levels_ref, b, width):
    return live_rows(count_of(levels_ref[b]), (PPAD, width))


def fold(value):
    total = value[:, 0:128]
    for n in range(128, value.shape[1], 128):
        total = total + value[:, n : n + 128]
    return total


def spread_sum(ref, factor):
    return jnp.broadcast_to(jnp.sum(ref[...], axis=-1, keepdims=True) * factor, ref.shape)


def wide(value, times):
    return jnp.concatenate([value] * times, axis=1)


def start_blocks(table_ref, pieces, rows, cols, target, sem, extra=0):
    copies = []
    k = 0
    for piece in pieces:
        for j in range(piece.shape[0] // 16):
            at = pl.multiple_of(table_ref[k] * rows, 16)
            c = pltpu.make_async_copy(
                piece.at[pl.ds(j * 16, 16), pl.ds(cols[0], cols[1])], target.at[pl.ds(at + extra, 16)], sem.at[k]
            )
            c.start()
            copies.append(c)
            k += 1
    return copies


def row_loop(step, body):
    def run(i, carry):
        body(pl.multiple_of(i * step, step))
        return carry

    lax.fori_loop(0, ROWS // step, run, 0)


def call(kernel, out_shape, in_specs, scratch, flops, nbytes, *args, room=12):
    vm = pl.BlockSpec(memory_space=pltpu.VMEM)
    return pl.pallas_call(
        kernel,
        out_shape=out_shape,
        in_specs=in_specs,
        out_specs=jax.tree.map(lambda _: vm, out_shape),
        scratch_shapes=scratch,
        compiler_params=pltpu.CompilerParams(vmem_limit_bytes=room * MIB),
        cost_estimate=pl.CostEstimate(flops=flops, bytes_accessed=nbytes, transcendentals=0),
    )(*args)


def norm_parts(values):
    center = values - jnp.mean(values, axis=-1, keepdims=True)
    scale = lax.rsqrt(jnp.mean(center * center, axis=-1, keepdims=True) + NORM_EPS)
    return center * scale, scale


VSEG = {
    "g1": (0, D),
    "b1": (D, D),
    "c1l": (2 * D, HALF),
    "c1r": (2 * D + HALF, HALF),
    "g2": (2 * D + FF, HALF),
    "b2": (2 * D + FF + HALF, HALF),
    "c2": (2 * D + FF + 2 * HALF, D),
}
VEC = 2 * D + FF + 2 * HALF + D


def seg(ref, name):
    start, size = VSEG[name]
    return ref[0:1, start : start + size]

def adamw(weight, grad, first, second, rate, decay):
    first = BETA_ONE * first + (1.0 - BETA_ONE) * grad
    second = BETA_TWO * second + (1.0 - BETA_TWO) * grad * grad
    first_hat = first / (1.0 - BETA_ONE**STEP)
    second_hat = second / (1.0 - BETA_TWO**STEP)
    weight = weight - rate * (first_hat / (jnp.sqrt(second_hat) + ADAM_EPS) + decay * weight)
    return (weight, first, second)


CHUNK = 16
TILE = 256
BODY = 32
STRIPE = 112
LO = 2 * HALF
SPC = 2 * SCOLS


def sds(shape, dtype):
    return jax.ShapeDtypeStruct(shape, dtype)


def pack_dense(dense_in, dense_out, vec_row):
    rows = dense_in.shape[0]
    per = vec_row.shape[1]

    def kernel(w_hbm, o_hbm, v_hbm, out_ref, w_ref, o_ref, v_ref, row, sem):
        copies = [
            pltpu.make_async_copy(src, dst, sem.at[k])
            for k, (src, dst) in enumerate(((w_hbm, w_ref), (o_hbm, o_ref), (v_hbm, v_ref)))
        ]
        for c in copies:
            c.start()
        row[...] = jnp.zeros_like(row)
        for c in copies:
            c.wait()
        out_ref[:, 0:HALF] = w_ref[:, HALF:].astype(BF)
        row[0:1, 0:per] = v_ref[...]
        out_ref[:, HALF : HALF + VCOLS] = row[...].astype(BF)
        start = HALF + VCOLS
        out_ref[:, start : start + HALF] = w_ref[:, 0:HALF].astype(BF)
        start += HALF
        for g in range(3):
            out_ref[:, start + g * D : start + (g + 1) * D] = o_ref[g * rows : (g + 1) * rows, :].astype(BF)

    scratch = [
        pltpu.VMEM(dense_in.shape, F32),
        pltpu.VMEM(dense_out.shape, F32),
        pltpu.VMEM(vec_row.shape, F32),
        pltpu.VMEM((rows, VCOLS), F32),
        pltpu.SemaphoreType.DMA((3,)),
    ]
    shape = sds((rows, HALF + VCOLS + LO), BF)
    return call(kernel, shape, [HB] * 3, scratch, 1000, 600000, dense_in, dense_out, vec_row, room=60)


def pack_images(sides, spatial, bias_col, patches, out_grad):
    half = patches.shape[1]

    def kernel(sides_ref, s_ref, b_ref, x_ref, g_ref, spat_ref, xs_ref, gs_ref, buf):
        away = 2 - 2 * sides_ref[0]
        for b in range(2):
            xs_ref[b] = x_ref[away + b]
            gs_ref[b] = g_ref[away + b]
        buf[...] = jnp.zeros_like(buf)
        for level in range(3):
            buf[:, 0:PMAX] = s_ref[level]
            rest = b_ref[level]
            for c in range(3):
                piece = rest.astype(BF).astype(F32)
                buf[:, BIAS_AT + c : BIAS_AT + c + 1] = piece
                rest = rest - piece
            spat_ref[level] = buf[...].astype(BF)

    pair = sds((2, half, D), BF)
    return call(
        kernel,
        (sds((3, half, SCOLS), BF), pair, pair),
        [SM] + [VM] * 4,
        [pltpu.VMEM((half, SCOLS), F32)],
        1000,
        3000000,
        sides,
        spatial,
        bias_col,
        patches,
        out_grad,
    )


def stack(pieces, start, width, after):
    count = len(pieces)
    rows = pieces[0].shape[0]

    def kernel(*refs):
        out = refs[count + len(after)]
        for k in range(count):
            out[k * rows : (k + 1) * rows, :] = refs[k][:, start : start + width]

    specs = [VM] * count + [HB] * len(after)
    return call(kernel, sds((count * rows, width), BF), specs, [], 1000, 1000000, *pieces, *after)


def two_halves(is_first, own, got):
    own = own.astype(F32)
    got = got.astype(F32)
    return jnp.where(is_first, own, got), jnp.where(is_first, got, own)


def gate_norm(levels, sides, vec, v, part, spat_own, spat_got, after):
    half = spat_own.shape[1]
    count = len(after)

    def kernel(levels_ref, sides_ref, vec_ref, v_ref, part_ref, so_ref, sg_ref, *refs):
        gate_ref, hat_ref, scale_ref, spat_ref, mm_ref, mixf, mean, buf = refs[count:]
        is_first = sides_ref[0] == 0
        g_start = VSEG["g2"][0]
        b_start = VSEG["b2"][0]
        mean[...] = spread_sum(part_ref, 1.0 / HALF)

        def square_rows(r):
            for k in range(0, BODY, CHUNK):
                rows = pl.ds(r + k, CHUNK)
                mid = mean[rows, :]
                total = jnp.zeros((CHUNK, 128), F32)
                for n in range(0, HALF, 128):
                    center = v_ref[rows, n : n + 128] - mid
                    total = total + center * center
                buf[rows, :] = total

        row_loop(BODY, square_rows)
        scale_ref[...] = lax.rsqrt(spread_sum(buf, 1.0 / HALF) + NORM_EPS)

        def gate_rows(r):
            for k in range(0, BODY, CHUNK):
                rows = pl.ds(r + k, CHUNK)
                mid = wide(mean[rows, :], 2)
                scale = wide(scale_ref[rows, :], 2)
                for n in range(0, HALF, TILE):
                    hat = (v_ref[rows, n : n + TILE] - mid) * scale
                    hat_ref[rows, n : n + TILE] = hat.astype(BF)
                    gate = hat * vec_ref[0:1, g_start + n : g_start + n + TILE]
                    gate = (gate + vec_ref[0:1, b_start + n : b_start + n + TILE]).astype(BF)
                    gate_ref[rows, n : n + TILE] = gate

        row_loop(BODY, gate_rows)
        gate_ref[ROWS:, :] = jnp.zeros((SCOLS - PPAD, HALF), BF)
        for b in range(2):
            level = levels_ref[b]
            live = count_of(level)
            one, two = two_halves(is_first, so_ref[level], sg_ref[level])
            mixf[0:half, :] = one
            mixf[half : 2 * half, :] = two
            mixf[2 * half :, :] = jnp.zeros((PPAD - 2 * half, SCOLS), F32)
            bias = jnp.sum(mixf[:, TOTAL_AT:], axis=-1, keepdims=True)
            mm_ref[b] = masked_mix(mixf[...], live)

            def mix_tile(n, carry):
                cols = pl.ds(pl.multiple_of(n * 512, 512), 512)
                got = dot(mm_ref[b], gate_ref[b * PPAD : b * PPAD + SCOLS, cols], NN) + bias
                got = jnp.where(live_rows(live, (PPAD, 512)), got, 0.0)
                spat_ref[b * PPAD : (b + 1) * PPAD, cols] = got.astype(BF)
                return carry

            lax.fori_loop(0, HALF // 512, mix_tile, 0)

    return call(
        kernel,
        (
            sds((ROWS + SCOLS - PPAD, HALF), BF),
            sds((ROWS, HALF), BF),
            sds((ROWS, 128), F32),
            sds((ROWS, HALF), BF),
            sds((2, PPAD, SCOLS), BF),
        ),
        [SM] * 2 + [VM] * 5 + [HB] * count,
        [pltpu.VMEM((PPAD, SCOLS), F32), pltpu.VMEM((ROWS, 128), F32), pltpu.VMEM((ROWS, 128), F32)],
        6000000000,
        12000000,
        levels,
        sides,
        vec,
        v,
        part,
        spat_own,
        spat_got,
        *after,
        room=22,
    )


def gate_forward(table, sides, patches, x_got, out_grad, g_got, pieces):
    count = len(pieces)
    half = patches.shape[1]

    def kernel(table_ref, sides_ref, p_ref, xg_ref, o_ref, gg_ref, *refs):
        ins = refs[:count]
        outs = refs[count : count + 8]
        x_ref, og_ref, h_ref, pre, slope_ref, part, w_ref, vec_ref = outs
        vblk, xbuf, sem, vsem = refs[count + 8 :]
        vcopies = start_blocks(table_ref, ins, 16, (HALF, VCOLS), vblk, vsem)
        copies = start_blocks(table_ref, ins, 16, (0, HALF), w_ref, sem)
        me = sides_ref[0]
        is_first = me == 0

        for src, got, target in ((o_ref, gg_ref, og_ref), (p_ref, xg_ref, x_ref)):
            for b in range(2):
                one, two = two_halves(is_first, src[2 * me + b], got[b])
                xbuf[b * PPAD : b * PPAD + half, :] = one
                xbuf[b * PPAD + half : b * PPAD + 2 * half, :] = two
                xbuf[b * PPAD + 2 * half : (b + 1) * PPAD, :] = jnp.zeros((PPAD - 2 * half, D), F32)
            target[...] = xbuf[...].astype(BF)
        for c in vcopies:
            c.wait()
        for s in range(DEVS):
            row = vblk[16 * s : 16 * s + 16, :].astype(F32)[0:1, :VPER]
            vec_ref[0:1, VPER * s : VPER * s + VPER] = row

        def norm_one(r):
            hat, _ = norm_parts(xbuf[pl.ds(r, STRIPE), :])
            h_ref[pl.ds(r, STRIPE), :] = (hat * seg(vec_ref, "g1") + seg(vec_ref, "b1")).astype(BF)

        row_loop(STRIPE, norm_one)
        for c in copies:
            c.wait()
        c_start = VSEG["c1r"][0]

        def matmul(n, carry):
            at = pl.multiple_of(n * TILE, TILE)
            pre[:, pl.ds(at, TILE)] = dot(h_ref[...], w_ref[:, pl.ds(at, TILE)], NN)
            return carry

        lax.fori_loop(0, HALF // TILE, matmul, 0)

        def gelu_rows(r):
            for k in range(0, BODY, CHUNK):
                rows = pl.ds(r + k, CHUNK)
                total = jnp.zeros((CHUNK, 128), F32)
                for n in range(0, HALF, TILE):
                    v, slope = gelu_parts(pre[rows, n : n + TILE] + vec_ref[0:1, c_start + n : c_start + n + TILE])
                    pre[rows, n : n + TILE] = v
                    slope_ref[rows, n : n + TILE] = slope.astype(BF)
                    total = total + fold(v)
                part[rows, :] = total

        row_loop(BODY, gelu_rows)

    broad = sds((ROWS, HALF), BF)
    narrow = sds((ROWS, D), BF)
    out_shape = (
        narrow,
        narrow,
        narrow,
        sds((ROWS, HALF), F32),
        broad,
        sds((ROWS, 128), F32),
        sds((D, HALF), BF),
        sds((1, VEC), F32),
    )
    scratch = [
        pltpu.VMEM((D, VCOLS), BF),
        pltpu.VMEM((ROWS, D), F32),
        pltpu.SemaphoreType.DMA((DEVS,)),
        pltpu.SemaphoreType.DMA((DEVS,)),
    ]
    return call(
        kernel,
        out_shape,
        [SM] * 2 + [VM] * 4 + [HB] * count,
        scratch,
        10000000000,
        20000000,
        table,
        sides,
        patches,
        x_got,
        out_grad,
        g_got,
        *pieces,
        room=26,
    )


def split_rows(target, first, second, seq, value):
    half = first.shape[1]
    target[...] = value
    for b in range(2):
        one = target[b * PPAD : b * PPAD + half, :]
        two = target[b * PPAD + half : b * PPAD + 2 * half, :]
        first[b] = jnp.where(seq == 0, one, two).astype(BF)
        second[b] = jnp.where(seq == 0, two, one).astype(BF)


def middle(table, levels, sides, vec, h, spat, gate, grad_out, pieces):
    count = len(pieces)

    def kernel(table_ref, levels_ref, sides_ref, vec_ref, h_ref, spat_ref, gate_ref, og_ref, *refs):
        ins = refs[:count]
        gs_ref, gated_ref, q_ref, gb, wl, wo, keep, send, gsum_ref = refs[count : count + 9]
        pbuf, gbuf, cells, flat, sem = refs[count + 9 :]
        copies = start_blocks(table_ref, ins, 16, (0, HALF), wl, sem.at[0])
        for g in range(3):
            copies += start_blocks(table_ref, ins, 48, (HALF + g * D, D), wo, sem.at[1 + g], 16 * g)
        for b in range(2):
            rows = slice(b * PPAD, (b + 1) * PPAD)
            gb[rows, :] = jnp.where(live_mask(levels_ref, b, D), og_ref[rows, :].astype(F32), 0.0).astype(BF)
        gsum_ref[0:1, HALF : HALF + D] = jnp.sum(gb[...].astype(F32), axis=0, keepdims=True)
        cells[...] = jnp.zeros_like(cells)
        flat[...] = jnp.zeros_like(flat)
        for c in copies:
            c.wait()
        c_start = VSEG["c1l"][0]

        def tile(n, carry):
            at = pl.multiple_of(n * TILE, TILE)
            cols = pl.ds(at, TILE)
            pbuf[...] = dot(h_ref[...], wl[:, cols], NN)
            gbuf[...] = dot(gb[...], wo[cols, :], NT)
            shift = vec_ref[0:1, pl.ds(c_start + at, TILE)]
            total = jnp.zeros((CHUNK, TILE), F32)
            for k in range(0, ROWS, CHUNK):
                r = slice(k, k + CHUNK)
                u, slope = gelu_parts(pbuf[r, :] + shift)
                sp = spat_ref[r, cols].astype(F32)
                gg = gbuf[r, :]
                gated_ref[r, cols] = (u * sp).astype(BF)
                gs_ref[r, cols] = (gg * u).astype(BF)
                q = (gg * sp * slope).astype(BF)
                q_ref[r, cols] = q
                total = total + q.astype(F32)
            gsum_ref[0:1, cols] = jnp.sum(total, axis=0, keepdims=True)
            return carry

        lax.fori_loop(0, HALF // TILE, tile, 0)

        me = sides_ref[0]
        for b in range(2):
            level = levels_ref[b]
            count_b = count_of(level)
            gs = gs_ref[b * PPAD : (b + 1) * PPAD, :]
            got = dot(gs, gate_ref[b * PPAD : (b + 1) * PPAD, :], NT)
            sums = jnp.sum(gs.astype(F32), axis=-1, keepdims=True)
            j = lax.broadcasted_iota(jnp.int32, (PPAD, PPAD), 1)
            got = jnp.where(j < count_b, got, jnp.where(j == TOTAL_AT, sums, 0.0))
            cells[level, :, 0:PPAD] += got
        part = PMAX // 2
        for level in range(3):
            for k in range(2):
                flat[k, level * LSTRIDE : level * LSTRIDE + part, 0:PPAD] = cells[level, k * part : (k + 1) * part, 0:PPAD]
        for k in range(DEVS):
            target, side = (keep, me) if k < GROUPS else (send, 1 - me)
            r = pl.ds(k % GROUPS * 16, 16)
            block = flat[side, pl.ds(pl.multiple_of(sides_ref[1 + k] * 32, 32), 32), :].astype(BF)
            target[r, 0:SCOLS] = block[0:16]
            target[r, SCOLS:SPC] = block[16:32]

    broad = sds((ROWS, HALF), BF)
    payload = sds((D // 2, SPC), BF)
    out_shape = (
        broad,
        broad,
        broad,
        sds((ROWS, D), BF),
        sds((D, HALF), BF),
        sds((HALF, D), BF),
        payload,
        payload,
        sds((1, HALF + D), F32),
    )
    scratch = [
        pltpu.VMEM((ROWS, TILE), F32),
        pltpu.VMEM((ROWS, TILE), F32),
        pltpu.VMEM((3, PPAD, SCOLS), F32),
        pltpu.VMEM((2, 512, SCOLS), F32),
        pltpu.SemaphoreType.DMA((4, DEVS)),
    ]
    return call(
        kernel,
        out_shape,
        [SM] * 3 + [VM] * 5 + [HB] * count,
        scratch,
        8000000000,
        16000000,
        table,
        levels,
        sides,
        vec,
        h,
        spat,
        gate,
        grad_out,
        *pieces,
        room=28,
    )


def weight_grads(table, levels, sides, vec, gated, q, gb, h, wl, wo, x, half):
    def kernel(
        table_ref, levels_ref, sides_ref, vec_ref, t_ref, q_ref, gb_ref, h_ref, wl_ref, wo_ref, x_ref,
        keep, send, stay_ref, away_ref, gh_ref, branch, gwo, gwl,
    ):
        def out_tile(n, carry):
            cols = pl.ds(pl.multiple_of(n * TILE, TILE), TILE)
            gwo[cols, :] = dot(t_ref[:, cols], gb_ref[...], TN).astype(BF)
            return carry

        lax.fori_loop(0, HALF // TILE, out_tile, 0)

        def in_tile(n, carry):
            cols = pl.ds(pl.multiple_of(n * TILE, TILE), TILE)
            gwl[cols, :] = dot(h_ref[:, cols], q_ref[...], TN).astype(BF)
            branch[:, cols] = dot(t_ref[...], wo_ref[:, cols], NN)
            gh_ref[:, cols] = dot(q_ref[...], wl_ref[cols, :], NT)
            return carry

        lax.fori_loop(0, D // TILE, in_tile, 0)
        me = sides_ref[0]
        live = jnp.concatenate([live_mask(levels_ref, b, D) for b in range(2)], axis=0)
        out = branch[...] + seg(vec_ref, "c2")
        split_rows(branch, stay_ref, away_ref, me, x_ref[...].astype(F32) + jnp.where(live, out, 0.0))
        for k in range(DEVS):
            dev = table_ref[k]
            target = keep if k < GROUPS else send
            r = pl.ds(k % GROUPS * 16, 16)
            target[r, 0:HALF] = gwl[pl.ds(pl.multiple_of(dev * 16, 16), 16), :]
            for g in range(3):
                target[r, HALF + g * D : HALF + (g + 1) * D] = gwo[pl.ds(pl.multiple_of(dev * 48 + 16 * g, 16), 16), :]

    pair = sds((2, half, D), BF)
    payload = sds((D // 2, LO), BF)
    return call(
        kernel,
        (payload, payload, pair, pair, sds((ROWS, D), F32)),
        [SM] * 3 + [VM] * 8,
        [pltpu.VMEM((ROWS, D), F32), pltpu.VMEM((HALF, D), BF), pltpu.VMEM((D, HALF), BF)],
        5000000000,
        15000000,
        table,
        levels,
        sides,
        vec,
        gated,
        q,
        gb,
        h,
        wl,
        wo,
        x,
        room=24,
    )


def gate_backward(vec, gs, mm, hat, slope, scale, after):
    count = len(after)

    def kernel(vec_ref, gs_ref, mm_ref, hat_ref, slope_ref, scale_ref, *refs):
        gp, gsum_ref, dbuf, one, two, acc = refs[count:]

        for b in range(2):

            def mix_tile(n, carry):
                cols = pl.ds(pl.multiple_of(n * 512, 512), 512)
                got = dot(mm_ref[b], gs_ref[b * PPAD : (b + 1) * PPAD, cols], TN)
                dbuf[b * PPAD : (b + 1) * PPAD, cols] = got[0:PPAD]
                return carry

            lax.fori_loop(0, HALF // 512, mix_tile, 0)
        g_start = VSEG["g2"][0]

        def sum_rows(r):
            for k in range(0, BODY, CHUNK):
                rows = pl.ds(r + k, CHUNK)
                a = jnp.zeros((CHUNK, 128), F32)
                c = jnp.zeros((CHUNK, 128), F32)
                for n in range(0, HALF, TILE):
                    e = dbuf[rows, n : n + TILE] * vec_ref[0:1, g_start + n : g_start + n + TILE]
                    a = a + fold(e)
                    c = c + fold(e * hat_ref[rows, n : n + TILE].astype(F32))
                one[rows, :] = a
                two[rows, :] = c

        row_loop(BODY, sum_rows)
        one[...] = spread_sum(one, 1.0 / HALF)
        two[...] = spread_sum(two, 1.0 / HALF)
        acc[...] = jnp.zeros_like(acc)

        def grad_rows(r):
            for n in range(0, HALF, TILE):
                gain = vec_ref[0:1, g_start + n : g_start + n + TILE]
                sums = [jnp.zeros((CHUNK, TILE), F32) for _ in range(3)]
                for k in range(0, BODY, CHUNK):
                    rows = pl.ds(r + k, CHUNK)
                    d = dbuf[rows, n : n + TILE]
                    xh = hat_ref[rows, n : n + TILE].astype(F32)
                    inner = d * gain - wide(one[rows, :], 2) - xh * wide(two[rows, :], 2)
                    q = inner * wide(scale_ref[rows, :], 2) * slope_ref[rows, n : n + TILE].astype(F32)
                    q = q.astype(BF)
                    gp[rows, n : n + TILE] = q
                    sums = [sums[0] + d * xh, sums[1] + d, sums[2] + q.astype(F32)]
                for i in range(3):
                    acc[i, :, n : n + TILE] += sums[i]

        row_loop(BODY, grad_rows)
        for i in range(3):
            gsum_ref[0:1, i * HALF : (i + 1) * HALF] = jnp.sum(acc[i], axis=0, keepdims=True)

    return call(
        kernel,
        (sds((ROWS, HALF), BF), sds((1, 3 * HALF), F32)),
        [VM] * 6 + [HB] * count,
        [
            pltpu.VMEM((ROWS, HALF), F32),
            pltpu.VMEM((ROWS, 128), F32),
            pltpu.VMEM((ROWS, 128), F32),
            pltpu.VMEM((3, CHUNK, HALF), F32),
        ],
        3000000000,
        10000000,
        vec,
        gs,
        mm,
        hat,
        slope,
        scale,
        *after,
        room=20,
    )


def in_grads(gp, h, w, gh, after):
    count = len(after)

    def kernel(gp_ref, h_ref, w_ref, gh_ref, *refs):
        gwr, ghb = refs[count:]

        def in_tile(n, carry):
            cols = pl.ds(pl.multiple_of(n * TILE, TILE), TILE)
            ghb[:, cols] = gh_ref[:, cols] + dot(gp_ref[...], w_ref[cols, :], NT)
            gwr[cols, :] = dot(h_ref[:, cols], gp_ref[...], TN).astype(BF)
            return carry

        lax.fori_loop(0, D // TILE, in_tile, 0)

    return call(
        kernel,
        (sds((D, HALF), BF), sds((ROWS, D), F32)),
        [VM] * 4 + [HB] * count,
        [],
        3000000000,
        8000000,
        gp,
        h,
        w,
        gh,
        *after,
        room=14,
    )


def in_backward(table, sides, vec, gsum, gate_sum, gwr, ghb, x, grad_out, half, after):
    count = len(after)

    def kernel(table_ref, sides_ref, vec_ref, gsum_ref, gate_ref, gwr, ghb, x_ref, og_ref, *refs):
        keep, send, send_up, stay_ref, away_ref, acc, gvec, blocks, pgb = refs[count:]

        def put(name, value):
            start, size = VSEG[name]
            gvec[0:1, start : start + size] = value

        put("g2", gate_ref[0:1, 0:HALF])
        put("b2", gate_ref[0:1, HALF : 2 * HALF])
        put("c1r", gate_ref[0:1, 2 * HALF : 3 * HALF])
        put("c1l", gsum_ref[0:1, 0:HALF])
        put("c2", gsum_ref[0:1, HALF : HALF + D])
        acc[...] = jnp.zeros_like(acc)
        def in_rows(r):
            rows = pl.ds(r, STRIPE)
            xh, scale = norm_parts(x_ref[rows, :].astype(F32))
            d = ghb[rows, :]
            e = d * seg(vec_ref, "g1")
            one = jnp.mean(e, axis=-1, keepdims=True)
            two = jnp.mean(e * xh, axis=-1, keepdims=True)
            pgb[rows, :] = og_ref[rows, :].astype(F32) + scale * (e - one - xh * two)
            acc[0:1, :] += jnp.sum(d * xh, axis=0, keepdims=True)
            acc[1:2, :] += jnp.sum(d, axis=0, keepdims=True)

        row_loop(STRIPE, in_rows)
        put("g1", acc[0:1, :])
        put("b1", acc[1:2, :])
        split_rows(pgb, stay_ref, away_ref, sides_ref[0], pgb[...])
        blocks[...] = jnp.zeros_like(blocks)
        for s in range(DEVS):
            blocks[s, 0:1, 0:VPER] = gvec[0:1, VPER * s : VPER * s + VPER]
        for k in range(DEVS):
            dev = table_ref[k]
            target = keep if k < GROUPS else send if k < GROUPS * 3 // 2 else send_up
            r = pl.ds(k % (GROUPS if k < GROUPS else GROUPS // 2) * 16, 16)
            target[r, 0:HALF] = gwr[pl.ds(pl.multiple_of(dev * 16, 16), 16), :]
            target[r, HALF : HALF + VCOLS] = blocks[dev].astype(BF)

    payload = sds((D // 2, HALF + VCOLS), BF)
    part = sds((D // 4, HALF + VCOLS), BF)
    pair = sds((2, half, D), BF)
    return call(
        kernel,
        (payload, part, part, pair, pair),
        [SM] * 2 + [VM] * 7 + [HB] * count,
        [
            pltpu.VMEM((8, D), F32),
            pltpu.VMEM((1, VEC), F32),
            pltpu.VMEM((DEVS, 16, VCOLS), F32),
            pltpu.VMEM((ROWS, D), F32),
        ],
        2000000000,
        6000000,
        table,
        sides,
        vec,
        gsum,
        gate_sum,
        gwr,
        ghb,
        x,
        grad_out,
        *after,
        room=16,
    )


def add_part(terms, size, after, places=None):
    cols = terms[0].shape[1]
    count = len(terms)

    def kernel(*refs):
        for r in range(0, size, 16):
            rows = slice(r, r + 16)
            value = refs[0][rows, :].astype(F32)
            for t in refs[1:count]:
                value = value + t[rows, :].astype(F32)
            refs[count + len(after)][rows, :] = value.astype(BF)

    places = places or [1] * count
    blocks = [pl.BlockSpec((size, cols), lambda i, p=p: (p, 0)) for p in places]
    return pl.pallas_call(
        kernel,
        grid=(1,),
        out_shape=sds((size, cols), BF),
        in_specs=blocks + [HB] * len(after),
        out_specs=pl.BlockSpec((size, cols), lambda i: (0, 0)),
        compiler_params=pltpu.CompilerParams(vmem_limit_bytes=10 * MIB),
        cost_estimate=pl.CostEstimate(flops=1000000, bytes_accessed=3000000, transcendentals=0),
    )(*terms, *after)


def line_parts(terms, after):
    cols = terms[0].shape[1]
    count = len(terms)

    def kernel(*refs):
        own, outs = refs[count + 1], refs[count + 2 :]
        for m in range(4):
            rows = slice(16 * m, 16 * (m + 1))
            value = refs[0][rows, :].astype(F32)
            for t in refs[1:count]:
                value = value + t[rows, :].astype(F32)
            if m == 0:
                own[...] = value
            else:
                outs[m - 1][...] = value.astype(BF)

    block = pl.BlockSpec((64, cols), lambda i: (0, 0))
    one = pl.BlockSpec((16, cols), lambda i: (0, 0))
    return pl.pallas_call(
        kernel,
        grid=(1,),
        out_shape=[sds((16, cols), F32)] + [sds((16, cols), BF)] * 3,
        in_specs=[block] * count + [HB],
        out_specs=[one] * 4,
        compiler_params=pltpu.CompilerParams(vmem_limit_bytes=8 * MIB),
        cost_estimate=pl.CostEstimate(flops=1000000, bytes_accessed=3000000, transcendentals=0),
    )(*terms, after)


def line_sum(total, got, after):
    rows = total.shape[0]

    def kernel(own_ref, a_ref, b_ref, c_ref, after_ref, out_ref):
        near = own_ref[...].astype(F32) + a_ref[...].astype(F32)
        far = b_ref[...].astype(F32) + c_ref[...].astype(F32)
        out_ref[...] = (near + far).astype(BF)

    return call(kernel, sds((rows, SPC), BF), [VM] * 4 + [HB], [], 1000000, 500000, total, *got, after)


def line_spread(terms, after):
    count = len(terms)
    cols = terms[0].shape[1]

    def kernel(*refs):
        outs = refs[count + 1 :]
        for m in range(4):
            rows = slice(16 * m, 16 * (m + 1))
            value = refs[0][rows, :].astype(F32)
            for t in refs[1:count]:
                value = value + t[rows, :].astype(F32)
            value = value.astype(BF)
            for j in range(4):
                at = 16 * (m ^ j)
                outs[j][at : at + 16, :] = value

    block = pl.BlockSpec((64, cols), lambda i: (0, 0))
    return pl.pallas_call(
        kernel,
        grid=(1,),
        out_shape=[sds((64, cols), BF)] * 4,
        in_specs=[block] * count + [HB],
        out_specs=[block] * 4,
        compiler_params=pltpu.CompilerParams(vmem_limit_bytes=8 * MIB),
        cost_estimate=pl.CostEstimate(flops=1000000, bytes_accessed=1000000, transcendentals=0),
    )(*terms, after)


def finish_out(own, got, weight, first, second, after):
    def kernel(own_ref, a_ref, b_ref, c_ref, w_ref, m_ref, s_ref, after_ref, left_ref, nw, nm, ns):
        total = own_ref[...] + a_ref[...].astype(F32)
        total = total + (b_ref[...].astype(F32) + c_ref[...].astype(F32))
        left_ref[...] = total[:, 0:HALF]
        for g in range(3):
            rows = slice(16 * g, 16 * (g + 1))
            grad = total[:, HALF + g * D : HALF + (g + 1) * D]
            new = adamw(w_ref[rows, :], grad, m_ref[rows, :], s_ref[rows, :], DENSE_RATE, DENSE_DECAY)
            nw[rows, :] = new[0]
            nm[rows, :] = new[1]
            ns[rows, :] = new[2]

    same = sds(weight.shape, F32)
    return call(
        kernel,
        (sds((16, HALF), F32), same, same, same),
        [VM] * 7 + [HB],
        [],
        1000000,
        2000000,
        own,
        *got,
        weight,
        first,
        second,
        after,
    )


def finish_in(own, got, left, weight, first, second, after):
    def kernel(own_ref, a_ref, b_ref, c_ref, l_ref, w_ref, m_ref, s_ref, after_ref, nw, nm, ns, vec_ref):
        total = own_ref[...] + a_ref[...].astype(F32)
        total = total + (b_ref[...].astype(F32) + c_ref[...].astype(F32))
        vec_ref[...] = total[0:1, HALF:]
        for cols, grad in ((slice(0, HALF), l_ref[...]), (slice(HALF, FF), total[:, 0:HALF])):
            new = adamw(w_ref[:, cols], grad, m_ref[:, cols], s_ref[:, cols], DENSE_RATE, DENSE_DECAY)
            nw[:, cols] = new[0]
            nm[:, cols] = new[1]
            ns[:, cols] = new[2]

    same = sds(weight.shape, F32)
    return call(
        kernel,
        (same, same, same, sds((1, VCOLS), F32)),
        [VM] * 8 + [HB],
        [],
        1000000,
        2000000,
        own,
        *got,
        left,
        weight,
        first,
        second,
        after,
    )


def spatial_update(order, pieces, spatial, first, second, bias, bias_first, bias_second, after):
    count = len(pieces)
    rows = spatial.shape[1]

    def kernel(order_ref, *refs):
        ins = refs[:count]
        w_ref, m_ref, s_ref, bw, bm, bs = refs[count : count + 6]
        nw, nm, ns, nbw, nbm, nbs, flat = refs[count + 6 + len(after) :]
        k = 0
        for piece in ins:
            for j in range(piece.shape[0] // 16):
                at = pl.multiple_of(order_ref[k] * 32, 32)
                block = piece[16 * j : 16 * j + 16, :].astype(F32)
                flat[pl.ds(at, 16), :] = block[:, 0:SCOLS]
                flat[pl.ds(at + 16, 16), :] = block[:, SCOLS:]
                k += 1
        at = TOTAL_AT // 128 * 128
        totals = flat[:, at : at + 128].T[TOTAL_AT - at : TOTAL_AT - at + 1, :]
        for level in range(3):
            got = flat[level * LSTRIDE : level * LSTRIDE + rows, :]
            new = adamw(w_ref[level], got[:, 0:PMAX], m_ref[level], s_ref[level], DENSE_RATE, DENSE_DECAY)
            nw[level] = new[0]
            nm[level] = new[1]
            ns[level] = new[2]
            got = totals[:, level * LSTRIDE : level * LSTRIDE + rows]
            r = slice(level, level + 1)
            new = adamw(bw[r, :], got, bm[r, :], bs[r, :], SMALL_RATE, 0.0)
            nbw[r, :] = new[0]
            nbm[r, :] = new[1]
            nbs[r, :] = new[2]

    same = sds(spatial.shape, F32)
    small = sds(bias.shape, F32)
    return call(
        kernel,
        (same, same, same, small, small, small),
        [SM] + [VM] * (count + 6) + [HB] * len(after),
        [pltpu.VMEM((512, SCOLS), F32)],
        10000000,
        6000000,
        order,
        *pieces,
        spatial,
        first,
        second,
        bias,
        bias_first,
        bias_second,
        *after,
    )


def in_order(blocks, table, rows):
    cols = blocks[0].shape[1]
    whole = jnp.concatenate(blocks, axis=0).reshape(-1, rows, cols)
    back = jnp.zeros_like(table).at[table].set(jnp.arange(table.shape[0], dtype=table.dtype))
    return jnp.take(whole, back, axis=0)


def local(
    patches,
    resolution,
    out_grad,
    dense_in,
    dense_out,
    vectors,
    spatial,
    spatial_bias,
    in_first,
    in_second,
    out_first,
    out_second,
    vec_first,
    vec_second,
    spat_first,
    spat_second,
    bias_first,
    bias_second,
):
    route = Route(lax.axis_size("dp"))
    ndev = 2 * route.n
    fits = route.n == GROUPS
    seq = lax.axis_index("seq").astype(jnp.int32)
    rows = patches.shape[1]
    table = route.table()
    order = route.order(False)[0]
    in_rows = dense_in.shape[0]
    out_rows = dense_out.shape[0]
    vec_len = vectors.shape[0]
    if fits:
        ktable = table
        korder = table // 2
    else:
        ktable = jnp.arange(DEVS, dtype=jnp.int32)
        korder = jnp.arange(DEVS, dtype=jnp.int32) % GROUPS
    sides = jnp.concatenate([seq[None], korder])
    levels = lax.dynamic_slice_in_dim(resolution, seq * 2, 2, 0)

    shard = pack_dense(dense_in, dense_out, vectors.reshape(1, vec_len))
    line = [shard] + [route.swap(shard, (m, m)) for m in route.direct]
    spat_own, x_send, g_send = pack_images(sides, spatial, spatial_bias.reshape(3, rows, 1), patches, out_grad)
    x_got = route.cross(x_send)
    g_got = route.cross(g_send)
    spat_got = route.cross(spat_own)
    first_cols = HALF + VCOLS
    if fits:
        right_blocks = route.widen_direct(stack(line, 0, first_cols, [x_send]))
        lo_blocks = route.widen_direct(stack(line, first_cols, LO, [right_blocks[1]]))
    else:
        whole = jnp.concatenate(line, axis=0)
        right_blocks = route.widen(whole[:, :first_cols])
        lo_blocks = route.widen(whole[:, first_cols:])
    right_blocks = right_blocks + [route.cross(b) for b in right_blocks]
    lo_blocks = lo_blocks + [route.cross(b) for b in lo_blocks]
    if not fits:
        whole = in_order(right_blocks, table, in_rows)
        all_vec = whole[:, 0, HALF : HALF + vec_len].reshape(DEVS, 1, VPER)
        all_vec = jnp.pad(all_vec, ((0, 0), (0, 15), (0, VCOLS - VPER))).reshape(D, VCOLS)
        right_blocks = [jnp.concatenate([whole[:, :, :HALF].reshape(D, HALF), all_vec], axis=1)]
        whole = in_order(lo_blocks, table, in_rows)
        outs = whole[:, :, HALF:].reshape(ndev, in_rows, 3, D).transpose(0, 2, 1, 3).reshape(DEVS, 3, 16, D)
        outs = outs.transpose(0, 2, 1, 3).reshape(D, HALF)
        lo_blocks = [jnp.concatenate([whole[:, :, :HALF].reshape(D, HALF), outs], axis=1)]

    x, grad_out, h, v, slope, part, weight_right, vec = gate_forward(
        ktable, sides, patches, x_got, out_grad, g_got, right_blocks
    )
    gate, hat, scale, spat, mm = gate_norm(levels, sides, vec, v, part, spat_own, spat_got, [])
    gs, gated, q, gb, wl, wo, sp_keep, sp_send, gsum = middle(ktable, levels, sides, vec, h, spat, gate, grad_out, lo_blocks)
    near, far = route.low[-1], route.low[0]
    if fits:
        sp_terms = [sp_keep, route.cross(sp_send)]
    lo_keep, lo_send, mixed_stay, mixed_away, gh = weight_grads(
        ktable, levels, sides, vec, gated, q, gb, h, wl, wo, x, rows
    )
    mixed_got = route.cross(mixed_away)
    after = [[], []]
    if fits:
        sp_part = add_part(sp_terms, 128, [])
        sp_terms.append(route.swap(sp_part, near))
        lo_terms = [lo_keep, route.cross(lo_send)]
        after[0] = [sp_part]
    gp, gate_sum = gate_backward(vec, gs, mm, hat, slope, scale, after[0])
    if fits:
        lo_part = add_part(lo_terms, 128, [gate_sum])
        lo_terms.append(route.swap(lo_part, near))
        sp_part = add_part(sp_terms, 64, [lo_part])
        sp_terms.append(route.swap(sp_part, far))
        after[1] = [sp_part]
    gwr, ghb = in_grads(gp, h, weight_right, gh, after[1])
    if fits:
        after[0] = [sp_terms[-1]]
    else:
        after[0] = []
    right_keep, right_send, right_up, grad_stay, grad_away = in_backward(
        ktable, sides, vec, gsum, gate_sum, gwr, ghb, x, grad_out, rows, after[0]
    )
    if fits:
        right_up = route.cross(right_up)
        right_terms = [right_keep, route.cross(right_send)]
        right_part = add_part([right_keep, right_up], 128, [], [1, 0])
        right_terms.append(route.swap(right_part, near))
        sp_own, *sends = line_spread(sp_terms, right_part)
        sp_got = [route.swap(p, (m, m)) for p, m in zip(sends, route.direct)]
        lo_part = add_part(lo_terms, 64, [sp_own])
        lo_terms.append(route.swap(lo_part, far))
        right_part = add_part(right_terms, 64, [lo_part])
        right_terms.append(route.swap(right_part, far))
        sp_sum = line_sum(sp_own, sp_got, right_part)
        spat_pieces = route.widen(sp_sum)
        lo_own, *sends = line_parts(lo_terms, sp_sum)
        lo_got = [route.swap(p, (m, m)) for p, m in zip(sends, route.direct)]
        right_own, *sends = line_parts(right_terms, lo_own)
        right_got = [route.swap(p, (m, m)) for p, m in zip(sends, route.direct)]
        left_sum, *new_out = finish_out(lo_own, lo_got, dense_out, out_first, out_second, right_own)
        korder = order
        after = [left_sum]
    else:
        both = jnp.concatenate([lo_keep, lo_send])
        outs = both[:, HALF:LO].reshape(DEVS, 16, 3, D).transpose(0, 2, 1, 3).reshape(ndev, out_rows, D)
        outs = jnp.take(outs, table, axis=0).reshape(HALF, D)
        out_sum = route.scatter(outs[: HALF // 2], outs[HALF // 2 :])
        lefts = jnp.take(both[:, :HALF].reshape(ndev, in_rows, HALF), table, axis=0).reshape(D, HALF)
        left_sum = route.scatter(lefts[: D // 2], lefts[D // 2 :])
        per = 512 // route.n

        def spat_blocks(part, flip):
            flat = part.reshape(GROUPS, 16, 2, SCOLS).transpose(0, 2, 1, 3).reshape(route.n, per, SCOLS)
            return jnp.take(flat, route.order(flip)[0], axis=0).reshape(512, SCOLS)

        spat_part = route.scatter(spat_blocks(sp_keep, False), spat_blocks(sp_send, True)).astype(BF)
        flat = in_order(route.spread(spat_part), order, per).reshape(GROUPS, 2, 16, SCOLS)
        spat_pieces = [flat.transpose(0, 2, 1, 3).reshape(GROUPS * 16, SPC)]
        korder = jnp.arange(GROUPS, dtype=jnp.int32)
        after = []
        both = jnp.concatenate([right_keep, right_send, right_up])
        vecs = jnp.take(both[::16, HALF : HALF + VPER].reshape(ndev, vec_len), table, axis=0)
        vec_sum = route.scatter(vecs[: route.n], vecs[route.n :]).reshape(vec_len)
        rights = jnp.take(both[:, :HALF].reshape(ndev, in_rows, HALF), table, axis=0).reshape(D, HALF)
        right_sum = route.scatter(rights[: D // 2], rights[D // 2 :])
        in_sum = jnp.concatenate([left_sum, right_sum], axis=1)
        new_in = adamw(dense_in, in_sum, in_first, in_second, DENSE_RATE, DENSE_DECAY)
        new_out = adamw(dense_out, out_sum, out_first, out_second, DENSE_RATE, DENSE_DECAY)

    def whole_images(stays, came):
        return jnp.concatenate([jnp.where(seq == 0, stays, came), jnp.where(seq == 0, came, stays)], axis=0)

    mixed = whole_images(mixed_stay, mixed_got)
    patches_grad = whole_images(grad_stay, route.cross(grad_away))
    spat_new = spatial_update(
        korder, spat_pieces, spatial, spat_first, spat_second, spatial_bias, bias_first, bias_second, after
    )
    if fits:
        *new_in, vec_sum = finish_in(right_own, right_got, left_sum, dense_in, in_first, in_second, spat_new[0])
        vec_sum = vec_sum[0, :vec_len]
    new_vec = adamw(vectors, vec_sum, vec_first, vec_second, SMALL_RATE, 0.0)
    return (mixed, patches_grad) + tuple(new_in) + tuple(new_out) + new_vec + tuple(spat_new)


def solution(mesh):
    rows3 = P("dp", "seq", None)
    dense = P(AXES, None)
    vec = P(AXES)
    spat = P(None, "seq", None)
    bias = P(None, "seq")
    in_specs = (rows3, P("dp"), rows3, dense, dense, vec, spat, bias)
    in_specs += (dense,) * 4 + (vec,) * 2 + (spat,) * 2 + (bias,) * 2
    out_specs = (rows3, rows3) + (dense,) * 6 + (vec,) * 3 + (spat,) * 3 + (bias,) * 3
    return jax.shard_map(local, mesh=mesh, in_specs=in_specs, out_specs=out_specs, check_vma=False)
```

```python
import functools

import jax
import jax.numpy as jnp
from jax import lax
from jax.experimental import pallas as pl
from jax.experimental.pallas import tpu as pltpu
from jax.sharding import PartitionSpec as P

D = 512
FF = 3072
HALF = 1536
PMAX = 324
PPAD = 336
P_MID = 196
P_LOW = 100
VCOLS = 256
ROWS = 2 * PPAD
GROUPS = 16
DEVS = 2 * GROUPS
VPER = 240
SCOLS = 384
BIAS_AT = 336
TOTAL_AT = 324
LSTRIDE = 168
MIB = 1024 * 1024
STEP = 10

NORM_EPS = 1e-05
BETA_ONE = 0.9
BETA_TWO = 0.99
ADAM_EPS = 1e-08
DENSE_RATE = 0.02
SMALL_RATE = 0.2
DENSE_DECAY = 0.05

BF = jnp.bfloat16
F32 = jnp.float32
AXES = ("dp", "seq")
VM = pl.BlockSpec(memory_space=pltpu.VMEM)
SM = pl.BlockSpec(memory_space=pltpu.SMEM)
HB = pl.BlockSpec(memory_space=pl.ANY)


class Route:
    def __init__(self, n):
        bits = n.bit_length() - 1
        assert n == 1 << bits and bits >= 2
        self.n = n
        top = n // 4
        self.direct = [top, 2 * top, 3 * top]
        low = [1 << b for b in range(bits - 2)]
        self.low = list(zip(low[::-1], low))
        masks = [(0, 0)] + [(m, m) for m in self.direct]
        for step in self.low:
            masks = masks + [(m[0] ^ step[0], m[1] ^ step[1]) for m in masks]
        self.masks = masks

    def swap(self, block, mask):
        pairs = []
        for dp in range(self.n):
            for seq in range(2):
                pairs.append((dp * 2 + seq, (dp ^ mask[seq]) * 2 + seq))
        return lax.ppermute(block, AXES, pairs)

    def cross(self, block):
        pairs = []
        for dp in range(self.n):
            for seq in range(2):
                pairs.append((dp * 2 + seq, dp * 2 + 1 - seq))
        return lax.ppermute(block, AXES, pairs)

    def order(self, seq_flip):
        place = lax.axis_index("dp")
        seq = lax.axis_index("seq")
        if seq_flip:
            seq = 1 - seq
        zero = jnp.array([m[0] for m in self.masks], jnp.int32)
        one = jnp.array([m[1] for m in self.masks], jnp.int32)
        return place ^ jnp.where(seq == 0, zero, one), seq

    def table(self):
        mine, seq = self.order(False)
        other, flip = self.order(True)
        return jnp.concatenate([mine * 2 + seq, other * 2 + flip])

    def spread(self, shard):
        first = jnp.concatenate([shard] + [self.swap(shard, (m, m)) for m in self.direct], axis=0)
        return self.widen(first)

    def widen(self, first):
        blocks = [first]
        for step in self.low:
            blocks = blocks + [self.swap(b, step) for b in blocks]
        return blocks

    def widen_direct(self, first):
        one, two = self.low
        return [first] + [self.swap(first, m) for m in (one, two, (one[0] ^ two[0], one[1] ^ two[1]))]

    def gather(self, shard):
        blocks = self.spread(shard)
        return blocks + [self.cross(b) for b in blocks]

    def collect(self, terms):
        cur = terms[0].shape[0]
        rows = cur // self.n

        def part(lower, upper):
            total = terms[0][lower:upper].astype(F32)
            for t in terms[1:]:
                total = total + t[lower:upper].astype(F32)
            return total

        terms = list(terms)
        for step in reversed(self.low):
            half = cur // 2
            terms.append(self.swap(part(half, cur).astype(BF), step))
            cur = half
        got = []
        for j, m in enumerate(self.direct):
            got.append(self.swap(part((j + 1) * rows, (j + 2) * rows).astype(BF), (m, m)))
        total = part(0, rows)
        return (total + got[0].astype(F32)) + (got[1].astype(F32) + got[2].astype(F32))

    def scatter(self, keep, send):
        return self.collect([keep, self.cross(send)])


def dot(a, b, dims):
    return lax.dot_general(a, b, (dims, ((), ())), preferred_element_type=F32)


NN = ((1,), (0,))
NT = ((1,), (1,))
TN = ((0,), (0,))


def gelu_parts(p):
    bell = jnp.exp(p * p * -0.5)
    d = 1.0 + jnp.abs(p) * (0.3275911 * 0.7071067811865476)
    t = pl.reciprocal(d, approx=True)
    t = t * (2.0 - d * t)
    poly = t * (
        0.127414796
        + t * (-0.142248368 + t * (0.7107068705 + t * (-0.7265760135 + t * 0.5307027145)))
    )
    tail = poly * bell
    phi_sum = jnp.where(p >= 0.0, 1.0 - tail, tail)
    return p * phi_sum, phi_sum + p * bell * 0.3989422804014327


def count_of(level):
    return jnp.where(level == 0, P_LOW, jnp.where(level == 1, P_MID, PMAX))


def masked_mix(mix, count):
    i = lax.broadcasted_iota(jnp.int32, (PPAD, SCOLS), 0)
    j = lax.broadcasted_iota(jnp.int32, (PPAD, SCOLS), 1)
    return jnp.where((i < count) & (j < count), mix.astype(F32), 0.0).astype(BF)


def live_rows(count, shape, start=0):
    return lax.broadcasted_iota(jnp.int32, shape, 0) + start < count


def live_mask(levels_ref, b, width):
    return live_rows(count_of(levels_ref[b]), (PPAD, width))


def fold(value):
    total = value[:, 0:128]
    for n in range(128, value.shape[1], 128):
        total = total + value[:, n : n + 128]
    return total


def spread_sum(ref, factor):
    return jnp.broadcast_to(jnp.sum(ref[...], axis=-1, keepdims=True) * factor, ref.shape)


def wide(value, times):
    return jnp.concatenate([value] * times, axis=1)


def start_blocks(table_ref, pieces, rows, cols, target, sem, extra=0):
    copies = []
    k = 0
    for piece in pieces:
        for j in range(piece.shape[0] // 16):
            at = pl.multiple_of(table_ref[k] * rows, 16)
            c = pltpu.make_async_copy(
                piece.at[pl.ds(j * 16, 16), pl.ds(cols[0], cols[1])], target.at[pl.ds(at + extra, 16)], sem.at[k]
            )
            c.start()
            copies.append(c)
            k += 1
    return copies


def row_loop(step, body):
    def run(i, carry):
        body(pl.multiple_of(i * step, step))
        return carry

    lax.fori_loop(0, ROWS // step, run, 0)


def call(kernel, out_shape, in_specs, scratch, flops, nbytes, *args, room=12):
    vm = pl.BlockSpec(memory_space=pltpu.VMEM)
    return pl.pallas_call(
        kernel,
        out_shape=out_shape,
        in_specs=in_specs,
        out_specs=jax.tree.map(lambda _: vm, out_shape),
        scratch_shapes=scratch,
        compiler_params=pltpu.CompilerParams(vmem_limit_bytes=room * MIB),
        cost_estimate=pl.CostEstimate(flops=flops, bytes_accessed=nbytes, transcendentals=0),
    )(*args)


def norm_parts(values):
    center = values - jnp.mean(values, axis=-1, keepdims=True)
    scale = lax.rsqrt(jnp.mean(center * center, axis=-1, keepdims=True) + NORM_EPS)
    return center * scale, scale


VSEG = {
    "g1": (0, D),
    "b1": (D, D),
    "c1l": (2 * D, HALF),
    "c1r": (2 * D + HALF, HALF),
    "g2": (2 * D + FF, HALF),
    "b2": (2 * D + FF + HALF, HALF),
    "c2": (2 * D + FF + 2 * HALF, D),
}
VEC = 2 * D + FF + 2 * HALF + D


def seg(ref, name):
    start, size = VSEG[name]
    return ref[0:1, start : start + size]

def adamw(weight, grad, first, second, rate, decay):
    first = BETA_ONE * first + (1.0 - BETA_ONE) * grad
    second = BETA_TWO * second + (1.0 - BETA_TWO) * grad * grad
    first_hat = first / (1.0 - BETA_ONE**STEP)
    second_hat = second / (1.0 - BETA_TWO**STEP)
    weight = weight - rate * (first_hat / (jnp.sqrt(second_hat) + ADAM_EPS) + decay * weight)
    return (weight, first, second)


CHUNK = 16
TILE = 256
BODY = 32
STRIPE = 112
LO = 2 * HALF
SPC = 2 * SCOLS


def sds(shape, dtype):
    return jax.ShapeDtypeStruct(shape, dtype)


def pack_dense(dense_in, dense_out, vec_row):
    rows = dense_in.shape[0]
    per = vec_row.shape[1]

    def kernel(w_hbm, o_hbm, v_hbm, out_ref, lo_ref, w_ref, o_ref, v_ref, row, sem):
        copies = [
            pltpu.make_async_copy(src, dst, sem.at[k])
            for k, (src, dst) in enumerate(((w_hbm, w_ref), (o_hbm, o_ref), (v_hbm, v_ref)))
        ]
        for c in copies:
            c.start()
        row[...] = jnp.zeros_like(row)
        for c in copies:
            c.wait()
        out_ref[:, 0:HALF] = w_ref[:, HALF:].astype(BF)
        row[0:1, 0:per] = v_ref[...]
        out_ref[:, HALF : HALF + VCOLS] = row[...].astype(BF)
        lo_ref[:, 0:HALF] = w_ref[:, 0:HALF].astype(BF)
        for g in range(3):
            lo_ref[:, HALF + g * D : HALF + (g + 1) * D] = o_ref[g * rows : (g + 1) * rows, :].astype(BF)

    scratch = [
        pltpu.VMEM(dense_in.shape, F32),
        pltpu.VMEM(dense_out.shape, F32),
        pltpu.VMEM(vec_row.shape, F32),
        pltpu.VMEM((rows, VCOLS), F32),
        pltpu.SemaphoreType.DMA((3,)),
    ]
    shape = (sds((rows, HALF + VCOLS), BF), sds((rows, LO), BF))
    return call(kernel, shape, [HB] * 3, scratch, 1000, 600000, dense_in, dense_out, vec_row, room=60)


def pack_images(sides, spatial, bias_col, patches, out_grad):
    half = patches.shape[1]

    def kernel(sides_ref, s_ref, b_ref, x_ref, g_ref, spat_ref, xs_ref, gs_ref, buf):
        away = 2 - 2 * sides_ref[0]
        for b in range(2):
            xs_ref[b] = x_ref[away + b]
            gs_ref[b] = g_ref[away + b]
        buf[...] = jnp.zeros_like(buf)
        for level in range(3):
            buf[:, 0:PMAX] = s_ref[level]
            rest = b_ref[level]
            for c in range(3):
                piece = rest.astype(BF).astype(F32)
                buf[:, BIAS_AT + c : BIAS_AT + c + 1] = piece
                rest = rest - piece
            spat_ref[level] = buf[...].astype(BF)

    pair = sds((2, half, D), BF)
    return call(
        kernel,
        (sds((3, half, SCOLS), BF), pair, pair),
        [SM] + [VM] * 4,
        [pltpu.VMEM((half, SCOLS), F32)],
        1000,
        3000000,
        sides,
        spatial,
        bias_col,
        patches,
        out_grad,
    )


def stack(pieces, after):
    count = len(pieces)
    rows, cols = pieces[0].shape

    def kernel(*refs):
        out = refs[count + len(after)]
        for k in range(count):
            out[k * rows : (k + 1) * rows, :] = refs[k][...]

    specs = [VM] * count + [HB] * len(after)
    return call(kernel, sds((count * rows, cols), BF), specs, [], 1000, 1000000, *pieces, *after)


def two_halves(is_first, own, got):
    own = own.astype(F32)
    got = got.astype(F32)
    return jnp.where(is_first, own, got), jnp.where(is_first, got, own)


def gate_norm(levels, sides, vec, v, part, spat_own, spat_got, after):
    half = spat_own.shape[1]
    count = len(after)

    def kernel(levels_ref, sides_ref, vec_ref, v_ref, part_ref, so_ref, sg_ref, *refs):
        gate_ref, hat_ref, scale_ref, spat_ref, mm_ref, mixf, mean, buf = refs[count:]
        is_first = sides_ref[0] == 0
        g_start = VSEG["g2"][0]
        b_start = VSEG["b2"][0]
        mean[...] = spread_sum(part_ref, 1.0 / HALF)

        def square_rows(r):
            for k in range(0, BODY, CHUNK):
                rows = pl.ds(r + k, CHUNK)
                mid = mean[rows, :]
                total = jnp.zeros((CHUNK, 128), F32)
                for n in range(0, HALF, 128):
                    center = v_ref[rows, n : n + 128] - mid
                    total = total + center * center
                buf[rows, :] = total

        row_loop(BODY, square_rows)
        scale_ref[...] = lax.rsqrt(spread_sum(buf, 1.0 / HALF) + NORM_EPS)

        def gate_rows(r):
            for k in range(0, BODY, CHUNK):
                rows = pl.ds(r + k, CHUNK)
                mid = wide(mean[rows, :], 2)
                scale = wide(scale_ref[rows, :], 2)
                for n in range(0, HALF, TILE):
                    hat = (v_ref[rows, n : n + TILE] - mid) * scale
                    hat_ref[rows, n : n + TILE] = hat.astype(BF)
                    gate = hat * vec_ref[0:1, g_start + n : g_start + n + TILE]
                    gate = (gate + vec_ref[0:1, b_start + n : b_start + n + TILE]).astype(BF)
                    gate_ref[rows, n : n + TILE] = gate

        row_loop(BODY, gate_rows)
        gate_ref[ROWS:, :] = jnp.zeros((SCOLS - PPAD, HALF), BF)
        for b in range(2):
            level = levels_ref[b]
            live = count_of(level)
            one, two = two_halves(is_first, so_ref[level], sg_ref[level])
            mixf[0:half, :] = one
            mixf[half : 2 * half, :] = two
            mixf[2 * half :, :] = jnp.zeros((PPAD - 2 * half, SCOLS), F32)
            bias = jnp.sum(mixf[:, TOTAL_AT:], axis=-1, keepdims=True)
            mm_ref[b] = masked_mix(mixf[...], live)

            def mix_tile(n, carry):
                cols = pl.ds(pl.multiple_of(n * 512, 512), 512)
                got = dot(mm_ref[b], gate_ref[b * PPAD : b * PPAD + SCOLS, cols], NN) + bias
                got = jnp.where(live_rows(live, (PPAD, 512)), got, 0.0)
                spat_ref[b * PPAD : (b + 1) * PPAD, cols] = got.astype(BF)
                return carry

            lax.fori_loop(0, HALF // 512, mix_tile, 0)

    return call(
        kernel,
        (
            sds((ROWS + SCOLS - PPAD, HALF), BF),
            sds((ROWS, HALF), BF),
            sds((ROWS, 128), F32),
            sds((ROWS, HALF), BF),
            sds((2, PPAD, SCOLS), BF),
        ),
        [SM] * 2 + [VM] * 5 + [HB] * count,
        [pltpu.VMEM((PPAD, SCOLS), F32), pltpu.VMEM((ROWS, 128), F32), pltpu.VMEM((ROWS, 128), F32)],
        6000000000,
        12000000,
        levels,
        sides,
        vec,
        v,
        part,
        spat_own,
        spat_got,
        *after,
        room=22,
    )


def gate_forward(table, sides, patches, x_got, out_grad, g_got, pieces):
    count = len(pieces)
    half = patches.shape[1]

    def kernel(table_ref, sides_ref, p_ref, xg_ref, o_ref, gg_ref, *refs):
        ins = refs[:count]
        outs = refs[count : count + 8]
        x_ref, og_ref, h_ref, pre, slope_ref, part, w_ref, vec_ref = outs
        vblk, xbuf, sem, vsem = refs[count + 8 :]
        vcopies = start_blocks(table_ref, ins, 16, (HALF, VCOLS), vblk, vsem)
        copies = start_blocks(table_ref, ins, 16, (0, HALF), w_ref, sem)
        me = sides_ref[0]
        is_first = me == 0

        for src, got, target in ((o_ref, gg_ref, og_ref), (p_ref, xg_ref, x_ref)):
            for b in range(2):
                one, two = two_halves(is_first, src[2 * me + b], got[b])
                xbuf[b * PPAD : b * PPAD + half, :] = one
                xbuf[b * PPAD + half : b * PPAD + 2 * half, :] = two
                xbuf[b * PPAD + 2 * half : (b + 1) * PPAD, :] = jnp.zeros((PPAD - 2 * half, D), F32)
            target[...] = xbuf[...].astype(BF)
        for c in vcopies:
            c.wait()
        for s in range(DEVS):
            row = vblk[16 * s : 16 * s + 16, :].astype(F32)[0:1, :VPER]
            vec_ref[0:1, VPER * s : VPER * s + VPER] = row

        def norm_one(r):
            hat, _ = norm_parts(xbuf[pl.ds(r, STRIPE), :])
            h_ref[pl.ds(r, STRIPE), :] = (hat * seg(vec_ref, "g1") + seg(vec_ref, "b1")).astype(BF)

        row_loop(STRIPE, norm_one)
        for c in copies:
            c.wait()
        c_start = VSEG["c1r"][0]

        def matmul(n, carry):
            at = pl.multiple_of(n * TILE, TILE)
            pre[:, pl.ds(at, TILE)] = dot(h_ref[...], w_ref[:, pl.ds(at, TILE)], NN)
            return carry

        lax.fori_loop(0, HALF // TILE, matmul, 0)

        def gelu_rows(r):
            for k in range(0, BODY, CHUNK):
                rows = pl.ds(r + k, CHUNK)
                total = jnp.zeros((CHUNK, 128), F32)
                for n in range(0, HALF, TILE):
                    v, slope = gelu_parts(pre[rows, n : n + TILE] + vec_ref[0:1, c_start + n : c_start + n + TILE])
                    pre[rows, n : n + TILE] = v
                    slope_ref[rows, n : n + TILE] = slope.astype(BF)
                    total = total + fold(v)
                part[rows, :] = total

        row_loop(BODY, gelu_rows)

    broad = sds((ROWS, HALF), BF)
    narrow = sds((ROWS, D), BF)
    out_shape = (
        narrow,
        narrow,
        narrow,
        sds((ROWS, HALF), F32),
        broad,
        sds((ROWS, 128), F32),
        sds((D, HALF), BF),
        sds((1, VEC), F32),
    )
    scratch = [
        pltpu.VMEM((D, VCOLS), BF),
        pltpu.VMEM((ROWS, D), F32),
        pltpu.SemaphoreType.DMA((DEVS,)),
        pltpu.SemaphoreType.DMA((DEVS,)),
    ]
    return call(
        kernel,
        out_shape,
        [SM] * 2 + [VM] * 4 + [HB] * count,
        scratch,
        10000000000,
        20000000,
        table,
        sides,
        patches,
        x_got,
        out_grad,
        g_got,
        *pieces,
        room=26,
    )


def split_rows(target, first, second, seq, value):
    half = first.shape[1]
    target[...] = value
    for b in range(2):
        one = target[b * PPAD : b * PPAD + half, :]
        two = target[b * PPAD + half : b * PPAD + 2 * half, :]
        first[b] = jnp.where(seq == 0, one, two).astype(BF)
        second[b] = jnp.where(seq == 0, two, one).astype(BF)


def middle(table, levels, sides, vec, h, spat, gate, grad_out, pieces):
    count = len(pieces)

    def kernel(table_ref, levels_ref, sides_ref, vec_ref, h_ref, spat_ref, gate_ref, og_ref, *refs):
        ins = refs[:count]
        gs_ref, gated_ref, q_ref, gb, wl, wo, keep, send, gsum_ref = refs[count : count + 9]
        pbuf, gbuf, cells, flat, sem = refs[count + 9 :]
        copies = start_blocks(table_ref, ins, 16, (0, HALF), wl, sem.at[0])
        for g in range(3):
            copies += start_blocks(table_ref, ins, 48, (HALF + g * D, D), wo, sem.at[1 + g], 16 * g)
        for b in range(2):
            rows = slice(b * PPAD, (b + 1) * PPAD)
            gb[rows, :] = jnp.where(live_mask(levels_ref, b, D), og_ref[rows, :].astype(F32), 0.0).astype(BF)
        gsum_ref[0:1, HALF : HALF + D] = jnp.sum(gb[...].astype(F32), axis=0, keepdims=True)
        cells[...] = jnp.zeros_like(cells)
        flat[...] = jnp.zeros_like(flat)
        for c in copies:
            c.wait()
        c_start = VSEG["c1l"][0]

        def tile(n, carry):
            at = pl.multiple_of(n * TILE, TILE)
            cols = pl.ds(at, TILE)
            pbuf[...] = dot(h_ref[...], wl[:, cols], NN)
            gbuf[...] = dot(gb[...], wo[cols, :], NT)
            shift = vec_ref[0:1, pl.ds(c_start + at, TILE)]
            total = jnp.zeros((CHUNK, TILE), F32)
            for k in range(0, ROWS, CHUNK):
                r = slice(k, k + CHUNK)
                u, slope = gelu_parts(pbuf[r, :] + shift)
                sp = spat_ref[r, cols].astype(F32)
                gg = gbuf[r, :]
                gated_ref[r, cols] = (u * sp).astype(BF)
                gs_ref[r, cols] = (gg * u).astype(BF)
                q = (gg * sp * slope).astype(BF)
                q_ref[r, cols] = q
                total = total + q.astype(F32)
            gsum_ref[0:1, cols] = jnp.sum(total, axis=0, keepdims=True)
            return carry

        lax.fori_loop(0, HALF // TILE, tile, 0)

        me = sides_ref[0]
        for b in range(2):
            level = levels_ref[b]
            count_b = count_of(level)
            gs = gs_ref[b * PPAD : (b + 1) * PPAD, :]
            got = dot(gs, gate_ref[b * PPAD : (b + 1) * PPAD, :], NT)
            sums = jnp.sum(gs.astype(F32), axis=-1, keepdims=True)
            j = lax.broadcasted_iota(jnp.int32, (PPAD, PPAD), 1)
            got = jnp.where(j < count_b, got, jnp.where(j == TOTAL_AT, sums, 0.0))
            cells[level, :, 0:PPAD] += got
        part = PMAX // 2
        for level in range(3):
            for k in range(2):
                flat[k, level * LSTRIDE : level * LSTRIDE + part, 0:PPAD] = cells[level, k * part : (k + 1) * part, 0:PPAD]
        for k in range(DEVS):
            target, side = (keep, me) if k < GROUPS else (send, 1 - me)
            r = pl.ds(k % GROUPS * 16, 16)
            block = flat[side, pl.ds(pl.multiple_of(sides_ref[1 + k] * 32, 32), 32), :].astype(BF)
            target[r, 0:SCOLS] = block[0:16]
            target[r, SCOLS:SPC] = block[16:32]

    broad = sds((ROWS, HALF), BF)
    payload = sds((D // 2, SPC), BF)
    out_shape = (
        broad,
        broad,
        broad,
        sds((ROWS, D), BF),
        sds((D, HALF), BF),
        sds((HALF, D), BF),
        payload,
        payload,
        sds((1, HALF + D), F32),
    )
    scratch = [
        pltpu.VMEM((ROWS, TILE), F32),
        pltpu.VMEM((ROWS, TILE), F32),
        pltpu.VMEM((3, PPAD, SCOLS), F32),
        pltpu.VMEM((2, 512, SCOLS), F32),
        pltpu.SemaphoreType.DMA((4, DEVS)),
    ]
    return call(
        kernel,
        out_shape,
        [SM] * 3 + [VM] * 5 + [HB] * count,
        scratch,
        8000000000,
        16000000,
        table,
        levels,
        sides,
        vec,
        h,
        spat,
        gate,
        grad_out,
        *pieces,
        room=28,
    )


def weight_grads(table, levels, sides, vec, gated, q, gb, h, wl, wo, x, half, after):
    count = len(after)

    def kernel(
        table_ref, levels_ref, sides_ref, vec_ref, t_ref, q_ref, gb_ref, h_ref, wl_ref, wo_ref, x_ref, *refs
    ):
        keep, send, send_up, stay_ref, away_ref, gh_ref, branch, gwo, gwl = refs[count:]

        def out_tile(n, carry):
            cols = pl.ds(pl.multiple_of(n * TILE, TILE), TILE)
            gwo[cols, :] = dot(t_ref[:, cols], gb_ref[...], TN).astype(BF)
            return carry

        lax.fori_loop(0, HALF // TILE, out_tile, 0)

        def in_tile(n, carry):
            cols = pl.ds(pl.multiple_of(n * TILE, TILE), TILE)
            gwl[cols, :] = dot(h_ref[:, cols], q_ref[...], TN).astype(BF)
            branch[:, cols] = dot(t_ref[...], wo_ref[:, cols], NN)
            gh_ref[:, cols] = dot(q_ref[...], wl_ref[cols, :], NT)
            return carry

        lax.fori_loop(0, D // TILE, in_tile, 0)
        me = sides_ref[0]
        live = jnp.concatenate([live_mask(levels_ref, b, D) for b in range(2)], axis=0)
        out = branch[...] + seg(vec_ref, "c2")
        split_rows(branch, stay_ref, away_ref, me, x_ref[...].astype(F32) + jnp.where(live, out, 0.0))
        for k in range(DEVS):
            dev = table_ref[k]
            target = keep if k < GROUPS else send if k < GROUPS * 3 // 2 else send_up
            r = pl.ds(k % (GROUPS if k < GROUPS else GROUPS // 2) * 16, 16)
            target[r, 0:HALF] = gwl[pl.ds(pl.multiple_of(dev * 16, 16), 16), :]
            for g in range(3):
                target[r, HALF + g * D : HALF + (g + 1) * D] = gwo[pl.ds(pl.multiple_of(dev * 48 + 16 * g, 16), 16), :]

    pair = sds((2, half, D), BF)
    payload = sds((D // 2, LO), BF)
    part = sds((D // 4, LO), BF)
    return call(
        kernel,
        (payload, part, part, pair, pair, sds((ROWS, D), F32)),
        [SM] * 3 + [VM] * 8 + [HB] * count,
        [pltpu.VMEM((ROWS, D), F32), pltpu.VMEM((HALF, D), BF), pltpu.VMEM((D, HALF), BF)],
        5000000000,
        15000000,
        table,
        levels,
        sides,
        vec,
        gated,
        q,
        gb,
        h,
        wl,
        wo,
        x,
        *after,
        room=24,
    )


def gate_backward(vec, gs, mm, hat, slope, scale, after):
    count = len(after)

    def kernel(vec_ref, gs_ref, mm_ref, hat_ref, slope_ref, scale_ref, *refs):
        gp, gsum_ref, dbuf, one, two, acc = refs[count:]

        for b in range(2):

            def mix_tile(n, carry):
                cols = pl.ds(pl.multiple_of(n * 512, 512), 512)
                got = dot(mm_ref[b], gs_ref[b * PPAD : (b + 1) * PPAD, cols], TN)
                dbuf[b * PPAD : (b + 1) * PPAD, cols] = got[0:PPAD]
                return carry

            lax.fori_loop(0, HALF // 512, mix_tile, 0)
        g_start = VSEG["g2"][0]

        def sum_rows(r):
            for k in range(0, BODY, CHUNK):
                rows = pl.ds(r + k, CHUNK)
                a = jnp.zeros((CHUNK, 128), F32)
                c = jnp.zeros((CHUNK, 128), F32)
                for n in range(0, HALF, TILE):
                    e = dbuf[rows, n : n + TILE] * vec_ref[0:1, g_start + n : g_start + n + TILE]
                    a = a + fold(e)
                    c = c + fold(e * hat_ref[rows, n : n + TILE].astype(F32))
                one[rows, :] = a
                two[rows, :] = c

        row_loop(BODY, sum_rows)
        one[...] = spread_sum(one, 1.0 / HALF)
        two[...] = spread_sum(two, 1.0 / HALF)
        acc[...] = jnp.zeros_like(acc)

        def grad_rows(r):
            for n in range(0, HALF, TILE):
                gain = vec_ref[0:1, g_start + n : g_start + n + TILE]
                sums = [jnp.zeros((CHUNK, TILE), F32) for _ in range(3)]
                for k in range(0, BODY, CHUNK):
                    rows = pl.ds(r + k, CHUNK)
                    d = dbuf[rows, n : n + TILE]
                    xh = hat_ref[rows, n : n + TILE].astype(F32)
                    inner = d * gain - wide(one[rows, :], 2) - xh * wide(two[rows, :], 2)
                    q = inner * wide(scale_ref[rows, :], 2) * slope_ref[rows, n : n + TILE].astype(F32)
                    q = q.astype(BF)
                    gp[rows, n : n + TILE] = q
                    sums = [sums[0] + d * xh, sums[1] + d, sums[2] + q.astype(F32)]
                for i in range(3):
                    acc[i, :, n : n + TILE] += sums[i]

        row_loop(BODY, grad_rows)
        for i in range(3):
            gsum_ref[0:1, i * HALF : (i + 1) * HALF] = jnp.sum(acc[i], axis=0, keepdims=True)

    return call(
        kernel,
        (sds((ROWS, HALF), BF), sds((1, 3 * HALF), F32)),
        [VM] * 6 + [HB] * count,
        [
            pltpu.VMEM((ROWS, HALF), F32),
            pltpu.VMEM((ROWS, 128), F32),
            pltpu.VMEM((ROWS, 128), F32),
            pltpu.VMEM((3, CHUNK, HALF), F32),
        ],
        3000000000,
        10000000,
        vec,
        gs,
        mm,
        hat,
        slope,
        scale,
        *after,
        room=20,
    )


def in_grads(gp, h, w, gh, after):
    count = len(after)

    def kernel(gp_ref, h_ref, w_ref, gh_ref, *refs):
        gwr, ghb = refs[count:]

        def in_tile(n, carry):
            cols = pl.ds(pl.multiple_of(n * TILE, TILE), TILE)
            ghb[:, cols] = gh_ref[:, cols] + dot(gp_ref[...], w_ref[cols, :], NT)
            gwr[cols, :] = dot(h_ref[:, cols], gp_ref[...], TN).astype(BF)
            return carry

        lax.fori_loop(0, D // TILE, in_tile, 0)

    return call(
        kernel,
        (sds((D, HALF), BF), sds((ROWS, D), F32)),
        [VM] * 4 + [HB] * count,
        [],
        3000000000,
        8000000,
        gp,
        h,
        w,
        gh,
        *after,
        room=14,
    )


def in_backward(table, sides, vec, gsum, gate_sum, gwr, ghb, x, grad_out, half, after):
    count = len(after)

    def kernel(table_ref, sides_ref, vec_ref, gsum_ref, gate_ref, gwr, ghb, x_ref, og_ref, *refs):
        keep, send, send_up, stay_ref, away_ref, acc, gvec, blocks, pgb = refs[count:]

        def put(name, value):
            start, size = VSEG[name]
            gvec[0:1, start : start + size] = value

        put("g2", gate_ref[0:1, 0:HALF])
        put("b2", gate_ref[0:1, HALF : 2 * HALF])
        put("c1r", gate_ref[0:1, 2 * HALF : 3 * HALF])
        put("c1l", gsum_ref[0:1, 0:HALF])
        put("c2", gsum_ref[0:1, HALF : HALF + D])
        acc[...] = jnp.zeros_like(acc)
        def in_rows(r):
            rows = pl.ds(r, STRIPE)
            xh, scale = norm_parts(x_ref[rows, :].astype(F32))
            d = ghb[rows, :]
            e = d * seg(vec_ref, "g1")
            one = jnp.mean(e, axis=-1, keepdims=True)
            two = jnp.mean(e * xh, axis=-1, keepdims=True)
            pgb[rows, :] = og_ref[rows, :].astype(F32) + scale * (e - one - xh * two)
            acc[0:1, :] += jnp.sum(d * xh, axis=0, keepdims=True)
            acc[1:2, :] += jnp.sum(d, axis=0, keepdims=True)

        row_loop(STRIPE, in_rows)
        put("g1", acc[0:1, :])
        put("b1", acc[1:2, :])
        split_rows(pgb, stay_ref, away_ref, sides_ref[0], pgb[...])
        blocks[...] = jnp.zeros_like(blocks)
        for s in range(DEVS):
            blocks[s, 0:1, 0:VPER] = gvec[0:1, VPER * s : VPER * s + VPER]
        for k in range(DEVS):
            dev = table_ref[k]
            target = keep if k < GROUPS else send if k < GROUPS * 3 // 2 else send_up
            r = pl.ds(k % (GROUPS if k < GROUPS else GROUPS // 2) * 16, 16)
            target[r, 0:HALF] = gwr[pl.ds(pl.multiple_of(dev * 16, 16), 16), :]
            target[r, HALF : HALF + VCOLS] = blocks[dev].astype(BF)

    payload = sds((D // 2, HALF + VCOLS), BF)
    part = sds((D // 4, HALF + VCOLS), BF)
    pair = sds((2, half, D), BF)
    return call(
        kernel,
        (payload, part, part, pair, pair),
        [SM] * 2 + [VM] * 7 + [HB] * count,
        [
            pltpu.VMEM((8, D), F32),
            pltpu.VMEM((1, VEC), F32),
            pltpu.VMEM((DEVS, 16, VCOLS), F32),
            pltpu.VMEM((ROWS, D), F32),
        ],
        2000000000,
        6000000,
        table,
        sides,
        vec,
        gsum,
        gate_sum,
        gwr,
        ghb,
        x,
        grad_out,
        *after,
        room=16,
    )


def add_part(terms, size, after, places=None):
    cols = terms[0].shape[1]
    count = len(terms)

    def kernel(*refs):
        for r in range(0, size, 16):
            rows = slice(r, r + 16)
            value = refs[0][rows, :].astype(F32)
            for t in refs[1:count]:
                value = value + t[rows, :].astype(F32)
            refs[count + len(after)][rows, :] = value.astype(BF)

    places = places or [1] * count
    blocks = [pl.BlockSpec((size, cols), lambda i, p=p: (p, 0)) for p in places]
    return pl.pallas_call(
        kernel,
        grid=(1,),
        out_shape=sds((size, cols), BF),
        in_specs=blocks + [HB] * len(after),
        out_specs=pl.BlockSpec((size, cols), lambda i: (0, 0)),
        compiler_params=pltpu.CompilerParams(vmem_limit_bytes=10 * MIB),
        cost_estimate=pl.CostEstimate(flops=1000000, bytes_accessed=3000000, transcendentals=0),
    )(*terms, *after)


def line_parts(terms, after):
    cols = terms[0].shape[1]
    count = len(terms)

    def kernel(*refs):
        own, outs = refs[count + 1], refs[count + 2 :]
        for m in range(4):
            rows = slice(16 * m, 16 * (m + 1))
            value = refs[0][rows, :].astype(F32)
            for t in refs[1:count]:
                value = value + t[rows, :].astype(F32)
            if m == 0:
                own[...] = value
            else:
                outs[m - 1][...] = value.astype(BF)

    block = pl.BlockSpec((64, cols), lambda i: (0, 0))
    one = pl.BlockSpec((16, cols), lambda i: (0, 0))
    return pl.pallas_call(
        kernel,
        grid=(1,),
        out_shape=[sds((16, cols), F32)] + [sds((16, cols), BF)] * 3,
        in_specs=[block] * count + [HB],
        out_specs=[one] * 4,
        compiler_params=pltpu.CompilerParams(vmem_limit_bytes=8 * MIB),
        cost_estimate=pl.CostEstimate(flops=1000000, bytes_accessed=3000000, transcendentals=0),
    )(*terms, after)


def line_sum(total, got, after):
    rows = total.shape[0]

    def kernel(own_ref, a_ref, b_ref, c_ref, after_ref, out_ref):
        near = own_ref[...].astype(F32) + a_ref[...].astype(F32)
        far = b_ref[...].astype(F32) + c_ref[...].astype(F32)
        out_ref[...] = (near + far).astype(BF)

    return call(kernel, sds((rows, SPC), BF), [VM] * 4 + [HB], [], 1000000, 500000, total, *got, after)


def line_spread(terms, after):
    count = len(terms)
    cols = terms[0].shape[1]

    def kernel(*refs):
        outs = refs[count + 1 :]
        for m in range(4):
            rows = slice(16 * m, 16 * (m + 1))
            value = refs[0][rows, :].astype(F32)
            for t in refs[1:count]:
                value = value + t[rows, :].astype(F32)
            value = value.astype(BF)
            for j in range(4):
                at = 16 * (m ^ j)
                outs[j][at : at + 16, :] = value

    block = pl.BlockSpec((64, cols), lambda i: (0, 0))
    return pl.pallas_call(
        kernel,
        grid=(1,),
        out_shape=[sds((64, cols), BF)] * 4,
        in_specs=[block] * count + [HB],
        out_specs=[block] * 4,
        compiler_params=pltpu.CompilerParams(vmem_limit_bytes=8 * MIB),
        cost_estimate=pl.CostEstimate(flops=1000000, bytes_accessed=1000000, transcendentals=0),
    )(*terms, after)


def finish_out(own, got, weight, first, second, after):
    def kernel(own_ref, a_ref, b_ref, c_ref, w_ref, m_ref, s_ref, after_ref, left_ref, nw, nm, ns):
        total = own_ref[...] + a_ref[...].astype(F32)
        total = total + (b_ref[...].astype(F32) + c_ref[...].astype(F32))
        left_ref[...] = total[:, 0:HALF]
        for g in range(3):
            rows = slice(16 * g, 16 * (g + 1))
            grad = total[:, HALF + g * D : HALF + (g + 1) * D]
            new = adamw(w_ref[rows, :], grad, m_ref[rows, :], s_ref[rows, :], DENSE_RATE, DENSE_DECAY)
            nw[rows, :] = new[0]
            nm[rows, :] = new[1]
            ns[rows, :] = new[2]

    same = sds(weight.shape, F32)
    return call(
        kernel,
        (sds((16, HALF), F32), same, same, same),
        [VM] * 7 + [HB],
        [],
        1000000,
        2000000,
        own,
        *got,
        weight,
        first,
        second,
        after,
    )


def finish_in(own, got, left, weight, first, second, after):
    def kernel(own_ref, a_ref, b_ref, c_ref, l_ref, w_ref, m_ref, s_ref, after_ref, nw, nm, ns, vec_ref):
        total = own_ref[...] + a_ref[...].astype(F32)
        total = total + (b_ref[...].astype(F32) + c_ref[...].astype(F32))
        vec_ref[...] = total[0:1, HALF:]
        for cols, grad in ((slice(0, HALF), l_ref[...]), (slice(HALF, FF), total[:, 0:HALF])):
            new = adamw(w_ref[:, cols], grad, m_ref[:, cols], s_ref[:, cols], DENSE_RATE, DENSE_DECAY)
            nw[:, cols] = new[0]
            nm[:, cols] = new[1]
            ns[:, cols] = new[2]

    same = sds(weight.shape, F32)
    return call(
        kernel,
        (same, same, same, sds((1, VCOLS), F32)),
        [VM] * 8 + [HB],
        [],
        1000000,
        2000000,
        own,
        *got,
        left,
        weight,
        first,
        second,
        after,
    )


def spatial_update(order, pieces, spatial, first, second, bias, bias_first, bias_second, after):
    count = len(pieces)
    rows = spatial.shape[1]

    def kernel(order_ref, *refs):
        ins = refs[:count]
        w_ref, m_ref, s_ref, bw, bm, bs = refs[count : count + 6]
        nw, nm, ns, nbw, nbm, nbs, flat = refs[count + 6 + len(after) :]
        k = 0
        for piece in ins:
            for j in range(piece.shape[0] // 16):
                at = pl.multiple_of(order_ref[k] * 32, 32)
                block = piece[16 * j : 16 * j + 16, :].astype(F32)
                flat[pl.ds(at, 16), :] = block[:, 0:SCOLS]
                flat[pl.ds(at + 16, 16), :] = block[:, SCOLS:]
                k += 1
        at = TOTAL_AT // 128 * 128
        totals = flat[:, at : at + 128].T[TOTAL_AT - at : TOTAL_AT - at + 1, :]
        for level in range(3):
            got = flat[level * LSTRIDE : level * LSTRIDE + rows, :]
            new = adamw(w_ref[level], got[:, 0:PMAX], m_ref[level], s_ref[level], DENSE_RATE, DENSE_DECAY)
            nw[level] = new[0]
            nm[level] = new[1]
            ns[level] = new[2]
            got = totals[:, level * LSTRIDE : level * LSTRIDE + rows]
            r = slice(level, level + 1)
            new = adamw(bw[r, :], got, bm[r, :], bs[r, :], SMALL_RATE, 0.0)
            nbw[r, :] = new[0]
            nbm[r, :] = new[1]
            nbs[r, :] = new[2]

    same = sds(spatial.shape, F32)
    small = sds(bias.shape, F32)
    return call(
        kernel,
        (same, same, same, small, small, small),
        [SM] + [VM] * (count + 6) + [HB] * len(after),
        [pltpu.VMEM((512, SCOLS), F32)],
        10000000,
        6000000,
        order,
        *pieces,
        spatial,
        first,
        second,
        bias,
        bias_first,
        bias_second,
        *after,
    )


def in_order(blocks, table, rows):
    cols = blocks[0].shape[1]
    whole = jnp.concatenate(blocks, axis=0).reshape(-1, rows, cols)
    back = jnp.zeros_like(table).at[table].set(jnp.arange(table.shape[0], dtype=table.dtype))
    return jnp.take(whole, back, axis=0)


def local(
    patches,
    resolution,
    out_grad,
    dense_in,
    dense_out,
    vectors,
    spatial,
    spatial_bias,
    in_first,
    in_second,
    out_first,
    out_second,
    vec_first,
    vec_second,
    spat_first,
    spat_second,
    bias_first,
    bias_second,
):
    route = Route(lax.axis_size("dp"))
    ndev = 2 * route.n
    fits = route.n == GROUPS
    seq = lax.axis_index("seq").astype(jnp.int32)
    rows = patches.shape[1]
    table = route.table()
    order = route.order(False)[0]
    in_rows = dense_in.shape[0]
    out_rows = dense_out.shape[0]
    vec_len = vectors.shape[0]
    if fits:
        ktable = table
        korder = table // 2
    else:
        ktable = jnp.arange(DEVS, dtype=jnp.int32)
        korder = jnp.arange(DEVS, dtype=jnp.int32) % GROUPS
    sides = jnp.concatenate([seq[None], korder])
    levels = lax.dynamic_slice_in_dim(resolution, seq * 2, 2, 0)

    right_shard, lo_shard = pack_dense(dense_in, dense_out, vectors.reshape(1, vec_len))
    line = [right_shard] + [route.swap(right_shard, (m, m)) for m in route.direct]
    lo_line = [lo_shard] + [route.swap(lo_shard, (m, m)) for m in route.direct]
    spat_own, x_send, g_send = pack_images(sides, spatial, spatial_bias.reshape(3, rows, 1), patches, out_grad)
    x_got = route.cross(x_send)
    g_got = route.cross(g_send)
    spat_got = route.cross(spat_own)
    if fits:
        right_blocks = route.widen_direct(stack(line, []))
        lo_blocks = route.widen_direct(stack(lo_line, [right_blocks[1]]))
    else:
        right_blocks = route.widen(jnp.concatenate(line, axis=0))
        lo_blocks = route.widen(jnp.concatenate(lo_line, axis=0))
    right_blocks = right_blocks + [route.cross(b) for b in right_blocks]
    lo_blocks = lo_blocks + [route.cross(b) for b in lo_blocks]
    if not fits:
        whole = in_order(right_blocks, table, in_rows)
        all_vec = whole[:, 0, HALF : HALF + vec_len].reshape(DEVS, 1, VPER)
        all_vec = jnp.pad(all_vec, ((0, 0), (0, 15), (0, VCOLS - VPER))).reshape(D, VCOLS)
        right_blocks = [jnp.concatenate([whole[:, :, :HALF].reshape(D, HALF), all_vec], axis=1)]
        whole = in_order(lo_blocks, table, in_rows)
        outs = whole[:, :, HALF:].reshape(ndev, in_rows, 3, D).transpose(0, 2, 1, 3).reshape(DEVS, 3, 16, D)
        outs = outs.transpose(0, 2, 1, 3).reshape(D, HALF)
        lo_blocks = [jnp.concatenate([whole[:, :, :HALF].reshape(D, HALF), outs], axis=1)]

    x, grad_out, h, v, slope, part, weight_right, vec = gate_forward(
        ktable, sides, patches, x_got, out_grad, g_got, right_blocks
    )
    gate, hat, scale, spat, mm = gate_norm(levels, sides, vec, v, part, spat_own, spat_got, [])
    gs, gated, q, gb, wl, wo, sp_keep, sp_send, gsum = middle(ktable, levels, sides, vec, h, spat, gate, grad_out, lo_blocks)
    near, far = route.low[-1], route.low[0]
    after = [[], [], [], []]
    if fits:
        sp_got = route.cross(sp_send)
        sp_part = add_part([sp_keep, sp_got], 128, [])
        sp_terms = [sp_keep, sp_got, route.swap(sp_part, near)]
        after[0] = [sp_part]
    lo_keep, lo_send, lo_up, mixed_stay, mixed_away, gh = weight_grads(
        ktable, levels, sides, vec, gated, q, gb, h, wl, wo, x, rows, after[0]
    )
    if fits:
        lo_up = route.cross(lo_up)
        lo_terms = [lo_keep, route.cross(lo_send)]
        sp_part = add_part(sp_terms, 64, [lo_keep])
        sp_terms.append(route.swap(sp_part, far))
        lo_part = add_part([lo_keep, lo_up], 128, [sp_part], [1, 0])
        lo_terms.append(route.swap(lo_part, near))
        after[1] = [lo_part]
    mixed_got = route.cross(mixed_away)
    gp, gate_sum = gate_backward(vec, gs, mm, hat, slope, scale, after[1])
    if fits:
        sp_own, *sends = line_spread(sp_terms, gate_sum)
        sp_got = [route.swap(p, (m, m)) for p, m in zip(sends, route.direct)]
        after[2] = [sp_own]
    gwr, ghb = in_grads(gp, h, weight_right, gh, after[2])
    if fits:
        lo_part = add_part(lo_terms, 64, [gwr])
        lo_terms.append(route.swap(lo_part, far))
        after[3] = [lo_part]
    right_keep, right_send, right_up, grad_stay, grad_away = in_backward(
        ktable, sides, vec, gsum, gate_sum, gwr, ghb, x, grad_out, rows, after[3]
    )
    if fits:
        right_up = route.cross(right_up)
        right_terms = [right_keep, route.cross(right_send)]
        right_part = add_part([right_keep, right_up], 128, [], [1, 0])
        right_terms.append(route.swap(right_part, near))
        lo_own, *sends = line_parts(lo_terms, right_part)
        lo_got = [route.swap(p, (m, m)) for p, m in zip(sends, route.direct)]
        sp_sum = line_sum(sp_own, sp_got, lo_own)
        spat_pieces = route.widen(sp_sum)
        right_part = add_part(right_terms, 64, [sp_sum])
        right_terms.append(route.swap(right_part, far))
        right_own, *sends = line_parts(right_terms, right_part)
        right_got = [route.swap(p, (m, m)) for p, m in zip(sends, route.direct)]
        left_sum, *new_out = finish_out(lo_own, lo_got, dense_out, out_first, out_second, right_own)
        korder = order
        after = [left_sum]
    else:
        both = jnp.concatenate([lo_keep, lo_send, lo_up])
        outs = both[:, HALF:LO].reshape(DEVS, 16, 3, D).transpose(0, 2, 1, 3).reshape(ndev, out_rows, D)
        outs = jnp.take(outs, table, axis=0).reshape(HALF, D)
        out_sum = route.scatter(outs[: HALF // 2], outs[HALF // 2 :])
        lefts = jnp.take(both[:, :HALF].reshape(ndev, in_rows, HALF), table, axis=0).reshape(D, HALF)
        left_sum = route.scatter(lefts[: D // 2], lefts[D // 2 :])
        per = 512 // route.n

        def spat_blocks(part, flip):
            flat = part.reshape(GROUPS, 16, 2, SCOLS).transpose(0, 2, 1, 3).reshape(route.n, per, SCOLS)
            return jnp.take(flat, route.order(flip)[0], axis=0).reshape(512, SCOLS)

        spat_part = route.scatter(spat_blocks(sp_keep, False), spat_blocks(sp_send, True)).astype(BF)
        flat = in_order(route.spread(spat_part), order, per).reshape(GROUPS, 2, 16, SCOLS)
        spat_pieces = [flat.transpose(0, 2, 1, 3).reshape(GROUPS * 16, SPC)]
        korder = jnp.arange(GROUPS, dtype=jnp.int32)
        after = []
        both = jnp.concatenate([right_keep, right_send, right_up])
        vecs = jnp.take(both[::16, HALF : HALF + VPER].reshape(ndev, vec_len), table, axis=0)
        vec_sum = route.scatter(vecs[: route.n], vecs[route.n :]).reshape(vec_len)
        rights = jnp.take(both[:, :HALF].reshape(ndev, in_rows, HALF), table, axis=0).reshape(D, HALF)
        right_sum = route.scatter(rights[: D // 2], rights[D // 2 :])
        in_sum = jnp.concatenate([left_sum, right_sum], axis=1)
        new_in = adamw(dense_in, in_sum, in_first, in_second, DENSE_RATE, DENSE_DECAY)
        new_out = adamw(dense_out, out_sum, out_first, out_second, DENSE_RATE, DENSE_DECAY)

    def whole_images(stays, came):
        return jnp.concatenate([jnp.where(seq == 0, stays, came), jnp.where(seq == 0, came, stays)], axis=0)

    mixed = whole_images(mixed_stay, mixed_got)
    patches_grad = whole_images(grad_stay, route.cross(grad_away))
    spat_new = spatial_update(
        korder, spat_pieces, spatial, spat_first, spat_second, spatial_bias, bias_first, bias_second, after
    )
    if fits:
        *new_in, vec_sum = finish_in(right_own, right_got, left_sum, dense_in, in_first, in_second, spat_new[0])
        vec_sum = vec_sum[0, :vec_len]
    new_vec = adamw(vectors, vec_sum, vec_first, vec_second, SMALL_RATE, 0.0)
    return (mixed, patches_grad) + tuple(new_in) + tuple(new_out) + new_vec + tuple(spat_new)


def solution(mesh):
    rows3 = P("dp", "seq", None)
    dense = P(AXES, None)
    vec = P(AXES)
    spat = P(None, "seq", None)
    bias = P(None, "seq")
    in_specs = (rows3, P("dp"), rows3, dense, dense, vec, spat, bias)
    in_specs += (dense,) * 4 + (vec,) * 2 + (spat,) * 2 + (bias,) * 2
    out_specs = (rows3, rows3) + (dense,) * 6 + (vec,) * 3 + (spat,) * 3 + (bias,) * 3
    return jax.shard_map(local, mesh=mesh, in_specs=in_specs, out_specs=out_specs, check_vma=False)
```

```python
import functools

import jax
import jax.numpy as jnp
from jax import lax
from jax.experimental import pallas as pl
from jax.experimental.pallas import tpu as pltpu
from jax.sharding import PartitionSpec as P

D = 512
FF = 3072
HALF = 1536
PMAX = 324
PPAD = 336
P_MID = 196
P_LOW = 100
VCOLS = 256
ROWS = 2 * PPAD
GROUPS = 16
DEVS = 2 * GROUPS
VPER = 240
SCOLS = 384
BIAS_AT = 336
TOTAL_AT = 324
LSTRIDE = 168
MIB = 1024 * 1024
STEP = 10

NORM_EPS = 1e-05
BETA_ONE = 0.9
BETA_TWO = 0.99
ADAM_EPS = 1e-08
DENSE_RATE = 0.02
SMALL_RATE = 0.2
DENSE_DECAY = 0.05

BF = jnp.bfloat16
F32 = jnp.float32
AXES = ("dp", "seq")
VM = pl.BlockSpec(memory_space=pltpu.VMEM)
SM = pl.BlockSpec(memory_space=pltpu.SMEM)
HB = pl.BlockSpec(memory_space=pl.ANY)


class Route:
    def __init__(self, n):
        bits = n.bit_length() - 1
        assert n == 1 << bits and bits >= 2
        self.n = n
        top = n // 4
        self.direct = [top, 2 * top, 3 * top]
        low = [1 << b for b in range(bits - 2)]
        self.low = list(zip(low[::-1], low))
        masks = [(0, 0)] + [(m, m) for m in self.direct]
        for step in self.low:
            masks = masks + [(m[0] ^ step[0], m[1] ^ step[1]) for m in masks]
        self.masks = masks

    def swap(self, block, mask):
        pairs = []
        for dp in range(self.n):
            for seq in range(2):
                pairs.append((dp * 2 + seq, (dp ^ mask[seq]) * 2 + seq))
        return lax.ppermute(block, AXES, pairs)

    def cross(self, block):
        pairs = []
        for dp in range(self.n):
            for seq in range(2):
                pairs.append((dp * 2 + seq, dp * 2 + 1 - seq))
        return lax.ppermute(block, AXES, pairs)

    def order(self, seq_flip):
        place = lax.axis_index("dp")
        seq = lax.axis_index("seq")
        if seq_flip:
            seq = 1 - seq
        zero = jnp.array([m[0] for m in self.masks], jnp.int32)
        one = jnp.array([m[1] for m in self.masks], jnp.int32)
        return place ^ jnp.where(seq == 0, zero, one), seq

    def table(self):
        mine, seq = self.order(False)
        other, flip = self.order(True)
        return jnp.concatenate([mine * 2 + seq, other * 2 + flip])

    def spread(self, shard):
        first = jnp.concatenate([shard] + [self.swap(shard, (m, m)) for m in self.direct], axis=0)
        return self.widen(first)

    def widen(self, first):
        blocks = [first]
        for step in self.low:
            blocks = blocks + [self.swap(b, step) for b in blocks]
        return blocks

    def widen_direct(self, first):
        one, two = self.low
        return [first] + [self.swap(first, m) for m in (one, two, (one[0] ^ two[0], one[1] ^ two[1]))]

    def gather(self, shard):
        blocks = self.spread(shard)
        return blocks + [self.cross(b) for b in blocks]

    def collect(self, terms):
        cur = terms[0].shape[0]
        rows = cur // self.n

        def part(lower, upper):
            total = terms[0][lower:upper].astype(F32)
            for t in terms[1:]:
                total = total + t[lower:upper].astype(F32)
            return total

        terms = list(terms)
        for step in reversed(self.low):
            half = cur // 2
            terms.append(self.swap(part(half, cur).astype(BF), step))
            cur = half
        got = []
        for j, m in enumerate(self.direct):
            got.append(self.swap(part((j + 1) * rows, (j + 2) * rows).astype(BF), (m, m)))
        total = part(0, rows)
        return (total + got[0].astype(F32)) + (got[1].astype(F32) + got[2].astype(F32))

    def scatter(self, keep, send):
        return self.collect([keep, self.cross(send)])


def dot(a, b, dims):
    return lax.dot_general(a, b, (dims, ((), ())), preferred_element_type=F32)


NN = ((1,), (0,))
NT = ((1,), (1,))
TN = ((0,), (0,))


def gelu_parts(p):
    bell = jnp.exp(p * p * -0.5)
    d = 1.0 + jnp.abs(p) * (0.3275911 * 0.7071067811865476)
    t = pl.reciprocal(d, approx=True)
    t = t * (2.0 - d * t)
    poly = t * (
        0.127414796
        + t * (-0.142248368 + t * (0.7107068705 + t * (-0.7265760135 + t * 0.5307027145)))
    )
    tail = poly * bell
    phi_sum = jnp.where(p >= 0.0, 1.0 - tail, tail)
    return p * phi_sum, phi_sum + p * bell * 0.3989422804014327


def count_of(level):
    return jnp.where(level == 0, P_LOW, jnp.where(level == 1, P_MID, PMAX))


def masked_mix(mix, count):
    i = lax.broadcasted_iota(jnp.int32, (PPAD, SCOLS), 0)
    j = lax.broadcasted_iota(jnp.int32, (PPAD, SCOLS), 1)
    return jnp.where((i < count) & (j < count), mix.astype(F32), 0.0).astype(BF)


def live_rows(count, shape, start=0):
    return lax.broadcasted_iota(jnp.int32, shape, 0) + start < count


def live_mask(levels_ref, b, width):
    return live_rows(count_of(levels_ref[b]), (PPAD, width))


def fold(value):
    total = value[:, 0:128]
    for n in range(128, value.shape[1], 128):
        total = total + value[:, n : n + 128]
    return total


def spread_sum(ref, factor):
    return jnp.broadcast_to(jnp.sum(ref[...], axis=-1, keepdims=True) * factor, ref.shape)


def wide(value, times):
    return jnp.concatenate([value] * times, axis=1)


def start_blocks(table_ref, pieces, rows, cols, target, sem, extra=0):
    copies = []
    k = 0
    for piece in pieces:
        for j in range(piece.shape[0] // 16):
            at = pl.multiple_of(table_ref[k] * rows, 16)
            c = pltpu.make_async_copy(
                piece.at[pl.ds(j * 16, 16), pl.ds(cols[0], cols[1])], target.at[pl.ds(at + extra, 16)], sem.at[k]
            )
            c.start()
            copies.append(c)
            k += 1
    return copies


def row_loop(step, body):
    def run(i, carry):
        body(pl.multiple_of(i * step, step))
        return carry

    lax.fori_loop(0, ROWS // step, run, 0)


def call(kernel, out_shape, in_specs, scratch, flops, nbytes, *args, room=12):
    vm = pl.BlockSpec(memory_space=pltpu.VMEM)
    return pl.pallas_call(
        kernel,
        out_shape=out_shape,
        in_specs=in_specs,
        out_specs=jax.tree.map(lambda _: vm, out_shape),
        scratch_shapes=scratch,
        compiler_params=pltpu.CompilerParams(vmem_limit_bytes=room * MIB),
        cost_estimate=pl.CostEstimate(flops=flops, bytes_accessed=nbytes, transcendentals=0),
    )(*args)


def norm_parts(values):
    center = values - jnp.mean(values, axis=-1, keepdims=True)
    scale = lax.rsqrt(jnp.mean(center * center, axis=-1, keepdims=True) + NORM_EPS)
    return center * scale, scale


VSEG = {
    "g1": (0, D),
    "b1": (D, D),
    "c1l": (2 * D, HALF),
    "c1r": (2 * D + HALF, HALF),
    "g2": (2 * D + FF, HALF),
    "b2": (2 * D + FF + HALF, HALF),
    "c2": (2 * D + FF + 2 * HALF, D),
}
VEC = 2 * D + FF + 2 * HALF + D


def seg(ref, name):
    start, size = VSEG[name]
    return ref[0:1, start : start + size]

def adamw(weight, grad, first, second, rate, decay):
    first = BETA_ONE * first + (1.0 - BETA_ONE) * grad
    second = BETA_TWO * second + (1.0 - BETA_TWO) * grad * grad
    first_hat = first / (1.0 - BETA_ONE**STEP)
    second_hat = second / (1.0 - BETA_TWO**STEP)
    weight = weight - rate * (first_hat / (jnp.sqrt(second_hat) + ADAM_EPS) + decay * weight)
    return (weight, first, second)


CHUNK = 16
TILE = 256
BODY = 32
STRIPE = 112
LO = 2 * HALF
SPC = 2 * SCOLS


def sds(shape, dtype):
    return jax.ShapeDtypeStruct(shape, dtype)


def pack_dense(dense_in, dense_out, vec_row):
    rows = dense_in.shape[0]
    per = vec_row.shape[1]

    def kernel(w_hbm, o_hbm, v_hbm, out_ref, lo_ref, w_ref, o_ref, v_ref, row, sem):
        copies = [
            pltpu.make_async_copy(src, dst, sem.at[k])
            for k, (src, dst) in enumerate(((w_hbm, w_ref), (o_hbm, o_ref), (v_hbm, v_ref)))
        ]
        for c in copies:
            c.start()
        row[...] = jnp.zeros_like(row)
        for c in copies:
            c.wait()
        out_ref[:, 0:HALF] = w_ref[:, HALF:].astype(BF)
        row[0:1, 0:per] = v_ref[...]
        out_ref[:, HALF : HALF + VCOLS] = row[...].astype(BF)
        lo_ref[:, 0:HALF] = w_ref[:, 0:HALF].astype(BF)
        for g in range(3):
            lo_ref[:, HALF + g * D : HALF + (g + 1) * D] = o_ref[g * rows : (g + 1) * rows, :].astype(BF)

    scratch = [
        pltpu.VMEM(dense_in.shape, F32),
        pltpu.VMEM(dense_out.shape, F32),
        pltpu.VMEM(vec_row.shape, F32),
        pltpu.VMEM((rows, VCOLS), F32),
        pltpu.SemaphoreType.DMA((3,)),
    ]
    shape = (sds((rows, HALF + VCOLS), BF), sds((rows, LO), BF))
    return call(kernel, shape, [HB] * 3, scratch, 1000, 600000, dense_in, dense_out, vec_row, room=60)


def pack_images(sides, spatial, bias_col, patches, out_grad):
    half = patches.shape[1]

    def kernel(sides_ref, s_ref, b_ref, x_ref, g_ref, spat_ref, xs_ref, gs_ref, buf):
        away = 2 - 2 * sides_ref[0]
        for b in range(2):
            xs_ref[b] = x_ref[away + b]
            gs_ref[b] = g_ref[away + b]
        buf[...] = jnp.zeros_like(buf)
        for level in range(3):
            buf[:, 0:PMAX] = s_ref[level]
            rest = b_ref[level]
            for c in range(3):
                piece = rest.astype(BF).astype(F32)
                buf[:, BIAS_AT + c : BIAS_AT + c + 1] = piece
                rest = rest - piece
            spat_ref[level] = buf[...].astype(BF)

    pair = sds((2, half, D), BF)
    return call(
        kernel,
        (sds((3, half, SCOLS), BF), pair, pair),
        [SM] + [VM] * 4,
        [pltpu.VMEM((half, SCOLS), F32)],
        1000,
        3000000,
        sides,
        spatial,
        bias_col,
        patches,
        out_grad,
    )


def stack(pieces, after):
    count = len(pieces)
    rows, cols = pieces[0].shape

    def kernel(*refs):
        out = refs[count + len(after)]
        for k in range(count):
            out[k * rows : (k + 1) * rows, :] = refs[k][...]

    specs = [VM] * count + [HB] * len(after)
    return call(kernel, sds((count * rows, cols), BF), specs, [], 1000, 1000000, *pieces, *after)


def two_halves(is_first, own, got):
    own = own.astype(F32)
    got = got.astype(F32)
    return jnp.where(is_first, own, got), jnp.where(is_first, got, own)


def gate_norm(levels, sides, vec, v, part, spat_own, spat_got, after):
    half = spat_own.shape[1]
    count = len(after)

    def kernel(levels_ref, sides_ref, vec_ref, v_ref, part_ref, so_ref, sg_ref, *refs):
        gate_ref, hat_ref, scale_ref, spat_ref, mm_ref, mixf, mean, buf = refs[count:]
        is_first = sides_ref[0] == 0
        g_start = VSEG["g2"][0]
        b_start = VSEG["b2"][0]
        mean[...] = spread_sum(part_ref, 1.0 / HALF)

        def square_rows(r):
            for k in range(0, BODY, CHUNK):
                rows = pl.ds(r + k, CHUNK)
                mid = mean[rows, :]
                total = jnp.zeros((CHUNK, 128), F32)
                for n in range(0, HALF, 128):
                    center = v_ref[rows, n : n + 128] - mid
                    total = total + center * center
                buf[rows, :] = total

        row_loop(BODY, square_rows)
        scale_ref[...] = lax.rsqrt(spread_sum(buf, 1.0 / HALF) + NORM_EPS)

        def gate_rows(r):
            for k in range(0, BODY, CHUNK):
                rows = pl.ds(r + k, CHUNK)
                mid = wide(mean[rows, :], 2)
                scale = wide(scale_ref[rows, :], 2)
                for n in range(0, HALF, TILE):
                    hat = (v_ref[rows, n : n + TILE] - mid) * scale
                    hat_ref[rows, n : n + TILE] = hat.astype(BF)
                    gate = hat * vec_ref[0:1, g_start + n : g_start + n + TILE]
                    gate = (gate + vec_ref[0:1, b_start + n : b_start + n + TILE]).astype(BF)
                    gate_ref[rows, n : n + TILE] = gate

        row_loop(BODY, gate_rows)
        gate_ref[ROWS:, :] = jnp.zeros((SCOLS - PPAD, HALF), BF)
        for b in range(2):
            level = levels_ref[b]
            live = count_of(level)
            one, two = two_halves(is_first, so_ref[level], sg_ref[level])
            mixf[0:half, :] = one
            mixf[half : 2 * half, :] = two
            mixf[2 * half :, :] = jnp.zeros((PPAD - 2 * half, SCOLS), F32)
            bias = jnp.sum(mixf[:, TOTAL_AT:], axis=-1, keepdims=True)
            mm_ref[b] = masked_mix(mixf[...], live)

            def mix_tile(n, carry):
                cols = pl.ds(pl.multiple_of(n * 512, 512), 512)
                got = dot(mm_ref[b], gate_ref[b * PPAD : b * PPAD + SCOLS, cols], NN) + bias
                got = jnp.where(live_rows(live, (PPAD, 512)), got, 0.0)
                spat_ref[b * PPAD : (b + 1) * PPAD, cols] = got.astype(BF)
                return carry

            lax.fori_loop(0, HALF // 512, mix_tile, 0)

    return call(
        kernel,
        (
            sds((ROWS + SCOLS - PPAD, HALF), BF),
            sds((ROWS, HALF), BF),
            sds((ROWS, 128), F32),
            sds((ROWS, HALF), BF),
            sds((2, PPAD, SCOLS), BF),
        ),
        [SM] * 2 + [VM] * 5 + [HB] * count,
        [pltpu.VMEM((PPAD, SCOLS), F32), pltpu.VMEM((ROWS, 128), F32), pltpu.VMEM((ROWS, 128), F32)],
        6000000000,
        12000000,
        levels,
        sides,
        vec,
        v,
        part,
        spat_own,
        spat_got,
        *after,
        room=22,
    )


def gate_forward(table, sides, patches, x_got, out_grad, g_got, pieces):
    count = len(pieces)
    half = patches.shape[1]

    def kernel(table_ref, sides_ref, p_ref, xg_ref, o_ref, gg_ref, *refs):
        ins = refs[:count]
        outs = refs[count : count + 8]
        x_ref, og_ref, h_ref, pre, slope_ref, part, w_ref, vec_ref = outs
        vblk, xbuf, sem, vsem = refs[count + 8 :]
        vcopies = start_blocks(table_ref, ins, 16, (HALF, VCOLS), vblk, vsem)
        copies = start_blocks(table_ref, ins, 16, (0, HALF), w_ref, sem)
        me = sides_ref[0]
        is_first = me == 0

        for src, got, target in ((o_ref, gg_ref, og_ref), (p_ref, xg_ref, x_ref)):
            for b in range(2):
                one, two = two_halves(is_first, src[2 * me + b], got[b])
                xbuf[b * PPAD : b * PPAD + half, :] = one
                xbuf[b * PPAD + half : b * PPAD + 2 * half, :] = two
                xbuf[b * PPAD + 2 * half : (b + 1) * PPAD, :] = jnp.zeros((PPAD - 2 * half, D), F32)
            target[...] = xbuf[...].astype(BF)
        for c in vcopies:
            c.wait()
        for s in range(DEVS):
            row = vblk[16 * s : 16 * s + 16, :].astype(F32)[0:1, :VPER]
            vec_ref[0:1, VPER * s : VPER * s + VPER] = row

        def norm_one(r):
            hat, _ = norm_parts(xbuf[pl.ds(r, STRIPE), :])
            h_ref[pl.ds(r, STRIPE), :] = (hat * seg(vec_ref, "g1") + seg(vec_ref, "b1")).astype(BF)

        row_loop(STRIPE, norm_one)
        for c in copies:
            c.wait()
        c_start = VSEG["c1r"][0]

        def matmul(n, carry):
            at = pl.multiple_of(n * TILE, TILE)
            pre[:, pl.ds(at, TILE)] = dot(h_ref[...], w_ref[:, pl.ds(at, TILE)], NN)
            return carry

        lax.fori_loop(0, HALF // TILE, matmul, 0)

        def gelu_rows(r):
            for k in range(0, BODY, CHUNK):
                rows = pl.ds(r + k, CHUNK)
                total = jnp.zeros((CHUNK, 128), F32)
                for n in range(0, HALF, TILE):
                    v, slope = gelu_parts(pre[rows, n : n + TILE] + vec_ref[0:1, c_start + n : c_start + n + TILE])
                    pre[rows, n : n + TILE] = v
                    slope_ref[rows, n : n + TILE] = slope.astype(BF)
                    total = total + fold(v)
                part[rows, :] = total

        row_loop(BODY, gelu_rows)

    broad = sds((ROWS, HALF), BF)
    narrow = sds((ROWS, D), BF)
    out_shape = (
        narrow,
        narrow,
        narrow,
        sds((ROWS, HALF), F32),
        broad,
        sds((ROWS, 128), F32),
        sds((D, HALF), BF),
        sds((1, VEC), F32),
    )
    scratch = [
        pltpu.VMEM((D, VCOLS), BF),
        pltpu.VMEM((ROWS, D), F32),
        pltpu.SemaphoreType.DMA((DEVS,)),
        pltpu.SemaphoreType.DMA((DEVS,)),
    ]
    return call(
        kernel,
        out_shape,
        [SM] * 2 + [VM] * 4 + [HB] * count,
        scratch,
        10000000000,
        20000000,
        table,
        sides,
        patches,
        x_got,
        out_grad,
        g_got,
        *pieces,
        room=26,
    )


def split_rows(target, first, second, seq, value):
    half = first.shape[1]
    target[...] = value
    for b in range(2):
        one = target[b * PPAD : b * PPAD + half, :]
        two = target[b * PPAD + half : b * PPAD + 2 * half, :]
        first[b] = jnp.where(seq == 0, one, two).astype(BF)
        second[b] = jnp.where(seq == 0, two, one).astype(BF)


def middle(table, levels, sides, vec, h, spat, gate, grad_out, pieces):
    count = len(pieces)

    def kernel(table_ref, levels_ref, sides_ref, vec_ref, h_ref, spat_ref, gate_ref, og_ref, *refs):
        ins = refs[:count]
        gs_ref, gated_ref, q_ref, gb, wl, wo, keep, send, gsum_ref = refs[count : count + 9]
        pbuf, gbuf, cells, flat, sem = refs[count + 9 :]
        copies = start_blocks(table_ref, ins, 16, (0, HALF), wl, sem.at[0])
        for g in range(3):
            copies += start_blocks(table_ref, ins, 48, (HALF + g * D, D), wo, sem.at[1 + g], 16 * g)
        for b in range(2):
            rows = slice(b * PPAD, (b + 1) * PPAD)
            gb[rows, :] = jnp.where(live_mask(levels_ref, b, D), og_ref[rows, :].astype(F32), 0.0).astype(BF)
        gsum_ref[0:1, HALF : HALF + D] = jnp.sum(gb[...].astype(F32), axis=0, keepdims=True)
        cells[...] = jnp.zeros_like(cells)
        flat[...] = jnp.zeros_like(flat)
        for c in copies:
            c.wait()
        c_start = VSEG["c1l"][0]

        def tile(n, carry):
            at = pl.multiple_of(n * TILE, TILE)
            cols = pl.ds(at, TILE)
            pbuf[...] = dot(h_ref[...], wl[:, cols], NN)
            gbuf[...] = dot(gb[...], wo[cols, :], NT)
            shift = vec_ref[0:1, pl.ds(c_start + at, TILE)]
            total = jnp.zeros((CHUNK, TILE), F32)
            for k in range(0, ROWS, CHUNK):
                r = slice(k, k + CHUNK)
                u, slope = gelu_parts(pbuf[r, :] + shift)
                sp = spat_ref[r, cols].astype(F32)
                gg = gbuf[r, :]
                gated_ref[r, cols] = (u * sp).astype(BF)
                gs_ref[r, cols] = (gg * u).astype(BF)
                q = (gg * sp * slope).astype(BF)
                q_ref[r, cols] = q
                total = total + q.astype(F32)
            gsum_ref[0:1, cols] = jnp.sum(total, axis=0, keepdims=True)
            return carry

        lax.fori_loop(0, HALF // TILE, tile, 0)

        me = sides_ref[0]
        for b in range(2):
            level = levels_ref[b]
            count_b = count_of(level)
            gs = gs_ref[b * PPAD : (b + 1) * PPAD, :]
            got = dot(gs, gate_ref[b * PPAD : (b + 1) * PPAD, :], NT)
            sums = jnp.sum(gs.astype(F32), axis=-1, keepdims=True)
            j = lax.broadcasted_iota(jnp.int32, (PPAD, PPAD), 1)
            got = jnp.where(j < count_b, got, jnp.where(j == TOTAL_AT, sums, 0.0))
            cells[level, :, 0:PPAD] += got
        part = PMAX // 2
        for level in range(3):
            for k in range(2):
                flat[k, level * LSTRIDE : level * LSTRIDE + part, 0:PPAD] = cells[level, k * part : (k + 1) * part, 0:PPAD]
        for k in range(DEVS):
            target, side = (keep, me) if k < GROUPS else (send, 1 - me)
            r = pl.ds(k % GROUPS * 16, 16)
            block = flat[side, pl.ds(pl.multiple_of(sides_ref[1 + k] * 32, 32), 32), :].astype(BF)
            target[r, 0:SCOLS] = block[0:16]
            target[r, SCOLS:SPC] = block[16:32]

    broad = sds((ROWS, HALF), BF)
    payload = sds((D // 2, SPC), BF)
    out_shape = (
        broad,
        broad,
        broad,
        sds((ROWS, D), BF),
        sds((D, HALF), BF),
        sds((HALF, D), BF),
        payload,
        payload,
        sds((1, HALF + D), F32),
    )
    scratch = [
        pltpu.VMEM((ROWS, TILE), F32),
        pltpu.VMEM((ROWS, TILE), F32),
        pltpu.VMEM((3, PPAD, SCOLS), F32),
        pltpu.VMEM((2, 512, SCOLS), F32),
        pltpu.SemaphoreType.DMA((4, DEVS)),
    ]
    return call(
        kernel,
        out_shape,
        [SM] * 3 + [VM] * 5 + [HB] * count,
        scratch,
        8000000000,
        16000000,
        table,
        levels,
        sides,
        vec,
        h,
        spat,
        gate,
        grad_out,
        *pieces,
        room=28,
    )


def out_grads(gated, gb, after):
    count = len(after)

    def kernel(t_ref, gb_ref, *refs):
        gwo = refs[count]

        def out_tile(n, carry):
            cols = pl.ds(pl.multiple_of(n * TILE, TILE), TILE)
            gwo[cols, :] = dot(t_ref[:, cols], gb_ref[...], TN).astype(BF)
            return carry

        lax.fori_loop(0, HALF // TILE, out_tile, 0)

    return call(
        kernel, sds((HALF, D), BF), [VM] * 2 + [HB] * count, [], 1000000000, 5000000, gated, gb, *after, room=10
    )


def weight_grads(table, levels, sides, vec, gated, q, gwo, h, wl, wo, x, half, after):
    count = len(after)

    def kernel(
        table_ref, levels_ref, sides_ref, vec_ref, t_ref, q_ref, gwo, h_ref, wl_ref, wo_ref, x_ref, *refs
    ):
        keep, send, send_up, stay_ref, away_ref, gh_ref, branch, gwl = refs[count:]

        def in_tile(n, carry):
            cols = pl.ds(pl.multiple_of(n * TILE, TILE), TILE)
            gwl[cols, :] = dot(h_ref[:, cols], q_ref[...], TN).astype(BF)
            branch[:, cols] = dot(t_ref[...], wo_ref[:, cols], NN)
            gh_ref[:, cols] = dot(q_ref[...], wl_ref[cols, :], NT)
            return carry

        lax.fori_loop(0, D // TILE, in_tile, 0)
        me = sides_ref[0]
        live = jnp.concatenate([live_mask(levels_ref, b, D) for b in range(2)], axis=0)
        out = branch[...] + seg(vec_ref, "c2")
        split_rows(branch, stay_ref, away_ref, me, x_ref[...].astype(F32) + jnp.where(live, out, 0.0))
        for k in range(DEVS):
            dev = table_ref[k]
            target = keep if k < GROUPS else send if k < GROUPS * 3 // 2 else send_up
            r = pl.ds(k % (GROUPS if k < GROUPS else GROUPS // 2) * 16, 16)
            target[r, 0:HALF] = gwl[pl.ds(pl.multiple_of(dev * 16, 16), 16), :]
            for g in range(3):
                target[r, HALF + g * D : HALF + (g + 1) * D] = gwo[pl.ds(pl.multiple_of(dev * 48 + 16 * g, 16), 16), :]

    pair = sds((2, half, D), BF)
    payload = sds((D // 2, LO), BF)
    part = sds((D // 4, LO), BF)
    return call(
        kernel,
        (payload, part, part, pair, pair, sds((ROWS, D), F32)),
        [SM] * 3 + [VM] * 8 + [HB] * count,
        [pltpu.VMEM((ROWS, D), F32), pltpu.VMEM((D, HALF), BF)],
        5000000000,
        15000000,
        table,
        levels,
        sides,
        vec,
        gated,
        q,
        gwo,
        h,
        wl,
        wo,
        x,
        *after,
        room=24,
    )


def gate_backward(vec, gs, mm, hat, slope, scale, after):
    count = len(after)

    def kernel(vec_ref, gs_ref, mm_ref, hat_ref, slope_ref, scale_ref, *refs):
        gp, gsum_ref, dbuf, one, two, acc = refs[count:]

        for b in range(2):

            def mix_tile(n, carry):
                cols = pl.ds(pl.multiple_of(n * 512, 512), 512)
                got = dot(mm_ref[b], gs_ref[b * PPAD : (b + 1) * PPAD, cols], TN)
                dbuf[b * PPAD : (b + 1) * PPAD, cols] = got[0:PPAD]
                return carry

            lax.fori_loop(0, HALF // 512, mix_tile, 0)
        g_start = VSEG["g2"][0]

        def sum_rows(r):
            for k in range(0, BODY, CHUNK):
                rows = pl.ds(r + k, CHUNK)
                a = jnp.zeros((CHUNK, 128), F32)
                c = jnp.zeros((CHUNK, 128), F32)
                for n in range(0, HALF, TILE):
                    e = dbuf[rows, n : n + TILE] * vec_ref[0:1, g_start + n : g_start + n + TILE]
                    a = a + fold(e)
                    c = c + fold(e * hat_ref[rows, n : n + TILE].astype(F32))
                one[rows, :] = a
                two[rows, :] = c

        row_loop(BODY, sum_rows)
        one[...] = spread_sum(one, 1.0 / HALF)
        two[...] = spread_sum(two, 1.0 / HALF)
        acc[...] = jnp.zeros_like(acc)

        def grad_rows(r):
            for n in range(0, HALF, TILE):
                gain = vec_ref[0:1, g_start + n : g_start + n + TILE]
                sums = [jnp.zeros((CHUNK, TILE), F32) for _ in range(3)]
                for k in range(0, BODY, CHUNK):
                    rows = pl.ds(r + k, CHUNK)
                    d = dbuf[rows, n : n + TILE]
                    xh = hat_ref[rows, n : n + TILE].astype(F32)
                    inner = d * gain - wide(one[rows, :], 2) - xh * wide(two[rows, :], 2)
                    q = inner * wide(scale_ref[rows, :], 2) * slope_ref[rows, n : n + TILE].astype(F32)
                    q = q.astype(BF)
                    gp[rows, n : n + TILE] = q
                    sums = [sums[0] + d * xh, sums[1] + d, sums[2] + q.astype(F32)]
                for i in range(3):
                    acc[i, :, n : n + TILE] += sums[i]

        row_loop(BODY, grad_rows)
        for i in range(3):
            gsum_ref[0:1, i * HALF : (i + 1) * HALF] = jnp.sum(acc[i], axis=0, keepdims=True)

    return call(
        kernel,
        (sds((ROWS, HALF), BF), sds((1, 3 * HALF), F32)),
        [VM] * 6 + [HB] * count,
        [
            pltpu.VMEM((ROWS, HALF), F32),
            pltpu.VMEM((ROWS, 128), F32),
            pltpu.VMEM((ROWS, 128), F32),
            pltpu.VMEM((3, CHUNK, HALF), F32),
        ],
        3000000000,
        10000000,
        vec,
        gs,
        mm,
        hat,
        slope,
        scale,
        *after,
        room=20,
    )


def in_grads(gp, h, w, gh, after):
    count = len(after)

    def kernel(gp_ref, h_ref, w_ref, gh_ref, *refs):
        gwr, ghb = refs[count:]

        def in_tile(n, carry):
            cols = pl.ds(pl.multiple_of(n * TILE, TILE), TILE)
            ghb[:, cols] = gh_ref[:, cols] + dot(gp_ref[...], w_ref[cols, :], NT)
            gwr[cols, :] = dot(h_ref[:, cols], gp_ref[...], TN).astype(BF)
            return carry

        lax.fori_loop(0, D // TILE, in_tile, 0)

    return call(
        kernel,
        (sds((D, HALF), BF), sds((ROWS, D), F32)),
        [VM] * 4 + [HB] * count,
        [],
        3000000000,
        8000000,
        gp,
        h,
        w,
        gh,
        *after,
        room=14,
    )


def in_backward(table, sides, vec, gsum, gate_sum, gwr, ghb, x, grad_out, half, after):
    count = len(after)

    def kernel(table_ref, sides_ref, vec_ref, gsum_ref, gate_ref, gwr, ghb, x_ref, og_ref, *refs):
        keep, send, send_up, stay_ref, away_ref, acc, gvec, blocks, pgb = refs[count:]

        def put(name, value):
            start, size = VSEG[name]
            gvec[0:1, start : start + size] = value

        put("g2", gate_ref[0:1, 0:HALF])
        put("b2", gate_ref[0:1, HALF : 2 * HALF])
        put("c1r", gate_ref[0:1, 2 * HALF : 3 * HALF])
        put("c1l", gsum_ref[0:1, 0:HALF])
        put("c2", gsum_ref[0:1, HALF : HALF + D])
        acc[...] = jnp.zeros_like(acc)
        def in_rows(r):
            rows = pl.ds(r, STRIPE)
            xh, scale = norm_parts(x_ref[rows, :].astype(F32))
            d = ghb[rows, :]
            e = d * seg(vec_ref, "g1")
            one = jnp.mean(e, axis=-1, keepdims=True)
            two = jnp.mean(e * xh, axis=-1, keepdims=True)
            pgb[rows, :] = og_ref[rows, :].astype(F32) + scale * (e - one - xh * two)
            acc[0:1, :] += jnp.sum(d * xh, axis=0, keepdims=True)
            acc[1:2, :] += jnp.sum(d, axis=0, keepdims=True)

        row_loop(STRIPE, in_rows)
        put("g1", acc[0:1, :])
        put("b1", acc[1:2, :])
        split_rows(pgb, stay_ref, away_ref, sides_ref[0], pgb[...])
        blocks[...] = jnp.zeros_like(blocks)
        for s in range(DEVS):
            blocks[s, 0:1, 0:VPER] = gvec[0:1, VPER * s : VPER * s + VPER]
        for k in range(DEVS):
            dev = table_ref[k]
            target = keep if k < GROUPS else send if k < GROUPS * 3 // 2 else send_up
            r = pl.ds(k % (GROUPS if k < GROUPS else GROUPS // 2) * 16, 16)
            target[r, 0:HALF] = gwr[pl.ds(pl.multiple_of(dev * 16, 16), 16), :]
            target[r, HALF : HALF + VCOLS] = blocks[dev].astype(BF)

    payload = sds((D // 2, HALF + VCOLS), BF)
    part = sds((D // 4, HALF + VCOLS), BF)
    pair = sds((2, half, D), BF)
    return call(
        kernel,
        (payload, part, part, pair, pair),
        [SM] * 2 + [VM] * 7 + [HB] * count,
        [
            pltpu.VMEM((8, D), F32),
            pltpu.VMEM((1, VEC), F32),
            pltpu.VMEM((DEVS, 16, VCOLS), F32),
            pltpu.VMEM((ROWS, D), F32),
        ],
        2000000000,
        6000000,
        table,
        sides,
        vec,
        gsum,
        gate_sum,
        gwr,
        ghb,
        x,
        grad_out,
        *after,
        room=16,
    )


def add_part(terms, size, after, places=None):
    cols = terms[0].shape[1]
    count = len(terms)

    def kernel(*refs):
        for r in range(0, size, 16):
            rows = slice(r, r + 16)
            value = refs[0][rows, :].astype(F32)
            for t in refs[1:count]:
                value = value + t[rows, :].astype(F32)
            refs[count + len(after)][rows, :] = value.astype(BF)

    places = places or [1] * count
    blocks = [pl.BlockSpec((size, cols), lambda i, p=p: (p, 0)) for p in places]
    return pl.pallas_call(
        kernel,
        grid=(1,),
        out_shape=sds((size, cols), BF),
        in_specs=blocks + [HB] * len(after),
        out_specs=pl.BlockSpec((size, cols), lambda i: (0, 0)),
        compiler_params=pltpu.CompilerParams(vmem_limit_bytes=10 * MIB),
        cost_estimate=pl.CostEstimate(flops=1000000, bytes_accessed=3000000, transcendentals=0),
    )(*terms, *after)


def line_parts(terms, after):
    cols = terms[0].shape[1]
    count = len(terms)

    def kernel(*refs):
        own, *outs = refs[count + len(after) :]
        for m in range(4):
            rows = slice(16 * m, 16 * (m + 1))
            value = refs[0][rows, :].astype(F32)
            for t in refs[1:count]:
                value = value + t[rows, :].astype(F32)
            if m == 0:
                own[...] = value
            else:
                outs[m - 1][...] = value.astype(BF)

    block = pl.BlockSpec((64, cols), lambda i: (0, 0))
    one = pl.BlockSpec((16, cols), lambda i: (0, 0))
    return pl.pallas_call(
        kernel,
        grid=(1,),
        out_shape=[sds((16, cols), F32)] + [sds((16, cols), BF)] * 3,
        in_specs=[block] * count + [HB] * len(after),
        out_specs=[one] * 4,
        compiler_params=pltpu.CompilerParams(vmem_limit_bytes=8 * MIB),
        cost_estimate=pl.CostEstimate(flops=1000000, bytes_accessed=3000000, transcendentals=0),
    )(*terms, *after)


def line_turn(terms, flip, after):
    count = len(terms)
    cols = terms[0].shape[1]

    def kernel(*refs):
        outs = refs[count + len(after) :]
        for m in range(4):
            rows = slice(16 * m, 16 * (m + 1))
            value = refs[0][rows, :].astype(F32)
            for t in refs[1:count]:
                value = value + t[rows, :].astype(F32)
            value = value.astype(BF)
            outs[0][rows, :] = value
            if flip:
                at = 16 * (m ^ flip)
                outs[1][at : at + 16, :] = value

    block = pl.BlockSpec((64, cols), lambda i: (0, 0))
    number = 2 if flip else 1
    return pl.pallas_call(
        kernel,
        grid=(1,),
        out_shape=[sds((64, cols), BF)] * number,
        in_specs=[block] * count + [HB] * len(after),
        out_specs=[block] * number,
        compiler_params=pltpu.CompilerParams(vmem_limit_bytes=8 * MIB),
        cost_estimate=pl.CostEstimate(flops=1000000, bytes_accessed=1000000, transcendentals=0),
    )(*terms, *after)


def finish_out(own, got, weight, first, second, after):
    def kernel(own_ref, a_ref, b_ref, c_ref, w_ref, m_ref, s_ref, after_ref, left_ref, nw, nm, ns):
        total = own_ref[...] + a_ref[...].astype(F32)
        total = total + (b_ref[...].astype(F32) + c_ref[...].astype(F32))
        left_ref[...] = total[:, 0:HALF]
        for g in range(3):
            rows = slice(16 * g, 16 * (g + 1))
            grad = total[:, HALF + g * D : HALF + (g + 1) * D]
            new = adamw(w_ref[rows, :], grad, m_ref[rows, :], s_ref[rows, :], DENSE_RATE, DENSE_DECAY)
            nw[rows, :] = new[0]
            nm[rows, :] = new[1]
            ns[rows, :] = new[2]

    same = sds(weight.shape, F32)
    return call(
        kernel,
        (sds((16, HALF), F32), same, same, same),
        [VM] * 7 + [HB],
        [],
        1000000,
        2000000,
        own,
        *got,
        weight,
        first,
        second,
        after,
    )


def finish_in(own, got, left, weight, first, second, after):
    def kernel(own_ref, a_ref, b_ref, c_ref, l_ref, w_ref, m_ref, s_ref, after_ref, nw, nm, ns, vec_ref):
        total = own_ref[...] + a_ref[...].astype(F32)
        total = total + (b_ref[...].astype(F32) + c_ref[...].astype(F32))
        vec_ref[...] = total[0:1, HALF:]
        for cols, grad in ((slice(0, HALF), l_ref[...]), (slice(HALF, FF), total[:, 0:HALF])):
            new = adamw(w_ref[:, cols], grad, m_ref[:, cols], s_ref[:, cols], DENSE_RATE, DENSE_DECAY)
            nw[:, cols] = new[0]
            nm[:, cols] = new[1]
            ns[:, cols] = new[2]

    same = sds(weight.shape, F32)
    return call(
        kernel,
        (same, same, same, sds((1, VCOLS), F32)),
        [VM] * 8 + [HB],
        [],
        1000000,
        2000000,
        own,
        *got,
        left,
        weight,
        first,
        second,
        after,
    )


def spatial_update(order, pieces, spatial, first, second, bias, bias_first, bias_second, after):
    count = len(pieces)
    rows = spatial.shape[1]

    def kernel(order_ref, *refs):
        ins = refs[:count]
        w_ref, m_ref, s_ref, bw, bm, bs = refs[count : count + 6]
        nw, nm, ns, nbw, nbm, nbs, flat = refs[count + 6 + len(after) :]
        k = 0
        for piece in ins:
            for j in range(piece.shape[0] // 16):
                at = pl.multiple_of(order_ref[k] * 32, 32)
                block = piece[16 * j : 16 * j + 16, :].astype(F32)
                flat[pl.ds(at, 16), :] = block[:, 0:SCOLS]
                flat[pl.ds(at + 16, 16), :] = block[:, SCOLS:]
                k += 1
        at = TOTAL_AT // 128 * 128
        totals = flat[:, at : at + 128].T[TOTAL_AT - at : TOTAL_AT - at + 1, :]
        for level in range(3):
            got = flat[level * LSTRIDE : level * LSTRIDE + rows, :]
            new = adamw(w_ref[level], got[:, 0:PMAX], m_ref[level], s_ref[level], DENSE_RATE, DENSE_DECAY)
            nw[level] = new[0]
            nm[level] = new[1]
            ns[level] = new[2]
            got = totals[:, level * LSTRIDE : level * LSTRIDE + rows]
            r = slice(level, level + 1)
            new = adamw(bw[r, :], got, bm[r, :], bs[r, :], SMALL_RATE, 0.0)
            nbw[r, :] = new[0]
            nbm[r, :] = new[1]
            nbs[r, :] = new[2]

    same = sds(spatial.shape, F32)
    small = sds(bias.shape, F32)
    return call(
        kernel,
        (same, same, same, small, small, small),
        [SM] + [VM] * (count + 6) + [HB] * len(after),
        [pltpu.VMEM((512, SCOLS), F32)],
        10000000,
        6000000,
        order,
        *pieces,
        spatial,
        first,
        second,
        bias,
        bias_first,
        bias_second,
        *after,
    )


def in_order(blocks, table, rows):
    cols = blocks[0].shape[1]
    whole = jnp.concatenate(blocks, axis=0).reshape(-1, rows, cols)
    back = jnp.zeros_like(table).at[table].set(jnp.arange(table.shape[0], dtype=table.dtype))
    return jnp.take(whole, back, axis=0)


def local(
    patches,
    resolution,
    out_grad,
    dense_in,
    dense_out,
    vectors,
    spatial,
    spatial_bias,
    in_first,
    in_second,
    out_first,
    out_second,
    vec_first,
    vec_second,
    spat_first,
    spat_second,
    bias_first,
    bias_second,
):
    route = Route(lax.axis_size("dp"))
    ndev = 2 * route.n
    fits = route.n == GROUPS
    seq = lax.axis_index("seq").astype(jnp.int32)
    rows = patches.shape[1]
    table = route.table()
    order = route.order(False)[0]
    in_rows = dense_in.shape[0]
    out_rows = dense_out.shape[0]
    vec_len = vectors.shape[0]
    if fits:
        ktable = table
        korder = table // 2
    else:
        ktable = jnp.arange(DEVS, dtype=jnp.int32)
        korder = jnp.arange(DEVS, dtype=jnp.int32) % GROUPS
    sides = jnp.concatenate([seq[None], korder])
    levels = lax.dynamic_slice_in_dim(resolution, seq * 2, 2, 0)

    right_shard, lo_shard = pack_dense(dense_in, dense_out, vectors.reshape(1, vec_len))
    line = [right_shard] + [route.swap(right_shard, (m, m)) for m in route.direct]
    lo_line = [lo_shard] + [route.swap(lo_shard, (m, m)) for m in route.direct]
    spat_own, x_send, g_send = pack_images(sides, spatial, spatial_bias.reshape(3, rows, 1), patches, out_grad)
    x_got = route.cross(x_send)
    g_got = route.cross(g_send)
    spat_got = route.cross(spat_own)
    if fits:
        right_blocks = route.widen_direct(stack(line, []))
        lo_blocks = route.widen_direct(stack(lo_line, [right_blocks[1]]))
    else:
        right_blocks = route.widen(jnp.concatenate(line, axis=0))
        lo_blocks = route.widen(jnp.concatenate(lo_line, axis=0))
    right_blocks = right_blocks + [route.cross(b) for b in right_blocks]
    lo_blocks = lo_blocks + [route.cross(b) for b in lo_blocks]
    if not fits:
        whole = in_order(right_blocks, table, in_rows)
        all_vec = whole[:, 0, HALF : HALF + vec_len].reshape(DEVS, 1, VPER)
        all_vec = jnp.pad(all_vec, ((0, 0), (0, 15), (0, VCOLS - VPER))).reshape(D, VCOLS)
        right_blocks = [jnp.concatenate([whole[:, :, :HALF].reshape(D, HALF), all_vec], axis=1)]
        whole = in_order(lo_blocks, table, in_rows)
        outs = whole[:, :, HALF:].reshape(ndev, in_rows, 3, D).transpose(0, 2, 1, 3).reshape(DEVS, 3, 16, D)
        outs = outs.transpose(0, 2, 1, 3).reshape(D, HALF)
        lo_blocks = [jnp.concatenate([whole[:, :, :HALF].reshape(D, HALF), outs], axis=1)]

    x, grad_out, h, v, slope, part, weight_right, vec = gate_forward(
        ktable, sides, patches, x_got, out_grad, g_got, right_blocks
    )
    gate, hat, scale, spat, mm = gate_norm(levels, sides, vec, v, part, spat_own, spat_got, [])
    gs, gated, q, gb, wl, wo, sp_keep, sp_send, gsum = middle(ktable, levels, sides, vec, h, spat, gate, grad_out, lo_blocks)
    near, far = route.low[-1], route.low[0]
    after = [[] for _ in range(5)]
    if fits:
        sp_got = route.cross(sp_send)
        sp_part = add_part([sp_keep, sp_got], 128, [])
        sp_terms = [sp_keep, sp_got, route.swap(sp_part, near)]
        after[0] = [sp_part]
    gwo = out_grads(gated, gb, after[0])
    if fits:
        sp_part = add_part(sp_terms, 64, [gwo])
        sp_terms.append(route.swap(sp_part, far))
        after[1] = [sp_part]
    lo_keep, lo_send, lo_up, mixed_stay, mixed_away, gh = weight_grads(
        ktable, levels, sides, vec, gated, q, gwo, h, wl, wo, x, rows, after[1]
    )
    mixed_got = route.cross(mixed_away)
    if fits:
        lo_up = route.cross(lo_up)
        lo_terms = [lo_keep, route.cross(lo_send)]
        sp_own, sp_out = line_turn(sp_terms, 1, [lo_keep])
        sp_terms = [sp_own, route.swap(sp_out, (route.direct[0],) * 2)]
        lo_part = add_part([lo_keep, lo_up], 128, [sp_own], [1, 0])
        lo_terms.append(route.swap(lo_part, near))
        after[2] = [lo_part]
    gp, gate_sum = gate_backward(vec, gs, mm, hat, slope, scale, after[2])
    if fits:
        sp_own, sp_out = line_turn(sp_terms, 2, [gate_sum])
        sp_terms = [sp_own, route.swap(sp_out, (route.direct[1],) * 2)]
        after[3] = [sp_own, mixed_got]
    gwr, ghb = in_grads(gp, h, weight_right, gh, after[3])
    if fits:
        lo_part = add_part(lo_terms, 64, [gwr])
        lo_terms.append(route.swap(lo_part, far))
        after[4] = [lo_part]
    right_keep, right_send, right_up, grad_stay, grad_away = in_backward(
        ktable, sides, vec, gsum, gate_sum, gwr, ghb, x, grad_out, rows, after[4]
    )
    grad_got = route.cross(grad_away)
    if fits:
        right_up = route.cross(right_up)
        right_terms = [right_keep, route.cross(right_send)]
        right_part = add_part([right_keep, right_up], 128, [], [1, 0])
        right_terms.append(route.swap(right_part, near))
        (sp_sum,) = line_turn(sp_terms, 0, [right_part])
        spat_pieces = route.widen(sp_sum)
        lo_own, *sends = line_parts(lo_terms, [sp_sum, grad_got])
        lo_got = [route.swap(p, (m, m)) for p, m in zip(sends, route.direct)]
        right_part = add_part(right_terms, 64, [lo_own])
        right_terms.append(route.swap(right_part, far))
        right_own, *sends = line_parts(right_terms, [right_part])
        right_got = [route.swap(p, (m, m)) for p, m in zip(sends, route.direct)]
        left_sum, *new_out = finish_out(lo_own, lo_got, dense_out, out_first, out_second, right_own)
        korder = order
        after = [left_sum]
    else:
        both = jnp.concatenate([lo_keep, lo_send, lo_up])
        outs = both[:, HALF:LO].reshape(DEVS, 16, 3, D).transpose(0, 2, 1, 3).reshape(ndev, out_rows, D)
        outs = jnp.take(outs, table, axis=0).reshape(HALF, D)
        out_sum = route.scatter(outs[: HALF // 2], outs[HALF // 2 :])
        lefts = jnp.take(both[:, :HALF].reshape(ndev, in_rows, HALF), table, axis=0).reshape(D, HALF)
        left_sum = route.scatter(lefts[: D // 2], lefts[D // 2 :])
        per = 512 // route.n

        def spat_blocks(part, flip):
            flat = part.reshape(GROUPS, 16, 2, SCOLS).transpose(0, 2, 1, 3).reshape(route.n, per, SCOLS)
            return jnp.take(flat, route.order(flip)[0], axis=0).reshape(512, SCOLS)

        spat_part = route.scatter(spat_blocks(sp_keep, False), spat_blocks(sp_send, True)).astype(BF)
        flat = in_order(route.spread(spat_part), order, per).reshape(GROUPS, 2, 16, SCOLS)
        spat_pieces = [flat.transpose(0, 2, 1, 3).reshape(GROUPS * 16, SPC)]
        korder = jnp.arange(GROUPS, dtype=jnp.int32)
        after = []
        both = jnp.concatenate([right_keep, right_send, right_up])
        vecs = jnp.take(both[::16, HALF : HALF + VPER].reshape(ndev, vec_len), table, axis=0)
        vec_sum = route.scatter(vecs[: route.n], vecs[route.n :]).reshape(vec_len)
        rights = jnp.take(both[:, :HALF].reshape(ndev, in_rows, HALF), table, axis=0).reshape(D, HALF)
        right_sum = route.scatter(rights[: D // 2], rights[D // 2 :])
        in_sum = jnp.concatenate([left_sum, right_sum], axis=1)
        new_in = adamw(dense_in, in_sum, in_first, in_second, DENSE_RATE, DENSE_DECAY)
        new_out = adamw(dense_out, out_sum, out_first, out_second, DENSE_RATE, DENSE_DECAY)

    def whole_images(stays, came):
        return jnp.concatenate([jnp.where(seq == 0, stays, came), jnp.where(seq == 0, came, stays)], axis=0)

    mixed = whole_images(mixed_stay, mixed_got)
    patches_grad = whole_images(grad_stay, grad_got)
    spat_new = spatial_update(
        korder, spat_pieces, spatial, spat_first, spat_second, spatial_bias, bias_first, bias_second, after
    )
    if fits:
        *new_in, vec_sum = finish_in(right_own, right_got, left_sum, dense_in, in_first, in_second, spat_new[0])
        vec_sum = vec_sum[0, :vec_len]
    new_vec = adamw(vectors, vec_sum, vec_first, vec_second, SMALL_RATE, 0.0)
    return (mixed, patches_grad) + tuple(new_in) + tuple(new_out) + new_vec + tuple(spat_new)


def solution(mesh):
    rows3 = P("dp", "seq", None)
    dense = P(AXES, None)
    vec = P(AXES)
    spat = P(None, "seq", None)
    bias = P(None, "seq")
    in_specs = (rows3, P("dp"), rows3, dense, dense, vec, spat, bias)
    in_specs += (dense,) * 4 + (vec,) * 2 + (spat,) * 2 + (bias,) * 2
    out_specs = (rows3, rows3) + (dense,) * 6 + (vec,) * 3 + (spat,) * 3 + (bias,) * 3
    return jax.shard_map(local, mesh=mesh, in_specs=in_specs, out_specs=out_specs, check_vma=False)
```

```python
import functools

import jax
import jax.numpy as jnp
from jax import lax
from jax.experimental import pallas as pl
from jax.experimental.pallas import tpu as pltpu
from jax.sharding import PartitionSpec as P

D = 512
FF = 3072
HALF = 1536
PMAX = 324
PPAD = 336
P_MID = 196
P_LOW = 100
VCOLS = 256
ROWS = 2 * PPAD
GROUPS = 16
DEVS = 2 * GROUPS
VPER = 240
SCOLS = 384
BIAS_AT = 336
TOTAL_AT = 324
LSTRIDE = 168
MIB = 1024 * 1024
STEP = 10

NORM_EPS = 1e-05
BETA_ONE = 0.9
BETA_TWO = 0.99
ADAM_EPS = 1e-08
DENSE_RATE = 0.02
SMALL_RATE = 0.2
DENSE_DECAY = 0.05

BF = jnp.bfloat16
F32 = jnp.float32
AXES = ("dp", "seq")
VM = pl.BlockSpec(memory_space=pltpu.VMEM)
SM = pl.BlockSpec(memory_space=pltpu.SMEM)
HB = pl.BlockSpec(memory_space=pl.ANY)


class Route:
    def __init__(self, n):
        bits = n.bit_length() - 1
        assert n == 1 << bits and bits >= 2
        self.n = n
        top = n // 4
        self.direct = [top, 2 * top, 3 * top]
        low = [1 << b for b in range(bits - 2)]
        self.low = list(zip(low[::-1], low))
        masks = [(0, 0)] + [(m, m) for m in self.direct]
        for step in self.low:
            masks = masks + [(m[0] ^ step[0], m[1] ^ step[1]) for m in masks]
        self.masks = masks

    def swap(self, block, mask):
        pairs = []
        for dp in range(self.n):
            for seq in range(2):
                pairs.append((dp * 2 + seq, (dp ^ mask[seq]) * 2 + seq))
        return lax.ppermute(block, AXES, pairs)

    def cross(self, block):
        pairs = []
        for dp in range(self.n):
            for seq in range(2):
                pairs.append((dp * 2 + seq, dp * 2 + 1 - seq))
        return lax.ppermute(block, AXES, pairs)

    def order(self, seq_flip):
        place = lax.axis_index("dp")
        seq = lax.axis_index("seq")
        if seq_flip:
            seq = 1 - seq
        zero = jnp.array([m[0] for m in self.masks], jnp.int32)
        one = jnp.array([m[1] for m in self.masks], jnp.int32)
        return place ^ jnp.where(seq == 0, zero, one), seq

    def table(self):
        mine, seq = self.order(False)
        other, flip = self.order(True)
        return jnp.concatenate([mine * 2 + seq, other * 2 + flip])

    def spread(self, shard):
        first = jnp.concatenate([shard] + [self.swap(shard, (m, m)) for m in self.direct], axis=0)
        return self.widen(first)

    def widen(self, first):
        blocks = [first]
        for step in self.low:
            blocks = blocks + [self.swap(b, step) for b in blocks]
        return blocks

    def widen_in_turn(self, first):
        second = self.swap(first, self.low[0])
        third = self.swap(first, self.low[1])
        passed = stack([second], [third])
        return [first, second, third, self.swap(passed, self.low[1])], passed

    def widen_direct(self, first):
        return [first] + [self.swap(first, m) for m in self.plane()]

    def plane(self):
        one, two = self.low
        return [one, two, (one[0] ^ two[0], one[1] ^ two[1])]

    def gather(self, shard):
        blocks = self.spread(shard)
        return blocks + [self.cross(b) for b in blocks]

    def collect(self, terms):
        cur = terms[0].shape[0]
        rows = cur // self.n

        def part(lower, upper):
            total = terms[0][lower:upper].astype(F32)
            for t in terms[1:]:
                total = total + t[lower:upper].astype(F32)
            return total

        terms = list(terms)
        for step in reversed(self.low):
            half = cur // 2
            terms.append(self.swap(part(half, cur).astype(BF), step))
            cur = half
        got = []
        for j, m in enumerate(self.direct):
            got.append(self.swap(part((j + 1) * rows, (j + 2) * rows).astype(BF), (m, m)))
        total = part(0, rows)
        return (total + got[0].astype(F32)) + (got[1].astype(F32) + got[2].astype(F32))

    def scatter(self, keep, send):
        return self.collect([keep, self.cross(send)])


def dot(a, b, dims):
    return lax.dot_general(a, b, (dims, ((), ())), preferred_element_type=F32)


NN = ((1,), (0,))
NT = ((1,), (1,))
TN = ((0,), (0,))


def gelu_parts(p):
    bell = jnp.exp(p * p * -0.5)
    d = 1.0 + jnp.abs(p) * (0.3275911 * 0.7071067811865476)
    t = pl.reciprocal(d, approx=True)
    t = t * (2.0 - d * t)
    poly = t * (
        0.127414796
        + t * (-0.142248368 + t * (0.7107068705 + t * (-0.7265760135 + t * 0.5307027145)))
    )
    tail = poly * bell
    phi_sum = jnp.where(p >= 0.0, 1.0 - tail, tail)
    return p * phi_sum, phi_sum + p * bell * 0.3989422804014327


def count_of(level):
    return jnp.where(level == 0, P_LOW, jnp.where(level == 1, P_MID, PMAX))


def masked_mix(mix, count):
    i = lax.broadcasted_iota(jnp.int32, (PPAD, SCOLS), 0)
    j = lax.broadcasted_iota(jnp.int32, (PPAD, SCOLS), 1)
    return jnp.where((i < count) & (j < count), mix.astype(F32), 0.0).astype(BF)


def live_rows(count, shape, start=0):
    return lax.broadcasted_iota(jnp.int32, shape, 0) + start < count


def live_mask(levels_ref, b, width):
    return live_rows(count_of(levels_ref[b]), (PPAD, width))


def fold(value):
    total = value[:, 0:128]
    for n in range(128, value.shape[1], 128):
        total = total + value[:, n : n + 128]
    return total


def spread_sum(ref, factor):
    return jnp.broadcast_to(jnp.sum(ref[...], axis=-1, keepdims=True) * factor, ref.shape)


def wide(value, times):
    return jnp.concatenate([value] * times, axis=1)


def start_blocks(table_ref, pieces, rows, cols, target, sem, extra=0):
    copies = []
    k = 0
    for piece in pieces:
        for j in range(piece.shape[0] // 16):
            at = pl.multiple_of(table_ref[k] * rows, 16)
            c = pltpu.make_async_copy(
                piece.at[pl.ds(j * 16, 16), pl.ds(cols[0], cols[1])], target.at[pl.ds(at + extra, 16)], sem.at[k]
            )
            c.start()
            copies.append(c)
            k += 1
    return copies


def row_loop(step, body):
    def run(i, carry):
        body(pl.multiple_of(i * step, step))
        return carry

    lax.fori_loop(0, ROWS // step, run, 0)


def call(kernel, out_shape, in_specs, scratch, flops, nbytes, *args, room=12):
    vm = pl.BlockSpec(memory_space=pltpu.VMEM)
    return pl.pallas_call(
        kernel,
        out_shape=out_shape,
        in_specs=in_specs,
        out_specs=jax.tree.map(lambda _: vm, out_shape),
        scratch_shapes=scratch,
        compiler_params=pltpu.CompilerParams(vmem_limit_bytes=room * MIB),
        cost_estimate=pl.CostEstimate(flops=flops, bytes_accessed=nbytes, transcendentals=0),
    )(*args)


def norm_parts(values):
    center = values - jnp.mean(values, axis=-1, keepdims=True)
    scale = lax.rsqrt(jnp.mean(center * center, axis=-1, keepdims=True) + NORM_EPS)
    return center * scale, scale


VSEG = {
    "g1": (0, D),
    "b1": (D, D),
    "c1l": (2 * D, HALF),
    "c1r": (2 * D + HALF, HALF),
    "g2": (2 * D + FF, HALF),
    "b2": (2 * D + FF + HALF, HALF),
    "c2": (2 * D + FF + 2 * HALF, D),
}
VEC = 2 * D + FF + 2 * HALF + D


def seg(ref, name):
    start, size = VSEG[name]
    return ref[0:1, start : start + size]

def adamw(weight, grad, first, second, rate, decay):
    first = BETA_ONE * first + (1.0 - BETA_ONE) * grad
    second = BETA_TWO * second + (1.0 - BETA_TWO) * grad * grad
    first_hat = first / (1.0 - BETA_ONE**STEP)
    second_hat = second / (1.0 - BETA_TWO**STEP)
    weight = weight - rate * (first_hat / (jnp.sqrt(second_hat) + ADAM_EPS) + decay * weight)
    return (weight, first, second)


CHUNK = 16
TILE = 256
BODY = 32
STRIPE = 112
LO = 2 * HALF
SPC = 2 * SCOLS


def sds(shape, dtype):
    return jax.ShapeDtypeStruct(shape, dtype)


def pack_dense(dense_in, dense_out, vec_row):
    rows = dense_in.shape[0]
    per = vec_row.shape[1]

    def kernel(w_hbm, o_hbm, v_hbm, out_ref, lo_ref, w_ref, o_ref, v_ref, row, sem):
        copies = [
            pltpu.make_async_copy(src, dst, sem.at[k])
            for k, (src, dst) in enumerate(((w_hbm, w_ref), (o_hbm, o_ref), (v_hbm, v_ref)))
        ]
        for c in copies:
            c.start()
        row[...] = jnp.zeros_like(row)
        for c in copies:
            c.wait()
        out_ref[:, 0:HALF] = w_ref[:, HALF:].astype(BF)
        row[0:1, 0:per] = v_ref[...]
        out_ref[:, HALF : HALF + VCOLS] = row[...].astype(BF)
        lo_ref[:, 0:HALF] = w_ref[:, 0:HALF].astype(BF)
        for g in range(3):
            lo_ref[:, HALF + g * D : HALF + (g + 1) * D] = o_ref[g * rows : (g + 1) * rows, :].astype(BF)

    scratch = [
        pltpu.VMEM(dense_in.shape, F32),
        pltpu.VMEM(dense_out.shape, F32),
        pltpu.VMEM(vec_row.shape, F32),
        pltpu.VMEM((rows, VCOLS), F32),
        pltpu.SemaphoreType.DMA((3,)),
    ]
    shape = (sds((rows, HALF + VCOLS), BF), sds((rows, LO), BF))
    return call(kernel, shape, [HB] * 3, scratch, 1000, 600000, dense_in, dense_out, vec_row, room=60)


def pack_images(sides, spatial, bias_col, patches, out_grad):
    half = patches.shape[1]

    def kernel(sides_ref, s_ref, b_ref, x_ref, g_ref, spat_ref, xs_ref, gs_ref, buf):
        away = 2 - 2 * sides_ref[0]
        for b in range(2):
            xs_ref[b] = x_ref[away + b]
            gs_ref[b] = g_ref[away + b]
        buf[...] = jnp.zeros_like(buf)
        for level in range(3):
            buf[:, 0:PMAX] = s_ref[level]
            rest = b_ref[level]
            for c in range(3):
                piece = rest.astype(BF).astype(F32)
                buf[:, BIAS_AT + c : BIAS_AT + c + 1] = piece
                rest = rest - piece
            spat_ref[level] = buf[...].astype(BF)

    pair = sds((2, half, D), BF)
    return call(
        kernel,
        (sds((3, half, SCOLS), BF), pair, pair),
        [SM] + [VM] * 4,
        [pltpu.VMEM((half, SCOLS), F32)],
        1000,
        3000000,
        sides,
        spatial,
        bias_col,
        patches,
        out_grad,
    )


def stack(pieces, after):
    count = len(pieces)
    rows, cols = pieces[0].shape

    def kernel(*refs):
        out = refs[count + len(after)]
        for k in range(count):
            out[k * rows : (k + 1) * rows, :] = refs[k][...]

    specs = [VM] * count + [HB] * len(after)
    return call(kernel, sds((count * rows, cols), BF), specs, [], 1000, 1000000, *pieces, *after)


def two_halves(is_first, own, got):
    own = own.astype(F32)
    got = got.astype(F32)
    return jnp.where(is_first, own, got), jnp.where(is_first, got, own)


def gate_norm(levels, sides, vec, v, part, spat_own, spat_got, after):
    half = spat_own.shape[1]
    count = len(after)

    def kernel(levels_ref, sides_ref, vec_ref, v_ref, part_ref, so_ref, sg_ref, *refs):
        gate_ref, hat_ref, scale_ref, spat_ref, mm_ref, mixf, mean, buf = refs[count:]
        is_first = sides_ref[0] == 0
        g_start = VSEG["g2"][0]
        b_start = VSEG["b2"][0]
        mean[...] = spread_sum(part_ref, 1.0 / HALF)

        def square_rows(r):
            for k in range(0, BODY, CHUNK):
                rows = pl.ds(r + k, CHUNK)
                mid = mean[rows, :]
                total = jnp.zeros((CHUNK, 128), F32)
                for n in range(0, HALF, 128):
                    center = v_ref[rows, n : n + 128] - mid
                    total = total + center * center
                buf[rows, :] = total

        row_loop(BODY, square_rows)
        scale_ref[...] = lax.rsqrt(spread_sum(buf, 1.0 / HALF) + NORM_EPS)

        def gate_rows(r):
            for k in range(0, BODY, CHUNK):
                rows = pl.ds(r + k, CHUNK)
                mid = wide(mean[rows, :], 2)
                scale = wide(scale_ref[rows, :], 2)
                for n in range(0, HALF, TILE):
                    hat = (v_ref[rows, n : n + TILE] - mid) * scale
                    hat_ref[rows, n : n + TILE] = hat.astype(BF)
                    gate = hat * vec_ref[0:1, g_start + n : g_start + n + TILE]
                    gate = (gate + vec_ref[0:1, b_start + n : b_start + n + TILE]).astype(BF)
                    gate_ref[rows, n : n + TILE] = gate

        row_loop(BODY, gate_rows)
        gate_ref[ROWS:, :] = jnp.zeros((SCOLS - PPAD, HALF), BF)
        for b in range(2):
            level = levels_ref[b]
            live = count_of(level)
            one, two = two_halves(is_first, so_ref[level], sg_ref[level])
            mixf[0:half, :] = one
            mixf[half : 2 * half, :] = two
            mixf[2 * half :, :] = jnp.zeros((PPAD - 2 * half, SCOLS), F32)
            bias = jnp.sum(mixf[:, TOTAL_AT:], axis=-1, keepdims=True)
            mm_ref[b] = masked_mix(mixf[...], live)

            def mix_tile(n, carry):
                cols = pl.ds(pl.multiple_of(n * 512, 512), 512)
                got = dot(mm_ref[b], gate_ref[b * PPAD : b * PPAD + SCOLS, cols], NN) + bias
                got = jnp.where(live_rows(live, (PPAD, 512)), got, 0.0)
                spat_ref[b * PPAD : (b + 1) * PPAD, cols] = got.astype(BF)
                return carry

            lax.fori_loop(0, HALF // 512, mix_tile, 0)

    return call(
        kernel,
        (
            sds((ROWS + SCOLS - PPAD, HALF), BF),
            sds((ROWS, HALF), BF),
            sds((ROWS, 128), F32),
            sds((ROWS, HALF), BF),
            sds((2, PPAD, SCOLS), BF),
        ),
        [SM] * 2 + [VM] * 5 + [HB] * count,
        [pltpu.VMEM((PPAD, SCOLS), F32), pltpu.VMEM((ROWS, 128), F32), pltpu.VMEM((ROWS, 128), F32)],
        6000000000,
        12000000,
        levels,
        sides,
        vec,
        v,
        part,
        spat_own,
        spat_got,
        *after,
        room=22,
    )


def gate_forward(table, sides, patches, x_got, out_grad, g_got, pieces):
    count = len(pieces)
    half = patches.shape[1]

    def kernel(table_ref, sides_ref, p_ref, xg_ref, o_ref, gg_ref, *refs):
        ins = refs[:count]
        outs = refs[count : count + 8]
        x_ref, og_ref, h_ref, pre, slope_ref, part, w_ref, vec_ref = outs
        vblk, xbuf, sem, vsem = refs[count + 8 :]
        vcopies = start_blocks(table_ref, ins, 16, (HALF, VCOLS), vblk, vsem)
        copies = start_blocks(table_ref, ins, 16, (0, HALF), w_ref, sem)
        me = sides_ref[0]
        is_first = me == 0

        for src, got, target in ((o_ref, gg_ref, og_ref), (p_ref, xg_ref, x_ref)):
            for b in range(2):
                one, two = two_halves(is_first, src[2 * me + b], got[b])
                xbuf[b * PPAD : b * PPAD + half, :] = one
                xbuf[b * PPAD + half : b * PPAD + 2 * half, :] = two
                xbuf[b * PPAD + 2 * half : (b + 1) * PPAD, :] = jnp.zeros((PPAD - 2 * half, D), F32)
            target[...] = xbuf[...].astype(BF)
        for c in vcopies:
            c.wait()
        for s in range(DEVS):
            row = vblk[16 * s : 16 * s + 16, :].astype(F32)[0:1, :VPER]
            vec_ref[0:1, VPER * s : VPER * s + VPER] = row

        def norm_one(r):
            hat, _ = norm_parts(xbuf[pl.ds(r, STRIPE), :])
            h_ref[pl.ds(r, STRIPE), :] = (hat * seg(vec_ref, "g1") + seg(vec_ref, "b1")).astype(BF)

        row_loop(STRIPE, norm_one)
        for c in copies:
            c.wait()
        c_start = VSEG["c1r"][0]

        def matmul(n, carry):
            at = pl.multiple_of(n * TILE, TILE)
            pre[:, pl.ds(at, TILE)] = dot(h_ref[...], w_ref[:, pl.ds(at, TILE)], NN)
            return carry

        lax.fori_loop(0, HALF // TILE, matmul, 0)

        def gelu_rows(r):
            for k in range(0, BODY, CHUNK):
                rows = pl.ds(r + k, CHUNK)
                total = jnp.zeros((CHUNK, 128), F32)
                for n in range(0, HALF, TILE):
                    v, slope = gelu_parts(pre[rows, n : n + TILE] + vec_ref[0:1, c_start + n : c_start + n + TILE])
                    pre[rows, n : n + TILE] = v
                    slope_ref[rows, n : n + TILE] = slope.astype(BF)
                    total = total + fold(v)
                part[rows, :] = total

        row_loop(BODY, gelu_rows)

    broad = sds((ROWS, HALF), BF)
    narrow = sds((ROWS, D), BF)
    out_shape = (
        narrow,
        narrow,
        narrow,
        sds((ROWS, HALF), F32),
        broad,
        sds((ROWS, 128), F32),
        sds((D, HALF), BF),
        sds((1, VEC), F32),
    )
    scratch = [
        pltpu.VMEM((D, VCOLS), BF),
        pltpu.VMEM((ROWS, D), F32),
        pltpu.SemaphoreType.DMA((DEVS,)),
        pltpu.SemaphoreType.DMA((DEVS,)),
    ]
    return call(
        kernel,
        out_shape,
        [SM] * 2 + [VM] * 4 + [HB] * count,
        scratch,
        10000000000,
        20000000,
        table,
        sides,
        patches,
        x_got,
        out_grad,
        g_got,
        *pieces,
        room=26,
    )


def split_rows(target, first, second, seq, value):
    half = first.shape[1]
    target[...] = value
    for b in range(2):
        one = target[b * PPAD : b * PPAD + half, :]
        two = target[b * PPAD + half : b * PPAD + 2 * half, :]
        first[b] = jnp.where(seq == 0, one, two).astype(BF)
        second[b] = jnp.where(seq == 0, two, one).astype(BF)


def middle(table, levels, sides, vec, h, spat, gate, grad_out, pieces):
    count = len(pieces)

    def kernel(table_ref, levels_ref, sides_ref, vec_ref, h_ref, spat_ref, gate_ref, og_ref, *refs):
        ins = refs[:count]
        gs_ref, gated_ref, q_ref, gb, wl, wo, keep, send, gsum_ref = refs[count : count + 9]
        pbuf, gbuf, cells, flat, sem = refs[count + 9 :]
        copies = start_blocks(table_ref, ins, 16, (0, HALF), wl, sem.at[0])
        for g in range(3):
            copies += start_blocks(table_ref, ins, 48, (HALF + g * D, D), wo, sem.at[1 + g], 16 * g)
        for b in range(2):
            rows = slice(b * PPAD, (b + 1) * PPAD)
            gb[rows, :] = jnp.where(live_mask(levels_ref, b, D), og_ref[rows, :].astype(F32), 0.0).astype(BF)
        gsum_ref[0:1, HALF : HALF + D] = jnp.sum(gb[...].astype(F32), axis=0, keepdims=True)
        cells[...] = jnp.zeros_like(cells)
        flat[...] = jnp.zeros_like(flat)
        for c in copies:
            c.wait()
        c_start = VSEG["c1l"][0]

        def tile(n, carry):
            at = pl.multiple_of(n * TILE, TILE)
            cols = pl.ds(at, TILE)
            pbuf[...] = dot(h_ref[...], wl[:, cols], NN)
            gbuf[...] = dot(gb[...], wo[cols, :], NT)
            shift = vec_ref[0:1, pl.ds(c_start + at, TILE)]
            total = jnp.zeros((CHUNK, TILE), F32)
            for k in range(0, ROWS, CHUNK):
                r = slice(k, k + CHUNK)
                u, slope = gelu_parts(pbuf[r, :] + shift)
                sp = spat_ref[r, cols].astype(F32)
                gg = gbuf[r, :]
                gated_ref[r, cols] = (u * sp).astype(BF)
                gs_ref[r, cols] = (gg * u).astype(BF)
                q = (gg * sp * slope).astype(BF)
                q_ref[r, cols] = q
                total = total + q.astype(F32)
            gsum_ref[0:1, cols] = jnp.sum(total, axis=0, keepdims=True)
            return carry

        lax.fori_loop(0, HALF // TILE, tile, 0)

        me = sides_ref[0]
        for b in range(2):
            level = levels_ref[b]
            count_b = count_of(level)
            gs = gs_ref[b * PPAD : (b + 1) * PPAD, :]
            got = dot(gs, gate_ref[b * PPAD : (b + 1) * PPAD, :], NT)
            sums = jnp.sum(gs.astype(F32), axis=-1, keepdims=True)
            j = lax.broadcasted_iota(jnp.int32, (PPAD, PPAD), 1)
            got = jnp.where(j < count_b, got, jnp.where(j == TOTAL_AT, sums, 0.0))
            cells[level, :, 0:PPAD] += got
        part = PMAX // 2
        for level in range(3):
            for k in range(2):
                flat[k, level * LSTRIDE : level * LSTRIDE + part, 0:PPAD] = cells[level, k * part : (k + 1) * part, 0:PPAD]
        for k in range(DEVS):
            target, side = (keep, me) if k < GROUPS else (send, 1 - me)
            r = pl.ds(k % GROUPS * 16, 16)
            block = flat[side, pl.ds(pl.multiple_of(sides_ref[1 + k] * 32, 32), 32), :].astype(BF)
            target[r, 0:SCOLS] = block[0:16]
            target[r, SCOLS:SPC] = block[16:32]

    broad = sds((ROWS, HALF), BF)
    payload = sds((D // 2, SPC), BF)
    out_shape = (
        broad,
        broad,
        broad,
        sds((ROWS, D), BF),
        sds((D, HALF), BF),
        sds((HALF, D), BF),
        payload,
        payload,
        sds((1, HALF + D), F32),
    )
    scratch = [
        pltpu.VMEM((ROWS, TILE), F32),
        pltpu.VMEM((ROWS, TILE), F32),
        pltpu.VMEM((3, PPAD, SCOLS), F32),
        pltpu.VMEM((2, 512, SCOLS), F32),
        pltpu.SemaphoreType.DMA((4, DEVS)),
    ]
    return call(
        kernel,
        out_shape,
        [SM] * 3 + [VM] * 5 + [HB] * count,
        scratch,
        8000000000,
        16000000,
        table,
        levels,
        sides,
        vec,
        h,
        spat,
        gate,
        grad_out,
        *pieces,
        room=28,
    )


def out_grads(gated, gb, after):
    count = len(after)

    def kernel(t_ref, gb_ref, *refs):
        gwo = refs[count]

        def out_tile(n, carry):
            cols = pl.ds(pl.multiple_of(n * TILE, TILE), TILE)
            gwo[cols, :] = dot(t_ref[:, cols], gb_ref[...], TN).astype(BF)
            return carry

        lax.fori_loop(0, HALF // TILE, out_tile, 0)

    return call(
        kernel, sds((HALF, D), BF), [VM] * 2 + [HB] * count, [], 1000000000, 5000000, gated, gb, *after, room=10
    )


def weight_grads(table, levels, sides, vec, gated, q, gwo, h, wl, wo, x, half, after):
    count = len(after)

    def kernel(
        table_ref, levels_ref, sides_ref, vec_ref, t_ref, q_ref, gwo, h_ref, wl_ref, wo_ref, x_ref, *refs
    ):
        keep, send, send_up, stay_ref, away_ref, gh_ref, branch, gwl = refs[count:]

        def in_tile(n, carry):
            cols = pl.ds(pl.multiple_of(n * TILE, TILE), TILE)
            gwl[cols, :] = dot(h_ref[:, cols], q_ref[...], TN).astype(BF)
            branch[:, cols] = dot(t_ref[...], wo_ref[:, cols], NN)
            gh_ref[:, cols] = dot(q_ref[...], wl_ref[cols, :], NT)
            return carry

        lax.fori_loop(0, D // TILE, in_tile, 0)
        me = sides_ref[0]
        live = jnp.concatenate([live_mask(levels_ref, b, D) for b in range(2)], axis=0)
        out = branch[...] + seg(vec_ref, "c2")
        split_rows(branch, stay_ref, away_ref, me, x_ref[...].astype(F32) + jnp.where(live, out, 0.0))
        for k in range(DEVS):
            dev = table_ref[k]
            target = keep if k < GROUPS else send if k < GROUPS * 3 // 2 else send_up
            r = pl.ds(k % (GROUPS if k < GROUPS else GROUPS // 2) * 16, 16)
            target[r, 0:HALF] = gwl[pl.ds(pl.multiple_of(dev * 16, 16), 16), :]
            for g in range(3):
                target[r, HALF + g * D : HALF + (g + 1) * D] = gwo[pl.ds(pl.multiple_of(dev * 48 + 16 * g, 16), 16), :]

    pair = sds((2, half, D), BF)
    payload = sds((D // 2, LO), BF)
    part = sds((D // 4, LO), BF)
    return call(
        kernel,
        (payload, part, part, pair, pair, sds((ROWS, D), F32)),
        [SM] * 3 + [VM] * 8 + [HB] * count,
        [pltpu.VMEM((ROWS, D), F32), pltpu.VMEM((D, HALF), BF)],
        5000000000,
        15000000,
        table,
        levels,
        sides,
        vec,
        gated,
        q,
        gwo,
        h,
        wl,
        wo,
        x,
        *after,
        room=24,
    )


def gate_backward(vec, gs, mm, hat, slope, scale, after):
    count = len(after)

    def kernel(vec_ref, gs_ref, mm_ref, hat_ref, slope_ref, scale_ref, *refs):
        gp, gsum_ref, dbuf, one, two, acc = refs[count:]

        for b in range(2):

            def mix_tile(n, carry):
                cols = pl.ds(pl.multiple_of(n * 512, 512), 512)
                got = dot(mm_ref[b], gs_ref[b * PPAD : (b + 1) * PPAD, cols], TN)
                dbuf[b * PPAD : (b + 1) * PPAD, cols] = got[0:PPAD]
                return carry

            lax.fori_loop(0, HALF // 512, mix_tile, 0)
        g_start = VSEG["g2"][0]

        def sum_rows(r):
            for k in range(0, BODY, CHUNK):
                rows = pl.ds(r + k, CHUNK)
                a = jnp.zeros((CHUNK, 128), F32)
                c = jnp.zeros((CHUNK, 128), F32)
                for n in range(0, HALF, TILE):
                    e = dbuf[rows, n : n + TILE] * vec_ref[0:1, g_start + n : g_start + n + TILE]
                    a = a + fold(e)
                    c = c + fold(e * hat_ref[rows, n : n + TILE].astype(F32))
                one[rows, :] = a
                two[rows, :] = c

        row_loop(BODY, sum_rows)
        one[...] = spread_sum(one, 1.0 / HALF)
        two[...] = spread_sum(two, 1.0 / HALF)
        acc[...] = jnp.zeros_like(acc)

        def grad_rows(r):
            for n in range(0, HALF, TILE):
                gain = vec_ref[0:1, g_start + n : g_start + n + TILE]
                sums = [jnp.zeros((CHUNK, TILE), F32) for _ in range(3)]
                for k in range(0, BODY, CHUNK):
                    rows = pl.ds(r + k, CHUNK)
                    d = dbuf[rows, n : n + TILE]
                    xh = hat_ref[rows, n : n + TILE].astype(F32)
                    inner = d * gain - wide(one[rows, :], 2) - xh * wide(two[rows, :], 2)
                    q = inner * wide(scale_ref[rows, :], 2) * slope_ref[rows, n : n + TILE].astype(F32)
                    q = q.astype(BF)
                    gp[rows, n : n + TILE] = q
                    sums = [sums[0] + d * xh, sums[1] + d, sums[2] + q.astype(F32)]
                for i in range(3):
                    acc[i, :, n : n + TILE] += sums[i]

        row_loop(BODY, grad_rows)
        for i in range(3):
            gsum_ref[0:1, i * HALF : (i + 1) * HALF] = jnp.sum(acc[i], axis=0, keepdims=True)

    return call(
        kernel,
        (sds((ROWS, HALF), BF), sds((1, 3 * HALF), F32)),
        [VM] * 6 + [HB] * count,
        [
            pltpu.VMEM((ROWS, HALF), F32),
            pltpu.VMEM((ROWS, 128), F32),
            pltpu.VMEM((ROWS, 128), F32),
            pltpu.VMEM((3, CHUNK, HALF), F32),
        ],
        3000000000,
        10000000,
        vec,
        gs,
        mm,
        hat,
        slope,
        scale,
        *after,
        room=20,
    )


def in_grads(gp, h, w, gh, after):
    count = len(after)

    def kernel(gp_ref, h_ref, w_ref, gh_ref, *refs):
        gwr, ghb = refs[count:]

        def in_tile(n, carry):
            cols = pl.ds(pl.multiple_of(n * TILE, TILE), TILE)
            ghb[:, cols] = gh_ref[:, cols] + dot(gp_ref[...], w_ref[cols, :], NT)
            gwr[cols, :] = dot(h_ref[:, cols], gp_ref[...], TN).astype(BF)
            return carry

        lax.fori_loop(0, D // TILE, in_tile, 0)

    return call(
        kernel,
        (sds((D, HALF), BF), sds((ROWS, D), F32)),
        [VM] * 4 + [HB] * count,
        [],
        3000000000,
        8000000,
        gp,
        h,
        w,
        gh,
        *after,
        room=14,
    )


def in_backward(table, sides, vec, gsum, gate_sum, gwr, ghb, x, grad_out, half, after):
    count = len(after)

    def kernel(table_ref, sides_ref, vec_ref, gsum_ref, gate_ref, gwr, ghb, x_ref, og_ref, *refs):
        keep, send, up_a, up_b, stay_ref, away_ref, acc, gvec, blocks, pgb = refs[count:]

        def put(name, value):
            start, size = VSEG[name]
            gvec[0:1, start : start + size] = value

        put("g2", gate_ref[0:1, 0:HALF])
        put("b2", gate_ref[0:1, HALF : 2 * HALF])
        put("c1r", gate_ref[0:1, 2 * HALF : 3 * HALF])
        put("c1l", gsum_ref[0:1, 0:HALF])
        put("c2", gsum_ref[0:1, HALF : HALF + D])
        acc[...] = jnp.zeros_like(acc)
        def in_rows(r):
            rows = pl.ds(r, STRIPE)
            xh, scale = norm_parts(x_ref[rows, :].astype(F32))
            d = ghb[rows, :]
            e = d * seg(vec_ref, "g1")
            one = jnp.mean(e, axis=-1, keepdims=True)
            two = jnp.mean(e * xh, axis=-1, keepdims=True)
            pgb[rows, :] = og_ref[rows, :].astype(F32) + scale * (e - one - xh * two)
            acc[0:1, :] += jnp.sum(d * xh, axis=0, keepdims=True)
            acc[1:2, :] += jnp.sum(d, axis=0, keepdims=True)

        row_loop(STRIPE, in_rows)
        put("g1", acc[0:1, :])
        put("b1", acc[1:2, :])
        split_rows(pgb, stay_ref, away_ref, sides_ref[0], pgb[...])
        blocks[...] = jnp.zeros_like(blocks)
        for s in range(DEVS):
            blocks[s, 0:1, 0:VPER] = gvec[0:1, VPER * s : VPER * s + VPER]
        for k in range(DEVS):
            dev = table_ref[k]
            target, first = next((t, f) for t, f in ((up_b, 28), (up_a, 24), (send, GROUPS), (keep, 0)) if k >= f)
            r = pl.ds((k - first) * 16, 16)
            target[r, 0:HALF] = gwr[pl.ds(pl.multiple_of(dev * 16, 16), 16), :]
            target[r, HALF : HALF + VCOLS] = blocks[dev].astype(BF)

    payload = sds((D // 2, HALF + VCOLS), BF)
    part = sds((D // 4, HALF + VCOLS), BF)
    eighth = sds((D // 8, HALF + VCOLS), BF)
    pair = sds((2, half, D), BF)
    return call(
        kernel,
        (payload, part, eighth, eighth, pair, pair),
        [SM] * 2 + [VM] * 7 + [HB] * count,
        [
            pltpu.VMEM((8, D), F32),
            pltpu.VMEM((1, VEC), F32),
            pltpu.VMEM((DEVS, 16, VCOLS), F32),
            pltpu.VMEM((ROWS, D), F32),
        ],
        2000000000,
        6000000,
        table,
        sides,
        vec,
        gsum,
        gate_sum,
        gwr,
        ghb,
        x,
        grad_out,
        *after,
        room=16,
    )


def add_upper(keep, upper, after):
    cols = keep.shape[1]
    size = keep.shape[0] // 2

    def kernel(keep_ref, a_ref, b_ref, *refs):
        for r in range(0, size, 16):
            piece = a_ref if r < size // 2 else b_ref
            value = keep_ref[r : r + 16, :].astype(F32) + piece[r % (size // 2) : r % (size // 2) + 16, :].astype(F32)
            refs[len(after)][r : r + 16, :] = value.astype(BF)

    specs = [pl.BlockSpec((size, cols), lambda i: (1, 0))] + [pl.BlockSpec((size // 2, cols), lambda i: (0, 0))] * 2
    return pl.pallas_call(
        kernel,
        grid=(1,),
        out_shape=sds((size, cols), BF),
        in_specs=specs + [HB] * len(after),
        out_specs=pl.BlockSpec((size, cols), lambda i: (0, 0)),
        compiler_params=pltpu.CompilerParams(vmem_limit_bytes=10 * MIB),
        cost_estimate=pl.CostEstimate(flops=1000000, bytes_accessed=2000000, transcendentals=0),
    )(keep, *upper, *after)


def add_part(terms, size, after, places=None):
    cols = terms[0].shape[1]
    count = len(terms)

    def kernel(*refs):
        for r in range(0, size, 16):
            rows = slice(r, r + 16)
            value = refs[0][rows, :].astype(F32)
            for t in refs[1:count]:
                value = value + t[rows, :].astype(F32)
            refs[count + len(after)][rows, :] = value.astype(BF)

    places = places or [1] * count
    blocks = [pl.BlockSpec((size, cols), lambda i, p=p: (p, 0)) for p in places]
    return pl.pallas_call(
        kernel,
        grid=(1,),
        out_shape=sds((size, cols), BF),
        in_specs=blocks + [HB] * len(after),
        out_specs=pl.BlockSpec((size, cols), lambda i: (0, 0)),
        compiler_params=pltpu.CompilerParams(vmem_limit_bytes=10 * MIB),
        cost_estimate=pl.CostEstimate(flops=1000000, bytes_accessed=3000000, transcendentals=0),
    )(*terms, *after)


def line_parts(terms, after):
    cols = terms[0].shape[1]
    count = len(terms)

    def kernel(*refs):
        own, *outs = refs[count + len(after) :]
        for m in range(4):
            rows = slice(16 * m, 16 * (m + 1))
            value = refs[0][rows, :].astype(F32)
            for t in refs[1:count]:
                value = value + t[rows, :].astype(F32)
            if m == 0:
                own[...] = value
            else:
                outs[m - 1][...] = value.astype(BF)

    block = pl.BlockSpec((64, cols), lambda i: (0, 0))
    one = pl.BlockSpec((16, cols), lambda i: (0, 0))
    return pl.pallas_call(
        kernel,
        grid=(1,),
        out_shape=[sds((16, cols), F32)] + [sds((16, cols), BF)] * 3,
        in_specs=[block] * count + [HB] * len(after),
        out_specs=[one] * 4,
        compiler_params=pltpu.CompilerParams(vmem_limit_bytes=8 * MIB),
        cost_estimate=pl.CostEstimate(flops=1000000, bytes_accessed=3000000, transcendentals=0),
    )(*terms, *after)


def line_turn(terms, flip, after):
    count = len(terms)
    cols = terms[0].shape[1]

    def kernel(*refs):
        outs = refs[count + len(after) :]
        for m in range(4):
            rows = slice(16 * m, 16 * (m + 1))
            value = refs[0][rows, :].astype(F32)
            for t in refs[1:count]:
                value = value + t[rows, :].astype(F32)
            value = value.astype(BF)
            outs[0][rows, :] = value
            if flip:
                at = 16 * (m ^ flip)
                outs[1][at : at + 16, :] = value

    block = pl.BlockSpec((64, cols), lambda i: (0, 0))
    number = 2 if flip else 1
    return pl.pallas_call(
        kernel,
        grid=(1,),
        out_shape=[sds((64, cols), BF)] * number,
        in_specs=[block] * count + [HB] * len(after),
        out_specs=[block] * number,
        compiler_params=pltpu.CompilerParams(vmem_limit_bytes=8 * MIB),
        cost_estimate=pl.CostEstimate(flops=1000000, bytes_accessed=1000000, transcendentals=0),
    )(*terms, *after)


def finish_out(own, got, weight, first, second, after):
    def kernel(own_ref, a_ref, b_ref, c_ref, w_ref, m_ref, s_ref, after_ref, left_ref, nw, nm, ns):
        total = own_ref[...] + a_ref[...].astype(F32)
        total = total + (b_ref[...].astype(F32) + c_ref[...].astype(F32))
        left_ref[...] = total[:, 0:HALF]
        for g in range(3):
            rows = slice(16 * g, 16 * (g + 1))
            grad = total[:, HALF + g * D : HALF + (g + 1) * D]
            new = adamw(w_ref[rows, :], grad, m_ref[rows, :], s_ref[rows, :], DENSE_RATE, DENSE_DECAY)
            nw[rows, :] = new[0]
            nm[rows, :] = new[1]
            ns[rows, :] = new[2]

    same = sds(weight.shape, F32)
    return call(
        kernel,
        (sds((16, HALF), F32), same, same, same),
        [VM] * 7 + [HB],
        [],
        1000000,
        2000000,
        own,
        *got,
        weight,
        first,
        second,
        after,
    )


def finish_in(own, got, left, weight, first, second, after):
    def kernel(own_ref, a_ref, b_ref, c_ref, l_ref, w_ref, m_ref, s_ref, after_ref, nw, nm, ns, vec_ref):
        total = own_ref[...] + a_ref[...].astype(F32)
        total = total + (b_ref[...].astype(F32) + c_ref[...].astype(F32))
        vec_ref[...] = total[0:1, HALF:]
        for cols, grad in ((slice(0, HALF), l_ref[...]), (slice(HALF, FF), total[:, 0:HALF])):
            new = adamw(w_ref[:, cols], grad, m_ref[:, cols], s_ref[:, cols], DENSE_RATE, DENSE_DECAY)
            nw[:, cols] = new[0]
            nm[:, cols] = new[1]
            ns[:, cols] = new[2]

    same = sds(weight.shape, F32)
    return call(
        kernel,
        (same, same, same, sds((1, VCOLS), F32)),
        [VM] * 8 + [HB],
        [],
        1000000,
        2000000,
        own,
        *got,
        left,
        weight,
        first,
        second,
        after,
    )


def spatial_update(order, pieces, spatial, first, second, bias, bias_first, bias_second, after):
    count = len(pieces)
    rows = spatial.shape[1]

    def kernel(order_ref, *refs):
        ins = refs[:count]
        w_ref, m_ref, s_ref, bw, bm, bs = refs[count : count + 6]
        nw, nm, ns, nbw, nbm, nbs, flat = refs[count + 6 + len(after) :]
        k = 0
        for piece in ins:
            for j in range(piece.shape[0] // 16):
                at = pl.multiple_of(order_ref[k] * 32, 32)
                block = piece[16 * j : 16 * j + 16, :].astype(F32)
                flat[pl.ds(at, 16), :] = block[:, 0:SCOLS]
                flat[pl.ds(at + 16, 16), :] = block[:, SCOLS:]
                k += 1
        at = TOTAL_AT // 128 * 128
        totals = flat[:, at : at + 128].T[TOTAL_AT - at : TOTAL_AT - at + 1, :]
        for level in range(3):
            got = flat[level * LSTRIDE : level * LSTRIDE + rows, :]
            new = adamw(w_ref[level], got[:, 0:PMAX], m_ref[level], s_ref[level], DENSE_RATE, DENSE_DECAY)
            nw[level] = new[0]
            nm[level] = new[1]
            ns[level] = new[2]
            got = totals[:, level * LSTRIDE : level * LSTRIDE + rows]
            r = slice(level, level + 1)
            new = adamw(bw[r, :], got, bm[r, :], bs[r, :], SMALL_RATE, 0.0)
            nbw[r, :] = new[0]
            nbm[r, :] = new[1]
            nbs[r, :] = new[2]

    same = sds(spatial.shape, F32)
    small = sds(bias.shape, F32)
    return call(
        kernel,
        (same, same, same, small, small, small),
        [SM] + [VM] * (count + 6) + [HB] * len(after),
        [pltpu.VMEM((512, SCOLS), F32)],
        10000000,
        6000000,
        order,
        *pieces,
        spatial,
        first,
        second,
        bias,
        bias_first,
        bias_second,
        *after,
    )


def in_order(blocks, table, rows):
    cols = blocks[0].shape[1]
    whole = jnp.concatenate(blocks, axis=0).reshape(-1, rows, cols)
    back = jnp.zeros_like(table).at[table].set(jnp.arange(table.shape[0], dtype=table.dtype))
    return jnp.take(whole, back, axis=0)


def local(
    patches,
    resolution,
    out_grad,
    dense_in,
    dense_out,
    vectors,
    spatial,
    spatial_bias,
    in_first,
    in_second,
    out_first,
    out_second,
    vec_first,
    vec_second,
    spat_first,
    spat_second,
    bias_first,
    bias_second,
):
    route = Route(lax.axis_size("dp"))
    ndev = 2 * route.n
    fits = route.n == GROUPS
    seq = lax.axis_index("seq").astype(jnp.int32)
    rows = patches.shape[1]
    table = route.table()
    order = route.order(False)[0]
    in_rows = dense_in.shape[0]
    out_rows = dense_out.shape[0]
    vec_len = vectors.shape[0]
    if fits:
        ktable = table
        korder = table // 2
    else:
        ktable = jnp.arange(DEVS, dtype=jnp.int32)
        korder = jnp.arange(DEVS, dtype=jnp.int32) % GROUPS
    sides = jnp.concatenate([seq[None], korder])
    levels = lax.dynamic_slice_in_dim(resolution, seq * 2, 2, 0)

    right_shard, lo_shard = pack_dense(dense_in, dense_out, vectors.reshape(1, vec_len))
    line = [right_shard] + [route.swap(right_shard, (m, m)) for m in route.direct]
    lo_line = [lo_shard] + [route.swap(lo_shard, (m, m)) for m in route.direct]
    spat_own, x_send, g_send = pack_images(sides, spatial, spatial_bias.reshape(3, rows, 1), patches, out_grad)
    x_got = route.cross(x_send)
    g_got = route.cross(g_send)
    spat_got = route.cross(spat_own)
    if fits:
        right_blocks, passed = route.widen_in_turn(stack(line, []))
        lo_blocks = route.widen_direct(stack(lo_line, [passed]))
    else:
        right_blocks = route.widen(jnp.concatenate(line, axis=0))
        lo_blocks = route.widen(jnp.concatenate(lo_line, axis=0))
    right_blocks = right_blocks + [route.cross(b) for b in right_blocks]
    if not fits:
        lo_blocks = lo_blocks + [route.cross(b) for b in lo_blocks]
    if not fits:
        whole = in_order(right_blocks, table, in_rows)
        all_vec = whole[:, 0, HALF : HALF + vec_len].reshape(DEVS, 1, VPER)
        all_vec = jnp.pad(all_vec, ((0, 0), (0, 15), (0, VCOLS - VPER))).reshape(D, VCOLS)
        right_blocks = [jnp.concatenate([whole[:, :, :HALF].reshape(D, HALF), all_vec], axis=1)]
        whole = in_order(lo_blocks, table, in_rows)
        outs = whole[:, :, HALF:].reshape(ndev, in_rows, 3, D).transpose(0, 2, 1, 3).reshape(DEVS, 3, 16, D)
        outs = outs.transpose(0, 2, 1, 3).reshape(D, HALF)
        lo_blocks = [jnp.concatenate([whole[:, :, :HALF].reshape(D, HALF), outs], axis=1)]

    x, grad_out, h, v, slope, part, weight_right, vec = gate_forward(
        ktable, sides, patches, x_got, out_grad, g_got, right_blocks
    )
    gate, hat, scale, spat, mm = gate_norm(levels, sides, vec, v, part, spat_own, spat_got, [])
    if fits:
        lo_blocks = lo_blocks + [route.cross(lo_blocks[0]), route.cross(stack(lo_blocks[1:], [mm]))]
    gs, gated, q, gb, wl, wo, sp_keep, sp_send, gsum = middle(ktable, levels, sides, vec, h, spat, gate, grad_out, lo_blocks)
    near, far = route.low[-1], route.low[0]
    after = [[] for _ in range(5)]
    if fits:
        sp_got = route.cross(sp_send)
        sp_part = add_part([sp_keep, sp_got], 128, [])
        sp_terms = [sp_keep, sp_got, route.swap(sp_part, near)]
        after[0] = [sp_part]
    gwo = out_grads(gated, gb, after[0])
    if fits:
        sp_part = add_part(sp_terms, 64, [gwo])
        sp_terms.append(route.swap(sp_part, far))
        after[1] = [sp_part]
    lo_keep, lo_send, lo_up, mixed_stay, mixed_away, gh = weight_grads(
        ktable, levels, sides, vec, gated, q, gwo, h, wl, wo, x, rows, after[1]
    )
    mixed_got = route.cross(mixed_away)
    if fits:
        lo_up = route.cross(lo_up)
        lo_terms = [lo_keep, route.cross(lo_send)]
        lo_part = add_part([lo_keep, lo_up], 128, [], [1, 0])
        lo_terms.append(route.swap(lo_part, near))
        sp_own, sp_out = line_turn(sp_terms, 1, [lo_part])
        sp_terms = [sp_own, route.swap(sp_out, (route.direct[0],) * 2)]
        after[2] = [sp_own]
    gp, gate_sum = gate_backward(vec, gs, mm, hat, slope, scale, after[2])
    if fits:
        sp_own, sp_out = line_turn(sp_terms, 2, [gate_sum])
        sp_terms = [sp_own, route.swap(sp_out, (route.direct[1],) * 2)]
        after[3] = [sp_own, mixed_got]
    gwr, ghb = in_grads(gp, h, weight_right, gh, after[3])
    if fits:
        lo_part = add_part(lo_terms, 64, [gwr])
        lo_terms.append(route.swap(lo_part, far))
        after[4] = [lo_part]
    right_keep, right_send, up_a, up_b, grad_stay, grad_away = in_backward(
        ktable, sides, vec, gsum, gate_sum, gwr, ghb, x, grad_out, rows, after[4]
    )
    grad_got = route.cross(grad_away)
    if fits:
        upper = [route.cross(up_a), route.cross(up_b)]
        right_terms = [right_keep, route.cross(right_send)]
        lo_own, *sends = line_parts(lo_terms, [right_keep])
        lo_got = [route.swap(p, (m, m)) for p, m in zip(sends, route.direct)]
        right_part = add_upper(right_keep, upper, [lo_own])
        right_terms.append(route.swap(right_part, near))
        (sp_sum,) = line_turn(sp_terms, 0, [right_part, grad_got])
        spat_pieces = route.widen(sp_sum)
        right_part = add_part(right_terms, 64, [sp_sum])
        right_terms.append(route.swap(right_part, far))
        right_own, *sends = line_parts(right_terms, [right_part])
        right_got = [route.swap(p, (m, m)) for p, m in zip(sends, route.direct)]
        left_sum, *new_out = finish_out(lo_own, lo_got, dense_out, out_first, out_second, right_own)
        korder = order
        after = [left_sum]
    else:
        both = jnp.concatenate([lo_keep, lo_send, lo_up])
        outs = both[:, HALF:LO].reshape(DEVS, 16, 3, D).transpose(0, 2, 1, 3).reshape(ndev, out_rows, D)
        outs = jnp.take(outs, table, axis=0).reshape(HALF, D)
        out_sum = route.scatter(outs[: HALF // 2], outs[HALF // 2 :])
        lefts = jnp.take(both[:, :HALF].reshape(ndev, in_rows, HALF), table, axis=0).reshape(D, HALF)
        left_sum = route.scatter(lefts[: D // 2], lefts[D // 2 :])
        per = 512 // route.n

        def spat_blocks(part, flip):
            flat = part.reshape(GROUPS, 16, 2, SCOLS).transpose(0, 2, 1, 3).reshape(route.n, per, SCOLS)
            return jnp.take(flat, route.order(flip)[0], axis=0).reshape(512, SCOLS)

        spat_part = route.scatter(spat_blocks(sp_keep, False), spat_blocks(sp_send, True)).astype(BF)
        flat = in_order(route.spread(spat_part), order, per).reshape(GROUPS, 2, 16, SCOLS)
        spat_pieces = [flat.transpose(0, 2, 1, 3).reshape(GROUPS * 16, SPC)]
        korder = jnp.arange(GROUPS, dtype=jnp.int32)
        after = []
        both = jnp.concatenate([right_keep, right_send, up_a, up_b])
        vecs = jnp.take(both[::16, HALF : HALF + VPER].reshape(ndev, vec_len), table, axis=0)
        vec_sum = route.scatter(vecs[: route.n], vecs[route.n :]).reshape(vec_len)
        rights = jnp.take(both[:, :HALF].reshape(ndev, in_rows, HALF), table, axis=0).reshape(D, HALF)
        right_sum = route.scatter(rights[: D // 2], rights[D // 2 :])
        in_sum = jnp.concatenate([left_sum, right_sum], axis=1)
        new_in = adamw(dense_in, in_sum, in_first, in_second, DENSE_RATE, DENSE_DECAY)
        new_out = adamw(dense_out, out_sum, out_first, out_second, DENSE_RATE, DENSE_DECAY)

    def whole_images(stays, came):
        return jnp.concatenate([jnp.where(seq == 0, stays, came), jnp.where(seq == 0, came, stays)], axis=0)

    mixed = whole_images(mixed_stay, mixed_got)
    patches_grad = whole_images(grad_stay, grad_got)
    spat_new = spatial_update(
        korder, spat_pieces, spatial, spat_first, spat_second, spatial_bias, bias_first, bias_second, after
    )
    if fits:
        *new_in, vec_sum = finish_in(right_own, right_got, left_sum, dense_in, in_first, in_second, spat_new[0])
        vec_sum = vec_sum[0, :vec_len]
    new_vec = adamw(vectors, vec_sum, vec_first, vec_second, SMALL_RATE, 0.0)
    return (mixed, patches_grad) + tuple(new_in) + tuple(new_out) + new_vec + tuple(spat_new)


def solution(mesh):
    rows3 = P("dp", "seq", None)
    dense = P(AXES, None)
    vec = P(AXES)
    spat = P(None, "seq", None)
    bias = P(None, "seq")
    in_specs = (rows3, P("dp"), rows3, dense, dense, vec, spat, bias)
    in_specs += (dense,) * 4 + (vec,) * 2 + (spat,) * 2 + (bias,) * 2
    out_specs = (rows3, rows3) + (dense,) * 6 + (vec,) * 3 + (spat,) * 3 + (bias,) * 3
    return jax.shard_map(local, mesh=mesh, in_specs=in_specs, out_specs=out_specs, check_vma=False)
```

```python
import functools

import jax
import jax.numpy as jnp
from jax import lax
from jax.experimental import pallas as pl
from jax.experimental.pallas import tpu as pltpu
from jax.sharding import PartitionSpec as P

D = 512
FF = 3072
HALF = 1536
PMAX = 324
PPAD = 336
P_MID = 196
P_LOW = 100
VCOLS = 256
ROWS = 2 * PPAD
GROUPS = 16
DEVS = 2 * GROUPS
VPER = 240
SCOLS = 384
BIAS_AT = 336
TOTAL_AT = 324
LSTRIDE = 168
MIB = 1024 * 1024
STEP = 10

NORM_EPS = 1e-05
BETA_ONE = 0.9
BETA_TWO = 0.99
ADAM_EPS = 1e-08
DENSE_RATE = 0.02
SMALL_RATE = 0.2
DENSE_DECAY = 0.05

BF = jnp.bfloat16
F32 = jnp.float32
AXES = ("dp", "seq")
VM = pl.BlockSpec(memory_space=pltpu.VMEM)
SM = pl.BlockSpec(memory_space=pltpu.SMEM)
HB = pl.BlockSpec(memory_space=pl.ANY)


class Route:
    def __init__(self, n):
        bits = n.bit_length() - 1
        assert n == 1 << bits and bits >= 2
        self.n = n
        top = n // 4
        self.direct = [top, 2 * top, 3 * top]
        low = [1 << b for b in range(bits - 2)]
        self.low = list(zip(low[::-1], low))
        masks = [(0, 0)] + [(m, m) for m in self.direct]
        for step in self.low:
            masks = masks + [(m[0] ^ step[0], m[1] ^ step[1]) for m in masks]
        self.masks = masks

    def swap(self, block, mask):
        pairs = []
        for dp in range(self.n):
            for seq in range(2):
                pairs.append((dp * 2 + seq, (dp ^ mask[seq]) * 2 + seq))
        return lax.ppermute(block, AXES, pairs)

    def cross(self, block):
        pairs = []
        for dp in range(self.n):
            for seq in range(2):
                pairs.append((dp * 2 + seq, dp * 2 + 1 - seq))
        return lax.ppermute(block, AXES, pairs)

    def order(self, seq_flip):
        place = lax.axis_index("dp")
        seq = lax.axis_index("seq")
        if seq_flip:
            seq = 1 - seq
        zero = jnp.array([m[0] for m in self.masks], jnp.int32)
        one = jnp.array([m[1] for m in self.masks], jnp.int32)
        return place ^ jnp.where(seq == 0, zero, one), seq

    def table(self):
        mine, seq = self.order(False)
        other, flip = self.order(True)
        return jnp.concatenate([mine * 2 + seq, other * 2 + flip])

    def spread(self, shard):
        first = jnp.concatenate([shard] + [self.swap(shard, (m, m)) for m in self.direct], axis=0)
        return self.widen(first)

    def widen(self, first):
        blocks = [first]
        for step in self.low:
            blocks = blocks + [self.swap(b, step) for b in blocks]
        return blocks

    def widen_in_turn(self, first):
        second = self.swap(first, self.low[0])
        third = self.swap(first, self.low[1])
        passed = stack([second], [third])
        return [first, second, third, self.swap(passed, self.low[1])], passed

    def widen_direct(self, first):
        return [first] + [self.swap(first, m) for m in self.plane()]

    def plane(self):
        one, two = self.low
        return [one, two, (one[0] ^ two[0], one[1] ^ two[1])]

    def gather(self, shard):
        blocks = self.spread(shard)
        return blocks + [self.cross(b) for b in blocks]

    def collect(self, terms):
        cur = terms[0].shape[0]
        rows = cur // self.n

        def part(lower, upper):
            total = terms[0][lower:upper].astype(F32)
            for t in terms[1:]:
                total = total + t[lower:upper].astype(F32)
            return total

        terms = list(terms)
        for step in reversed(self.low):
            half = cur // 2
            terms.append(self.swap(part(half, cur).astype(BF), step))
            cur = half
        got = []
        for j, m in enumerate(self.direct):
            got.append(self.swap(part((j + 1) * rows, (j + 2) * rows).astype(BF), (m, m)))
        total = part(0, rows)
        return (total + got[0].astype(F32)) + (got[1].astype(F32) + got[2].astype(F32))

    def scatter(self, keep, send):
        return self.collect([keep, self.cross(send)])


def dot(a, b, dims):
    return lax.dot_general(a, b, (dims, ((), ())), preferred_element_type=F32)


NN = ((1,), (0,))
NT = ((1,), (1,))
TN = ((0,), (0,))


def gelu_parts(p):
    bell = jnp.exp(p * p * -0.5)
    d = 1.0 + jnp.abs(p) * (0.3275911 * 0.7071067811865476)
    t = pl.reciprocal(d, approx=True)
    t = t * (2.0 - d * t)
    poly = t * (
        0.127414796
        + t * (-0.142248368 + t * (0.7107068705 + t * (-0.7265760135 + t * 0.5307027145)))
    )
    tail = poly * bell
    phi_sum = jnp.where(p >= 0.0, 1.0 - tail, tail)
    return p * phi_sum, phi_sum + p * bell * 0.3989422804014327


def count_of(level):
    return jnp.where(level == 0, P_LOW, jnp.where(level == 1, P_MID, PMAX))


def masked_mix(mix, count):
    i = lax.broadcasted_iota(jnp.int32, (PPAD, SCOLS), 0)
    j = lax.broadcasted_iota(jnp.int32, (PPAD, SCOLS), 1)
    return jnp.where((i < count) & (j < count), mix.astype(F32), 0.0).astype(BF)


def live_rows(count, shape, start=0):
    return lax.broadcasted_iota(jnp.int32, shape, 0) + start < count


def live_mask(levels_ref, b, width):
    return live_rows(count_of(levels_ref[b]), (PPAD, width))


def fold(value):
    total = value[:, 0:128]
    for n in range(128, value.shape[1], 128):
        total = total + value[:, n : n + 128]
    return total


def spread_sum(ref, factor):
    return jnp.broadcast_to(jnp.sum(ref[...], axis=-1, keepdims=True) * factor, ref.shape)


def wide(value, times):
    return jnp.concatenate([value] * times, axis=1)


def start_blocks(table_ref, pieces, rows, cols, target, sem, extra=0):
    copies = []
    k = 0
    for piece in pieces:
        for j in range(piece.shape[0] // 16):
            at = pl.multiple_of(table_ref[k] * rows, 16)
            c = pltpu.make_async_copy(
                piece.at[pl.ds(j * 16, 16), pl.ds(cols[0], cols[1])], target.at[pl.ds(at + extra, 16)], sem.at[k]
            )
            c.start()
            copies.append(c)
            k += 1
    return copies


def row_loop(step, body):
    def run(i, carry):
        body(pl.multiple_of(i * step, step))
        return carry

    lax.fori_loop(0, ROWS // step, run, 0)


def call(kernel, out_shape, in_specs, scratch, flops, nbytes, *args, room=12):
    vm = pl.BlockSpec(memory_space=pltpu.VMEM)
    return pl.pallas_call(
        kernel,
        out_shape=out_shape,
        in_specs=in_specs,
        out_specs=jax.tree.map(lambda _: vm, out_shape),
        scratch_shapes=scratch,
        compiler_params=pltpu.CompilerParams(vmem_limit_bytes=room * MIB),
        cost_estimate=pl.CostEstimate(flops=flops, bytes_accessed=nbytes, transcendentals=0),
    )(*args)


def norm_parts(values):
    center = values - jnp.mean(values, axis=-1, keepdims=True)
    scale = lax.rsqrt(jnp.mean(center * center, axis=-1, keepdims=True) + NORM_EPS)
    return center * scale, scale


VSEG = {
    "g1": (0, D),
    "b1": (D, D),
    "c1l": (2 * D, HALF),
    "c1r": (2 * D + HALF, HALF),
    "g2": (2 * D + FF, HALF),
    "b2": (2 * D + FF + HALF, HALF),
    "c2": (2 * D + FF + 2 * HALF, D),
}
VEC = 2 * D + FF + 2 * HALF + D


def seg(ref, name):
    start, size = VSEG[name]
    return ref[0:1, start : start + size]

def adamw(weight, grad, first, second, rate, decay):
    first = BETA_ONE * first + (1.0 - BETA_ONE) * grad
    second = BETA_TWO * second + (1.0 - BETA_TWO) * grad * grad
    first_hat = first / (1.0 - BETA_ONE**STEP)
    second_hat = second / (1.0 - BETA_TWO**STEP)
    weight = weight - rate * (first_hat / (jnp.sqrt(second_hat) + ADAM_EPS) + decay * weight)
    return (weight, first, second)


CHUNK = 16
TILE = 256
BODY = 32
STRIPE = 112
LO = 2 * HALF
SPC = 2 * SCOLS


def sds(shape, dtype):
    return jax.ShapeDtypeStruct(shape, dtype)


def pack_dense(dense_in, dense_out, vec_row):
    rows = dense_in.shape[0]
    per = vec_row.shape[1]

    def kernel(w_hbm, o_hbm, v_hbm, out_ref, lo_ref, w_ref, o_ref, v_ref, row, sem):
        copies = [
            pltpu.make_async_copy(src, dst, sem.at[k])
            for k, (src, dst) in enumerate(((w_hbm, w_ref), (o_hbm, o_ref), (v_hbm, v_ref)))
        ]
        for c in copies:
            c.start()
        row[...] = jnp.zeros_like(row)
        for c in copies:
            c.wait()
        out_ref[:, 0:HALF] = w_ref[:, HALF:].astype(BF)
        row[0:1, 0:per] = v_ref[...]
        out_ref[:, HALF : HALF + VCOLS] = row[...].astype(BF)
        lo_ref[:, 0:HALF] = w_ref[:, 0:HALF].astype(BF)
        for g in range(3):
            lo_ref[:, HALF + g * D : HALF + (g + 1) * D] = o_ref[g * rows : (g + 1) * rows, :].astype(BF)

    scratch = [
        pltpu.VMEM(dense_in.shape, F32),
        pltpu.VMEM(dense_out.shape, F32),
        pltpu.VMEM(vec_row.shape, F32),
        pltpu.VMEM((rows, VCOLS), F32),
        pltpu.SemaphoreType.DMA((3,)),
    ]
    shape = (sds((rows, HALF + VCOLS), BF), sds((rows, LO), BF))
    return call(kernel, shape, [HB] * 3, scratch, 1000, 600000, dense_in, dense_out, vec_row, room=60)


def pack_images(sides, spatial, bias_col, patches, out_grad):
    half = patches.shape[1]

    def kernel(sides_ref, s_ref, b_ref, x_ref, g_ref, spat_ref, xs_ref, gs_ref, buf):
        away = 2 - 2 * sides_ref[0]
        for b in range(2):
            xs_ref[b] = x_ref[away + b]
            gs_ref[b] = g_ref[away + b]
        buf[...] = jnp.zeros_like(buf)
        for level in range(3):
            buf[:, 0:PMAX] = s_ref[level]
            rest = b_ref[level]
            for c in range(3):
                piece = rest.astype(BF).astype(F32)
                buf[:, BIAS_AT + c : BIAS_AT + c + 1] = piece
                rest = rest - piece
            spat_ref[level] = buf[...].astype(BF)

    pair = sds((2, half, D), BF)
    return call(
        kernel,
        (sds((3, half, SCOLS), BF), pair, pair),
        [SM] + [VM] * 4,
        [pltpu.VMEM((half, SCOLS), F32)],
        1000,
        3000000,
        sides,
        spatial,
        bias_col,
        patches,
        out_grad,
    )


def stack(pieces, after):
    count = len(pieces)
    rows, cols = pieces[0].shape

    def kernel(*refs):
        out = refs[count + len(after)]
        for k in range(count):
            out[k * rows : (k + 1) * rows, :] = refs[k][...]

    specs = [VM] * count + [HB] * len(after)
    return call(kernel, sds((count * rows, cols), BF), specs, [], 1000, 1000000, *pieces, *after)


def two_halves(is_first, own, got):
    own = own.astype(F32)
    got = got.astype(F32)
    return jnp.where(is_first, own, got), jnp.where(is_first, got, own)


def gate_norm(levels, sides, vec, v, part, spat_own, spat_got, after):
    half = spat_own.shape[1]
    count = len(after)

    def kernel(levels_ref, sides_ref, vec_ref, v_ref, part_ref, so_ref, sg_ref, *refs):
        gate_ref, hat_ref, scale_ref, spat_ref, mm_ref, mixf, mean, buf = refs[count:]
        is_first = sides_ref[0] == 0
        g_start = VSEG["g2"][0]
        b_start = VSEG["b2"][0]
        mean[...] = spread_sum(part_ref, 1.0 / HALF)

        def square_rows(r):
            for k in range(0, BODY, CHUNK):
                rows = pl.ds(r + k, CHUNK)
                mid = mean[rows, :]
                total = jnp.zeros((CHUNK, 128), F32)
                for n in range(0, HALF, 128):
                    center = v_ref[rows, n : n + 128] - mid
                    total = total + center * center
                buf[rows, :] = total

        row_loop(BODY, square_rows)
        scale_ref[...] = lax.rsqrt(spread_sum(buf, 1.0 / HALF) + NORM_EPS)

        def gate_rows(r):
            for k in range(0, BODY, CHUNK):
                rows = pl.ds(r + k, CHUNK)
                mid = wide(mean[rows, :], 2)
                scale = wide(scale_ref[rows, :], 2)
                for n in range(0, HALF, TILE):
                    hat = (v_ref[rows, n : n + TILE] - mid) * scale
                    hat_ref[rows, n : n + TILE] = hat.astype(BF)
                    gate = hat * vec_ref[0:1, g_start + n : g_start + n + TILE]
                    gate = (gate + vec_ref[0:1, b_start + n : b_start + n + TILE]).astype(BF)
                    gate_ref[rows, n : n + TILE] = gate

        row_loop(BODY, gate_rows)
        gate_ref[ROWS:, :] = jnp.zeros((SCOLS - PPAD, HALF), BF)
        for b in range(2):
            level = levels_ref[b]
            live = count_of(level)
            one, two = two_halves(is_first, so_ref[level], sg_ref[level])
            mixf[0:half, :] = one
            mixf[half : 2 * half, :] = two
            mixf[2 * half :, :] = jnp.zeros((PPAD - 2 * half, SCOLS), F32)
            bias = jnp.sum(mixf[:, TOTAL_AT:], axis=-1, keepdims=True)
            mm_ref[b] = masked_mix(mixf[...], live)

            def mix_tile(n, carry):
                cols = pl.ds(pl.multiple_of(n * 512, 512), 512)
                got = dot(mm_ref[b], gate_ref[b * PPAD : b * PPAD + SCOLS, cols], NN) + bias
                got = jnp.where(live_rows(live, (PPAD, 512)), got, 0.0)
                spat_ref[b * PPAD : (b + 1) * PPAD, cols] = got.astype(BF)
                return carry

            lax.fori_loop(0, HALF // 512, mix_tile, 0)

    return call(
        kernel,
        (
            sds((ROWS + SCOLS - PPAD, HALF), BF),
            sds((ROWS, HALF), BF),
            sds((ROWS, 128), F32),
            sds((ROWS, HALF), BF),
            sds((2, PPAD, SCOLS), BF),
        ),
        [SM] * 2 + [VM] * 5 + [HB] * count,
        [pltpu.VMEM((PPAD, SCOLS), F32), pltpu.VMEM((ROWS, 128), F32), pltpu.VMEM((ROWS, 128), F32)],
        6000000000,
        12000000,
        levels,
        sides,
        vec,
        v,
        part,
        spat_own,
        spat_got,
        *after,
        room=22,
    )


def gate_forward(table, sides, patches, x_got, out_grad, g_got, pieces):
    count = len(pieces)
    half = patches.shape[1]

    def kernel(table_ref, sides_ref, p_ref, xg_ref, o_ref, gg_ref, *refs):
        ins = refs[:count]
        outs = refs[count : count + 8]
        x_ref, og_ref, h_ref, pre, slope_ref, part, w_ref, vec_ref = outs
        vblk, xbuf, sem, vsem = refs[count + 8 :]
        vcopies = start_blocks(table_ref, ins, 16, (HALF, VCOLS), vblk, vsem)
        copies = start_blocks(table_ref, ins, 16, (0, HALF), w_ref, sem)
        me = sides_ref[0]
        is_first = me == 0

        for src, got, target in ((o_ref, gg_ref, og_ref), (p_ref, xg_ref, x_ref)):
            for b in range(2):
                one, two = two_halves(is_first, src[2 * me + b], got[b])
                xbuf[b * PPAD : b * PPAD + half, :] = one
                xbuf[b * PPAD + half : b * PPAD + 2 * half, :] = two
                xbuf[b * PPAD + 2 * half : (b + 1) * PPAD, :] = jnp.zeros((PPAD - 2 * half, D), F32)
            target[...] = xbuf[...].astype(BF)
        for c in vcopies:
            c.wait()
        for s in range(DEVS):
            row = vblk[16 * s : 16 * s + 16, :].astype(F32)[0:1, :VPER]
            vec_ref[0:1, VPER * s : VPER * s + VPER] = row

        def norm_one(r):
            hat, _ = norm_parts(xbuf[pl.ds(r, STRIPE), :])
            h_ref[pl.ds(r, STRIPE), :] = (hat * seg(vec_ref, "g1") + seg(vec_ref, "b1")).astype(BF)

        row_loop(STRIPE, norm_one)
        for c in copies:
            c.wait()
        c_start = VSEG["c1r"][0]

        def matmul(n, carry):
            at = pl.multiple_of(n * TILE, TILE)
            pre[:, pl.ds(at, TILE)] = dot(h_ref[...], w_ref[:, pl.ds(at, TILE)], NN)
            return carry

        lax.fori_loop(0, HALF // TILE, matmul, 0)

        def gelu_rows(r):
            for k in range(0, BODY, CHUNK):
                rows = pl.ds(r + k, CHUNK)
                total = jnp.zeros((CHUNK, 128), F32)
                for n in range(0, HALF, TILE):
                    v, slope = gelu_parts(pre[rows, n : n + TILE] + vec_ref[0:1, c_start + n : c_start + n + TILE])
                    pre[rows, n : n + TILE] = v
                    slope_ref[rows, n : n + TILE] = slope.astype(BF)
                    total = total + fold(v)
                part[rows, :] = total

        row_loop(BODY, gelu_rows)

    broad = sds((ROWS, HALF), BF)
    narrow = sds((ROWS, D), BF)
    out_shape = (
        narrow,
        narrow,
        narrow,
        sds((ROWS, HALF), F32),
        broad,
        sds((ROWS, 128), F32),
        sds((D, HALF), BF),
        sds((1, VEC), F32),
    )
    scratch = [
        pltpu.VMEM((D, VCOLS), BF),
        pltpu.VMEM((ROWS, D), F32),
        pltpu.SemaphoreType.DMA((DEVS,)),
        pltpu.SemaphoreType.DMA((DEVS,)),
    ]
    return call(
        kernel,
        out_shape,
        [SM] * 2 + [VM] * 4 + [HB] * count,
        scratch,
        10000000000,
        20000000,
        table,
        sides,
        patches,
        x_got,
        out_grad,
        g_got,
        *pieces,
        room=26,
    )


def split_rows(target, first, second, seq, value):
    half = first.shape[1]
    target[...] = value
    for b in range(2):
        one = target[b * PPAD : b * PPAD + half, :]
        two = target[b * PPAD + half : b * PPAD + 2 * half, :]
        first[b] = jnp.where(seq == 0, one, two).astype(BF)
        second[b] = jnp.where(seq == 0, two, one).astype(BF)


def middle(table, levels, sides, vec, h, spat, gate, grad_out, pieces):
    count = len(pieces)

    def kernel(table_ref, levels_ref, sides_ref, vec_ref, h_ref, spat_ref, gate_ref, og_ref, *refs):
        ins = refs[:count]
        gs_ref, gated_ref, q_ref, gb, wl, wo, keep, send, gsum_ref = refs[count : count + 9]
        pbuf, gbuf, cells, flat, sem = refs[count + 9 :]
        copies = start_blocks(table_ref, ins, 16, (0, HALF), wl, sem.at[0])
        for g in range(3):
            copies += start_blocks(table_ref, ins, 48, (HALF + g * D, D), wo, sem.at[1 + g], 16 * g)
        for b in range(2):
            rows = slice(b * PPAD, (b + 1) * PPAD)
            gb[rows, :] = jnp.where(live_mask(levels_ref, b, D), og_ref[rows, :].astype(F32), 0.0).astype(BF)
        gsum_ref[0:1, HALF : HALF + D] = jnp.sum(gb[...].astype(F32), axis=0, keepdims=True)
        cells[...] = jnp.zeros_like(cells)
        flat[...] = jnp.zeros_like(flat)
        for c in copies:
            c.wait()
        c_start = VSEG["c1l"][0]

        def tile(n, carry):
            at = pl.multiple_of(n * TILE, TILE)
            cols = pl.ds(at, TILE)
            pbuf[...] = dot(h_ref[...], wl[:, cols], NN)
            gbuf[...] = dot(gb[...], wo[cols, :], NT)
            shift = vec_ref[0:1, pl.ds(c_start + at, TILE)]
            total = jnp.zeros((CHUNK, TILE), F32)
            for k in range(0, ROWS, CHUNK):
                r = slice(k, k + CHUNK)
                u, slope = gelu_parts(pbuf[r, :] + shift)
                sp = spat_ref[r, cols].astype(F32)
                gg = gbuf[r, :]
                gated_ref[r, cols] = (u * sp).astype(BF)
                gs_ref[r, cols] = (gg * u).astype(BF)
                q = (gg * sp * slope).astype(BF)
                q_ref[r, cols] = q
                total = total + q.astype(F32)
            gsum_ref[0:1, cols] = jnp.sum(total, axis=0, keepdims=True)
            return carry

        lax.fori_loop(0, HALF // TILE, tile, 0)

        me = sides_ref[0]
        for b in range(2):
            level = levels_ref[b]
            count_b = count_of(level)
            gs = gs_ref[b * PPAD : (b + 1) * PPAD, :]
            got = dot(gs, gate_ref[b * PPAD : (b + 1) * PPAD, :], NT)
            sums = jnp.sum(gs.astype(F32), axis=-1, keepdims=True)
            j = lax.broadcasted_iota(jnp.int32, (PPAD, PPAD), 1)
            got = jnp.where(j < count_b, got, jnp.where(j == TOTAL_AT, sums, 0.0))
            cells[level, :, 0:PPAD] += got
        part = PMAX // 2
        for level in range(3):
            for k in range(2):
                flat[k, level * LSTRIDE : level * LSTRIDE + part, 0:PPAD] = cells[level, k * part : (k + 1) * part, 0:PPAD]
        for k in range(DEVS):
            target, side = (keep, me) if k < GROUPS else (send, 1 - me)
            r = pl.ds(k % GROUPS * 16, 16)
            block = flat[side, pl.ds(pl.multiple_of(sides_ref[1 + k] * 32, 32), 32), :].astype(BF)
            target[r, 0:SCOLS] = block[0:16]
            target[r, SCOLS:SPC] = block[16:32]

    broad = sds((ROWS, HALF), BF)
    payload = sds((D // 2, SPC), BF)
    out_shape = (
        broad,
        broad,
        broad,
        sds((ROWS, D), BF),
        sds((D, HALF), BF),
        sds((HALF, D), BF),
        payload,
        payload,
        sds((1, HALF + D), F32),
    )
    scratch = [
        pltpu.VMEM((ROWS, TILE), F32),
        pltpu.VMEM((ROWS, TILE), F32),
        pltpu.VMEM((3, PPAD, SCOLS), F32),
        pltpu.VMEM((2, 512, SCOLS), F32),
        pltpu.SemaphoreType.DMA((4, DEVS)),
    ]
    return call(
        kernel,
        out_shape,
        [SM] * 3 + [VM] * 5 + [HB] * count,
        scratch,
        8000000000,
        16000000,
        table,
        levels,
        sides,
        vec,
        h,
        spat,
        gate,
        grad_out,
        *pieces,
        room=28,
    )


def weight_grads(levels, sides, vec, gated, q, h, wl, wo, x, half, after):
    count = len(after)

    def kernel(levels_ref, sides_ref, vec_ref, t_ref, q_ref, h_ref, wl_ref, wo_ref, x_ref, *refs):
        gwl, stay_ref, away_ref, gh_ref, branch = refs[count:]

        def in_tile(n, carry):
            cols = pl.ds(pl.multiple_of(n * TILE, TILE), TILE)
            gwl[cols, :] = dot(h_ref[:, cols], q_ref[...], TN).astype(BF)
            branch[:, cols] = dot(t_ref[...], wo_ref[:, cols], NN)
            gh_ref[:, cols] = dot(q_ref[...], wl_ref[cols, :], NT)
            return carry

        lax.fori_loop(0, D // TILE, in_tile, 0)
        me = sides_ref[0]
        live = jnp.concatenate([live_mask(levels_ref, b, D) for b in range(2)], axis=0)
        out = branch[...] + seg(vec_ref, "c2")
        split_rows(branch, stay_ref, away_ref, me, x_ref[...].astype(F32) + jnp.where(live, out, 0.0))

    pair = sds((2, half, D), BF)
    return call(
        kernel,
        (sds((D, HALF), BF), pair, pair, sds((ROWS, D), F32)),
        [SM] * 2 + [VM] * 7 + [HB] * count,
        [pltpu.VMEM((ROWS, D), F32)],
        4000000000,
        12000000,
        levels,
        sides,
        vec,
        gated,
        q,
        h,
        wl,
        wo,
        x,
        *after,
        room=12,
    )


def out_grads(table, gated, gb, gwl, after):
    count = len(after)

    def kernel(table_ref, t_ref, gb_ref, gwl_ref, *refs):
        keep, send, send_up, gwo = refs[count:]

        def out_tile(n, carry):
            cols = pl.ds(pl.multiple_of(n * TILE, TILE), TILE)
            gwo[cols, :] = dot(t_ref[:, cols], gb_ref[...], TN).astype(BF)
            return carry

        lax.fori_loop(0, HALF // TILE, out_tile, 0)
        for k in range(DEVS):
            dev = table_ref[k]
            target = keep if k < GROUPS else send if k < GROUPS * 3 // 2 else send_up
            r = pl.ds(k % (GROUPS if k < GROUPS else GROUPS // 2) * 16, 16)
            target[r, 0:HALF] = gwl_ref[pl.ds(pl.multiple_of(dev * 16, 16), 16), :]
            for g in range(3):
                target[r, HALF + g * D : HALF + (g + 1) * D] = gwo[pl.ds(pl.multiple_of(dev * 48 + 16 * g, 16), 16), :]

    payload = sds((D // 2, LO), BF)
    part = sds((D // 4, LO), BF)
    return call(
        kernel,
        (payload, part, part),
        [SM] + [VM] * 3 + [HB] * count,
        [pltpu.VMEM((HALF, D), BF)],
        2000000000,
        8000000,
        table,
        gated,
        gb,
        gwl,
        *after,
        room=10,
    )


def gate_backward(vec, gs, mm, hat, slope, scale, after):
    count = len(after)

    def kernel(vec_ref, gs_ref, mm_ref, hat_ref, slope_ref, scale_ref, *refs):
        gp, gsum_ref, dbuf, one, two, acc = refs[count:]

        for b in range(2):

            def mix_tile(n, carry):
                cols = pl.ds(pl.multiple_of(n * 512, 512), 512)
                got = dot(mm_ref[b], gs_ref[b * PPAD : (b + 1) * PPAD, cols], TN)
                dbuf[b * PPAD : (b + 1) * PPAD, cols] = got[0:PPAD]
                return carry

            lax.fori_loop(0, HALF // 512, mix_tile, 0)
        g_start = VSEG["g2"][0]

        def sum_rows(r):
            for k in range(0, BODY, CHUNK):
                rows = pl.ds(r + k, CHUNK)
                a = jnp.zeros((CHUNK, 128), F32)
                c = jnp.zeros((CHUNK, 128), F32)
                for n in range(0, HALF, TILE):
                    e = dbuf[rows, n : n + TILE] * vec_ref[0:1, g_start + n : g_start + n + TILE]
                    a = a + fold(e)
                    c = c + fold(e * hat_ref[rows, n : n + TILE].astype(F32))
                one[rows, :] = a
                two[rows, :] = c

        row_loop(BODY, sum_rows)
        one[...] = spread_sum(one, 1.0 / HALF)
        two[...] = spread_sum(two, 1.0 / HALF)
        acc[...] = jnp.zeros_like(acc)

        def grad_rows(r):
            for n in range(0, HALF, TILE):
                gain = vec_ref[0:1, g_start + n : g_start + n + TILE]
                sums = [jnp.zeros((CHUNK, TILE), F32) for _ in range(3)]
                for k in range(0, BODY, CHUNK):
                    rows = pl.ds(r + k, CHUNK)
                    d = dbuf[rows, n : n + TILE]
                    xh = hat_ref[rows, n : n + TILE].astype(F32)
                    inner = d * gain - wide(one[rows, :], 2) - xh * wide(two[rows, :], 2)
                    q = inner * wide(scale_ref[rows, :], 2) * slope_ref[rows, n : n + TILE].astype(F32)
                    q = q.astype(BF)
                    gp[rows, n : n + TILE] = q
                    sums = [sums[0] + d * xh, sums[1] + d, sums[2] + q.astype(F32)]
                for i in range(3):
                    acc[i, :, n : n + TILE] += sums[i]

        row_loop(BODY, grad_rows)
        for i in range(3):
            gsum_ref[0:1, i * HALF : (i + 1) * HALF] = jnp.sum(acc[i], axis=0, keepdims=True)

    return call(
        kernel,
        (sds((ROWS, HALF), BF), sds((1, 3 * HALF), F32)),
        [VM] * 6 + [HB] * count,
        [
            pltpu.VMEM((ROWS, HALF), F32),
            pltpu.VMEM((ROWS, 128), F32),
            pltpu.VMEM((ROWS, 128), F32),
            pltpu.VMEM((3, CHUNK, HALF), F32),
        ],
        3000000000,
        10000000,
        vec,
        gs,
        mm,
        hat,
        slope,
        scale,
        *after,
        room=20,
    )


def in_grads(gp, h, w, gh, after):
    count = len(after)

    def kernel(gp_ref, h_ref, w_ref, gh_ref, *refs):
        gwr, ghb = refs[count:]

        def in_tile(n, carry):
            cols = pl.ds(pl.multiple_of(n * TILE, TILE), TILE)
            ghb[:, cols] = gh_ref[:, cols] + dot(gp_ref[...], w_ref[cols, :], NT)
            gwr[cols, :] = dot(h_ref[:, cols], gp_ref[...], TN).astype(BF)
            return carry

        lax.fori_loop(0, D // TILE, in_tile, 0)

    return call(
        kernel,
        (sds((D, HALF), BF), sds((ROWS, D), F32)),
        [VM] * 4 + [HB] * count,
        [],
        3000000000,
        8000000,
        gp,
        h,
        w,
        gh,
        *after,
        room=14,
    )


def in_backward(table, sides, vec, gsum, gate_sum, gwr, ghb, x, grad_out, half, after):
    count = len(after)

    def kernel(table_ref, sides_ref, vec_ref, gsum_ref, gate_ref, gwr, ghb, x_ref, og_ref, *refs):
        keep, send, up_a, up_b, stay_ref, away_ref, acc, gvec, blocks, pgb = refs[count:]

        def put(name, value):
            start, size = VSEG[name]
            gvec[0:1, start : start + size] = value

        put("g2", gate_ref[0:1, 0:HALF])
        put("b2", gate_ref[0:1, HALF : 2 * HALF])
        put("c1r", gate_ref[0:1, 2 * HALF : 3 * HALF])
        put("c1l", gsum_ref[0:1, 0:HALF])
        put("c2", gsum_ref[0:1, HALF : HALF + D])
        acc[...] = jnp.zeros_like(acc)
        def in_rows(r):
            rows = pl.ds(r, STRIPE)
            xh, scale = norm_parts(x_ref[rows, :].astype(F32))
            d = ghb[rows, :]
            e = d * seg(vec_ref, "g1")
            one = jnp.mean(e, axis=-1, keepdims=True)
            two = jnp.mean(e * xh, axis=-1, keepdims=True)
            pgb[rows, :] = og_ref[rows, :].astype(F32) + scale * (e - one - xh * two)
            acc[0:1, :] += jnp.sum(d * xh, axis=0, keepdims=True)
            acc[1:2, :] += jnp.sum(d, axis=0, keepdims=True)

        row_loop(STRIPE, in_rows)
        put("g1", acc[0:1, :])
        put("b1", acc[1:2, :])
        split_rows(pgb, stay_ref, away_ref, sides_ref[0], pgb[...])
        blocks[...] = jnp.zeros_like(blocks)
        for s in range(DEVS):
            blocks[s, 0:1, 0:VPER] = gvec[0:1, VPER * s : VPER * s + VPER]
        for k in range(DEVS):
            dev = table_ref[k]
            target, first = next((t, f) for t, f in ((up_b, 28), (up_a, 24), (send, GROUPS), (keep, 0)) if k >= f)
            r = pl.ds((k - first) * 16, 16)
            target[r, 0:HALF] = gwr[pl.ds(pl.multiple_of(dev * 16, 16), 16), :]
            target[r, HALF : HALF + VCOLS] = blocks[dev].astype(BF)

    payload = sds((D // 2, HALF + VCOLS), BF)
    part = sds((D // 4, HALF + VCOLS), BF)
    eighth = sds((D // 8, HALF + VCOLS), BF)
    pair = sds((2, half, D), BF)
    return call(
        kernel,
        (payload, part, eighth, eighth, pair, pair),
        [SM] * 2 + [VM] * 7 + [HB] * count,
        [
            pltpu.VMEM((8, D), F32),
            pltpu.VMEM((1, VEC), F32),
            pltpu.VMEM((DEVS, 16, VCOLS), F32),
            pltpu.VMEM((ROWS, D), F32),
        ],
        2000000000,
        6000000,
        table,
        sides,
        vec,
        gsum,
        gate_sum,
        gwr,
        ghb,
        x,
        grad_out,
        *after,
        room=16,
    )


def add_upper(keep, upper, after):
    cols = keep.shape[1]
    size = keep.shape[0] // 2

    def kernel(keep_ref, a_ref, b_ref, *refs):
        for r in range(0, size, 16):
            piece = a_ref if r < size // 2 else b_ref
            value = keep_ref[r : r + 16, :].astype(F32) + piece[r % (size // 2) : r % (size // 2) + 16, :].astype(F32)
            refs[len(after)][r : r + 16, :] = value.astype(BF)

    specs = [pl.BlockSpec((size, cols), lambda i: (1, 0))] + [pl.BlockSpec((size // 2, cols), lambda i: (0, 0))] * 2
    return pl.pallas_call(
        kernel,
        grid=(1,),
        out_shape=sds((size, cols), BF),
        in_specs=specs + [HB] * len(after),
        out_specs=pl.BlockSpec((size, cols), lambda i: (0, 0)),
        compiler_params=pltpu.CompilerParams(vmem_limit_bytes=10 * MIB),
        cost_estimate=pl.CostEstimate(flops=1000000, bytes_accessed=2000000, transcendentals=0),
    )(keep, *upper, *after)


def add_part(terms, size, after, places=None):
    cols = terms[0].shape[1]
    count = len(terms)

    def kernel(*refs):
        for r in range(0, size, 16):
            rows = slice(r, r + 16)
            value = refs[0][rows, :].astype(F32)
            for t in refs[1:count]:
                value = value + t[rows, :].astype(F32)
            refs[count + len(after)][rows, :] = value.astype(BF)

    places = places or [1] * count
    blocks = [pl.BlockSpec((size, cols), lambda i, p=p: (p, 0)) for p in places]
    return pl.pallas_call(
        kernel,
        grid=(1,),
        out_shape=sds((size, cols), BF),
        in_specs=blocks + [HB] * len(after),
        out_specs=pl.BlockSpec((size, cols), lambda i: (0, 0)),
        compiler_params=pltpu.CompilerParams(vmem_limit_bytes=10 * MIB),
        cost_estimate=pl.CostEstimate(flops=1000000, bytes_accessed=3000000, transcendentals=0),
    )(*terms, *after)


def line_parts(terms, after):
    cols = terms[0].shape[1]
    count = len(terms)

    def kernel(*refs):
        own, *outs = refs[count + len(after) :]
        for m in range(4):
            rows = slice(16 * m, 16 * (m + 1))
            value = refs[0][rows, :].astype(F32)
            for t in refs[1:count]:
                value = value + t[rows, :].astype(F32)
            if m == 0:
                own[...] = value
            else:
                outs[m - 1][...] = value.astype(BF)

    block = pl.BlockSpec((64, cols), lambda i: (0, 0))
    one = pl.BlockSpec((16, cols), lambda i: (0, 0))
    return pl.pallas_call(
        kernel,
        grid=(1,),
        out_shape=[sds((16, cols), F32)] + [sds((16, cols), BF)] * 3,
        in_specs=[block] * count + [HB] * len(after),
        out_specs=[one] * 4,
        compiler_params=pltpu.CompilerParams(vmem_limit_bytes=8 * MIB),
        cost_estimate=pl.CostEstimate(flops=1000000, bytes_accessed=3000000, transcendentals=0),
    )(*terms, *after)


def line_turn(terms, flip, after):
    count = len(terms)
    cols = terms[0].shape[1]

    def kernel(*refs):
        outs = refs[count + len(after) :]
        for m in range(4):
            rows = slice(16 * m, 16 * (m + 1))
            value = refs[0][rows, :].astype(F32)
            for t in refs[1:count]:
                value = value + t[rows, :].astype(F32)
            value = value.astype(BF)
            outs[0][rows, :] = value
            if flip:
                at = 16 * (m ^ flip)
                outs[1][at : at + 16, :] = value

    block = pl.BlockSpec((64, cols), lambda i: (0, 0))
    number = 2 if flip else 1
    return pl.pallas_call(
        kernel,
        grid=(1,),
        out_shape=[sds((64, cols), BF)] * number,
        in_specs=[block] * count + [HB] * len(after),
        out_specs=[block] * number,
        compiler_params=pltpu.CompilerParams(vmem_limit_bytes=8 * MIB),
        cost_estimate=pl.CostEstimate(flops=1000000, bytes_accessed=1000000, transcendentals=0),
    )(*terms, *after)


def finish_out(own, got, weight, first, second, after):
    def kernel(own_ref, a_ref, b_ref, c_ref, w_ref, m_ref, s_ref, after_ref, left_ref, nw, nm, ns):
        total = own_ref[...] + a_ref[...].astype(F32)
        total = total + (b_ref[...].astype(F32) + c_ref[...].astype(F32))
        left_ref[...] = total[:, 0:HALF]
        for g in range(3):
            rows = slice(16 * g, 16 * (g + 1))
            grad = total[:, HALF + g * D : HALF + (g + 1) * D]
            new = adamw(w_ref[rows, :], grad, m_ref[rows, :], s_ref[rows, :], DENSE_RATE, DENSE_DECAY)
            nw[rows, :] = new[0]
            nm[rows, :] = new[1]
            ns[rows, :] = new[2]

    same = sds(weight.shape, F32)
    return call(
        kernel,
        (sds((16, HALF), F32), same, same, same),
        [VM] * 7 + [HB],
        [],
        1000000,
        2000000,
        own,
        *got,
        weight,
        first,
        second,
        after,
    )


def finish_in(own, got, left, weight, first, second, after):
    def kernel(own_ref, a_ref, b_ref, c_ref, l_ref, w_ref, m_ref, s_ref, after_ref, nw, nm, ns, vec_ref):
        total = own_ref[...] + a_ref[...].astype(F32)
        total = total + (b_ref[...].astype(F32) + c_ref[...].astype(F32))
        vec_ref[...] = total[0:1, HALF:]
        for cols, grad in ((slice(0, HALF), l_ref[...]), (slice(HALF, FF), total[:, 0:HALF])):
            new = adamw(w_ref[:, cols], grad, m_ref[:, cols], s_ref[:, cols], DENSE_RATE, DENSE_DECAY)
            nw[:, cols] = new[0]
            nm[:, cols] = new[1]
            ns[:, cols] = new[2]

    same = sds(weight.shape, F32)
    return call(
        kernel,
        (same, same, same, sds((1, VCOLS), F32)),
        [VM] * 8 + [HB],
        [],
        1000000,
        2000000,
        own,
        *got,
        left,
        weight,
        first,
        second,
        after,
    )


def spatial_update(order, pieces, spatial, first, second, bias, bias_first, bias_second, after):
    count = len(pieces)
    rows = spatial.shape[1]

    def kernel(order_ref, *refs):
        ins = refs[:count]
        w_ref, m_ref, s_ref, bw, bm, bs = refs[count : count + 6]
        nw, nm, ns, nbw, nbm, nbs, flat = refs[count + 6 + len(after) :]
        k = 0
        for piece in ins:
            for j in range(piece.shape[0] // 16):
                at = pl.multiple_of(order_ref[k] * 32, 32)
                block = piece[16 * j : 16 * j + 16, :].astype(F32)
                flat[pl.ds(at, 16), :] = block[:, 0:SCOLS]
                flat[pl.ds(at + 16, 16), :] = block[:, SCOLS:]
                k += 1
        at = TOTAL_AT // 128 * 128
        totals = flat[:, at : at + 128].T[TOTAL_AT - at : TOTAL_AT - at + 1, :]
        for level in range(3):
            got = flat[level * LSTRIDE : level * LSTRIDE + rows, :]
            new = adamw(w_ref[level], got[:, 0:PMAX], m_ref[level], s_ref[level], DENSE_RATE, DENSE_DECAY)
            nw[level] = new[0]
            nm[level] = new[1]
            ns[level] = new[2]
            got = totals[:, level * LSTRIDE : level * LSTRIDE + rows]
            r = slice(level, level + 1)
            new = adamw(bw[r, :], got, bm[r, :], bs[r, :], SMALL_RATE, 0.0)
            nbw[r, :] = new[0]
            nbm[r, :] = new[1]
            nbs[r, :] = new[2]

    same = sds(spatial.shape, F32)
    small = sds(bias.shape, F32)
    return call(
        kernel,
        (same, same, same, small, small, small),
        [SM] + [VM] * (count + 6) + [HB] * len(after),
        [pltpu.VMEM((512, SCOLS), F32)],
        10000000,
        6000000,
        order,
        *pieces,
        spatial,
        first,
        second,
        bias,
        bias_first,
        bias_second,
        *after,
    )


def in_order(blocks, table, rows):
    cols = blocks[0].shape[1]
    whole = jnp.concatenate(blocks, axis=0).reshape(-1, rows, cols)
    back = jnp.zeros_like(table).at[table].set(jnp.arange(table.shape[0], dtype=table.dtype))
    return jnp.take(whole, back, axis=0)


def local(
    patches,
    resolution,
    out_grad,
    dense_in,
    dense_out,
    vectors,
    spatial,
    spatial_bias,
    in_first,
    in_second,
    out_first,
    out_second,
    vec_first,
    vec_second,
    spat_first,
    spat_second,
    bias_first,
    bias_second,
):
    route = Route(lax.axis_size("dp"))
    ndev = 2 * route.n
    fits = route.n == GROUPS
    seq = lax.axis_index("seq").astype(jnp.int32)
    rows = patches.shape[1]
    table = route.table()
    order = route.order(False)[0]
    in_rows = dense_in.shape[0]
    out_rows = dense_out.shape[0]
    vec_len = vectors.shape[0]
    if fits:
        ktable = table
        korder = table // 2
    else:
        ktable = jnp.arange(DEVS, dtype=jnp.int32)
        korder = jnp.arange(DEVS, dtype=jnp.int32) % GROUPS
    sides = jnp.concatenate([seq[None], korder])
    levels = lax.dynamic_slice_in_dim(resolution, seq * 2, 2, 0)

    right_shard, lo_shard = pack_dense(dense_in, dense_out, vectors.reshape(1, vec_len))
    line = [right_shard] + [route.swap(right_shard, (m, m)) for m in route.direct]
    lo_line = [lo_shard] + [route.swap(lo_shard, (m, m)) for m in route.direct]
    spat_own, x_send, g_send = pack_images(sides, spatial, spatial_bias.reshape(3, rows, 1), patches, out_grad)
    x_got = route.cross(x_send)
    g_got = route.cross(g_send)
    spat_got = route.cross(spat_own)
    if fits:
        right_blocks, passed = route.widen_in_turn(stack(line, []))
        lo_blocks = route.widen_direct(stack(lo_line, [passed]))
    else:
        right_blocks = route.widen(jnp.concatenate(line, axis=0))
        lo_blocks = route.widen(jnp.concatenate(lo_line, axis=0))
    right_blocks = right_blocks + [route.cross(b) for b in right_blocks]
    if not fits:
        lo_blocks = lo_blocks + [route.cross(b) for b in lo_blocks]
    if not fits:
        whole = in_order(right_blocks, table, in_rows)
        all_vec = whole[:, 0, HALF : HALF + vec_len].reshape(DEVS, 1, VPER)
        all_vec = jnp.pad(all_vec, ((0, 0), (0, 15), (0, VCOLS - VPER))).reshape(D, VCOLS)
        right_blocks = [jnp.concatenate([whole[:, :, :HALF].reshape(D, HALF), all_vec], axis=1)]
        whole = in_order(lo_blocks, table, in_rows)
        outs = whole[:, :, HALF:].reshape(ndev, in_rows, 3, D).transpose(0, 2, 1, 3).reshape(DEVS, 3, 16, D)
        outs = outs.transpose(0, 2, 1, 3).reshape(D, HALF)
        lo_blocks = [jnp.concatenate([whole[:, :, :HALF].reshape(D, HALF), outs], axis=1)]

    x, grad_out, h, v, slope, part, weight_right, vec = gate_forward(
        ktable, sides, patches, x_got, out_grad, g_got, right_blocks
    )
    gate, hat, scale, spat, mm = gate_norm(levels, sides, vec, v, part, spat_own, spat_got, [])
    if fits:
        lo_blocks = lo_blocks + [route.cross(lo_blocks[0]), route.cross(stack(lo_blocks[1:], [mm]))]
    gs, gated, q, gb, wl, wo, sp_keep, sp_send, gsum = middle(ktable, levels, sides, vec, h, spat, gate, grad_out, lo_blocks)
    near, far = route.low[-1], route.low[0]
    after = [[] for _ in range(5)]
    if fits:
        sp_got = route.cross(sp_send)
        sp_part = add_part([sp_keep, sp_got], 128, [])
        sp_terms = [sp_keep, sp_got, route.swap(sp_part, near)]
        after[0] = [sp_part]
    gwl, mixed_stay, mixed_away, gh = weight_grads(levels, sides, vec, gated, q, h, wl, wo, x, rows, after[0])
    if fits:
        sp_part = add_part(sp_terms, 64, [gh])
        sp_terms.append(route.swap(sp_part, far))
        after[1] = [sp_part]
    lo_keep, lo_send, lo_up = out_grads(ktable, gated, gb, gwl, after[1])
    mixed_got = route.cross(mixed_away)
    if fits:
        lo_up = route.cross(lo_up)
        lo_terms = [lo_keep, route.cross(lo_send)]
        lo_part = add_part([lo_keep, lo_up], 128, [], [1, 0])
        lo_terms.append(route.swap(lo_part, near))
        after[2] = [lo_part]
    gp, gate_sum = gate_backward(vec, gs, mm, hat, slope, scale, after[2])
    if fits:
        sp_own, sp_out = line_turn(sp_terms, 1, [gate_sum])
        sp_terms = [sp_own, route.swap(sp_out, (route.direct[0],) * 2)]
        after[3] = [sp_own, mixed_got]
    gwr, ghb = in_grads(gp, h, weight_right, gh, after[3])
    if fits:
        sp_own, sp_out = line_turn(sp_terms, 2, [gwr])
        sp_terms = [sp_own, route.swap(sp_out, (route.direct[1],) * 2)]
        lo_part = add_part(lo_terms, 64, [sp_own])
        lo_terms.append(route.swap(lo_part, far))
        after[4] = [lo_part]
    right_keep, right_send, up_a, up_b, grad_stay, grad_away = in_backward(
        ktable, sides, vec, gsum, gate_sum, gwr, ghb, x, grad_out, rows, after[4]
    )
    grad_got = route.cross(grad_away)
    if fits:
        upper = [route.cross(up_a), route.cross(up_b)]
        right_terms = [right_keep, route.cross(right_send)]
        lo_own, *sends = line_parts(lo_terms, [right_keep])
        lo_got = [route.swap(p, (m, m)) for p, m in zip(sends, route.direct)]
        right_part = add_upper(right_keep, upper, [lo_own])
        right_terms.append(route.swap(right_part, near))
        right_part = add_part(right_terms, 64, [grad_got])
        right_terms.append(route.swap(right_part, far))
        (sp_sum,) = line_turn(sp_terms, 0, [right_part])
        spat_pieces = route.widen(sp_sum)
        right_own, *sends = line_parts(right_terms, [sp_sum])
        right_got = [route.swap(p, (m, m)) for p, m in zip(sends, route.direct)]
        left_sum, *new_out = finish_out(lo_own, lo_got, dense_out, out_first, out_second, right_own)
        korder = order
        after = [left_sum]
    else:
        both = jnp.concatenate([lo_keep, lo_send, lo_up])
        outs = both[:, HALF:LO].reshape(DEVS, 16, 3, D).transpose(0, 2, 1, 3).reshape(ndev, out_rows, D)
        outs = jnp.take(outs, table, axis=0).reshape(HALF, D)
        out_sum = route.scatter(outs[: HALF // 2], outs[HALF // 2 :])
        lefts = jnp.take(both[:, :HALF].reshape(ndev, in_rows, HALF), table, axis=0).reshape(D, HALF)
        left_sum = route.scatter(lefts[: D // 2], lefts[D // 2 :])
        per = 512 // route.n

        def spat_blocks(part, flip):
            flat = part.reshape(GROUPS, 16, 2, SCOLS).transpose(0, 2, 1, 3).reshape(route.n, per, SCOLS)
            return jnp.take(flat, route.order(flip)[0], axis=0).reshape(512, SCOLS)

        spat_part = route.scatter(spat_blocks(sp_keep, False), spat_blocks(sp_send, True)).astype(BF)
        flat = in_order(route.spread(spat_part), order, per).reshape(GROUPS, 2, 16, SCOLS)
        spat_pieces = [flat.transpose(0, 2, 1, 3).reshape(GROUPS * 16, SPC)]
        korder = jnp.arange(GROUPS, dtype=jnp.int32)
        after = []
        both = jnp.concatenate([right_keep, right_send, up_a, up_b])
        vecs = jnp.take(both[::16, HALF : HALF + VPER].reshape(ndev, vec_len), table, axis=0)
        vec_sum = route.scatter(vecs[: route.n], vecs[route.n :]).reshape(vec_len)
        rights = jnp.take(both[:, :HALF].reshape(ndev, in_rows, HALF), table, axis=0).reshape(D, HALF)
        right_sum = route.scatter(rights[: D // 2], rights[D // 2 :])
        in_sum = jnp.concatenate([left_sum, right_sum], axis=1)
        new_in = adamw(dense_in, in_sum, in_first, in_second, DENSE_RATE, DENSE_DECAY)
        new_out = adamw(dense_out, out_sum, out_first, out_second, DENSE_RATE, DENSE_DECAY)

    def whole_images(stays, came):
        return jnp.concatenate([jnp.where(seq == 0, stays, came), jnp.where(seq == 0, came, stays)], axis=0)

    mixed = whole_images(mixed_stay, mixed_got)
    patches_grad = whole_images(grad_stay, grad_got)
    spat_new = spatial_update(
        korder, spat_pieces, spatial, spat_first, spat_second, spatial_bias, bias_first, bias_second, after
    )
    if fits:
        *new_in, vec_sum = finish_in(right_own, right_got, left_sum, dense_in, in_first, in_second, spat_new[0])
        vec_sum = vec_sum[0, :vec_len]
    new_vec = adamw(vectors, vec_sum, vec_first, vec_second, SMALL_RATE, 0.0)
    return (mixed, patches_grad) + tuple(new_in) + tuple(new_out) + new_vec + tuple(spat_new)


def solution(mesh):
    rows3 = P("dp", "seq", None)
    dense = P(AXES, None)
    vec = P(AXES)
    spat = P(None, "seq", None)
    bias = P(None, "seq")
    in_specs = (rows3, P("dp"), rows3, dense, dense, vec, spat, bias)
    in_specs += (dense,) * 4 + (vec,) * 2 + (spat,) * 2 + (bias,) * 2
    out_specs = (rows3, rows3) + (dense,) * 6 + (vec,) * 3 + (spat,) * 3 + (bias,) * 3
    return jax.shard_map(local, mesh=mesh, in_specs=in_specs, out_specs=out_specs, check_vma=False)
```

```python
import functools

import jax
import jax.numpy as jnp
from jax import lax
from jax.experimental import pallas as pl
from jax.experimental.pallas import tpu as pltpu
from jax.sharding import PartitionSpec as P

D = 512
FF = 3072
HALF = 1536
PMAX = 324
PPAD = 336
P_MID = 196
P_LOW = 100
VCOLS = 128
VSUB = 120
ROWS = 2 * PPAD
GROUPS = 16
DEVS = 2 * GROUPS
VPER = 240
SCOLS = 384
BIAS_AT = 336
TOTAL_AT = 324
LSTRIDE = 168
MIB = 1024 * 1024
STEP = 10

NORM_EPS = 1e-05
BETA_ONE = 0.9
BETA_TWO = 0.99
ADAM_EPS = 1e-08
DENSE_RATE = 0.02
SMALL_RATE = 0.2
DENSE_DECAY = 0.05

BF = jnp.bfloat16
F32 = jnp.float32
AXES = ("dp", "seq")
VM = pl.BlockSpec(memory_space=pltpu.VMEM)
SM = pl.BlockSpec(memory_space=pltpu.SMEM)
HB = pl.BlockSpec(memory_space=pl.ANY)


class Route:
    def __init__(self, n):
        bits = n.bit_length() - 1
        assert n == 1 << bits and bits >= 2
        self.n = n
        top = n // 4
        self.direct = [top, 2 * top, 3 * top]
        low = [1 << b for b in range(bits - 2)]
        self.low = list(zip(low[::-1], low))
        masks = [(0, 0)] + [(m, m) for m in self.direct]
        for step in self.low:
            masks = masks + [(m[0] ^ step[0], m[1] ^ step[1]) for m in masks]
        self.masks = masks

    def swap(self, block, mask):
        pairs = []
        for dp in range(self.n):
            for seq in range(2):
                pairs.append((dp * 2 + seq, (dp ^ mask[seq]) * 2 + seq))
        return lax.ppermute(block, AXES, pairs)

    def cross(self, block):
        pairs = []
        for dp in range(self.n):
            for seq in range(2):
                pairs.append((dp * 2 + seq, dp * 2 + 1 - seq))
        return lax.ppermute(block, AXES, pairs)

    def order(self, seq_flip):
        place = lax.axis_index("dp")
        seq = lax.axis_index("seq")
        if seq_flip:
            seq = 1 - seq
        zero = jnp.array([m[0] for m in self.masks], jnp.int32)
        one = jnp.array([m[1] for m in self.masks], jnp.int32)
        return place ^ jnp.where(seq == 0, zero, one), seq

    def table(self):
        mine, seq = self.order(False)
        other, flip = self.order(True)
        return jnp.concatenate([mine * 2 + seq, other * 2 + flip])

    def spread(self, shard):
        first = jnp.concatenate([shard] + [self.swap(shard, (m, m)) for m in self.direct], axis=0)
        return self.widen(first)

    def widen(self, first):
        blocks = [first]
        for step in self.low:
            blocks = blocks + [self.swap(b, step) for b in blocks]
        return blocks

    def widen_in_turn(self, first):
        second = self.swap(first, self.low[0])
        third = self.swap(first, self.low[1])
        passed = stack([second], [third])
        return [first, second, third, self.swap(passed, self.low[1])], passed

    def widen_direct(self, first):
        return [first] + [self.swap(first, m) for m in self.plane()]

    def plane(self):
        one, two = self.low
        return [one, two, (one[0] ^ two[0], one[1] ^ two[1])]

    def gather(self, shard):
        blocks = self.spread(shard)
        return blocks + [self.cross(b) for b in blocks]

    def collect(self, terms):
        cur = terms[0].shape[0]
        rows = cur // self.n

        def part(lower, upper):
            total = terms[0][lower:upper].astype(F32)
            for t in terms[1:]:
                total = total + t[lower:upper].astype(F32)
            return total

        terms = list(terms)
        for step in reversed(self.low):
            half = cur // 2
            terms.append(self.swap(part(half, cur).astype(BF), step))
            cur = half
        got = []
        for j, m in enumerate(self.direct):
            got.append(self.swap(part((j + 1) * rows, (j + 2) * rows).astype(BF), (m, m)))
        total = part(0, rows)
        return (total + got[0].astype(F32)) + (got[1].astype(F32) + got[2].astype(F32))

    def scatter(self, keep, send):
        return self.collect([keep, self.cross(send)])


def dot(a, b, dims):
    return lax.dot_general(a, b, (dims, ((), ())), preferred_element_type=F32)


NN = ((1,), (0,))
NT = ((1,), (1,))
TN = ((0,), (0,))


def gelu_parts(p):
    bell = jnp.exp(p * p * -0.5)
    d = 1.0 + jnp.abs(p) * (0.3275911 * 0.7071067811865476)
    t = pl.reciprocal(d, approx=True)
    t = t * (2.0 - d * t)
    poly = t * (
        0.127414796
        + t * (-0.142248368 + t * (0.7107068705 + t * (-0.7265760135 + t * 0.5307027145)))
    )
    tail = poly * bell
    phi_sum = jnp.where(p >= 0.0, 1.0 - tail, tail)
    return p * phi_sum, phi_sum + p * bell * 0.3989422804014327


def count_of(level):
    return jnp.where(level == 0, P_LOW, jnp.where(level == 1, P_MID, PMAX))


def masked_mix(mix, count):
    i = lax.broadcasted_iota(jnp.int32, (PPAD, SCOLS), 0)
    j = lax.broadcasted_iota(jnp.int32, (PPAD, SCOLS), 1)
    return jnp.where((i < count) & (j < count), mix.astype(F32), 0.0).astype(BF)


def live_rows(count, shape, start=0):
    return lax.broadcasted_iota(jnp.int32, shape, 0) + start < count


def live_mask(levels_ref, b, width):
    return live_rows(count_of(levels_ref[b]), (PPAD, width))


def fold(value):
    total = value[:, 0:128]
    for n in range(128, value.shape[1], 128):
        total = total + value[:, n : n + 128]
    return total


def spread_sum(ref, factor):
    return jnp.broadcast_to(jnp.sum(ref[...], axis=-1, keepdims=True) * factor, ref.shape)


def wide(value, times):
    return jnp.concatenate([value] * times, axis=1)


def start_blocks(table_ref, pieces, rows, cols, target, sem, extra=0):
    copies = []
    k = 0
    for piece in pieces:
        for j in range(piece.shape[0] // 16):
            at = pl.multiple_of(table_ref[k] * rows, 16)
            c = pltpu.make_async_copy(
                piece.at[pl.ds(j * 16, 16), pl.ds(cols[0], cols[1])], target.at[pl.ds(at + extra, 16)], sem.at[k]
            )
            c.start()
            copies.append(c)
            k += 1
    return copies


def row_loop(step, body):
    def run(i, carry):
        body(pl.multiple_of(i * step, step))
        return carry

    lax.fori_loop(0, ROWS // step, run, 0)


def call(kernel, out_shape, in_specs, scratch, flops, nbytes, *args, room=12):
    vm = pl.BlockSpec(memory_space=pltpu.VMEM)
    return pl.pallas_call(
        kernel,
        out_shape=out_shape,
        in_specs=in_specs,
        out_specs=jax.tree.map(lambda _: vm, out_shape),
        scratch_shapes=scratch,
        compiler_params=pltpu.CompilerParams(vmem_limit_bytes=room * MIB),
        cost_estimate=pl.CostEstimate(flops=flops, bytes_accessed=nbytes, transcendentals=0),
    )(*args)


def norm_parts(values):
    center = values - jnp.mean(values, axis=-1, keepdims=True)
    scale = lax.rsqrt(jnp.mean(center * center, axis=-1, keepdims=True) + NORM_EPS)
    return center * scale, scale


VSEG = {
    "g1": (0, D),
    "b1": (D, D),
    "c1l": (2 * D, HALF),
    "c1r": (2 * D + HALF, HALF),
    "g2": (2 * D + FF, HALF),
    "b2": (2 * D + FF + HALF, HALF),
    "c2": (2 * D + FF + 2 * HALF, D),
}
VEC = 2 * D + FF + 2 * HALF + D


def seg(ref, name):
    start, size = VSEG[name]
    return ref[0:1, start : start + size]

def adamw(weight, grad, first, second, rate, decay):
    first = BETA_ONE * first + (1.0 - BETA_ONE) * grad
    second = BETA_TWO * second + (1.0 - BETA_TWO) * grad * grad
    first_hat = first / (1.0 - BETA_ONE**STEP)
    second_hat = second / (1.0 - BETA_TWO**STEP)
    weight = weight - rate * (first_hat / (jnp.sqrt(second_hat) + ADAM_EPS) + decay * weight)
    return (weight, first, second)


CHUNK = 16
TILE = 256
BODY = 32
STRIPE = 112
LO = 2 * HALF
SPC = 2 * SCOLS


def sds(shape, dtype):
    return jax.ShapeDtypeStruct(shape, dtype)


def pack_dense(dense_in, dense_out, vec_row):
    rows = dense_in.shape[0]
    per = vec_row.shape[1]

    def kernel(w_hbm, o_hbm, v_hbm, out_ref, lo_ref, w_ref, o_ref, v_ref, row, sem):
        copies = [
            pltpu.make_async_copy(src, dst, sem.at[k])
            for k, (src, dst) in enumerate(((w_hbm, w_ref), (o_hbm, o_ref), (v_hbm, v_ref)))
        ]
        for c in copies:
            c.start()
        row[...] = jnp.zeros_like(row)
        for c in copies:
            c.wait()
        out_ref[:, 0:HALF] = w_ref[:, HALF:].astype(BF)
        for i in range(-(-per // VSUB)):
            size = min(VSUB, per - i * VSUB)
            row[i : i + 1, 0:size] = v_ref[:, i * VSUB : i * VSUB + size]
        out_ref[:, HALF : HALF + VCOLS] = row[...].astype(BF)
        lo_ref[:, 0:HALF] = w_ref[:, 0:HALF].astype(BF)
        for g in range(3):
            lo_ref[:, HALF + g * D : HALF + (g + 1) * D] = o_ref[g * rows : (g + 1) * rows, :].astype(BF)

    scratch = [
        pltpu.VMEM(dense_in.shape, F32),
        pltpu.VMEM(dense_out.shape, F32),
        pltpu.VMEM(vec_row.shape, F32),
        pltpu.VMEM((rows, VCOLS), F32),
        pltpu.SemaphoreType.DMA((3,)),
    ]
    shape = (sds((rows, HALF + VCOLS), BF), sds((rows, LO), BF))
    return call(kernel, shape, [HB] * 3, scratch, 1000, 600000, dense_in, dense_out, vec_row, room=60)


def pack_images(sides, spatial, bias_col, patches, out_grad):
    half = patches.shape[1]

    def kernel(sides_ref, s_ref, b_ref, x_ref, g_ref, spat_ref, xs_ref, gs_ref, buf):
        away = 2 - 2 * sides_ref[0]
        for b in range(2):
            xs_ref[b] = x_ref[away + b]
            gs_ref[b] = g_ref[away + b]
        buf[...] = jnp.zeros_like(buf)
        for level in range(3):
            buf[:, 0:PMAX] = s_ref[level]
            rest = b_ref[level]
            for c in range(3):
                piece = rest.astype(BF).astype(F32)
                buf[:, BIAS_AT + c : BIAS_AT + c + 1] = piece
                rest = rest - piece
            spat_ref[level] = buf[...].astype(BF)

    pair = sds((2, half, D), BF)
    return call(
        kernel,
        (sds((3, half, SCOLS), BF), pair, pair),
        [SM] + [VM] * 4,
        [pltpu.VMEM((half, SCOLS), F32)],
        1000,
        3000000,
        sides,
        spatial,
        bias_col,
        patches,
        out_grad,
    )


def stack(pieces, after):
    count = len(pieces)
    rows, cols = pieces[0].shape

    def kernel(*refs):
        out = refs[count + len(after)]
        for k in range(count):
            out[k * rows : (k + 1) * rows, :] = refs[k][...]

    specs = [VM] * count + [HB] * len(after)
    return call(kernel, sds((count * rows, cols), BF), specs, [], 1000, 1000000, *pieces, *after)


def two_halves(is_first, own, got):
    own = own.astype(F32)
    got = got.astype(F32)
    return jnp.where(is_first, own, got), jnp.where(is_first, got, own)


def gate_norm(levels, sides, vec, v, part, spat_own, spat_got, after):
    half = spat_own.shape[1]
    count = len(after)

    def kernel(levels_ref, sides_ref, vec_ref, v_ref, part_ref, so_ref, sg_ref, *refs):
        gate_ref, hat_ref, scale_ref, spat_ref, mm_ref, mixf, mean, buf = refs[count:]
        is_first = sides_ref[0] == 0
        g_start = VSEG["g2"][0]
        b_start = VSEG["b2"][0]
        mean[...] = spread_sum(part_ref, 1.0 / HALF)

        def square_rows(r):
            for k in range(0, BODY, CHUNK):
                rows = pl.ds(r + k, CHUNK)
                mid = mean[rows, :]
                total = jnp.zeros((CHUNK, 128), F32)
                for n in range(0, HALF, 128):
                    center = v_ref[rows, n : n + 128] - mid
                    total = total + center * center
                buf[rows, :] = total

        row_loop(BODY, square_rows)
        scale_ref[...] = lax.rsqrt(spread_sum(buf, 1.0 / HALF) + NORM_EPS)

        def gate_rows(r):
            for k in range(0, BODY, CHUNK):
                rows = pl.ds(r + k, CHUNK)
                mid = wide(mean[rows, :], 2)
                scale = wide(scale_ref[rows, :], 2)
                for n in range(0, HALF, TILE):
                    hat = (v_ref[rows, n : n + TILE] - mid) * scale
                    hat_ref[rows, n : n + TILE] = hat.astype(BF)
                    gate = hat * vec_ref[0:1, g_start + n : g_start + n + TILE]
                    gate = (gate + vec_ref[0:1, b_start + n : b_start + n + TILE]).astype(BF)
                    gate_ref[rows, n : n + TILE] = gate

        row_loop(BODY, gate_rows)
        gate_ref[ROWS:, :] = jnp.zeros((SCOLS - PPAD, HALF), BF)
        for b in range(2):
            level = levels_ref[b]
            live = count_of(level)
            one, two = two_halves(is_first, so_ref[level], sg_ref[level])
            mixf[0:half, :] = one
            mixf[half : 2 * half, :] = two
            mixf[2 * half :, :] = jnp.zeros((PPAD - 2 * half, SCOLS), F32)
            bias = jnp.sum(mixf[:, TOTAL_AT:], axis=-1, keepdims=True)
            mm_ref[b] = masked_mix(mixf[...], live)

            def mix_tile(n, carry):
                cols = pl.ds(pl.multiple_of(n * 512, 512), 512)
                got = dot(mm_ref[b], gate_ref[b * PPAD : b * PPAD + SCOLS, cols], NN) + bias
                got = jnp.where(live_rows(live, (PPAD, 512)), got, 0.0)
                spat_ref[b * PPAD : (b + 1) * PPAD, cols] = got.astype(BF)
                return carry

            lax.fori_loop(0, HALF // 512, mix_tile, 0)

    return call(
        kernel,
        (
            sds((ROWS + SCOLS - PPAD, HALF), BF),
            sds((ROWS, HALF), BF),
            sds((ROWS, 128), F32),
            sds((ROWS, HALF), BF),
            sds((2, PPAD, SCOLS), BF),
        ),
        [SM] * 2 + [VM] * 5 + [HB] * count,
        [pltpu.VMEM((PPAD, SCOLS), F32), pltpu.VMEM((ROWS, 128), F32), pltpu.VMEM((ROWS, 128), F32)],
        6000000000,
        12000000,
        levels,
        sides,
        vec,
        v,
        part,
        spat_own,
        spat_got,
        *after,
        room=22,
    )


def gate_forward(table, sides, patches, x_got, out_grad, g_got, pieces):
    count = len(pieces)
    half = patches.shape[1]

    def kernel(table_ref, sides_ref, p_ref, xg_ref, o_ref, gg_ref, *refs):
        ins = refs[:count]
        outs = refs[count : count + 8]
        x_ref, og_ref, h_ref, pre, slope_ref, part, w_ref, vec_ref = outs
        vblk, xbuf, sem, vsem = refs[count + 8 :]
        vcopies = start_blocks(table_ref, ins, 16, (HALF, VCOLS), vblk, vsem)
        copies = start_blocks(table_ref, ins, 16, (0, HALF), w_ref, sem)
        me = sides_ref[0]
        is_first = me == 0

        for src, got, target in ((o_ref, gg_ref, og_ref), (p_ref, xg_ref, x_ref)):
            for b in range(2):
                one, two = two_halves(is_first, src[2 * me + b], got[b])
                xbuf[b * PPAD : b * PPAD + half, :] = one
                xbuf[b * PPAD + half : b * PPAD + 2 * half, :] = two
                xbuf[b * PPAD + 2 * half : (b + 1) * PPAD, :] = jnp.zeros((PPAD - 2 * half, D), F32)
            target[...] = xbuf[...].astype(BF)
        for c in vcopies:
            c.wait()
        for s in range(DEVS):
            rows = vblk[16 * s : 16 * s + 16, :].astype(F32)
            for i in range(VPER // VSUB):
                at = VPER * s + VSUB * i
                vec_ref[0:1, at : at + VSUB] = rows[i : i + 1, :VSUB]

        def norm_one(r):
            hat, _ = norm_parts(xbuf[pl.ds(r, STRIPE), :])
            h_ref[pl.ds(r, STRIPE), :] = (hat * seg(vec_ref, "g1") + seg(vec_ref, "b1")).astype(BF)

        row_loop(STRIPE, norm_one)
        for c in copies:
            c.wait()
        c_start = VSEG["c1r"][0]

        def matmul(n, carry):
            at = pl.multiple_of(n * TILE, TILE)
            pre[:, pl.ds(at, TILE)] = dot(h_ref[...], w_ref[:, pl.ds(at, TILE)], NN)
            return carry

        lax.fori_loop(0, HALF // TILE, matmul, 0)

        def gelu_rows(r):
            for k in range(0, BODY, CHUNK):
                rows = pl.ds(r + k, CHUNK)
                total = jnp.zeros((CHUNK, 128), F32)
                for n in range(0, HALF, TILE):
                    v, slope = gelu_parts(pre[rows, n : n + TILE] + vec_ref[0:1, c_start + n : c_start + n + TILE])
                    pre[rows, n : n + TILE] = v
                    slope_ref[rows, n : n + TILE] = slope.astype(BF)
                    total = total + fold(v)
                part[rows, :] = total

        row_loop(BODY, gelu_rows)

    broad = sds((ROWS, HALF), BF)
    narrow = sds((ROWS, D), BF)
    out_shape = (
        narrow,
        narrow,
        narrow,
        sds((ROWS, HALF), F32),
        broad,
        sds((ROWS, 128), F32),
        sds((D, HALF), BF),
        sds((1, VEC), F32),
    )
    scratch = [
        pltpu.VMEM((D, VCOLS), BF),
        pltpu.VMEM((ROWS, D), F32),
        pltpu.SemaphoreType.DMA((DEVS,)),
        pltpu.SemaphoreType.DMA((DEVS,)),
    ]
    return call(
        kernel,
        out_shape,
        [SM] * 2 + [VM] * 4 + [HB] * count,
        scratch,
        10000000000,
        20000000,
        table,
        sides,
        patches,
        x_got,
        out_grad,
        g_got,
        *pieces,
        room=26,
    )


def split_rows(target, first, second, seq, value):
    half = first.shape[1]
    target[...] = value
    for b in range(2):
        one = target[b * PPAD : b * PPAD + half, :]
        two = target[b * PPAD + half : b * PPAD + 2 * half, :]
        first[b] = jnp.where(seq == 0, one, two).astype(BF)
        second[b] = jnp.where(seq == 0, two, one).astype(BF)


def middle(table, levels, sides, vec, h, spat, gate, grad_out, pieces):
    count = len(pieces)

    def kernel(table_ref, levels_ref, sides_ref, vec_ref, h_ref, spat_ref, gate_ref, og_ref, *refs):
        ins = refs[:count]
        gs_ref, gated_ref, q_ref, gb, wl, wo, keep, send, gsum_ref = refs[count : count + 9]
        pbuf, gbuf, cells, flat, sem = refs[count + 9 :]
        copies = start_blocks(table_ref, ins, 16, (0, HALF), wl, sem.at[0])
        for g in range(3):
            copies += start_blocks(table_ref, ins, 48, (HALF + g * D, D), wo, sem.at[1 + g], 16 * g)
        for b in range(2):
            rows = slice(b * PPAD, (b + 1) * PPAD)
            gb[rows, :] = jnp.where(live_mask(levels_ref, b, D), og_ref[rows, :].astype(F32), 0.0).astype(BF)
        gsum_ref[0:1, HALF : HALF + D] = jnp.sum(gb[...].astype(F32), axis=0, keepdims=True)
        cells[...] = jnp.zeros_like(cells)
        flat[...] = jnp.zeros_like(flat)
        for c in copies:
            c.wait()
        c_start = VSEG["c1l"][0]

        def tile(n, carry):
            at = pl.multiple_of(n * TILE, TILE)
            cols = pl.ds(at, TILE)
            pbuf[...] = dot(h_ref[...], wl[:, cols], NN)
            gbuf[...] = dot(gb[...], wo[cols, :], NT)
            shift = vec_ref[0:1, pl.ds(c_start + at, TILE)]
            total = jnp.zeros((CHUNK, TILE), F32)
            for k in range(0, ROWS, CHUNK):
                r = slice(k, k + CHUNK)
                u, slope = gelu_parts(pbuf[r, :] + shift)
                sp = spat_ref[r, cols].astype(F32)
                gg = gbuf[r, :]
                gated_ref[r, cols] = (u * sp).astype(BF)
                gs_ref[r, cols] = (gg * u).astype(BF)
                q = (gg * sp * slope).astype(BF)
                q_ref[r, cols] = q
                total = total + q.astype(F32)
            gsum_ref[0:1, cols] = jnp.sum(total, axis=0, keepdims=True)
            return carry

        lax.fori_loop(0, HALF // TILE, tile, 0)

        me = sides_ref[0]
        for b in range(2):
            level = levels_ref[b]
            count_b = count_of(level)
            gs = gs_ref[b * PPAD : (b + 1) * PPAD, :]
            got = dot(gs, gate_ref[b * PPAD : (b + 1) * PPAD, :], NT)
            sums = jnp.sum(gs.astype(F32), axis=-1, keepdims=True)
            j = lax.broadcasted_iota(jnp.int32, (PPAD, PPAD), 1)
            got = jnp.where(j < count_b, got, jnp.where(j == TOTAL_AT, sums, 0.0))
            cells[level, :, 0:PPAD] += got
        part = PMAX // 2
        for level in range(3):
            for k in range(2):
                flat[k, level * LSTRIDE : level * LSTRIDE + part, 0:PPAD] = cells[level, k * part : (k + 1) * part, 0:PPAD]
        for k in range(DEVS):
            target, side = (keep, me) if k < GROUPS else (send, 1 - me)
            r = pl.ds(k % GROUPS * 16, 16)
            block = flat[side, pl.ds(pl.multiple_of(sides_ref[1 + k] * 32, 32), 32), :].astype(BF)
            target[r, 0:SCOLS] = block[0:16]
            target[r, SCOLS:SPC] = block[16:32]

    broad = sds((ROWS, HALF), BF)
    payload = sds((D // 2, SPC), BF)
    out_shape = (
        broad,
        broad,
        broad,
        sds((ROWS, D), BF),
        sds((D, HALF), BF),
        sds((HALF, D), BF),
        payload,
        payload,
        sds((1, HALF + D), F32),
    )
    scratch = [
        pltpu.VMEM((ROWS, TILE), F32),
        pltpu.VMEM((ROWS, TILE), F32),
        pltpu.VMEM((3, PPAD, SCOLS), F32),
        pltpu.VMEM((2, 512, SCOLS), F32),
        pltpu.SemaphoreType.DMA((4, DEVS)),
    ]
    return call(
        kernel,
        out_shape,
        [SM] * 3 + [VM] * 5 + [HB] * count,
        scratch,
        8000000000,
        16000000,
        table,
        levels,
        sides,
        vec,
        h,
        spat,
        gate,
        grad_out,
        *pieces,
        room=28,
    )


def weight_grads(levels, sides, vec, gated, q, h, wl, wo, x, half, after):
    count = len(after)

    def kernel(levels_ref, sides_ref, vec_ref, t_ref, q_ref, h_ref, wl_ref, wo_ref, x_ref, *refs):
        gwl, stay_ref, away_ref, gh_ref, branch = refs[count:]

        def in_tile(n, carry):
            cols = pl.ds(pl.multiple_of(n * TILE, TILE), TILE)
            gwl[cols, :] = dot(h_ref[:, cols], q_ref[...], TN).astype(BF)
            branch[:, cols] = dot(t_ref[...], wo_ref[:, cols], NN)
            gh_ref[:, cols] = dot(q_ref[...], wl_ref[cols, :], NT)
            return carry

        lax.fori_loop(0, D // TILE, in_tile, 0)
        me = sides_ref[0]
        live = jnp.concatenate([live_mask(levels_ref, b, D) for b in range(2)], axis=0)
        out = branch[...] + seg(vec_ref, "c2")
        split_rows(branch, stay_ref, away_ref, me, x_ref[...].astype(F32) + jnp.where(live, out, 0.0))

    pair = sds((2, half, D), BF)
    return call(
        kernel,
        (sds((D, HALF), BF), pair, pair, sds((ROWS, D), F32)),
        [SM] * 2 + [VM] * 7 + [HB] * count,
        [pltpu.VMEM((ROWS, D), F32)],
        4000000000,
        12000000,
        levels,
        sides,
        vec,
        gated,
        q,
        h,
        wl,
        wo,
        x,
        *after,
        room=12,
    )


def out_grads(table, gated, gb, gwl, after):
    count = len(after)

    def kernel(table_ref, t_ref, gb_ref, gwl_ref, *refs):
        keep, send, send_up, gwo = refs[count:]

        def out_tile(n, carry):
            cols = pl.ds(pl.multiple_of(n * TILE, TILE), TILE)
            gwo[cols, :] = dot(t_ref[:, cols], gb_ref[...], TN).astype(BF)
            return carry

        lax.fori_loop(0, HALF // TILE, out_tile, 0)
        for k in range(DEVS):
            dev = table_ref[k]
            target = keep if k < GROUPS else send if k < GROUPS * 3 // 2 else send_up
            r = pl.ds(k % (GROUPS if k < GROUPS else GROUPS // 2) * 16, 16)
            target[r, 0:HALF] = gwl_ref[pl.ds(pl.multiple_of(dev * 16, 16), 16), :]
            for g in range(3):
                target[r, HALF + g * D : HALF + (g + 1) * D] = gwo[pl.ds(pl.multiple_of(dev * 48 + 16 * g, 16), 16), :]

    payload = sds((D // 2, LO), BF)
    part = sds((D // 4, LO), BF)
    return call(
        kernel,
        (payload, part, part),
        [SM] + [VM] * 3 + [HB] * count,
        [pltpu.VMEM((HALF, D), BF)],
        2000000000,
        8000000,
        table,
        gated,
        gb,
        gwl,
        *after,
        room=10,
    )


def gate_backward(vec, gs, mm, hat, slope, scale, after):
    count = len(after)

    def kernel(vec_ref, gs_ref, mm_ref, hat_ref, slope_ref, scale_ref, *refs):
        gp, gsum_ref, dbuf, one, two, acc = refs[count:]

        for b in range(2):

            def mix_tile(n, carry):
                cols = pl.ds(pl.multiple_of(n * 512, 512), 512)
                got = dot(mm_ref[b], gs_ref[b * PPAD : (b + 1) * PPAD, cols], TN)
                dbuf[b * PPAD : (b + 1) * PPAD, cols] = got[0:PPAD]
                return carry

            lax.fori_loop(0, HALF // 512, mix_tile, 0)
        g_start = VSEG["g2"][0]

        def sum_rows(r):
            for k in range(0, BODY, CHUNK):
                rows = pl.ds(r + k, CHUNK)
                a = jnp.zeros((CHUNK, 128), F32)
                c = jnp.zeros((CHUNK, 128), F32)
                for n in range(0, HALF, TILE):
                    e = dbuf[rows, n : n + TILE] * vec_ref[0:1, g_start + n : g_start + n + TILE]
                    a = a + fold(e)
                    c = c + fold(e * hat_ref[rows, n : n + TILE].astype(F32))
                one[rows, :] = a
                two[rows, :] = c

        row_loop(BODY, sum_rows)
        one[...] = spread_sum(one, 1.0 / HALF)
        two[...] = spread_sum(two, 1.0 / HALF)
        acc[...] = jnp.zeros_like(acc)

        def grad_rows(r):
            for n in range(0, HALF, TILE):
                gain = vec_ref[0:1, g_start + n : g_start + n + TILE]
                sums = [jnp.zeros((CHUNK, TILE), F32) for _ in range(3)]
                for k in range(0, BODY, CHUNK):
                    rows = pl.ds(r + k, CHUNK)
                    d = dbuf[rows, n : n + TILE]
                    xh = hat_ref[rows, n : n + TILE].astype(F32)
                    inner = d * gain - wide(one[rows, :], 2) - xh * wide(two[rows, :], 2)
                    q = inner * wide(scale_ref[rows, :], 2) * slope_ref[rows, n : n + TILE].astype(F32)
                    q = q.astype(BF)
                    gp[rows, n : n + TILE] = q
                    sums = [sums[0] + d * xh, sums[1] + d, sums[2] + q.astype(F32)]
                for i in range(3):
                    acc[i, :, n : n + TILE] += sums[i]

        row_loop(BODY, grad_rows)
        for i in range(3):
            gsum_ref[0:1, i * HALF : (i + 1) * HALF] = jnp.sum(acc[i], axis=0, keepdims=True)

    return call(
        kernel,
        (sds((ROWS, HALF), BF), sds((1, 3 * HALF), F32)),
        [VM] * 6 + [HB] * count,
        [
            pltpu.VMEM((ROWS, HALF), F32),
            pltpu.VMEM((ROWS, 128), F32),
            pltpu.VMEM((ROWS, 128), F32),
            pltpu.VMEM((3, CHUNK, HALF), F32),
        ],
        3000000000,
        10000000,
        vec,
        gs,
        mm,
        hat,
        slope,
        scale,
        *after,
        room=20,
    )


def in_grads(gp, h, w, gh, after):
    count = len(after)

    def kernel(gp_ref, h_ref, w_ref, gh_ref, *refs):
        gwr, ghb = refs[count:]

        def in_tile(n, carry):
            cols = pl.ds(pl.multiple_of(n * TILE, TILE), TILE)
            ghb[:, cols] = gh_ref[:, cols] + dot(gp_ref[...], w_ref[cols, :], NT)
            gwr[cols, :] = dot(h_ref[:, cols], gp_ref[...], TN).astype(BF)
            return carry

        lax.fori_loop(0, D // TILE, in_tile, 0)

    return call(
        kernel,
        (sds((D, HALF), BF), sds((ROWS, D), F32)),
        [VM] * 4 + [HB] * count,
        [],
        3000000000,
        8000000,
        gp,
        h,
        w,
        gh,
        *after,
        room=14,
    )


def in_backward(table, sides, vec, gsum, gate_sum, gwr, ghb, x, grad_out, half, after):
    count = len(after)

    def kernel(table_ref, sides_ref, vec_ref, gsum_ref, gate_ref, gwr, ghb, x_ref, og_ref, *refs):
        keep, send, up_a, up_b, stay_ref, away_ref, acc, gvec, blocks, pgb = refs[count:]

        def put(name, value):
            start, size = VSEG[name]
            gvec[0:1, start : start + size] = value

        put("g2", gate_ref[0:1, 0:HALF])
        put("b2", gate_ref[0:1, HALF : 2 * HALF])
        put("c1r", gate_ref[0:1, 2 * HALF : 3 * HALF])
        put("c1l", gsum_ref[0:1, 0:HALF])
        put("c2", gsum_ref[0:1, HALF : HALF + D])
        acc[...] = jnp.zeros_like(acc)
        def in_rows(r):
            rows = pl.ds(r, STRIPE)
            xh, scale = norm_parts(x_ref[rows, :].astype(F32))
            d = ghb[rows, :]
            e = d * seg(vec_ref, "g1")
            one = jnp.mean(e, axis=-1, keepdims=True)
            two = jnp.mean(e * xh, axis=-1, keepdims=True)
            pgb[rows, :] = og_ref[rows, :].astype(F32) + scale * (e - one - xh * two)
            acc[0:1, :] += jnp.sum(d * xh, axis=0, keepdims=True)
            acc[1:2, :] += jnp.sum(d, axis=0, keepdims=True)

        row_loop(STRIPE, in_rows)
        put("g1", acc[0:1, :])
        put("b1", acc[1:2, :])
        split_rows(pgb, stay_ref, away_ref, sides_ref[0], pgb[...])
        blocks[...] = jnp.zeros_like(blocks)
        for s in range(DEVS):
            for i in range(VPER // VSUB):
                at = VPER * s + VSUB * i
                blocks[s, i : i + 1, 0:VSUB] = gvec[0:1, at : at + VSUB]
        for k in range(DEVS):
            dev = table_ref[k]
            target, first = next((t, f) for t, f in ((up_b, 28), (up_a, 24), (send, GROUPS), (keep, 0)) if k >= f)
            r = pl.ds((k - first) * 16, 16)
            target[r, 0:HALF] = gwr[pl.ds(pl.multiple_of(dev * 16, 16), 16), :]
            target[r, HALF : HALF + VCOLS] = blocks[dev].astype(BF)

    payload = sds((D // 2, HALF + VCOLS), BF)
    part = sds((D // 4, HALF + VCOLS), BF)
    eighth = sds((D // 8, HALF + VCOLS), BF)
    pair = sds((2, half, D), BF)
    return call(
        kernel,
        (payload, part, eighth, eighth, pair, pair),
        [SM] * 2 + [VM] * 7 + [HB] * count,
        [
            pltpu.VMEM((8, D), F32),
            pltpu.VMEM((1, VEC), F32),
            pltpu.VMEM((DEVS, 16, VCOLS), F32),
            pltpu.VMEM((ROWS, D), F32),
        ],
        2000000000,
        6000000,
        table,
        sides,
        vec,
        gsum,
        gate_sum,
        gwr,
        ghb,
        x,
        grad_out,
        *after,
        room=16,
    )


def add_upper(keep, upper, after):
    cols = keep.shape[1]
    size = keep.shape[0] // 2

    def kernel(keep_ref, a_ref, b_ref, *refs):
        for r in range(0, size, 16):
            piece = a_ref if r < size // 2 else b_ref
            value = keep_ref[r : r + 16, :].astype(F32) + piece[r % (size // 2) : r % (size // 2) + 16, :].astype(F32)
            refs[len(after)][r : r + 16, :] = value.astype(BF)

    specs = [pl.BlockSpec((size, cols), lambda i: (1, 0))] + [pl.BlockSpec((size // 2, cols), lambda i: (0, 0))] * 2
    return pl.pallas_call(
        kernel,
        grid=(1,),
        out_shape=sds((size, cols), BF),
        in_specs=specs + [HB] * len(after),
        out_specs=pl.BlockSpec((size, cols), lambda i: (0, 0)),
        compiler_params=pltpu.CompilerParams(vmem_limit_bytes=10 * MIB),
        cost_estimate=pl.CostEstimate(flops=1000000, bytes_accessed=2000000, transcendentals=0),
    )(keep, *upper, *after)


def add_part(terms, size, after, places=None):
    cols = terms[0].shape[1]
    count = len(terms)

    def kernel(*refs):
        for r in range(0, size, 16):
            rows = slice(r, r + 16)
            value = refs[0][rows, :].astype(F32)
            for t in refs[1:count]:
                value = value + t[rows, :].astype(F32)
            refs[count + len(after)][rows, :] = value.astype(BF)

    places = places or [1] * count
    blocks = [pl.BlockSpec((size, cols), lambda i, p=p: (p, 0)) for p in places]
    return pl.pallas_call(
        kernel,
        grid=(1,),
        out_shape=sds((size, cols), BF),
        in_specs=blocks + [HB] * len(after),
        out_specs=pl.BlockSpec((size, cols), lambda i: (0, 0)),
        compiler_params=pltpu.CompilerParams(vmem_limit_bytes=10 * MIB),
        cost_estimate=pl.CostEstimate(flops=1000000, bytes_accessed=3000000, transcendentals=0),
    )(*terms, *after)


def line_parts(terms, after):
    cols = terms[0].shape[1]
    count = len(terms)

    def kernel(*refs):
        own, *outs = refs[count + len(after) :]
        for m in range(4):
            rows = slice(16 * m, 16 * (m + 1))
            value = refs[0][rows, :].astype(F32)
            for t in refs[1:count]:
                value = value + t[rows, :].astype(F32)
            if m == 0:
                own[...] = value
            else:
                outs[m - 1][...] = value.astype(BF)

    block = pl.BlockSpec((64, cols), lambda i: (0, 0))
    one = pl.BlockSpec((16, cols), lambda i: (0, 0))
    return pl.pallas_call(
        kernel,
        grid=(1,),
        out_shape=[sds((16, cols), F32)] + [sds((16, cols), BF)] * 3,
        in_specs=[block] * count + [HB] * len(after),
        out_specs=[one] * 4,
        compiler_params=pltpu.CompilerParams(vmem_limit_bytes=8 * MIB),
        cost_estimate=pl.CostEstimate(flops=1000000, bytes_accessed=3000000, transcendentals=0),
    )(*terms, *after)


def line_turn(terms, flip, after):
    count = len(terms)
    cols = terms[0].shape[1]

    def kernel(*refs):
        outs = refs[count + len(after) :]
        for m in range(4):
            rows = slice(16 * m, 16 * (m + 1))
            value = refs[0][rows, :].astype(F32)
            for t in refs[1:count]:
                value = value + t[rows, :].astype(F32)
            value = value.astype(BF)
            outs[0][rows, :] = value
            if flip:
                at = 16 * (m ^ flip)
                outs[1][at : at + 16, :] = value

    block = pl.BlockSpec((64, cols), lambda i: (0, 0))
    number = 2 if flip else 1
    return pl.pallas_call(
        kernel,
        grid=(1,),
        out_shape=[sds((64, cols), BF)] * number,
        in_specs=[block] * count + [HB] * len(after),
        out_specs=[block] * number,
        compiler_params=pltpu.CompilerParams(vmem_limit_bytes=8 * MIB),
        cost_estimate=pl.CostEstimate(flops=1000000, bytes_accessed=1000000, transcendentals=0),
    )(*terms, *after)


def finish_out(own, got, weight, first, second, after):
    def kernel(own_ref, a_ref, b_ref, c_ref, w_ref, m_ref, s_ref, after_ref, left_ref, nw, nm, ns):
        total = own_ref[...] + a_ref[...].astype(F32)
        total = total + (b_ref[...].astype(F32) + c_ref[...].astype(F32))
        left_ref[...] = total[:, 0:HALF]
        for g in range(3):
            rows = slice(16 * g, 16 * (g + 1))
            grad = total[:, HALF + g * D : HALF + (g + 1) * D]
            new = adamw(w_ref[rows, :], grad, m_ref[rows, :], s_ref[rows, :], DENSE_RATE, DENSE_DECAY)
            nw[rows, :] = new[0]
            nm[rows, :] = new[1]
            ns[rows, :] = new[2]

    same = sds(weight.shape, F32)
    return call(
        kernel,
        (sds((16, HALF), F32), same, same, same),
        [VM] * 7 + [HB],
        [],
        1000000,
        2000000,
        own,
        *got,
        weight,
        first,
        second,
        after,
    )


def finish_in(own, got, left, weight, first, second, after):
    def kernel(own_ref, a_ref, b_ref, c_ref, l_ref, w_ref, m_ref, s_ref, after_ref, nw, nm, ns, vec_ref):
        total = own_ref[...] + a_ref[...].astype(F32)
        total = total + (b_ref[...].astype(F32) + c_ref[...].astype(F32))
        for i in range(VPER // VSUB):
            vec_ref[0:1, i * VSUB : (i + 1) * VSUB] = total[i : i + 1, HALF : HALF + VSUB]
        for cols, grad in ((slice(0, HALF), l_ref[...]), (slice(HALF, FF), total[:, 0:HALF])):
            new = adamw(w_ref[:, cols], grad, m_ref[:, cols], s_ref[:, cols], DENSE_RATE, DENSE_DECAY)
            nw[:, cols] = new[0]
            nm[:, cols] = new[1]
            ns[:, cols] = new[2]

    same = sds(weight.shape, F32)
    return call(
        kernel,
        (same, same, same, sds((1, VPER), F32)),
        [VM] * 8 + [HB],
        [],
        1000000,
        2000000,
        own,
        *got,
        left,
        weight,
        first,
        second,
        after,
    )


def spatial_update(order, pieces, spatial, first, second, bias, bias_first, bias_second, after):
    count = len(pieces)
    rows = spatial.shape[1]

    def kernel(order_ref, *refs):
        ins = refs[:count]
        w_ref, m_ref, s_ref, bw, bm, bs = refs[count : count + 6]
        nw, nm, ns, nbw, nbm, nbs, flat = refs[count + 6 + len(after) :]
        k = 0
        for piece in ins:
            for j in range(piece.shape[0] // 16):
                at = pl.multiple_of(order_ref[k] * 32, 32)
                block = piece[16 * j : 16 * j + 16, :].astype(F32)
                flat[pl.ds(at, 16), :] = block[:, 0:SCOLS]
                flat[pl.ds(at + 16, 16), :] = block[:, SCOLS:]
                k += 1
        at = TOTAL_AT // 128 * 128
        totals = flat[:, at : at + 128].T[TOTAL_AT - at : TOTAL_AT - at + 1, :]
        for level in range(3):
            got = flat[level * LSTRIDE : level * LSTRIDE + rows, :]
            new = adamw(w_ref[level], got[:, 0:PMAX], m_ref[level], s_ref[level], DENSE_RATE, DENSE_DECAY)
            nw[level] = new[0]
            nm[level] = new[1]
            ns[level] = new[2]
            got = totals[:, level * LSTRIDE : level * LSTRIDE + rows]
            r = slice(level, level + 1)
            new = adamw(bw[r, :], got, bm[r, :], bs[r, :], SMALL_RATE, 0.0)
            nbw[r, :] = new[0]
            nbm[r, :] = new[1]
            nbs[r, :] = new[2]

    same = sds(spatial.shape, F32)
    small = sds(bias.shape, F32)
    return call(
        kernel,
        (same, same, same, small, small, small),
        [SM] + [VM] * (count + 6) + [HB] * len(after),
        [pltpu.VMEM((512, SCOLS), F32)],
        10000000,
        6000000,
        order,
        *pieces,
        spatial,
        first,
        second,
        bias,
        bias_first,
        bias_second,
        *after,
    )


def in_order(blocks, table, rows):
    cols = blocks[0].shape[1]
    whole = jnp.concatenate(blocks, axis=0).reshape(-1, rows, cols)
    back = jnp.zeros_like(table).at[table].set(jnp.arange(table.shape[0], dtype=table.dtype))
    return jnp.take(whole, back, axis=0)


def local(
    patches,
    resolution,
    out_grad,
    dense_in,
    dense_out,
    vectors,
    spatial,
    spatial_bias,
    in_first,
    in_second,
    out_first,
    out_second,
    vec_first,
    vec_second,
    spat_first,
    spat_second,
    bias_first,
    bias_second,
):
    route = Route(lax.axis_size("dp"))
    ndev = 2 * route.n
    fits = route.n == GROUPS
    seq = lax.axis_index("seq").astype(jnp.int32)
    rows = patches.shape[1]
    table = route.table()
    order = route.order(False)[0]
    in_rows = dense_in.shape[0]
    out_rows = dense_out.shape[0]
    vec_len = vectors.shape[0]
    if fits:
        ktable = table
        korder = table // 2
    else:
        ktable = jnp.arange(DEVS, dtype=jnp.int32)
        korder = jnp.arange(DEVS, dtype=jnp.int32) % GROUPS
    sides = jnp.concatenate([seq[None], korder])
    levels = lax.dynamic_slice_in_dim(resolution, seq * 2, 2, 0)

    right_shard, lo_shard = pack_dense(dense_in, dense_out, vectors.reshape(1, vec_len))
    line = [right_shard] + [route.swap(right_shard, (m, m)) for m in route.direct]
    lo_line = [lo_shard] + [route.swap(lo_shard, (m, m)) for m in route.direct]
    spat_own, x_send, g_send = pack_images(sides, spatial, spatial_bias.reshape(3, rows, 1), patches, out_grad)
    x_got = route.cross(x_send)
    g_got = route.cross(g_send)
    spat_got = route.cross(spat_own)
    if fits:
        right_blocks, passed = route.widen_in_turn(stack(line, []))
        lo_blocks = route.widen_direct(stack(lo_line, [passed]))
    else:
        right_blocks = route.widen(jnp.concatenate(line, axis=0))
        lo_blocks = route.widen(jnp.concatenate(lo_line, axis=0))
    right_blocks = right_blocks + [route.cross(b) for b in right_blocks]
    if not fits:
        lo_blocks = lo_blocks + [route.cross(b) for b in lo_blocks]
    if not fits:
        whole = in_order(right_blocks, table, in_rows)
        all_vec = whole[:, 0, HALF : HALF + vec_len].reshape(DEVS, VPER // VSUB, VSUB)
        all_vec = jnp.pad(all_vec, ((0, 0), (0, 16 - VPER // VSUB), (0, VCOLS - VSUB))).reshape(D, VCOLS)
        right_blocks = [jnp.concatenate([whole[:, :, :HALF].reshape(D, HALF), all_vec], axis=1)]
        whole = in_order(lo_blocks, table, in_rows)
        outs = whole[:, :, HALF:].reshape(ndev, in_rows, 3, D).transpose(0, 2, 1, 3).reshape(DEVS, 3, 16, D)
        outs = outs.transpose(0, 2, 1, 3).reshape(D, HALF)
        lo_blocks = [jnp.concatenate([whole[:, :, :HALF].reshape(D, HALF), outs], axis=1)]

    x, grad_out, h, v, slope, part, weight_right, vec = gate_forward(
        ktable, sides, patches, x_got, out_grad, g_got, right_blocks
    )
    gate, hat, scale, spat, mm = gate_norm(levels, sides, vec, v, part, spat_own, spat_got, [])
    if fits:
        lo_blocks = lo_blocks + [route.cross(lo_blocks[0]), route.cross(stack(lo_blocks[1:], [mm]))]
    gs, gated, q, gb, wl, wo, sp_keep, sp_send, gsum = middle(ktable, levels, sides, vec, h, spat, gate, grad_out, lo_blocks)
    near, far = route.low[-1], route.low[0]
    after = [[] for _ in range(5)]
    if fits:
        sp_got = route.cross(sp_send)
        sp_part = add_part([sp_keep, sp_got], 128, [])
        sp_terms = [sp_keep, sp_got, route.swap(sp_part, near)]
        after[0] = [sp_part]
    gwl, mixed_stay, mixed_away, gh = weight_grads(levels, sides, vec, gated, q, h, wl, wo, x, rows, after[0])
    if fits:
        sp_part = add_part(sp_terms, 64, [gh])
        sp_terms.append(route.swap(sp_part, far))
        after[1] = [sp_part]
    lo_keep, lo_send, lo_up = out_grads(ktable, gated, gb, gwl, after[1])
    mixed_got = route.cross(mixed_away)
    if fits:
        lo_up = route.cross(lo_up)
        lo_terms = [lo_keep, route.cross(lo_send)]
        lo_part = add_part([lo_keep, lo_up], 128, [], [1, 0])
        lo_terms.append(route.swap(lo_part, near))
        after[2] = [lo_part]
    gp, gate_sum = gate_backward(vec, gs, mm, hat, slope, scale, after[2])
    if fits:
        sp_own, sp_out = line_turn(sp_terms, 1, [gate_sum])
        sp_terms = [sp_own, route.swap(sp_out, (route.direct[0],) * 2)]
        after[3] = [sp_own, mixed_got]
    gwr, ghb = in_grads(gp, h, weight_right, gh, after[3])
    if fits:
        sp_own, sp_out = line_turn(sp_terms, 2, [gwr])
        sp_terms = [sp_own, route.swap(sp_out, (route.direct[1],) * 2)]
        lo_part = add_part(lo_terms, 64, [sp_own])
        lo_terms.append(route.swap(lo_part, far))
        after[4] = [lo_part]
    right_keep, right_send, up_a, up_b, grad_stay, grad_away = in_backward(
        ktable, sides, vec, gsum, gate_sum, gwr, ghb, x, grad_out, rows, after[4]
    )
    grad_got = route.cross(grad_away)
    if fits:
        upper = [route.cross(up_a), route.cross(up_b)]
        right_terms = [right_keep, route.cross(right_send)]
        lo_own, *sends = line_parts(lo_terms, [right_keep])
        lo_got = [route.swap(p, (m, m)) for p, m in zip(sends, route.direct)]
        right_part = add_upper(right_keep, upper, [lo_own])
        right_terms.append(route.swap(right_part, near))
        right_part = add_part(right_terms, 64, [grad_got])
        right_terms.append(route.swap(right_part, far))
        (sp_sum,) = line_turn(sp_terms, 0, [right_part])
        spat_pieces = route.widen_direct(sp_sum)
        right_own, *sends = line_parts(right_terms, [sp_sum])
        right_got = [route.swap(p, (m, m)) for p, m in zip(sends, route.direct)]
        left_sum, *new_out = finish_out(lo_own, lo_got, dense_out, out_first, out_second, right_own)
        korder = order
        after = [left_sum]
    else:
        both = jnp.concatenate([lo_keep, lo_send, lo_up])
        outs = both[:, HALF:LO].reshape(DEVS, 16, 3, D).transpose(0, 2, 1, 3).reshape(ndev, out_rows, D)
        outs = jnp.take(outs, table, axis=0).reshape(HALF, D)
        out_sum = route.scatter(outs[: HALF // 2], outs[HALF // 2 :])
        lefts = jnp.take(both[:, :HALF].reshape(ndev, in_rows, HALF), table, axis=0).reshape(D, HALF)
        left_sum = route.scatter(lefts[: D // 2], lefts[D // 2 :])
        per = 512 // route.n

        def spat_blocks(part, flip):
            flat = part.reshape(GROUPS, 16, 2, SCOLS).transpose(0, 2, 1, 3).reshape(route.n, per, SCOLS)
            return jnp.take(flat, route.order(flip)[0], axis=0).reshape(512, SCOLS)

        spat_part = route.scatter(spat_blocks(sp_keep, False), spat_blocks(sp_send, True)).astype(BF)
        flat = in_order(route.spread(spat_part), order, per).reshape(GROUPS, 2, 16, SCOLS)
        spat_pieces = [flat.transpose(0, 2, 1, 3).reshape(GROUPS * 16, SPC)]
        korder = jnp.arange(GROUPS, dtype=jnp.int32)
        after = []
        both = jnp.concatenate([right_keep, right_send, up_a, up_b])
        vecs = both.reshape(DEVS, 16, -1)[:, : VPER // VSUB, HALF : HALF + VSUB]
        vecs = jnp.take(vecs.reshape(ndev, vec_len), table, axis=0)
        vec_sum = route.scatter(vecs[: route.n], vecs[route.n :]).reshape(vec_len)
        rights = jnp.take(both[:, :HALF].reshape(ndev, in_rows, HALF), table, axis=0).reshape(D, HALF)
        right_sum = route.scatter(rights[: D // 2], rights[D // 2 :])
        in_sum = jnp.concatenate([left_sum, right_sum], axis=1)
        new_in = adamw(dense_in, in_sum, in_first, in_second, DENSE_RATE, DENSE_DECAY)
        new_out = adamw(dense_out, out_sum, out_first, out_second, DENSE_RATE, DENSE_DECAY)

    def whole_images(stays, came):
        return jnp.concatenate([jnp.where(seq == 0, stays, came), jnp.where(seq == 0, came, stays)], axis=0)

    mixed = whole_images(mixed_stay, mixed_got)
    patches_grad = whole_images(grad_stay, grad_got)
    spat_new = spatial_update(
        korder, spat_pieces, spatial, spat_first, spat_second, spatial_bias, bias_first, bias_second, after
    )
    if fits:
        *new_in, vec_sum = finish_in(right_own, right_got, left_sum, dense_in, in_first, in_second, spat_new[0])
        vec_sum = vec_sum[0, :vec_len]
    new_vec = adamw(vectors, vec_sum, vec_first, vec_second, SMALL_RATE, 0.0)
    return (mixed, patches_grad) + tuple(new_in) + tuple(new_out) + new_vec + tuple(spat_new)


def solution(mesh):
    rows3 = P("dp", "seq", None)
    dense = P(AXES, None)
    vec = P(AXES)
    spat = P(None, "seq", None)
    bias = P(None, "seq")
    in_specs = (rows3, P("dp"), rows3, dense, dense, vec, spat, bias)
    in_specs += (dense,) * 4 + (vec,) * 2 + (spat,) * 2 + (bias,) * 2
    out_specs = (rows3, rows3) + (dense,) * 6 + (vec,) * 3 + (spat,) * 3 + (bias,) * 3
    return jax.shard_map(local, mesh=mesh, in_specs=in_specs, out_specs=out_specs, check_vma=False)
```

```python
import functools

import jax
import jax.numpy as jnp
from jax import lax
from jax.experimental import pallas as pl
from jax.experimental.pallas import tpu as pltpu
from jax.sharding import PartitionSpec as P

D = 512
FF = 3072
HALF = 1536
PMAX = 324
PPAD = 336
P_MID = 196
P_LOW = 100
VCOLS = 256
ROWS = 2 * PPAD
GROUPS = 16
DEVS = 2 * GROUPS
VPER = 240
SCOLS = 384
BIAS_AT = 336
TOTAL_AT = 324
LSTRIDE = 168
MIB = 1024 * 1024
STEP = 10

NORM_EPS = 1e-05
BETA_ONE = 0.9
BETA_TWO = 0.99
ADAM_EPS = 1e-08
DENSE_RATE = 0.02
SMALL_RATE = 0.2
DENSE_DECAY = 0.05

BF = jnp.bfloat16
F32 = jnp.float32
AXES = ("dp", "seq")
VM = pl.BlockSpec(memory_space=pltpu.VMEM)
SM = pl.BlockSpec(memory_space=pltpu.SMEM)
HB = pl.BlockSpec(memory_space=pl.ANY)


class Route:
    def __init__(self, n):
        bits = n.bit_length() - 1
        assert n == 1 << bits and bits >= 2
        self.n = n
        top = n // 4
        self.direct = [top, 2 * top, 3 * top]
        low = [1 << b for b in range(bits - 2)]
        self.low = list(zip(low[::-1], low))
        masks = [(0, 0)] + [(m, m) for m in self.direct]
        for step in self.low:
            masks = masks + [(m[0] ^ step[0], m[1] ^ step[1]) for m in masks]
        self.masks = masks

    def swap(self, block, mask):
        pairs = []
        for dp in range(self.n):
            for seq in range(2):
                pairs.append((dp * 2 + seq, (dp ^ mask[seq]) * 2 + seq))
        return lax.ppermute(block, AXES, pairs)

    def cross(self, block):
        pairs = []
        for dp in range(self.n):
            for seq in range(2):
                pairs.append((dp * 2 + seq, dp * 2 + 1 - seq))
        return lax.ppermute(block, AXES, pairs)

    def order(self, seq_flip):
        place = lax.axis_index("dp")
        seq = lax.axis_index("seq")
        if seq_flip:
            seq = 1 - seq
        zero = jnp.array([m[0] for m in self.masks], jnp.int32)
        one = jnp.array([m[1] for m in self.masks], jnp.int32)
        return place ^ jnp.where(seq == 0, zero, one), seq

    def table(self):
        mine, seq = self.order(False)
        other, flip = self.order(True)
        return jnp.concatenate([mine * 2 + seq, other * 2 + flip])

    def spread(self, shard):
        first = jnp.concatenate([shard] + [self.swap(shard, (m, m)) for m in self.direct], axis=0)
        return self.widen(first)

    def widen(self, first):
        blocks = [first]
        for step in self.low:
            blocks = blocks + [self.swap(b, step) for b in blocks]
        return blocks

    def widen_in_turn(self, first):
        second = self.swap(first, self.low[0])
        third = self.swap(first, self.low[1])
        passed = stack([second], [third])
        return [first, second, third, self.swap(passed, self.low[1])], passed

    def widen_direct(self, first):
        return [first] + [self.swap(first, m) for m in self.plane()]

    def plane(self):
        one, two = self.low
        return [one, two, (one[0] ^ two[0], one[1] ^ two[1])]

    def gather(self, shard):
        blocks = self.spread(shard)
        return blocks + [self.cross(b) for b in blocks]

    def collect(self, terms):
        cur = terms[0].shape[0]
        rows = cur // self.n

        def part(lower, upper):
            total = terms[0][lower:upper].astype(F32)
            for t in terms[1:]:
                total = total + t[lower:upper].astype(F32)
            return total

        terms = list(terms)
        for step in reversed(self.low):
            half = cur // 2
            terms.append(self.swap(part(half, cur).astype(BF), step))
            cur = half
        got = []
        for j, m in enumerate(self.direct):
            got.append(self.swap(part((j + 1) * rows, (j + 2) * rows).astype(BF), (m, m)))
        total = part(0, rows)
        return (total + got[0].astype(F32)) + (got[1].astype(F32) + got[2].astype(F32))

    def scatter(self, keep, send):
        return self.collect([keep, self.cross(send)])


def dot(a, b, dims):
    return lax.dot_general(a, b, (dims, ((), ())), preferred_element_type=F32)


NN = ((1,), (0,))
NT = ((1,), (1,))
TN = ((0,), (0,))


def gelu_parts(p):
    bell = jnp.exp(p * p * -0.5)
    d = 1.0 + jnp.abs(p) * (0.3275911 * 0.7071067811865476)
    t = pl.reciprocal(d, approx=True)
    t = t * (2.0 - d * t)
    poly = t * (
        0.127414796
        + t * (-0.142248368 + t * (0.7107068705 + t * (-0.7265760135 + t * 0.5307027145)))
    )
    tail = poly * bell
    phi_sum = jnp.where(p >= 0.0, 1.0 - tail, tail)
    return p * phi_sum, phi_sum + p * bell * 0.3989422804014327


def count_of(level):
    return jnp.where(level == 0, P_LOW, jnp.where(level == 1, P_MID, PMAX))


def masked_mix(mix, count):
    i = lax.broadcasted_iota(jnp.int32, (PPAD, SCOLS), 0)
    j = lax.broadcasted_iota(jnp.int32, (PPAD, SCOLS), 1)
    return jnp.where((i < count) & (j < count), mix.astype(F32), 0.0).astype(BF)


def live_rows(count, shape, start=0):
    return lax.broadcasted_iota(jnp.int32, shape, 0) + start < count


def live_mask(levels_ref, b, width):
    return live_rows(count_of(levels_ref[b]), (PPAD, width))


def fold(value):
    total = value[:, 0:128]
    for n in range(128, value.shape[1], 128):
        total = total + value[:, n : n + 128]
    return total


def spread_sum(ref, factor):
    return jnp.broadcast_to(jnp.sum(ref[...], axis=-1, keepdims=True) * factor, ref.shape)


def wide(value, times):
    return jnp.concatenate([value] * times, axis=1)


def start_blocks(table_ref, pieces, rows, cols, target, sem, extra=0):
    copies = []
    k = 0
    for piece in pieces:
        for j in range(piece.shape[0] // 16):
            at = pl.multiple_of(table_ref[k] * rows, 16)
            c = pltpu.make_async_copy(
                piece.at[pl.ds(j * 16, 16), pl.ds(cols[0], cols[1])], target.at[pl.ds(at + extra, 16)], sem.at[k]
            )
            c.start()
            copies.append(c)
            k += 1
    return copies


def row_loop(step, body):
    def run(i, carry):
        body(pl.multiple_of(i * step, step))
        return carry

    lax.fori_loop(0, ROWS // step, run, 0)


def call(kernel, out_shape, in_specs, scratch, flops, nbytes, *args, room=12):
    vm = pl.BlockSpec(memory_space=pltpu.VMEM)
    return pl.pallas_call(
        kernel,
        out_shape=out_shape,
        in_specs=in_specs,
        out_specs=jax.tree.map(lambda _: vm, out_shape),
        scratch_shapes=scratch,
        compiler_params=pltpu.CompilerParams(vmem_limit_bytes=room * MIB),
        cost_estimate=pl.CostEstimate(flops=flops, bytes_accessed=nbytes, transcendentals=0),
    )(*args)


def norm_parts(values):
    center = values - jnp.mean(values, axis=-1, keepdims=True)
    scale = lax.rsqrt(jnp.mean(center * center, axis=-1, keepdims=True) + NORM_EPS)
    return center * scale, scale


VSEG = {
    "g1": (0, D),
    "b1": (D, D),
    "c1l": (2 * D, HALF),
    "c1r": (2 * D + HALF, HALF),
    "g2": (2 * D + FF, HALF),
    "b2": (2 * D + FF + HALF, HALF),
    "c2": (2 * D + FF + 2 * HALF, D),
}
VEC = 2 * D + FF + 2 * HALF + D


def seg(ref, name):
    start, size = VSEG[name]
    return ref[0:1, start : start + size]

def adamw(weight, grad, first, second, rate, decay):
    first = BETA_ONE * first + (1.0 - BETA_ONE) * grad
    second = BETA_TWO * second + (1.0 - BETA_TWO) * grad * grad
    first_hat = first / (1.0 - BETA_ONE**STEP)
    second_hat = second / (1.0 - BETA_TWO**STEP)
    weight = weight - rate * (first_hat / (jnp.sqrt(second_hat) + ADAM_EPS) + decay * weight)
    return (weight, first, second)


CHUNK = 16
TILE = 256
BODY = 32
STRIPE = 112
LO = 2 * HALF
SPC = 2 * SCOLS


def sds(shape, dtype):
    return jax.ShapeDtypeStruct(shape, dtype)


def pack_dense(dense_in, dense_out, vec_row):
    rows = dense_in.shape[0]
    per = vec_row.shape[1]

    def kernel(w_hbm, o_hbm, v_hbm, out_ref, lo_ref, w_ref, o_ref, v_ref, row, sem):
        copies = [
            pltpu.make_async_copy(src, dst, sem.at[k])
            for k, (src, dst) in enumerate(((w_hbm, w_ref), (o_hbm, o_ref), (v_hbm, v_ref)))
        ]
        for c in copies:
            c.start()
        row[...] = jnp.zeros_like(row)
        for c in copies:
            c.wait()
        out_ref[:, 0:HALF] = w_ref[:, HALF:].astype(BF)
        row[0:1, 0:per] = v_ref[...]
        out_ref[:, HALF : HALF + VCOLS] = row[...].astype(BF)
        lo_ref[:, 0:HALF] = w_ref[:, 0:HALF].astype(BF)
        for g in range(3):
            lo_ref[:, HALF + g * D : HALF + (g + 1) * D] = o_ref[g * rows : (g + 1) * rows, :].astype(BF)

    scratch = [
        pltpu.VMEM(dense_in.shape, F32),
        pltpu.VMEM(dense_out.shape, F32),
        pltpu.VMEM(vec_row.shape, F32),
        pltpu.VMEM((rows, VCOLS), F32),
        pltpu.SemaphoreType.DMA((3,)),
    ]
    shape = (sds((rows, HALF + VCOLS), BF), sds((rows, LO), BF))
    return call(kernel, shape, [HB] * 3, scratch, 1000, 600000, dense_in, dense_out, vec_row, room=60)


def pack_images(sides, spatial, bias_col, patches, out_grad):
    half = patches.shape[1]

    def kernel(sides_ref, s_ref, b_ref, x_ref, g_ref, spat_ref, xs_ref, gs_ref, buf):
        away = 2 - 2 * sides_ref[0]
        for b in range(2):
            xs_ref[b] = x_ref[away + b]
            gs_ref[b] = g_ref[away + b]
        buf[...] = jnp.zeros_like(buf)
        for level in range(3):
            buf[:, 0:PMAX] = s_ref[level]
            rest = b_ref[level]
            for c in range(3):
                piece = rest.astype(BF).astype(F32)
                buf[:, BIAS_AT + c : BIAS_AT + c + 1] = piece
                rest = rest - piece
            spat_ref[level] = buf[...].astype(BF)

    pair = sds((2, half, D), BF)
    return call(
        kernel,
        (sds((3, half, SCOLS), BF), pair, pair),
        [SM] + [VM] * 4,
        [pltpu.VMEM((half, SCOLS), F32)],
        1000,
        3000000,
        sides,
        spatial,
        bias_col,
        patches,
        out_grad,
    )


def stack(pieces, after):
    count = len(pieces)
    rows, cols = pieces[0].shape

    def kernel(*refs):
        out = refs[count + len(after)]
        for k in range(count):
            out[k * rows : (k + 1) * rows, :] = refs[k][...]

    specs = [VM] * count + [HB] * len(after)
    return call(kernel, sds((count * rows, cols), BF), specs, [], 1000, 1000000, *pieces, *after)


def two_halves(is_first, own, got):
    own = own.astype(F32)
    got = got.astype(F32)
    return jnp.where(is_first, own, got), jnp.where(is_first, got, own)


def gate_norm(levels, sides, vec, v, part, spat_own, spat_got, after):
    half = spat_own.shape[1]
    count = len(after)

    def kernel(levels_ref, sides_ref, vec_ref, v_ref, part_ref, so_ref, sg_ref, *refs):
        gate_ref, hat_ref, scale_ref, spat_ref, mm_ref, mixf, mean, buf = refs[count:]
        is_first = sides_ref[0] == 0
        g_start = VSEG["g2"][0]
        b_start = VSEG["b2"][0]
        mean[...] = spread_sum(part_ref, 1.0 / HALF)

        def square_rows(r):
            for k in range(0, BODY, CHUNK):
                rows = pl.ds(r + k, CHUNK)
                mid = mean[rows, :]
                total = jnp.zeros((CHUNK, 128), F32)
                for n in range(0, HALF, 128):
                    center = v_ref[rows, n : n + 128] - mid
                    total = total + center * center
                buf[rows, :] = total

        row_loop(BODY, square_rows)
        scale_ref[...] = lax.rsqrt(spread_sum(buf, 1.0 / HALF) + NORM_EPS)

        def gate_rows(r):
            for k in range(0, BODY, CHUNK):
                rows = pl.ds(r + k, CHUNK)
                mid = wide(mean[rows, :], 2)
                scale = wide(scale_ref[rows, :], 2)
                for n in range(0, HALF, TILE):
                    hat = (v_ref[rows, n : n + TILE] - mid) * scale
                    hat_ref[rows, n : n + TILE] = hat.astype(BF)
                    gate = hat * vec_ref[0:1, g_start + n : g_start + n + TILE]
                    gate = (gate + vec_ref[0:1, b_start + n : b_start + n + TILE]).astype(BF)
                    gate_ref[rows, n : n + TILE] = gate

        row_loop(BODY, gate_rows)
        gate_ref[ROWS:, :] = jnp.zeros((SCOLS - PPAD, HALF), BF)
        for b in range(2):
            level = levels_ref[b]
            live = count_of(level)
            one, two = two_halves(is_first, so_ref[level], sg_ref[level])
            mixf[0:half, :] = one
            mixf[half : 2 * half, :] = two
            mixf[2 * half :, :] = jnp.zeros((PPAD - 2 * half, SCOLS), F32)
            bias = jnp.sum(mixf[:, TOTAL_AT:], axis=-1, keepdims=True)
            mm_ref[b] = masked_mix(mixf[...], live)

            def mix_tile(n, carry):
                cols = pl.ds(pl.multiple_of(n * 512, 512), 512)
                got = dot(mm_ref[b], gate_ref[b * PPAD : b * PPAD + SCOLS, cols], NN) + bias
                got = jnp.where(live_rows(live, (PPAD, 512)), got, 0.0)
                spat_ref[b * PPAD : (b + 1) * PPAD, cols] = got.astype(BF)
                return carry

            lax.fori_loop(0, HALF // 512, mix_tile, 0)

    return call(
        kernel,
        (
            sds((ROWS + SCOLS - PPAD, HALF), BF),
            sds((ROWS, HALF), BF),
            sds((ROWS, 128), F32),
            sds((ROWS, HALF), BF),
            sds((2, PPAD, SCOLS), BF),
        ),
        [SM] * 2 + [VM] * 5 + [HB] * count,
        [pltpu.VMEM((PPAD, SCOLS), F32), pltpu.VMEM((ROWS, 128), F32), pltpu.VMEM((ROWS, 128), F32)],
        6000000000,
        12000000,
        levels,
        sides,
        vec,
        v,
        part,
        spat_own,
        spat_got,
        *after,
        room=22,
    )


def gate_forward(table, sides, patches, x_got, out_grad, g_got, pieces):
    count = len(pieces)
    half = patches.shape[1]

    def kernel(table_ref, sides_ref, p_ref, xg_ref, o_ref, gg_ref, *refs):
        ins = refs[:count]
        outs = refs[count : count + 8]
        x_ref, og_ref, h_ref, pre, slope_ref, part, w_ref, vec_ref = outs
        vblk, xbuf, sem, vsem = refs[count + 8 :]
        vcopies = start_blocks(table_ref, ins, 16, (HALF, VCOLS), vblk, vsem)
        copies = start_blocks(table_ref, ins, 16, (0, HALF), w_ref, sem)
        me = sides_ref[0]
        is_first = me == 0

        for src, got, target in ((o_ref, gg_ref, og_ref), (p_ref, xg_ref, x_ref)):
            for b in range(2):
                one, two = two_halves(is_first, src[2 * me + b], got[b])
                xbuf[b * PPAD : b * PPAD + half, :] = one
                xbuf[b * PPAD + half : b * PPAD + 2 * half, :] = two
                xbuf[b * PPAD + 2 * half : (b + 1) * PPAD, :] = jnp.zeros((PPAD - 2 * half, D), F32)
            target[...] = xbuf[...].astype(BF)
        for c in vcopies:
            c.wait()
        for s in range(DEVS):
            row = vblk[16 * s : 16 * s + 16, :].astype(F32)[0:1, :VPER]
            vec_ref[0:1, VPER * s : VPER * s + VPER] = row

        def norm_one(r):
            hat, _ = norm_parts(xbuf[pl.ds(r, STRIPE), :])
            h_ref[pl.ds(r, STRIPE), :] = (hat * seg(vec_ref, "g1") + seg(vec_ref, "b1")).astype(BF)

        row_loop(STRIPE, norm_one)
        for c in copies:
            c.wait()
        c_start = VSEG["c1r"][0]

        def matmul(n, carry):
            at = pl.multiple_of(n * TILE, TILE)
            pre[:, pl.ds(at, TILE)] = dot(h_ref[...], w_ref[:, pl.ds(at, TILE)], NN)
            return carry

        lax.fori_loop(0, HALF // TILE, matmul, 0)

        def gelu_rows(r):
            for k in range(0, BODY, CHUNK):
                rows = pl.ds(r + k, CHUNK)
                total = jnp.zeros((CHUNK, 128), F32)
                for n in range(0, HALF, TILE):
                    v, slope = gelu_parts(pre[rows, n : n + TILE] + vec_ref[0:1, c_start + n : c_start + n + TILE])
                    pre[rows, n : n + TILE] = v
                    slope_ref[rows, n : n + TILE] = slope.astype(BF)
                    total = total + fold(v)
                part[rows, :] = total

        row_loop(BODY, gelu_rows)

    broad = sds((ROWS, HALF), BF)
    narrow = sds((ROWS, D), BF)
    out_shape = (
        narrow,
        narrow,
        narrow,
        sds((ROWS, HALF), F32),
        broad,
        sds((ROWS, 128), F32),
        sds((D, HALF), BF),
        sds((1, VEC), F32),
    )
    scratch = [
        pltpu.VMEM((D, VCOLS), BF),
        pltpu.VMEM((ROWS, D), F32),
        pltpu.SemaphoreType.DMA((DEVS,)),
        pltpu.SemaphoreType.DMA((DEVS,)),
    ]
    return call(
        kernel,
        out_shape,
        [SM] * 2 + [VM] * 4 + [HB] * count,
        scratch,
        10000000000,
        20000000,
        table,
        sides,
        patches,
        x_got,
        out_grad,
        g_got,
        *pieces,
        room=26,
    )


def split_rows(target, first, second, seq, value):
    half = first.shape[1]
    target[...] = value
    for b in range(2):
        one = target[b * PPAD : b * PPAD + half, :]
        two = target[b * PPAD + half : b * PPAD + 2 * half, :]
        first[b] = jnp.where(seq == 0, one, two).astype(BF)
        second[b] = jnp.where(seq == 0, two, one).astype(BF)


def middle(table, levels, sides, vec, h, spat, gate, grad_out, pieces):
    count = len(pieces)

    def kernel(table_ref, levels_ref, sides_ref, vec_ref, h_ref, spat_ref, gate_ref, og_ref, *refs):
        ins = refs[:count]
        gs_ref, gated_ref, q_ref, gb, wl, wo, keep, send, gsum_ref = refs[count : count + 9]
        pbuf, gbuf, cells, flat, sem = refs[count + 9 :]
        copies = start_blocks(table_ref, ins, 16, (0, HALF), wl, sem.at[0])
        for g in range(3):
            copies += start_blocks(table_ref, ins, 48, (HALF + g * D, D), wo, sem.at[1 + g], 16 * g)
        for b in range(2):
            rows = slice(b * PPAD, (b + 1) * PPAD)
            gb[rows, :] = jnp.where(live_mask(levels_ref, b, D), og_ref[rows, :].astype(F32), 0.0).astype(BF)
        gsum_ref[0:1, HALF : HALF + D] = jnp.sum(gb[...].astype(F32), axis=0, keepdims=True)
        cells[...] = jnp.zeros_like(cells)
        flat[...] = jnp.zeros_like(flat)
        for c in copies:
            c.wait()
        c_start = VSEG["c1l"][0]

        def tile(n, carry):
            at = pl.multiple_of(n * TILE, TILE)
            cols = pl.ds(at, TILE)
            pbuf[...] = dot(h_ref[...], wl[:, cols], NN)
            gbuf[...] = dot(gb[...], wo[cols, :], NT)
            shift = vec_ref[0:1, pl.ds(c_start + at, TILE)]
            total = jnp.zeros((CHUNK, TILE), F32)
            for k in range(0, ROWS, CHUNK):
                r = slice(k, k + CHUNK)
                u, slope = gelu_parts(pbuf[r, :] + shift)
                sp = spat_ref[r, cols].astype(F32)
                gg = gbuf[r, :]
                gated_ref[r, cols] = (u * sp).astype(BF)
                gs_ref[r, cols] = (gg * u).astype(BF)
                q = (gg * sp * slope).astype(BF)
                q_ref[r, cols] = q
                total = total + q.astype(F32)
            gsum_ref[0:1, cols] = jnp.sum(total, axis=0, keepdims=True)
            return carry

        lax.fori_loop(0, HALF // TILE, tile, 0)

        me = sides_ref[0]
        for b in range(2):
            level = levels_ref[b]
            count_b = count_of(level)
            gs = gs_ref[b * PPAD : (b + 1) * PPAD, :]
            got = dot(gs, gate_ref[b * PPAD : (b + 1) * PPAD, :], NT)
            sums = jnp.sum(gs.astype(F32), axis=-1, keepdims=True)
            j = lax.broadcasted_iota(jnp.int32, (PPAD, PPAD), 1)
            got = jnp.where(j < count_b, got, jnp.where(j == TOTAL_AT, sums, 0.0))
            cells[level, :, 0:PPAD] += got
        part = PMAX // 2
        for level in range(3):
            for k in range(2):
                flat[k, level * LSTRIDE : level * LSTRIDE + part, 0:PPAD] = cells[level, k * part : (k + 1) * part, 0:PPAD]
        for k in range(DEVS):
            target, side = (keep, me) if k < GROUPS else (send, 1 - me)
            r = pl.ds(k % GROUPS * 16, 16)
            block = flat[side, pl.ds(pl.multiple_of(sides_ref[1 + k] * 32, 32), 32), :].astype(BF)
            target[r, 0:SCOLS] = block[0:16]
            target[r, SCOLS:SPC] = block[16:32]

    broad = sds((ROWS, HALF), BF)
    payload = sds((D // 2, SPC), BF)
    out_shape = (
        broad,
        broad,
        broad,
        sds((ROWS, D), BF),
        sds((D, HALF), BF),
        sds((HALF, D), BF),
        payload,
        payload,
        sds((1, HALF + D), F32),
    )
    scratch = [
        pltpu.VMEM((ROWS, TILE), F32),
        pltpu.VMEM((ROWS, TILE), F32),
        pltpu.VMEM((3, PPAD, SCOLS), F32),
        pltpu.VMEM((2, 512, SCOLS), F32),
        pltpu.SemaphoreType.DMA((4, DEVS)),
    ]
    return call(
        kernel,
        out_shape,
        [SM] * 3 + [VM] * 5 + [HB] * count,
        scratch,
        8000000000,
        16000000,
        table,
        levels,
        sides,
        vec,
        h,
        spat,
        gate,
        grad_out,
        *pieces,
        room=28,
    )


def weight_grads(levels, sides, vec, gated, q, h, wl, wo, x, half, after):
    count = len(after)

    def kernel(levels_ref, sides_ref, vec_ref, t_ref, q_ref, h_ref, wl_ref, wo_ref, x_ref, *refs):
        gwl, stay_ref, away_ref, gh_ref, branch = refs[count:]

        def in_tile(n, carry):
            cols = pl.ds(pl.multiple_of(n * TILE, TILE), TILE)
            gwl[cols, :] = dot(h_ref[:, cols], q_ref[...], TN).astype(BF)
            branch[:, cols] = dot(t_ref[...], wo_ref[:, cols], NN)
            gh_ref[:, cols] = dot(q_ref[...], wl_ref[cols, :], NT)
            return carry

        lax.fori_loop(0, D // TILE, in_tile, 0)
        me = sides_ref[0]
        live = jnp.concatenate([live_mask(levels_ref, b, D) for b in range(2)], axis=0)
        out = branch[...] + seg(vec_ref, "c2")
        split_rows(branch, stay_ref, away_ref, me, x_ref[...].astype(F32) + jnp.where(live, out, 0.0))

    pair = sds((2, half, D), BF)
    return call(
        kernel,
        (sds((D, HALF), BF), pair, pair, sds((ROWS, D), F32)),
        [SM] * 2 + [VM] * 7 + [HB] * count,
        [pltpu.VMEM((ROWS, D), F32)],
        4000000000,
        12000000,
        levels,
        sides,
        vec,
        gated,
        q,
        h,
        wl,
        wo,
        x,
        *after,
        room=12,
    )


def out_grads(table, gated, gb, gwl, after):
    count = len(after)

    def kernel(table_ref, t_ref, gb_ref, gwl_ref, *refs):
        keep, send, send_up, gwo = refs[count:]

        def out_tile(n, carry):
            cols = pl.ds(pl.multiple_of(n * TILE, TILE), TILE)
            gwo[cols, :] = dot(t_ref[:, cols], gb_ref[...], TN).astype(BF)
            return carry

        lax.fori_loop(0, HALF // TILE, out_tile, 0)
        for k in range(DEVS):
            dev = table_ref[k]
            target = keep if k < GROUPS else send if k < GROUPS * 3 // 2 else send_up
            r = pl.ds(k % (GROUPS if k < GROUPS else GROUPS // 2) * 16, 16)
            target[r, 0:HALF] = gwl_ref[pl.ds(pl.multiple_of(dev * 16, 16), 16), :]
            for g in range(3):
                target[r, HALF + g * D : HALF + (g + 1) * D] = gwo[pl.ds(pl.multiple_of(dev * 48 + 16 * g, 16), 16), :]

    payload = sds((D // 2, LO), BF)
    part = sds((D // 4, LO), BF)
    return call(
        kernel,
        (payload, part, part),
        [SM] + [VM] * 3 + [HB] * count,
        [pltpu.VMEM((HALF, D), BF)],
        2000000000,
        8000000,
        table,
        gated,
        gb,
        gwl,
        *after,
        room=10,
    )


def gate_backward(vec, gs, mm, hat, slope, scale, after):
    count = len(after)

    def kernel(vec_ref, gs_ref, mm_ref, hat_ref, slope_ref, scale_ref, *refs):
        gp, gsum_ref, dbuf, one, two, acc = refs[count:]

        for b in range(2):

            def mix_tile(n, carry):
                cols = pl.ds(pl.multiple_of(n * 512, 512), 512)
                got = dot(mm_ref[b], gs_ref[b * PPAD : (b + 1) * PPAD, cols], TN)
                dbuf[b * PPAD : (b + 1) * PPAD, cols] = got[0:PPAD]
                return carry

            lax.fori_loop(0, HALF // 512, mix_tile, 0)
        g_start = VSEG["g2"][0]

        def sum_rows(r):
            for k in range(0, BODY, CHUNK):
                rows = pl.ds(r + k, CHUNK)
                a = jnp.zeros((CHUNK, 128), F32)
                c = jnp.zeros((CHUNK, 128), F32)
                for n in range(0, HALF, TILE):
                    e = dbuf[rows, n : n + TILE] * vec_ref[0:1, g_start + n : g_start + n + TILE]
                    a = a + fold(e)
                    c = c + fold(e * hat_ref[rows, n : n + TILE].astype(F32))
                one[rows, :] = a
                two[rows, :] = c

        row_loop(BODY, sum_rows)
        one[...] = spread_sum(one, 1.0 / HALF)
        two[...] = spread_sum(two, 1.0 / HALF)
        acc[...] = jnp.zeros_like(acc)

        def grad_rows(r):
            for n in range(0, HALF, TILE):
                gain = vec_ref[0:1, g_start + n : g_start + n + TILE]
                sums = [jnp.zeros((CHUNK, TILE), F32) for _ in range(3)]
                for k in range(0, BODY, CHUNK):
                    rows = pl.ds(r + k, CHUNK)
                    d = dbuf[rows, n : n + TILE]
                    xh = hat_ref[rows, n : n + TILE].astype(F32)
                    inner = d * gain - wide(one[rows, :], 2) - xh * wide(two[rows, :], 2)
                    q = inner * wide(scale_ref[rows, :], 2) * slope_ref[rows, n : n + TILE].astype(F32)
                    q = q.astype(BF)
                    gp[rows, n : n + TILE] = q
                    sums = [sums[0] + d * xh, sums[1] + d, sums[2] + q.astype(F32)]
                for i in range(3):
                    acc[i, :, n : n + TILE] += sums[i]

        row_loop(BODY, grad_rows)
        for i in range(3):
            gsum_ref[0:1, i * HALF : (i + 1) * HALF] = jnp.sum(acc[i], axis=0, keepdims=True)

    return call(
        kernel,
        (sds((ROWS, HALF), BF), sds((1, 3 * HALF), F32)),
        [VM] * 6 + [HB] * count,
        [
            pltpu.VMEM((ROWS, HALF), F32),
            pltpu.VMEM((ROWS, 128), F32),
            pltpu.VMEM((ROWS, 128), F32),
            pltpu.VMEM((3, CHUNK, HALF), F32),
        ],
        3000000000,
        10000000,
        vec,
        gs,
        mm,
        hat,
        slope,
        scale,
        *after,
        room=20,
    )


def in_grads(gp, h, w, gh, after):
    count = len(after)

    def kernel(gp_ref, h_ref, w_ref, gh_ref, *refs):
        gwr, ghb = refs[count:]

        def in_tile(n, carry):
            cols = pl.ds(pl.multiple_of(n * TILE, TILE), TILE)
            ghb[:, cols] = gh_ref[:, cols] + dot(gp_ref[...], w_ref[cols, :], NT)
            gwr[cols, :] = dot(h_ref[:, cols], gp_ref[...], TN).astype(BF)
            return carry

        lax.fori_loop(0, D // TILE, in_tile, 0)

    return call(
        kernel,
        (sds((D, HALF), BF), sds((ROWS, D), F32)),
        [VM] * 4 + [HB] * count,
        [],
        3000000000,
        8000000,
        gp,
        h,
        w,
        gh,
        *after,
        room=14,
    )


def in_backward(table, sides, vec, gsum, gate_sum, gwr, ghb, x, grad_out, half, after):
    count = len(after)

    def kernel(table_ref, sides_ref, vec_ref, gsum_ref, gate_ref, gwr, ghb, x_ref, og_ref, *refs):
        keep, send, up_a, up_b, stay_ref, away_ref, acc, gvec, blocks, pgb = refs[count:]

        def put(name, value):
            start, size = VSEG[name]
            gvec[0:1, start : start + size] = value

        put("g2", gate_ref[0:1, 0:HALF])
        put("b2", gate_ref[0:1, HALF : 2 * HALF])
        put("c1r", gate_ref[0:1, 2 * HALF : 3 * HALF])
        put("c1l", gsum_ref[0:1, 0:HALF])
        put("c2", gsum_ref[0:1, HALF : HALF + D])
        acc[...] = jnp.zeros_like(acc)
        def in_rows(r):
            rows = pl.ds(r, STRIPE)
            xh, scale = norm_parts(x_ref[rows, :].astype(F32))
            d = ghb[rows, :]
            e = d * seg(vec_ref, "g1")
            one = jnp.mean(e, axis=-1, keepdims=True)
            two = jnp.mean(e * xh, axis=-1, keepdims=True)
            pgb[rows, :] = og_ref[rows, :].astype(F32) + scale * (e - one - xh * two)
            acc[0:1, :] += jnp.sum(d * xh, axis=0, keepdims=True)
            acc[1:2, :] += jnp.sum(d, axis=0, keepdims=True)

        row_loop(STRIPE, in_rows)
        put("g1", acc[0:1, :])
        put("b1", acc[1:2, :])
        split_rows(pgb, stay_ref, away_ref, sides_ref[0], pgb[...])
        blocks[...] = jnp.zeros_like(blocks)
        for s in range(DEVS):
            blocks[s, 0:1, 0:VPER] = gvec[0:1, VPER * s : VPER * s + VPER]
        for k in range(DEVS):
            dev = table_ref[k]
            target, first = next((t, f) for t, f in ((up_b, 28), (up_a, 24), (send, GROUPS), (keep, 0)) if k >= f)
            r = pl.ds((k - first) * 16, 16)
            target[r, 0:HALF] = gwr[pl.ds(pl.multiple_of(dev * 16, 16), 16), :]
            target[r, HALF : HALF + VCOLS] = blocks[dev].astype(BF)

    payload = sds((D // 2, HALF + VCOLS), BF)
    part = sds((D // 4, HALF + VCOLS), BF)
    eighth = sds((D // 8, HALF + VCOLS), BF)
    pair = sds((2, half, D), BF)
    return call(
        kernel,
        (payload, part, eighth, eighth, pair, pair),
        [SM] * 2 + [VM] * 7 + [HB] * count,
        [
            pltpu.VMEM((8, D), F32),
            pltpu.VMEM((1, VEC), F32),
            pltpu.VMEM((DEVS, 16, VCOLS), F32),
            pltpu.VMEM((ROWS, D), F32),
        ],
        2000000000,
        6000000,
        table,
        sides,
        vec,
        gsum,
        gate_sum,
        gwr,
        ghb,
        x,
        grad_out,
        *after,
        room=16,
    )


def add_upper(keep, upper, after):
    cols = keep.shape[1]
    size = keep.shape[0] // 2

    def kernel(keep_ref, a_ref, b_ref, *refs):
        for r in range(0, size, 16):
            piece = a_ref if r < size // 2 else b_ref
            value = keep_ref[r : r + 16, :].astype(F32) + piece[r % (size // 2) : r % (size // 2) + 16, :].astype(F32)
            refs[len(after)][r : r + 16, :] = value.astype(BF)

    specs = [pl.BlockSpec((size, cols), lambda i: (1, 0))] + [pl.BlockSpec((size // 2, cols), lambda i: (0, 0))] * 2
    return pl.pallas_call(
        kernel,
        grid=(1,),
        out_shape=sds((size, cols), BF),
        in_specs=specs + [HB] * len(after),
        out_specs=pl.BlockSpec((size, cols), lambda i: (0, 0)),
        compiler_params=pltpu.CompilerParams(vmem_limit_bytes=10 * MIB),
        cost_estimate=pl.CostEstimate(flops=1000000, bytes_accessed=2000000, transcendentals=0),
    )(keep, *upper, *after)


def add_part(terms, size, after, places=None):
    cols = terms[0].shape[1]
    count = len(terms)

    def kernel(*refs):
        for r in range(0, size, 16):
            rows = slice(r, r + 16)
            value = refs[0][rows, :].astype(F32)
            for t in refs[1:count]:
                value = value + t[rows, :].astype(F32)
            refs[count + len(after)][rows, :] = value.astype(BF)

    places = places or [1] * count
    blocks = [pl.BlockSpec((size, cols), lambda i, p=p: (p, 0)) for p in places]
    return pl.pallas_call(
        kernel,
        grid=(1,),
        out_shape=sds((size, cols), BF),
        in_specs=blocks + [HB] * len(after),
        out_specs=pl.BlockSpec((size, cols), lambda i: (0, 0)),
        compiler_params=pltpu.CompilerParams(vmem_limit_bytes=10 * MIB),
        cost_estimate=pl.CostEstimate(flops=1000000, bytes_accessed=3000000, transcendentals=0),
    )(*terms, *after)


def line_parts(terms, after):
    cols = terms[0].shape[1]
    count = len(terms)

    def kernel(*refs):
        own, *outs = refs[count + len(after) :]
        for m in range(4):
            rows = slice(16 * m, 16 * (m + 1))
            value = refs[0][rows, :].astype(F32)
            for t in refs[1:count]:
                value = value + t[rows, :].astype(F32)
            if m == 0:
                own[...] = value
            else:
                outs[m - 1][...] = value.astype(BF)

    block = pl.BlockSpec((64, cols), lambda i: (0, 0))
    one = pl.BlockSpec((16, cols), lambda i: (0, 0))
    return pl.pallas_call(
        kernel,
        grid=(1,),
        out_shape=[sds((16, cols), F32)] + [sds((16, cols), BF)] * 3,
        in_specs=[block] * count + [HB] * len(after),
        out_specs=[one] * 4,
        compiler_params=pltpu.CompilerParams(vmem_limit_bytes=8 * MIB),
        cost_estimate=pl.CostEstimate(flops=1000000, bytes_accessed=3000000, transcendentals=0),
    )(*terms, *after)


def line_turn(terms, flip, after):
    count = len(terms)
    cols = terms[0].shape[1]

    def kernel(*refs):
        outs = refs[count + len(after) :]
        for m in range(4):
            rows = slice(16 * m, 16 * (m + 1))
            value = refs[0][rows, :].astype(F32)
            for t in refs[1:count]:
                value = value + t[rows, :].astype(F32)
            value = value.astype(BF)
            outs[0][rows, :] = value
            if flip:
                at = 16 * (m ^ flip)
                outs[1][at : at + 16, :] = value

    block = pl.BlockSpec((64, cols), lambda i: (0, 0))
    number = 2 if flip else 1
    return pl.pallas_call(
        kernel,
        grid=(1,),
        out_shape=[sds((64, cols), BF)] * number,
        in_specs=[block] * count + [HB] * len(after),
        out_specs=[block] * number,
        compiler_params=pltpu.CompilerParams(vmem_limit_bytes=8 * MIB),
        cost_estimate=pl.CostEstimate(flops=1000000, bytes_accessed=1000000, transcendentals=0),
    )(*terms, *after)


def finish_out(own, got, weight, first, second, after):
    def kernel(own_ref, a_ref, b_ref, c_ref, w_ref, m_ref, s_ref, after_ref, left_ref, nw, nm, ns):
        total = own_ref[...] + a_ref[...].astype(F32)
        total = total + (b_ref[...].astype(F32) + c_ref[...].astype(F32))
        left_ref[...] = total[:, 0:HALF]
        for g in range(3):
            rows = slice(16 * g, 16 * (g + 1))
            grad = total[:, HALF + g * D : HALF + (g + 1) * D]
            new = adamw(w_ref[rows, :], grad, m_ref[rows, :], s_ref[rows, :], DENSE_RATE, DENSE_DECAY)
            nw[rows, :] = new[0]
            nm[rows, :] = new[1]
            ns[rows, :] = new[2]

    same = sds(weight.shape, F32)
    return call(
        kernel,
        (sds((16, HALF), F32), same, same, same),
        [VM] * 7 + [HB],
        [],
        1000000,
        2000000,
        own,
        *got,
        weight,
        first,
        second,
        after,
    )


def finish_in(own, got, left, weight, first, second, after):
    def kernel(own_ref, a_ref, b_ref, c_ref, l_ref, w_ref, m_ref, s_ref, after_ref, nw, nm, ns, vec_ref):
        total = own_ref[...] + a_ref[...].astype(F32)
        total = total + (b_ref[...].astype(F32) + c_ref[...].astype(F32))
        vec_ref[...] = total[0:1, HALF:]
        for cols, grad in ((slice(0, HALF), l_ref[...]), (slice(HALF, FF), total[:, 0:HALF])):
            new = adamw(w_ref[:, cols], grad, m_ref[:, cols], s_ref[:, cols], DENSE_RATE, DENSE_DECAY)
            nw[:, cols] = new[0]
            nm[:, cols] = new[1]
            ns[:, cols] = new[2]

    same = sds(weight.shape, F32)
    return call(
        kernel,
        (same, same, same, sds((1, VCOLS), F32)),
        [VM] * 8 + [HB],
        [],
        1000000,
        2000000,
        own,
        *got,
        left,
        weight,
        first,
        second,
        after,
    )


def spatial_update(order, pieces, spatial, first, second, bias, bias_first, bias_second, after):
    count = len(pieces)
    rows = spatial.shape[1]

    def kernel(order_ref, *refs):
        ins = refs[:count]
        w_ref, m_ref, s_ref, bw, bm, bs = refs[count : count + 6]
        nw, nm, ns, nbw, nbm, nbs, flat = refs[count + 6 + len(after) :]
        k = 0
        for piece in ins:
            for j in range(piece.shape[0] // 16):
                at = pl.multiple_of(order_ref[k] * 32, 32)
                block = piece[16 * j : 16 * j + 16, :].astype(F32)
                flat[pl.ds(at, 16), :] = block[:, 0:SCOLS]
                flat[pl.ds(at + 16, 16), :] = block[:, SCOLS:]
                k += 1
        at = TOTAL_AT // 128 * 128
        totals = flat[:, at : at + 128].T[TOTAL_AT - at : TOTAL_AT - at + 1, :]
        for level in range(3):
            got = flat[level * LSTRIDE : level * LSTRIDE + rows, :]
            new = adamw(w_ref[level], got[:, 0:PMAX], m_ref[level], s_ref[level], DENSE_RATE, DENSE_DECAY)
            nw[level] = new[0]
            nm[level] = new[1]
            ns[level] = new[2]
            got = totals[:, level * LSTRIDE : level * LSTRIDE + rows]
            r = slice(level, level + 1)
            new = adamw(bw[r, :], got, bm[r, :], bs[r, :], SMALL_RATE, 0.0)
            nbw[r, :] = new[0]
            nbm[r, :] = new[1]
            nbs[r, :] = new[2]

    same = sds(spatial.shape, F32)
    small = sds(bias.shape, F32)
    return call(
        kernel,
        (same, same, same, small, small, small),
        [SM] + [VM] * (count + 6) + [HB] * len(after),
        [pltpu.VMEM((512, SCOLS), F32)],
        10000000,
        6000000,
        order,
        *pieces,
        spatial,
        first,
        second,
        bias,
        bias_first,
        bias_second,
        *after,
    )


def in_order(blocks, table, rows):
    cols = blocks[0].shape[1]
    whole = jnp.concatenate(blocks, axis=0).reshape(-1, rows, cols)
    back = jnp.zeros_like(table).at[table].set(jnp.arange(table.shape[0], dtype=table.dtype))
    return jnp.take(whole, back, axis=0)


def local(
    patches,
    resolution,
    out_grad,
    dense_in,
    dense_out,
    vectors,
    spatial,
    spatial_bias,
    in_first,
    in_second,
    out_first,
    out_second,
    vec_first,
    vec_second,
    spat_first,
    spat_second,
    bias_first,
    bias_second,
):
    route = Route(lax.axis_size("dp"))
    ndev = 2 * route.n
    fits = route.n == GROUPS
    seq = lax.axis_index("seq").astype(jnp.int32)
    rows = patches.shape[1]
    table = route.table()
    order = route.order(False)[0]
    in_rows = dense_in.shape[0]
    out_rows = dense_out.shape[0]
    vec_len = vectors.shape[0]
    if fits:
        ktable = table
        korder = table // 2
    else:
        ktable = jnp.arange(DEVS, dtype=jnp.int32)
        korder = jnp.arange(DEVS, dtype=jnp.int32) % GROUPS
    sides = jnp.concatenate([seq[None], korder])
    levels = lax.dynamic_slice_in_dim(resolution, seq * 2, 2, 0)

    right_shard, lo_shard = pack_dense(dense_in, dense_out, vectors.reshape(1, vec_len))
    line = [right_shard] + [route.swap(right_shard, (m, m)) for m in route.direct]
    lo_line = [lo_shard] + [route.swap(lo_shard, (m, m)) for m in route.direct]
    spat_own, x_send, g_send = pack_images(sides, spatial, spatial_bias.reshape(3, rows, 1), patches, out_grad)
    x_got = route.cross(x_send)
    g_got = route.cross(g_send)
    spat_got = route.cross(spat_own)
    if fits:
        right_blocks, passed = route.widen_in_turn(stack(line, []))
        lo_blocks = route.widen_direct(stack(lo_line, [passed]))
    else:
        right_blocks = route.widen(jnp.concatenate(line, axis=0))
        lo_blocks = route.widen(jnp.concatenate(lo_line, axis=0))
    right_blocks = right_blocks + [route.cross(b) for b in right_blocks]
    if not fits:
        lo_blocks = lo_blocks + [route.cross(b) for b in lo_blocks]
    if not fits:
        whole = in_order(right_blocks, table, in_rows)
        all_vec = whole[:, 0, HALF : HALF + vec_len].reshape(DEVS, 1, VPER)
        all_vec = jnp.pad(all_vec, ((0, 0), (0, 15), (0, VCOLS - VPER))).reshape(D, VCOLS)
        right_blocks = [jnp.concatenate([whole[:, :, :HALF].reshape(D, HALF), all_vec], axis=1)]
        whole = in_order(lo_blocks, table, in_rows)
        outs = whole[:, :, HALF:].reshape(ndev, in_rows, 3, D).transpose(0, 2, 1, 3).reshape(DEVS, 3, 16, D)
        outs = outs.transpose(0, 2, 1, 3).reshape(D, HALF)
        lo_blocks = [jnp.concatenate([whole[:, :, :HALF].reshape(D, HALF), outs], axis=1)]

    x, grad_out, h, v, slope, part, weight_right, vec = gate_forward(
        ktable, sides, patches, x_got, out_grad, g_got, right_blocks
    )
    gate, hat, scale, spat, mm = gate_norm(levels, sides, vec, v, part, spat_own, spat_got, [])
    if fits:
        lo_blocks = lo_blocks + [route.cross(lo_blocks[0]), route.cross(stack(lo_blocks[1:], [mm]))]
    gs, gated, q, gb, wl, wo, sp_keep, sp_send, gsum = middle(ktable, levels, sides, vec, h, spat, gate, grad_out, lo_blocks)
    near, far = route.low[-1], route.low[0]
    after = [[] for _ in range(5)]
    if fits:
        sp_got = route.cross(sp_send)
        sp_part = add_part([sp_keep, sp_got], 128, [])
        sp_terms = [sp_keep, sp_got, route.swap(sp_part, near)]
        after[0] = [sp_part]
    gwl, mixed_stay, mixed_away, gh = weight_grads(levels, sides, vec, gated, q, h, wl, wo, x, rows, after[0])
    if fits:
        sp_part = add_part(sp_terms, 64, [gh])
        sp_terms.append(route.swap(sp_part, far))
        after[1] = [sp_part]
    lo_keep, lo_send, lo_up = out_grads(ktable, gated, gb, gwl, after[1])
    mixed_got = route.cross(mixed_away)
    if fits:
        lo_up = route.cross(lo_up)
        lo_terms = [lo_keep, route.cross(lo_send)]
        lo_part = add_part([lo_keep, lo_up], 128, [], [1, 0])
        lo_terms.append(route.swap(lo_part, near))
        after[2] = [lo_part]
    gp, gate_sum = gate_backward(vec, gs, mm, hat, slope, scale, after[2])
    if fits:
        sp_own, sp_out = line_turn(sp_terms, 1, [gate_sum])
        sp_terms = [sp_own, route.swap(sp_out, (route.direct[0],) * 2)]
        after[3] = [sp_own, mixed_got]
    gwr, ghb = in_grads(gp, h, weight_right, gh, after[3])
    if fits:
        sp_own, sp_out = line_turn(sp_terms, 2, [gwr])
        sp_terms = [sp_own, route.swap(sp_out, (route.direct[1],) * 2)]
        lo_part = add_part(lo_terms, 64, [sp_own])
        lo_terms.append(route.swap(lo_part, far))
        after[4] = [lo_part]
    right_keep, right_send, up_a, up_b, grad_stay, grad_away = in_backward(
        ktable, sides, vec, gsum, gate_sum, gwr, ghb, x, grad_out, rows, after[4]
    )
    grad_got = route.cross(grad_away)
    if fits:
        upper = [route.cross(up_a), route.cross(up_b)]
        right_terms = [right_keep, route.cross(right_send)]
        lo_own, *sends = line_parts(lo_terms, [right_keep])
        lo_got = [route.swap(p, (m, m)) for p, m in zip(sends, route.direct)]
        right_part = add_upper(right_keep, upper, [lo_own])
        right_terms.append(route.swap(right_part, near))
        right_part = add_part(right_terms, 64, [grad_got])
        right_terms.append(route.swap(right_part, far))
        (sp_sum,) = line_turn(sp_terms, 0, [right_part])
        spat_pieces = route.widen(sp_sum)
        left_sum, *new_out = finish_out(lo_own, lo_got, dense_out, out_first, out_second, sp_sum)
        right_own, *sends = line_parts(right_terms, [left_sum])
        right_got = [route.swap(p, (m, m)) for p, m in zip(sends, route.direct)]
        korder = order
        after = [left_sum]
    else:
        both = jnp.concatenate([lo_keep, lo_send, lo_up])
        outs = both[:, HALF:LO].reshape(DEVS, 16, 3, D).transpose(0, 2, 1, 3).reshape(ndev, out_rows, D)
        outs = jnp.take(outs, table, axis=0).reshape(HALF, D)
        out_sum = route.scatter(outs[: HALF // 2], outs[HALF // 2 :])
        lefts = jnp.take(both[:, :HALF].reshape(ndev, in_rows, HALF), table, axis=0).reshape(D, HALF)
        left_sum = route.scatter(lefts[: D // 2], lefts[D // 2 :])
        per = 512 // route.n

        def spat_blocks(part, flip):
            flat = part.reshape(GROUPS, 16, 2, SCOLS).transpose(0, 2, 1, 3).reshape(route.n, per, SCOLS)
            return jnp.take(flat, route.order(flip)[0], axis=0).reshape(512, SCOLS)

        spat_part = route.scatter(spat_blocks(sp_keep, False), spat_blocks(sp_send, True)).astype(BF)
        flat = in_order(route.spread(spat_part), order, per).reshape(GROUPS, 2, 16, SCOLS)
        spat_pieces = [flat.transpose(0, 2, 1, 3).reshape(GROUPS * 16, SPC)]
        korder = jnp.arange(GROUPS, dtype=jnp.int32)
        after = []
        both = jnp.concatenate([right_keep, right_send, up_a, up_b])
        vecs = jnp.take(both[::16, HALF : HALF + VPER].reshape(ndev, vec_len), table, axis=0)
        vec_sum = route.scatter(vecs[: route.n], vecs[route.n :]).reshape(vec_len)
        rights = jnp.take(both[:, :HALF].reshape(ndev, in_rows, HALF), table, axis=0).reshape(D, HALF)
        right_sum = route.scatter(rights[: D // 2], rights[D // 2 :])
        in_sum = jnp.concatenate([left_sum, right_sum], axis=1)
        new_in = adamw(dense_in, in_sum, in_first, in_second, DENSE_RATE, DENSE_DECAY)
        new_out = adamw(dense_out, out_sum, out_first, out_second, DENSE_RATE, DENSE_DECAY)

    def whole_images(stays, came):
        return jnp.concatenate([jnp.where(seq == 0, stays, came), jnp.where(seq == 0, came, stays)], axis=0)

    mixed = whole_images(mixed_stay, mixed_got)
    patches_grad = whole_images(grad_stay, grad_got)
    spat_new = spatial_update(
        korder, spat_pieces, spatial, spat_first, spat_second, spatial_bias, bias_first, bias_second, after
    )
    if fits:
        *new_in, vec_sum = finish_in(right_own, right_got, left_sum, dense_in, in_first, in_second, spat_new[0])
        vec_sum = vec_sum[0, :vec_len]
    new_vec = adamw(vectors, vec_sum, vec_first, vec_second, SMALL_RATE, 0.0)
    return (mixed, patches_grad) + tuple(new_in) + tuple(new_out) + new_vec + tuple(spat_new)


def solution(mesh):
    rows3 = P("dp", "seq", None)
    dense = P(AXES, None)
    vec = P(AXES)
    spat = P(None, "seq", None)
    bias = P(None, "seq")
    in_specs = (rows3, P("dp"), rows3, dense, dense, vec, spat, bias)
    in_specs += (dense,) * 4 + (vec,) * 2 + (spat,) * 2 + (bias,) * 2
    out_specs = (rows3, rows3) + (dense,) * 6 + (vec,) * 3 + (spat,) * 3 + (bias,) * 3
    return jax.shard_map(local, mesh=mesh, in_specs=in_specs, out_specs=out_specs, check_vma=False)
```

```python
import functools

import jax
import jax.numpy as jnp
from jax import lax
from jax.experimental import pallas as pl
from jax.experimental.pallas import tpu as pltpu
from jax.sharding import PartitionSpec as P

D = 512
FF = 3072
HALF = 1536
PMAX = 324
PPAD = 336
P_MID = 196
P_LOW = 100
VCOLS = 256
ROWS = 2 * PPAD
GROUPS = 16
DEVS = 2 * GROUPS
VPER = 240
SCOLS = 384
BIAS_AT = 336
TOTAL_AT = 324
LSTRIDE = 168
MIB = 1024 * 1024
STEP = 10

NORM_EPS = 1e-05
BETA_ONE = 0.9
BETA_TWO = 0.99
ADAM_EPS = 1e-08
DENSE_RATE = 0.02
SMALL_RATE = 0.2
DENSE_DECAY = 0.05

BF = jnp.bfloat16
F32 = jnp.float32
AXES = ("dp", "seq")
VM = pl.BlockSpec(memory_space=pltpu.VMEM)
SM = pl.BlockSpec(memory_space=pltpu.SMEM)
HB = pl.BlockSpec(memory_space=pl.ANY)


class Route:
    def __init__(self, n):
        bits = n.bit_length() - 1
        assert n == 1 << bits and bits >= 2
        self.n = n
        top = n // 4
        self.direct = [top, 2 * top, 3 * top]
        low = [1 << b for b in range(bits - 2)]
        self.low = list(zip(low[::-1], low))
        masks = [(0, 0)] + [(m, m) for m in self.direct]
        for step in self.low:
            masks = masks + [(m[0] ^ step[0], m[1] ^ step[1]) for m in masks]
        self.masks = masks

    def swap(self, block, mask):
        pairs = []
        for dp in range(self.n):
            for seq in range(2):
                pairs.append((dp * 2 + seq, (dp ^ mask[seq]) * 2 + seq))
        return lax.ppermute(block, AXES, pairs)

    def cross(self, block):
        pairs = []
        for dp in range(self.n):
            for seq in range(2):
                pairs.append((dp * 2 + seq, dp * 2 + 1 - seq))
        return lax.ppermute(block, AXES, pairs)

    def order(self, seq_flip):
        place = lax.axis_index("dp")
        seq = lax.axis_index("seq")
        if seq_flip:
            seq = 1 - seq
        zero = jnp.array([m[0] for m in self.masks], jnp.int32)
        one = jnp.array([m[1] for m in self.masks], jnp.int32)
        return place ^ jnp.where(seq == 0, zero, one), seq

    def table(self):
        mine, seq = self.order(False)
        other, flip = self.order(True)
        return jnp.concatenate([mine * 2 + seq, other * 2 + flip])

    def spread(self, shard):
        first = jnp.concatenate([shard] + [self.swap(shard, (m, m)) for m in self.direct], axis=0)
        return self.widen(first)

    def widen(self, first):
        blocks = [first]
        for step in self.low:
            blocks = blocks + [self.swap(b, step) for b in blocks]
        return blocks

    def widen_in_turn(self, first):
        second = self.swap(first, self.low[0])
        third = self.swap(first, self.low[1])
        passed = stack([second], [third])
        return [first, second, third, self.swap(passed, self.low[1])], passed

    def widen_direct(self, first):
        return [first] + [self.swap(first, m) for m in self.plane()]

    def plane(self):
        one, two = self.low
        return [one, two, (one[0] ^ two[0], one[1] ^ two[1])]

    def gather(self, shard):
        blocks = self.spread(shard)
        return blocks + [self.cross(b) for b in blocks]

    def collect(self, terms):
        cur = terms[0].shape[0]
        rows = cur // self.n

        def part(lower, upper):
            total = terms[0][lower:upper].astype(F32)
            for t in terms[1:]:
                total = total + t[lower:upper].astype(F32)
            return total

        terms = list(terms)
        for step in reversed(self.low):
            half = cur // 2
            terms.append(self.swap(part(half, cur).astype(BF), step))
            cur = half
        got = []
        for j, m in enumerate(self.direct):
            got.append(self.swap(part((j + 1) * rows, (j + 2) * rows).astype(BF), (m, m)))
        total = part(0, rows)
        return (total + got[0].astype(F32)) + (got[1].astype(F32) + got[2].astype(F32))

    def scatter(self, keep, send):
        return self.collect([keep, self.cross(send)])


def dot(a, b, dims):
    return lax.dot_general(a, b, (dims, ((), ())), preferred_element_type=F32)


NN = ((1,), (0,))
NT = ((1,), (1,))
TN = ((0,), (0,))


def gelu_parts(p):
    bell = jnp.exp(p * p * -0.5)
    d = 1.0 + jnp.abs(p) * (0.3275911 * 0.7071067811865476)
    t = pl.reciprocal(d, approx=True)
    t = t * (2.0 - d * t)
    poly = t * (
        0.127414796
        + t * (-0.142248368 + t * (0.7107068705 + t * (-0.7265760135 + t * 0.5307027145)))
    )
    tail = poly * bell
    phi_sum = jnp.where(p >= 0.0, 1.0 - tail, tail)
    return p * phi_sum, phi_sum + p * bell * 0.3989422804014327


def count_of(level):
    return jnp.where(level == 0, P_LOW, jnp.where(level == 1, P_MID, PMAX))


def masked_mix(mix, count):
    i = lax.broadcasted_iota(jnp.int32, (PPAD, SCOLS), 0)
    j = lax.broadcasted_iota(jnp.int32, (PPAD, SCOLS), 1)
    return jnp.where((i < count) & (j < count), mix.astype(F32), 0.0).astype(BF)


def live_rows(count, shape, start=0):
    return lax.broadcasted_iota(jnp.int32, shape, 0) + start < count


def live_mask(levels_ref, b, width):
    return live_rows(count_of(levels_ref[b]), (PPAD, width))


def fold(value):
    total = value[:, 0:128]
    for n in range(128, value.shape[1], 128):
        total = total + value[:, n : n + 128]
    return total


def spread_sum(ref, factor):
    return jnp.broadcast_to(jnp.sum(ref[...], axis=-1, keepdims=True) * factor, ref.shape)


def wide(value, times):
    return jnp.concatenate([value] * times, axis=1)


def start_blocks(table_ref, pieces, rows, cols, target, sem, extra=0):
    copies = []
    k = 0
    for piece in pieces:
        for j in range(piece.shape[0] // 16):
            at = pl.multiple_of(table_ref[k] * rows, 16)
            c = pltpu.make_async_copy(
                piece.at[pl.ds(j * 16, 16), pl.ds(cols[0], cols[1])], target.at[pl.ds(at + extra, 16)], sem.at[k]
            )
            c.start()
            copies.append(c)
            k += 1
    return copies


def row_loop(step, body):
    def run(i, carry):
        body(pl.multiple_of(i * step, step))
        return carry

    lax.fori_loop(0, ROWS // step, run, 0)


def call(kernel, out_shape, in_specs, scratch, flops, nbytes, *args, room=12):
    vm = pl.BlockSpec(memory_space=pltpu.VMEM)
    return pl.pallas_call(
        kernel,
        out_shape=out_shape,
        in_specs=in_specs,
        out_specs=jax.tree.map(lambda _: vm, out_shape),
        scratch_shapes=scratch,
        compiler_params=pltpu.CompilerParams(vmem_limit_bytes=room * MIB),
        cost_estimate=pl.CostEstimate(flops=flops, bytes_accessed=nbytes, transcendentals=0),
    )(*args)


def norm_parts(values):
    center = values - jnp.mean(values, axis=-1, keepdims=True)
    scale = lax.rsqrt(jnp.mean(center * center, axis=-1, keepdims=True) + NORM_EPS)
    return center * scale, scale


VSEG = {
    "g1": (0, D),
    "b1": (D, D),
    "c1l": (2 * D, HALF),
    "c1r": (2 * D + HALF, HALF),
    "g2": (2 * D + FF, HALF),
    "b2": (2 * D + FF + HALF, HALF),
    "c2": (2 * D + FF + 2 * HALF, D),
}
VEC = 2 * D + FF + 2 * HALF + D


def seg(ref, name):
    start, size = VSEG[name]
    return ref[0:1, start : start + size]

def adamw(weight, grad, first, second, rate, decay):
    first = BETA_ONE * first + (1.0 - BETA_ONE) * grad
    second = BETA_TWO * second + (1.0 - BETA_TWO) * grad * grad
    first_hat = first / (1.0 - BETA_ONE**STEP)
    second_hat = second / (1.0 - BETA_TWO**STEP)
    weight = weight - rate * (first_hat / (jnp.sqrt(second_hat) + ADAM_EPS) + decay * weight)
    return (weight, first, second)


CHUNK = 16
TILE = 256
BODY = 32
STRIPE = 112
LO = 2 * HALF
SPC = 2 * SCOLS


def sds(shape, dtype):
    return jax.ShapeDtypeStruct(shape, dtype)


def pack_dense(dense_in, dense_out, vec_row):
    rows = dense_in.shape[0]
    per = vec_row.shape[1]

    def kernel(w_hbm, o_hbm, v_hbm, out_ref, lo_ref, w_ref, o_ref, v_ref, row, sem):
        copies = [
            pltpu.make_async_copy(src, dst, sem.at[k])
            for k, (src, dst) in enumerate(((w_hbm, w_ref), (o_hbm, o_ref), (v_hbm, v_ref)))
        ]
        for c in copies:
            c.start()
        row[...] = jnp.zeros_like(row)
        for c in copies:
            c.wait()
        out_ref[:, 0:HALF] = w_ref[:, HALF:].astype(BF)
        row[0:1, 0:per] = v_ref[...]
        out_ref[:, HALF : HALF + VCOLS] = row[...].astype(BF)
        lo_ref[:, 0:HALF] = w_ref[:, 0:HALF].astype(BF)
        for g in range(3):
            lo_ref[:, HALF + g * D : HALF + (g + 1) * D] = o_ref[g * rows : (g + 1) * rows, :].astype(BF)

    scratch = [
        pltpu.VMEM(dense_in.shape, F32),
        pltpu.VMEM(dense_out.shape, F32),
        pltpu.VMEM(vec_row.shape, F32),
        pltpu.VMEM((rows, VCOLS), F32),
        pltpu.SemaphoreType.DMA((3,)),
    ]
    shape = (sds((rows, HALF + VCOLS), BF), sds((rows, LO), BF))
    return call(kernel, shape, [HB] * 3, scratch, 1000, 600000, dense_in, dense_out, vec_row, room=60)


def pack_images(sides, spatial, bias_col, patches, out_grad):
    half = patches.shape[1]

    def kernel(sides_ref, s_ref, b_ref, x_ref, g_ref, spat_ref, xs_ref, gs_ref, buf):
        away = 2 - 2 * sides_ref[0]
        for b in range(2):
            xs_ref[b] = x_ref[away + b]
            gs_ref[b] = g_ref[away + b]
        buf[...] = jnp.zeros_like(buf)
        for level in range(3):
            buf[:, 0:PMAX] = s_ref[level]
            rest = b_ref[level]
            for c in range(3):
                piece = rest.astype(BF).astype(F32)
                buf[:, BIAS_AT + c : BIAS_AT + c + 1] = piece
                rest = rest - piece
            spat_ref[level] = buf[...].astype(BF)

    pair = sds((2, half, D), BF)
    return call(
        kernel,
        (sds((3, half, SCOLS), BF), pair, pair),
        [SM] + [VM] * 4,
        [pltpu.VMEM((half, SCOLS), F32)],
        1000,
        3000000,
        sides,
        spatial,
        bias_col,
        patches,
        out_grad,
    )


def stack(pieces, after):
    count = len(pieces)
    rows, cols = pieces[0].shape

    def kernel(*refs):
        out = refs[count + len(after)]
        for k in range(count):
            out[k * rows : (k + 1) * rows, :] = refs[k][...]

    specs = [VM] * count + [HB] * len(after)
    return call(kernel, sds((count * rows, cols), BF), specs, [], 1000, 1000000, *pieces, *after)


def two_halves(is_first, own, got):
    own = own.astype(F32)
    got = got.astype(F32)
    return jnp.where(is_first, own, got), jnp.where(is_first, got, own)


def gate_norm(levels, sides, vec, v, part, spat_own, spat_got, after):
    half = spat_own.shape[1]
    count = len(after)

    def kernel(levels_ref, sides_ref, vec_ref, v_ref, part_ref, so_ref, sg_ref, *refs):
        gate_ref, hat_ref, scale_ref, spat_ref, mm_ref, mixf, mean, buf = refs[count:]
        is_first = sides_ref[0] == 0
        g_start = VSEG["g2"][0]
        b_start = VSEG["b2"][0]
        mean[...] = spread_sum(part_ref, 1.0 / HALF)

        def square_rows(r):
            for k in range(0, BODY, CHUNK):
                rows = pl.ds(r + k, CHUNK)
                mid = mean[rows, :]
                total = jnp.zeros((CHUNK, 128), F32)
                for n in range(0, HALF, 128):
                    center = v_ref[rows, n : n + 128] - mid
                    total = total + center * center
                buf[rows, :] = total

        row_loop(BODY, square_rows)
        scale_ref[...] = lax.rsqrt(spread_sum(buf, 1.0 / HALF) + NORM_EPS)

        def gate_rows(r):
            for k in range(0, BODY, CHUNK):
                rows = pl.ds(r + k, CHUNK)
                mid = wide(mean[rows, :], 2)
                scale = wide(scale_ref[rows, :], 2)
                for n in range(0, HALF, TILE):
                    hat = (v_ref[rows, n : n + TILE] - mid) * scale
                    hat_ref[rows, n : n + TILE] = hat.astype(BF)
                    gate = hat * vec_ref[0:1, g_start + n : g_start + n + TILE]
                    gate = (gate + vec_ref[0:1, b_start + n : b_start + n + TILE]).astype(BF)
                    gate_ref[rows, n : n + TILE] = gate

        row_loop(BODY, gate_rows)
        gate_ref[ROWS:, :] = jnp.zeros((SCOLS - PPAD, HALF), BF)
        for b in range(2):
            level = levels_ref[b]
            live = count_of(level)
            one, two = two_halves(is_first, so_ref[level], sg_ref[level])
            mixf[0:half, :] = one
            mixf[half : 2 * half, :] = two
            mixf[2 * half :, :] = jnp.zeros((PPAD - 2 * half, SCOLS), F32)
            bias = jnp.sum(mixf[:, TOTAL_AT:], axis=-1, keepdims=True)
            mm_ref[b] = masked_mix(mixf[...], live)

            def mix_tile(n, carry):
                cols = pl.ds(pl.multiple_of(n * 512, 512), 512)
                got = dot(mm_ref[b], gate_ref[b * PPAD : b * PPAD + SCOLS, cols], NN) + bias
                got = jnp.where(live_rows(live, (PPAD, 512)), got, 0.0)
                spat_ref[b * PPAD : (b + 1) * PPAD, cols] = got.astype(BF)
                return carry

            lax.fori_loop(0, HALF // 512, mix_tile, 0)

    return call(
        kernel,
        (
            sds((ROWS + SCOLS - PPAD, HALF), BF),
            sds((ROWS, HALF), BF),
            sds((ROWS, 128), F32),
            sds((ROWS, HALF), BF),
            sds((2, PPAD, SCOLS), BF),
        ),
        [SM] * 2 + [VM] * 5 + [HB] * count,
        [pltpu.VMEM((PPAD, SCOLS), F32), pltpu.VMEM((ROWS, 128), F32), pltpu.VMEM((ROWS, 128), F32)],
        6000000000,
        12000000,
        levels,
        sides,
        vec,
        v,
        part,
        spat_own,
        spat_got,
        *after,
        room=22,
    )


def gate_forward(table, sides, patches, x_got, out_grad, g_got, pieces):
    count = len(pieces)
    half = patches.shape[1]

    def kernel(table_ref, sides_ref, p_ref, xg_ref, o_ref, gg_ref, *refs):
        ins = refs[:count]
        outs = refs[count : count + 8]
        x_ref, og_ref, h_ref, pre, slope_ref, part, w_ref, vec_ref = outs
        vblk, xbuf, sem, vsem = refs[count + 8 :]
        vcopies = start_blocks(table_ref, ins, 16, (HALF, VCOLS), vblk, vsem)
        copies = start_blocks(table_ref, ins, 16, (0, HALF), w_ref, sem)
        me = sides_ref[0]
        is_first = me == 0

        for src, got, target in ((o_ref, gg_ref, og_ref), (p_ref, xg_ref, x_ref)):
            for b in range(2):
                one, two = two_halves(is_first, src[2 * me + b], got[b])
                xbuf[b * PPAD : b * PPAD + half, :] = one
                xbuf[b * PPAD + half : b * PPAD + 2 * half, :] = two
                xbuf[b * PPAD + 2 * half : (b + 1) * PPAD, :] = jnp.zeros((PPAD - 2 * half, D), F32)
            target[...] = xbuf[...].astype(BF)
        for c in vcopies:
            c.wait()
        for s in range(DEVS):
            row = vblk[16 * s : 16 * s + 16, :].astype(F32)[0:1, :VPER]
            vec_ref[0:1, VPER * s : VPER * s + VPER] = row

        def norm_one(r):
            hat, _ = norm_parts(xbuf[pl.ds(r, STRIPE), :])
            h_ref[pl.ds(r, STRIPE), :] = (hat * seg(vec_ref, "g1") + seg(vec_ref, "b1")).astype(BF)

        row_loop(STRIPE, norm_one)
        for c in copies:
            c.wait()
        c_start = VSEG["c1r"][0]

        def matmul(n, carry):
            at = pl.multiple_of(n * TILE, TILE)
            pre[:, pl.ds(at, TILE)] = dot(h_ref[...], w_ref[:, pl.ds(at, TILE)], NN)
            return carry

        lax.fori_loop(0, HALF // TILE, matmul, 0)

        def gelu_rows(r):
            for k in range(0, BODY, CHUNK):
                rows = pl.ds(r + k, CHUNK)
                total = jnp.zeros((CHUNK, 128), F32)
                for n in range(0, HALF, TILE):
                    v, slope = gelu_parts(pre[rows, n : n + TILE] + vec_ref[0:1, c_start + n : c_start + n + TILE])
                    pre[rows, n : n + TILE] = v
                    slope_ref[rows, n : n + TILE] = slope.astype(BF)
                    total = total + fold(v)
                part[rows, :] = total

        row_loop(BODY, gelu_rows)

    broad = sds((ROWS, HALF), BF)
    narrow = sds((ROWS, D), BF)
    out_shape = (
        narrow,
        narrow,
        narrow,
        sds((ROWS, HALF), F32),
        broad,
        sds((ROWS, 128), F32),
        sds((D, HALF), BF),
        sds((1, VEC), F32),
    )
    scratch = [
        pltpu.VMEM((D, VCOLS), BF),
        pltpu.VMEM((ROWS, D), F32),
        pltpu.SemaphoreType.DMA((DEVS,)),
        pltpu.SemaphoreType.DMA((DEVS,)),
    ]
    return call(
        kernel,
        out_shape,
        [SM] * 2 + [VM] * 4 + [HB] * count,
        scratch,
        10000000000,
        20000000,
        table,
        sides,
        patches,
        x_got,
        out_grad,
        g_got,
        *pieces,
        room=26,
    )


def split_rows(target, first, second, seq, value):
    half = first.shape[1]
    target[...] = value
    for b in range(2):
        one = target[b * PPAD : b * PPAD + half, :]
        two = target[b * PPAD + half : b * PPAD + 2 * half, :]
        first[b] = jnp.where(seq == 0, one, two).astype(BF)
        second[b] = jnp.where(seq == 0, two, one).astype(BF)


def middle(table, levels, sides, vec, h, spat, gate, grad_out, pieces):
    count = len(pieces)

    def kernel(table_ref, levels_ref, sides_ref, vec_ref, h_ref, spat_ref, gate_ref, og_ref, *refs):
        ins = refs[:count]
        gs_ref, gated_ref, q_ref, gb, wl, wo, keep, send, gsum_ref = refs[count : count + 9]
        pbuf, gbuf, cells, flat, sem = refs[count + 9 :]
        copies = start_blocks(table_ref, ins, 16, (0, HALF), wl, sem.at[0])
        for g in range(3):
            copies += start_blocks(table_ref, ins, 48, (HALF + g * D, D), wo, sem.at[1 + g], 16 * g)
        for b in range(2):
            rows = slice(b * PPAD, (b + 1) * PPAD)
            gb[rows, :] = jnp.where(live_mask(levels_ref, b, D), og_ref[rows, :].astype(F32), 0.0).astype(BF)
        gsum_ref[0:1, HALF : HALF + D] = jnp.sum(gb[...].astype(F32), axis=0, keepdims=True)
        cells[...] = jnp.zeros_like(cells)
        flat[...] = jnp.zeros_like(flat)
        for c in copies:
            c.wait()
        c_start = VSEG["c1l"][0]

        def tile(n, carry):
            at = pl.multiple_of(n * TILE, TILE)
            cols = pl.ds(at, TILE)
            pbuf[...] = dot(h_ref[...], wl[:, cols], NN)
            gbuf[...] = dot(gb[...], wo[cols, :], NT)
            shift = vec_ref[0:1, pl.ds(c_start + at, TILE)]
            total = jnp.zeros((CHUNK, TILE), F32)
            for k in range(0, ROWS, CHUNK):
                r = slice(k, k + CHUNK)
                u, slope = gelu_parts(pbuf[r, :] + shift)
                sp = spat_ref[r, cols].astype(F32)
                gg = gbuf[r, :]
                gated_ref[r, cols] = (u * sp).astype(BF)
                gs_ref[r, cols] = (gg * u).astype(BF)
                q = (gg * sp * slope).astype(BF)
                q_ref[r, cols] = q
                total = total + q.astype(F32)
            gsum_ref[0:1, cols] = jnp.sum(total, axis=0, keepdims=True)
            return carry

        lax.fori_loop(0, HALF // TILE, tile, 0)

        me = sides_ref[0]
        for b in range(2):
            level = levels_ref[b]
            count_b = count_of(level)
            gs = gs_ref[b * PPAD : (b + 1) * PPAD, :]
            got = dot(gs, gate_ref[b * PPAD : (b + 1) * PPAD, :], NT)
            sums = jnp.sum(gs.astype(F32), axis=-1, keepdims=True)
            j = lax.broadcasted_iota(jnp.int32, (PPAD, PPAD), 1)
            got = jnp.where(j < count_b, got, jnp.where(j == TOTAL_AT, sums, 0.0))
            cells[level, :, 0:PPAD] += got
        part = PMAX // 2
        for level in range(3):
            for k in range(2):
                flat[k, level * LSTRIDE : level * LSTRIDE + part, 0:PPAD] = cells[level, k * part : (k + 1) * part, 0:PPAD]
        for k in range(DEVS):
            target, side = (keep, me) if k < GROUPS else (send, 1 - me)
            r = pl.ds(k % GROUPS * 16, 16)
            block = flat[side, pl.ds(pl.multiple_of(sides_ref[1 + k] * 32, 32), 32), :].astype(BF)
            target[r, 0:SCOLS] = block[0:16]
            target[r, SCOLS:SPC] = block[16:32]

    broad = sds((ROWS, HALF), BF)
    payload = sds((D // 2, SPC), BF)
    out_shape = (
        broad,
        broad,
        broad,
        sds((ROWS, D), BF),
        sds((D, HALF), BF),
        sds((HALF, D), BF),
        payload,
        payload,
        sds((1, HALF + D), F32),
    )
    scratch = [
        pltpu.VMEM((ROWS, TILE), F32),
        pltpu.VMEM((ROWS, TILE), F32),
        pltpu.VMEM((3, PPAD, SCOLS), F32),
        pltpu.VMEM((2, 512, SCOLS), F32),
        pltpu.SemaphoreType.DMA((4, DEVS)),
    ]
    return call(
        kernel,
        out_shape,
        [SM] * 3 + [VM] * 5 + [HB] * count,
        scratch,
        8000000000,
        16000000,
        table,
        levels,
        sides,
        vec,
        h,
        spat,
        gate,
        grad_out,
        *pieces,
        room=28,
    )


def weight_grads(levels, sides, vec, gated, q, h, wl, wo, x, half, after):
    count = len(after)

    def kernel(levels_ref, sides_ref, vec_ref, t_ref, q_ref, h_ref, wl_ref, wo_ref, x_ref, *refs):
        gwl, stay_ref, away_ref, gh_ref, branch = refs[count:]

        def in_tile(n, carry):
            cols = pl.ds(pl.multiple_of(n * TILE, TILE), TILE)
            gwl[cols, :] = dot(h_ref[:, cols], q_ref[...], TN).astype(BF)
            branch[:, cols] = dot(t_ref[...], wo_ref[:, cols], NN)
            gh_ref[:, cols] = dot(q_ref[...], wl_ref[cols, :], NT)
            return carry

        lax.fori_loop(0, D // TILE, in_tile, 0)
        me = sides_ref[0]
        live = jnp.concatenate([live_mask(levels_ref, b, D) for b in range(2)], axis=0)
        out = branch[...] + seg(vec_ref, "c2")
        split_rows(branch, stay_ref, away_ref, me, x_ref[...].astype(F32) + jnp.where(live, out, 0.0))

    pair = sds((2, half, D), BF)
    return call(
        kernel,
        (sds((D, HALF), BF), pair, pair, sds((ROWS, D), F32)),
        [SM] * 2 + [VM] * 7 + [HB] * count,
        [pltpu.VMEM((ROWS, D), F32)],
        4000000000,
        12000000,
        levels,
        sides,
        vec,
        gated,
        q,
        h,
        wl,
        wo,
        x,
        *after,
        room=12,
    )


def out_grads(table, gated, gb, gwl, after):
    count = len(after)

    def kernel(table_ref, t_ref, gb_ref, gwl_ref, *refs):
        keep, send, send_up, gwo = refs[count:]

        def out_tile(n, carry):
            cols = pl.ds(pl.multiple_of(n * TILE, TILE), TILE)
            gwo[cols, :] = dot(t_ref[:, cols], gb_ref[...], TN).astype(BF)
            return carry

        lax.fori_loop(0, HALF // TILE, out_tile, 0)
        for k in range(DEVS):
            dev = table_ref[k]
            target = keep if k < GROUPS else send if k < GROUPS * 3 // 2 else send_up
            r = pl.ds(k % (GROUPS if k < GROUPS else GROUPS // 2) * 16, 16)
            target[r, 0:HALF] = gwl_ref[pl.ds(pl.multiple_of(dev * 16, 16), 16), :]
            for g in range(3):
                target[r, HALF + g * D : HALF + (g + 1) * D] = gwo[pl.ds(pl.multiple_of(dev * 48 + 16 * g, 16), 16), :]

    payload = sds((D // 2, LO), BF)
    part = sds((D // 4, LO), BF)
    return call(
        kernel,
        (payload, part, part),
        [SM] + [VM] * 3 + [HB] * count,
        [pltpu.VMEM((HALF, D), BF)],
        2000000000,
        8000000,
        table,
        gated,
        gb,
        gwl,
        *after,
        room=10,
    )


def gate_backward(vec, gs, mm, hat, slope, scale, after):
    count = len(after)

    def kernel(vec_ref, gs_ref, mm_ref, hat_ref, slope_ref, scale_ref, *refs):
        gp, gsum_ref, dbuf, one, two, acc = refs[count:]

        for b in range(2):

            def mix_tile(n, carry):
                cols = pl.ds(pl.multiple_of(n * 512, 512), 512)
                got = dot(mm_ref[b], gs_ref[b * PPAD : (b + 1) * PPAD, cols], TN)
                dbuf[b * PPAD : (b + 1) * PPAD, cols] = got[0:PPAD]
                return carry

            lax.fori_loop(0, HALF // 512, mix_tile, 0)
        g_start = VSEG["g2"][0]

        def sum_rows(r):
            for k in range(0, BODY, CHUNK):
                rows = pl.ds(r + k, CHUNK)
                a = jnp.zeros((CHUNK, 128), F32)
                c = jnp.zeros((CHUNK, 128), F32)
                for n in range(0, HALF, TILE):
                    e = dbuf[rows, n : n + TILE] * vec_ref[0:1, g_start + n : g_start + n + TILE]
                    a = a + fold(e)
                    c = c + fold(e * hat_ref[rows, n : n + TILE].astype(F32))
                one[rows, :] = a
                two[rows, :] = c

        row_loop(BODY, sum_rows)
        one[...] = spread_sum(one, 1.0 / HALF)
        two[...] = spread_sum(two, 1.0 / HALF)
        acc[...] = jnp.zeros_like(acc)

        def grad_rows(r):
            for n in range(0, HALF, TILE):
                gain = vec_ref[0:1, g_start + n : g_start + n + TILE]
                sums = [jnp.zeros((CHUNK, TILE), F32) for _ in range(3)]
                for k in range(0, BODY, CHUNK):
                    rows = pl.ds(r + k, CHUNK)
                    d = dbuf[rows, n : n + TILE]
                    xh = hat_ref[rows, n : n + TILE].astype(F32)
                    inner = d * gain - wide(one[rows, :], 2) - xh * wide(two[rows, :], 2)
                    q = inner * wide(scale_ref[rows, :], 2) * slope_ref[rows, n : n + TILE].astype(F32)
                    q = q.astype(BF)
                    gp[rows, n : n + TILE] = q
                    sums = [sums[0] + d * xh, sums[1] + d, sums[2] + q.astype(F32)]
                for i in range(3):
                    acc[i, :, n : n + TILE] += sums[i]

        row_loop(BODY, grad_rows)
        for i in range(3):
            gsum_ref[0:1, i * HALF : (i + 1) * HALF] = jnp.sum(acc[i], axis=0, keepdims=True)

    return call(
        kernel,
        (sds((ROWS, HALF), BF), sds((1, 3 * HALF), F32)),
        [VM] * 6 + [HB] * count,
        [
            pltpu.VMEM((ROWS, HALF), F32),
            pltpu.VMEM((ROWS, 128), F32),
            pltpu.VMEM((ROWS, 128), F32),
            pltpu.VMEM((3, CHUNK, HALF), F32),
        ],
        3000000000,
        10000000,
        vec,
        gs,
        mm,
        hat,
        slope,
        scale,
        *after,
        room=20,
    )


def in_grads(gp, h, w, gh, after):
    count = len(after)

    def kernel(gp_ref, h_ref, w_ref, gh_ref, *refs):
        gwr, ghb = refs[count:]

        def in_tile(n, carry):
            cols = pl.ds(pl.multiple_of(n * TILE, TILE), TILE)
            ghb[:, cols] = gh_ref[:, cols] + dot(gp_ref[...], w_ref[cols, :], NT)
            gwr[cols, :] = dot(h_ref[:, cols], gp_ref[...], TN).astype(BF)
            return carry

        lax.fori_loop(0, D // TILE, in_tile, 0)

    return call(
        kernel,
        (sds((D, HALF), BF), sds((ROWS, D), F32)),
        [VM] * 4 + [HB] * count,
        [],
        3000000000,
        8000000,
        gp,
        h,
        w,
        gh,
        *after,
        room=14,
    )


def in_backward(table, sides, vec, gsum, gate_sum, gwr, ghb, x, grad_out, half, after):
    count = len(after)

    def kernel(table_ref, sides_ref, vec_ref, gsum_ref, gate_ref, gwr, ghb, x_ref, og_ref, *refs):
        keep, send, up_a, up_b, stay_ref, away_ref, acc, gvec, blocks, pgb = refs[count:]

        def put(name, value):
            start, size = VSEG[name]
            gvec[0:1, start : start + size] = value

        put("g2", gate_ref[0:1, 0:HALF])
        put("b2", gate_ref[0:1, HALF : 2 * HALF])
        put("c1r", gate_ref[0:1, 2 * HALF : 3 * HALF])
        put("c1l", gsum_ref[0:1, 0:HALF])
        put("c2", gsum_ref[0:1, HALF : HALF + D])
        acc[...] = jnp.zeros_like(acc)
        def in_rows(r):
            rows = pl.ds(r, STRIPE)
            xh, scale = norm_parts(x_ref[rows, :].astype(F32))
            d = ghb[rows, :]
            e = d * seg(vec_ref, "g1")
            one = jnp.mean(e, axis=-1, keepdims=True)
            two = jnp.mean(e * xh, axis=-1, keepdims=True)
            pgb[rows, :] = og_ref[rows, :].astype(F32) + scale * (e - one - xh * two)
            acc[0:1, :] += jnp.sum(d * xh, axis=0, keepdims=True)
            acc[1:2, :] += jnp.sum(d, axis=0, keepdims=True)

        row_loop(STRIPE, in_rows)
        put("g1", acc[0:1, :])
        put("b1", acc[1:2, :])
        split_rows(pgb, stay_ref, away_ref, sides_ref[0], pgb[...])
        blocks[...] = jnp.zeros_like(blocks)
        for s in range(DEVS):
            blocks[s, 0:1, 0:VPER] = gvec[0:1, VPER * s : VPER * s + VPER]
        for k in range(DEVS):
            dev = table_ref[k]
            target, first = next((t, f) for t, f in ((up_b, 28), (up_a, 24), (send, GROUPS), (keep, 0)) if k >= f)
            r = pl.ds((k - first) * 16, 16)
            target[r, 0:HALF] = gwr[pl.ds(pl.multiple_of(dev * 16, 16), 16), :]
            target[r, HALF : HALF + VCOLS] = blocks[dev].astype(BF)

    payload = sds((D // 2, HALF + VCOLS), BF)
    part = sds((D // 4, HALF + VCOLS), BF)
    eighth = sds((D // 8, HALF + VCOLS), BF)
    pair = sds((2, half, D), BF)
    return call(
        kernel,
        (payload, part, eighth, eighth, pair, pair),
        [SM] * 2 + [VM] * 7 + [HB] * count,
        [
            pltpu.VMEM((8, D), F32),
            pltpu.VMEM((1, VEC), F32),
            pltpu.VMEM((DEVS, 16, VCOLS), F32),
            pltpu.VMEM((ROWS, D), F32),
        ],
        2000000000,
        6000000,
        table,
        sides,
        vec,
        gsum,
        gate_sum,
        gwr,
        ghb,
        x,
        grad_out,
        *after,
        room=16,
    )


def add_upper(keep, upper, after):
    cols = keep.shape[1]
    size = keep.shape[0] // 2

    def kernel(keep_ref, a_ref, b_ref, *refs):
        for r in range(0, size, 16):
            piece = a_ref if r < size // 2 else b_ref
            value = keep_ref[r : r + 16, :].astype(F32) + piece[r % (size // 2) : r % (size // 2) + 16, :].astype(F32)
            refs[len(after)][r : r + 16, :] = value.astype(BF)

    specs = [pl.BlockSpec((size, cols), lambda i: (1, 0))] + [pl.BlockSpec((size // 2, cols), lambda i: (0, 0))] * 2
    return pl.pallas_call(
        kernel,
        grid=(1,),
        out_shape=sds((size, cols), BF),
        in_specs=specs + [HB] * len(after),
        out_specs=pl.BlockSpec((size, cols), lambda i: (0, 0)),
        compiler_params=pltpu.CompilerParams(vmem_limit_bytes=10 * MIB),
        cost_estimate=pl.CostEstimate(flops=1000000, bytes_accessed=2000000, transcendentals=0),
    )(keep, *upper, *after)


def add_part(terms, size, after, places=None):
    cols = terms[0].shape[1]
    count = len(terms)

    def kernel(*refs):
        for r in range(0, size, 16):
            rows = slice(r, r + 16)
            value = refs[0][rows, :].astype(F32)
            for t in refs[1:count]:
                value = value + t[rows, :].astype(F32)
            refs[count + len(after)][rows, :] = value.astype(BF)

    places = places or [1] * count
    blocks = [pl.BlockSpec((size, cols), lambda i, p=p: (p, 0)) for p in places]
    return pl.pallas_call(
        kernel,
        grid=(1,),
        out_shape=sds((size, cols), BF),
        in_specs=blocks + [HB] * len(after),
        out_specs=pl.BlockSpec((size, cols), lambda i: (0, 0)),
        compiler_params=pltpu.CompilerParams(vmem_limit_bytes=10 * MIB),
        cost_estimate=pl.CostEstimate(flops=1000000, bytes_accessed=3000000, transcendentals=0),
    )(*terms, *after)


def line_parts(terms, after):
    cols = terms[0].shape[1]
    count = len(terms)

    def kernel(*refs):
        own, *outs = refs[count + len(after) :]
        for m in range(4):
            rows = slice(16 * m, 16 * (m + 1))
            value = refs[0][rows, :].astype(F32)
            for t in refs[1:count]:
                value = value + t[rows, :].astype(F32)
            if m == 0:
                own[...] = value
            else:
                outs[m - 1][...] = value.astype(BF)

    block = pl.BlockSpec((64, cols), lambda i: (0, 0))
    one = pl.BlockSpec((16, cols), lambda i: (0, 0))
    return pl.pallas_call(
        kernel,
        grid=(1,),
        out_shape=[sds((16, cols), F32)] + [sds((16, cols), BF)] * 3,
        in_specs=[block] * count + [HB] * len(after),
        out_specs=[one] * 4,
        compiler_params=pltpu.CompilerParams(vmem_limit_bytes=8 * MIB),
        cost_estimate=pl.CostEstimate(flops=1000000, bytes_accessed=3000000, transcendentals=0),
    )(*terms, *after)


def line_turn(terms, flip, after):
    count = len(terms)
    cols = terms[0].shape[1]

    def kernel(*refs):
        outs = refs[count + len(after) :]
        for m in range(4):
            rows = slice(16 * m, 16 * (m + 1))
            value = refs[0][rows, :].astype(F32)
            for t in refs[1:count]:
                value = value + t[rows, :].astype(F32)
            value = value.astype(BF)
            outs[0][rows, :] = value
            if flip:
                at = 16 * (m ^ flip)
                outs[1][at : at + 16, :] = value

    block = pl.BlockSpec((64, cols), lambda i: (0, 0))
    number = 2 if flip else 1
    return pl.pallas_call(
        kernel,
        grid=(1,),
        out_shape=[sds((64, cols), BF)] * number,
        in_specs=[block] * count + [HB] * len(after),
        out_specs=[block] * number,
        compiler_params=pltpu.CompilerParams(vmem_limit_bytes=8 * MIB),
        cost_estimate=pl.CostEstimate(flops=1000000, bytes_accessed=1000000, transcendentals=0),
    )(*terms, *after)


def finish_out(own, got, weight, first, second, after):
    def kernel(own_ref, a_ref, b_ref, c_ref, w_ref, m_ref, s_ref, after_ref, left_ref, nw, nm, ns):
        total = own_ref[...] + a_ref[...].astype(F32)
        total = total + (b_ref[...].astype(F32) + c_ref[...].astype(F32))
        left_ref[...] = total[:, 0:HALF]
        for g in range(3):
            rows = slice(16 * g, 16 * (g + 1))
            grad = total[:, HALF + g * D : HALF + (g + 1) * D]
            new = adamw(w_ref[rows, :], grad, m_ref[rows, :], s_ref[rows, :], DENSE_RATE, DENSE_DECAY)
            nw[rows, :] = new[0]
            nm[rows, :] = new[1]
            ns[rows, :] = new[2]

    same = sds(weight.shape, F32)
    return call(
        kernel,
        (sds((16, HALF), F32), same, same, same),
        [VM] * 7 + [HB],
        [],
        1000000,
        2000000,
        own,
        *got,
        weight,
        first,
        second,
        after,
    )


def finish_in(own, got, left, weight, first, second, after):
    def kernel(own_ref, a_ref, b_ref, c_ref, l_ref, w_ref, m_ref, s_ref, after_ref, nw, nm, ns, vec_ref):
        total = own_ref[...] + a_ref[...].astype(F32)
        total = total + (b_ref[...].astype(F32) + c_ref[...].astype(F32))
        vec_ref[...] = total[0:1, HALF:]
        for cols, grad in ((slice(0, HALF), l_ref[...]), (slice(HALF, FF), total[:, 0:HALF])):
            new = adamw(w_ref[:, cols], grad, m_ref[:, cols], s_ref[:, cols], DENSE_RATE, DENSE_DECAY)
            nw[:, cols] = new[0]
            nm[:, cols] = new[1]
            ns[:, cols] = new[2]

    same = sds(weight.shape, F32)
    return call(
        kernel,
        (same, same, same, sds((1, VCOLS), F32)),
        [VM] * 8 + [HB],
        [],
        1000000,
        2000000,
        own,
        *got,
        left,
        weight,
        first,
        second,
        after,
    )


def spatial_update(order, pieces, spatial, first, second, bias, bias_first, bias_second, after):
    count = len(pieces)
    rows = spatial.shape[1]

    def kernel(order_ref, *refs):
        ins = refs[:count]
        w_ref, m_ref, s_ref, bw, bm, bs = refs[count : count + 6]
        nw, nm, ns, nbw, nbm, nbs, flat = refs[count + 6 + len(after) :]
        k = 0
        for piece in ins:
            for j in range(piece.shape[0] // 16):
                at = pl.multiple_of(order_ref[k] * 32, 32)
                block = piece[16 * j : 16 * j + 16, :].astype(F32)
                flat[pl.ds(at, 16), :] = block[:, 0:SCOLS]
                flat[pl.ds(at + 16, 16), :] = block[:, SCOLS:]
                k += 1
        at = TOTAL_AT // 128 * 128
        totals = flat[:, at : at + 128].T[TOTAL_AT - at : TOTAL_AT - at + 1, :]
        for level in range(3):
            got = flat[level * LSTRIDE : level * LSTRIDE + rows, :]
            new = adamw(w_ref[level], got[:, 0:PMAX], m_ref[level], s_ref[level], DENSE_RATE, DENSE_DECAY)
            nw[level] = new[0]
            nm[level] = new[1]
            ns[level] = new[2]
            got = totals[:, level * LSTRIDE : level * LSTRIDE + rows]
            r = slice(level, level + 1)
            new = adamw(bw[r, :], got, bm[r, :], bs[r, :], SMALL_RATE, 0.0)
            nbw[r, :] = new[0]
            nbm[r, :] = new[1]
            nbs[r, :] = new[2]

    same = sds(spatial.shape, F32)
    small = sds(bias.shape, F32)
    return call(
        kernel,
        (same, same, same, small, small, small),
        [SM] + [VM] * (count + 6) + [HB] * len(after),
        [pltpu.VMEM((512, SCOLS), F32)],
        10000000,
        6000000,
        order,
        *pieces,
        spatial,
        first,
        second,
        bias,
        bias_first,
        bias_second,
        *after,
    )


def in_order(blocks, table, rows):
    cols = blocks[0].shape[1]
    whole = jnp.concatenate(blocks, axis=0).reshape(-1, rows, cols)
    back = jnp.zeros_like(table).at[table].set(jnp.arange(table.shape[0], dtype=table.dtype))
    return jnp.take(whole, back, axis=0)


def local(
    patches,
    resolution,
    out_grad,
    dense_in,
    dense_out,
    vectors,
    spatial,
    spatial_bias,
    in_first,
    in_second,
    out_first,
    out_second,
    vec_first,
    vec_second,
    spat_first,
    spat_second,
    bias_first,
    bias_second,
):
    route = Route(lax.axis_size("dp"))
    ndev = 2 * route.n
    fits = route.n == GROUPS
    seq = lax.axis_index("seq").astype(jnp.int32)
    rows = patches.shape[1]
    table = route.table()
    order = route.order(False)[0]
    in_rows = dense_in.shape[0]
    out_rows = dense_out.shape[0]
    vec_len = vectors.shape[0]
    if fits:
        ktable = table
        korder = table // 2
    else:
        ktable = jnp.arange(DEVS, dtype=jnp.int32)
        korder = jnp.arange(DEVS, dtype=jnp.int32) % GROUPS
    sides = jnp.concatenate([seq[None], korder])
    levels = lax.dynamic_slice_in_dim(resolution, seq * 2, 2, 0)

    right_shard, lo_shard = pack_dense(dense_in, dense_out, vectors.reshape(1, vec_len))
    line = [right_shard] + [route.swap(right_shard, (m, m)) for m in route.direct]
    lo_line = [lo_shard] + [route.swap(lo_shard, (m, m)) for m in route.direct]
    spat_own, x_send, g_send = pack_images(sides, spatial, spatial_bias.reshape(3, rows, 1), patches, out_grad)
    x_got = route.cross(x_send)
    g_got = route.cross(g_send)
    spat_got = route.cross(spat_own)
    if fits:
        right_blocks, passed = route.widen_in_turn(stack(line, []))
        lo_blocks = route.widen_direct(stack(lo_line, [passed]))
    else:
        right_blocks = route.widen(jnp.concatenate(line, axis=0))
        lo_blocks = route.widen(jnp.concatenate(lo_line, axis=0))
    right_blocks = right_blocks + [route.cross(b) for b in right_blocks]
    if not fits:
        lo_blocks = lo_blocks + [route.cross(b) for b in lo_blocks]
    if not fits:
        whole = in_order(right_blocks, table, in_rows)
        all_vec = whole[:, 0, HALF : HALF + vec_len].reshape(DEVS, 1, VPER)
        all_vec = jnp.pad(all_vec, ((0, 0), (0, 15), (0, VCOLS - VPER))).reshape(D, VCOLS)
        right_blocks = [jnp.concatenate([whole[:, :, :HALF].reshape(D, HALF), all_vec], axis=1)]
        whole = in_order(lo_blocks, table, in_rows)
        outs = whole[:, :, HALF:].reshape(ndev, in_rows, 3, D).transpose(0, 2, 1, 3).reshape(DEVS, 3, 16, D)
        outs = outs.transpose(0, 2, 1, 3).reshape(D, HALF)
        lo_blocks = [jnp.concatenate([whole[:, :, :HALF].reshape(D, HALF), outs], axis=1)]

    x, grad_out, h, v, slope, part, weight_right, vec = gate_forward(
        ktable, sides, patches, x_got, out_grad, g_got, right_blocks
    )
    gate, hat, scale, spat, mm = gate_norm(levels, sides, vec, v, part, spat_own, spat_got, [])
    if fits:
        lo_blocks = lo_blocks + [route.cross(lo_blocks[0]), route.cross(stack(lo_blocks[1:], [mm]))]
    gs, gated, q, gb, wl, wo, sp_keep, sp_send, gsum = middle(ktable, levels, sides, vec, h, spat, gate, grad_out, lo_blocks)
    near, far = route.low[-1], route.low[0]
    after = [[] for _ in range(5)]
    if fits:
        sp_got = route.cross(sp_send)
        sp_part = add_part([sp_keep, sp_got], 128, [])
        sp_terms = [sp_keep, sp_got, route.swap(sp_part, near)]
        after[0] = [sp_part]
    gwl, mixed_stay, mixed_away, gh = weight_grads(levels, sides, vec, gated, q, h, wl, wo, x, rows, after[0])
    if fits:
        sp_part = add_part(sp_terms, 64, [gh])
        sp_terms.append(route.swap(sp_part, far))
        after[1] = [sp_part]
    lo_keep, lo_send, lo_up = out_grads(ktable, gated, gb, gwl, after[1])
    mixed_got = route.cross(mixed_away)
    if fits:
        lo_up = route.cross(lo_up)
        lo_terms = [lo_keep, route.cross(lo_send)]
        lo_part = add_part([lo_keep, lo_up], 128, [], [1, 0])
        lo_terms.append(route.swap(lo_part, near))
        after[2] = [lo_part]
    gp, gate_sum = gate_backward(vec, gs, mm, hat, slope, scale, after[2])
    if fits:
        sp_own, sp_out = line_turn(sp_terms, 1, [gate_sum])
        sp_terms = [sp_own, route.swap(sp_out, (route.direct[0],) * 2)]
        after[3] = [sp_own, mixed_got]
    gwr, ghb = in_grads(gp, h, weight_right, gh, after[3])
    if fits:
        sp_own, sp_out = line_turn(sp_terms, 2, [gwr])
        sp_terms = [sp_own, route.swap(sp_out, (route.direct[1],) * 2)]
        lo_part = add_part(lo_terms, 64, [sp_own])
        lo_terms.append(route.swap(lo_part, far))
        after[4] = [lo_part]
    right_keep, right_send, up_a, up_b, grad_stay, grad_away = in_backward(
        ktable, sides, vec, gsum, gate_sum, gwr, ghb, x, grad_out, rows, after[4]
    )
    grad_got = route.cross(grad_away)
    if fits:
        upper = [route.cross(up_a), route.cross(up_b)]
        right_terms = [right_keep, route.cross(right_send)]
        lo_own, *sends = line_parts(lo_terms, [right_keep])
        lo_got = [route.swap(p, (m, m)) for p, m in zip(sends, route.direct)]
        right_part = add_upper(right_keep, upper, [lo_own])
        right_terms.append(route.swap(right_part, near))
        right_part = add_part(right_terms, 64, [grad_got])
        right_terms.append(route.swap(right_part, far))
        (sp_sum,) = line_turn(sp_terms, 0, [right_part])
        spat_pieces = route.widen(sp_sum)
        left_sum, *new_out = finish_out(lo_own, lo_got, dense_out, out_first, out_second, sp_sum)
        right_own, *sends = line_parts(right_terms, [left_sum])
        right_got = [route.swap(p, (m, m)) for p, m in zip(sends, route.direct)]
        korder = order
        after = [left_sum]
    else:
        both = jnp.concatenate([lo_keep, lo_send, lo_up])
        outs = both[:, HALF:LO].reshape(DEVS, 16, 3, D).transpose(0, 2, 1, 3).reshape(ndev, out_rows, D)
        outs = jnp.take(outs, table, axis=0).reshape(HALF, D)
        out_sum = route.scatter(outs[: HALF // 2], outs[HALF // 2 :])
        lefts = jnp.take(both[:, :HALF].reshape(ndev, in_rows, HALF), table, axis=0).reshape(D, HALF)
        left_sum = route.scatter(lefts[: D // 2], lefts[D // 2 :])
        per = 512 // route.n

        def spat_blocks(part, flip):
            flat = part.reshape(GROUPS, 16, 2, SCOLS).transpose(0, 2, 1, 3).reshape(route.n, per, SCOLS)
            return jnp.take(flat, route.order(flip)[0], axis=0).reshape(512, SCOLS)

        spat_part = route.scatter(spat_blocks(sp_keep, False), spat_blocks(sp_send, True)).astype(BF)
        flat = in_order(route.spread(spat_part), order, per).reshape(GROUPS, 2, 16, SCOLS)
        spat_pieces = [flat.transpose(0, 2, 1, 3).reshape(GROUPS * 16, SPC)]
        korder = jnp.arange(GROUPS, dtype=jnp.int32)
        after = []
        both = jnp.concatenate([right_keep, right_send, up_a, up_b])
        vecs = jnp.take(both[::16, HALF : HALF + VPER].reshape(ndev, vec_len), table, axis=0)
        vec_sum = route.scatter(vecs[: route.n], vecs[route.n :]).reshape(vec_len)
        rights = jnp.take(both[:, :HALF].reshape(ndev, in_rows, HALF), table, axis=0).reshape(D, HALF)
        right_sum = route.scatter(rights[: D // 2], rights[D // 2 :])
        in_sum = jnp.concatenate([left_sum, right_sum], axis=1)
        new_in = adamw(dense_in, in_sum, in_first, in_second, DENSE_RATE, DENSE_DECAY)
        new_out = adamw(dense_out, out_sum, out_first, out_second, DENSE_RATE, DENSE_DECAY)

    def whole_images(stays, came):
        return jnp.concatenate([jnp.where(seq == 0, stays, came), jnp.where(seq == 0, came, stays)], axis=0)

    mixed = whole_images(mixed_stay, mixed_got)
    patches_grad = whole_images(grad_stay, grad_got)
    spat_new = spatial_update(
        korder, spat_pieces, spatial, spat_first, spat_second, spatial_bias, bias_first, bias_second, after
    )
    if fits:
        *new_in, vec_sum = finish_in(right_own, right_got, left_sum, dense_in, in_first, in_second, left_sum)
        vec_sum = vec_sum[0, :vec_len]
    new_vec = adamw(vectors, vec_sum, vec_first, vec_second, SMALL_RATE, 0.0)
    return (mixed, patches_grad) + tuple(new_in) + tuple(new_out) + new_vec + tuple(spat_new)


def solution(mesh):
    rows3 = P("dp", "seq", None)
    dense = P(AXES, None)
    vec = P(AXES)
    spat = P(None, "seq", None)
    bias = P(None, "seq")
    in_specs = (rows3, P("dp"), rows3, dense, dense, vec, spat, bias)
    in_specs += (dense,) * 4 + (vec,) * 2 + (spat,) * 2 + (bias,) * 2
    out_specs = (rows3, rows3) + (dense,) * 6 + (vec,) * 3 + (spat,) * 3 + (bias,) * 3
    return jax.shard_map(local, mesh=mesh, in_specs=in_specs, out_specs=out_specs, check_vma=False)
```
